32 devices in a mesh: dp: 8 (over z, x), seq: 4 (over y, core).
Axes of the slice: x: 2, y: 2, z: 4, core: 2. Of those that a mesh axis runs over, the one named last changes fastest.
Arguments:
- media: bfloat16 [192, 128, 1536], P(('dp', 'seq')), may hold values from -6 to 6
- latents: bfloat16 [32, 64, 1536], P(('dp', 'seq')), may hold values from -6 to 6
- out_grad: bfloat16 [32, 64, 1536], P(('dp', 'seq')), may hold values from -6 to 6
- frame_counts: int32 [8, 4], P('dp'), may hold values from 1 to 8, 12 in all within a row
- block_position: int32 [8, 24], P('dp'), may hold values from 0 to 23, as said below
- w_query: bfloat16 [1536, 1536], P(('dp', 'seq')), may hold values from -0.3125 to 0.3125
- w_key: bfloat16 [1536, 1536], P(('dp', 'seq')), may hold values from -0.15625 to 0.15625
- w_value: bfloat16 [1536, 1536], P(('dp', 'seq')), may hold values from -0.15625 to 0.15625
- w_out: bfloat16 [1536, 1536], P(('dp', 'seq')), may hold values from -0.625 to 0.625
- w_up: bfloat16 [1536, 6144], P(('dp', 'seq')), may hold values from -0.15625 to 0.15625
- w_down: bfloat16 [6144, 1536], P(('dp', 'seq')), may hold values from -0.078125 to 0.078125
- gain_lat: bfloat16 [1536], P(('dp', 'seq')), may hold values from 0.5 to 1.5
- shift_lat: bfloat16 [1536], P(('dp', 'seq')), may hold values from -3 to 3
- gain_media: bfloat16 [1536], P(('dp', 'seq')), may hold values from 0.5 to 1.5
- shift_media: bfloat16 [1536], P(('dp', 'seq')), may hold values from -3 to 3
- gain_ffn: bfloat16 [1536], P(('dp', 'seq')), may hold values from 0.5 to 1.5
- shift_ffn: bfloat16 [1536], P(('dp', 'seq')), may hold values from -3 to 3
Outputs:
- latents_out: bfloat16 [32, 64, 1536], P(('dp', 'seq'))
- latents_grad: float32 [32, 64, 1536], P(('dp', 'seq'))
- media_grad: float32 [192, 128, 1536], P(('dp', 'seq'))
- grad_w_query: float32 [1536, 1536], P(('dp', 'seq'))
- grad_w_key: float32 [1536, 1536], P(('dp', 'seq'))
- grad_w_value: float32 [1536, 1536], P(('dp', 'seq'))
- grad_w_out: float32 [1536, 1536], P(('dp', 'seq'))
- grad_w_up: float32 [1536, 6144], P(('dp', 'seq'))
- grad_w_down: float32 [6144, 1536], P(('dp', 'seq'))
- grad_gain_lat: float32 [1536], P(('dp', 'seq'))
- grad_shift_lat: float32 [1536], P(('dp', 'seq'))
- grad_gain_media: float32 [1536], P(('dp', 'seq'))
- grad_shift_media: float32 [1536], P(('dp', 'seq'))
- grad_gain_ffn: float32 [1536], P(('dp', 'seq'))
- grad_shift_ffn: float32 [1536], P(('dp', 'seq'))
The draws below stay inside these ranges and needn't reach their ends.
Inputs may be any that keep to these rules, and one draw needn't show every extreme that they name: `frame_counts`: row g gives the frames of the 4 items of group g in order; an item holds 2 blocks a frame; each row sums to 12 and its largest entry is 8. `block_position`: each row is a permutation of 0 to 23; the 6 blocks stored at seq index r all have positions with one common remainder modulo 4.
All inputs are finite; a program needn't handle non-finite values.
Results may differ from the reference program's by a relative error of at most 0.02.
Values may be sent and summed in bfloat16 or wider, within the bound.
A program may use at most 200 MiB of HBM per device.

```python
import math
import jax
import jax.numpy as jnp
import numpy as np
from jax import lax

D = 1536
HEADS = 16
HEAD_DIM = 96
FF = 6144
LATENTS = 64
BLOCK_ROWS = 128
FRAME_BLOCKS = 2
MOST_FRAMES = 8
BLK_DEV = 6
GROUPS = 8
SEQ_DEVS = 4
ITEM_DEV = 4
GROUP_BLOCKS = 24
ITEMS = 32
BLOCKS = 192


def draw_block_position(key, part):
    key = jax.random.fold_in(key, 11)
    shift_key, order_key = jax.random.split(key)
    offsets = jax.random.randint(shift_key, (GROUPS, 1, 1), 0, SEQ_DEVS)
    order_keys = jax.random.split(order_key, GROUPS * SEQ_DEVS)

    def shuffled(single_key):
        return jax.random.permutation(single_key, BLK_DEV)
    orders = jax.vmap(shuffled)(order_keys).reshape(GROUPS, SEQ_DEVS, BLK_DEV)
    ranks = jnp.arange(SEQ_DEVS, dtype=jnp.int32)[None, :, None]
    places = (ranks + offsets) % SEQ_DEVS + SEQ_DEVS * orders
    return places.reshape(GROUPS, GROUP_BLOCKS).astype(jnp.int32)


def steps_of(key, shape, cuts, least, largest):
    level, own = 1.0, jax.random.fold_in(key, 6)
    for position, shards_of in cuts:
        draws = jnp.exp(jax.random.uniform(jax.random.fold_in(own, position), (shards_of,), jnp.float32, least / len(cuts), largest / len(cuts)))
        level = level * jnp.repeat(draws, shape[position] // shards_of).reshape([-1 if axis == position else 1 for axis in range(len(shape))])
    return level


def split_up(count, total, most, slope):
    loads = [(1 << 20) // math.isqrt(rank ** slope) + 1 for rank in range(2, count + 1)]
    rest, counts = total - most - (count - 1), [1] * (count - 1)
    while rest > 0:
        movable = [i for i in range(count - 1) if counts[i] < most]
        whole, remaining = sum([loads[i] for i in movable]), rest
        for i in movable:
            addition = min(most - counts[i], max(1, remaining * loads[i] // whole), rest)
            counts[i] = counts[i] + addition
            rest = rest - addition
    return np.array([most] + counts)


def ragged(key, number_of, total, limit, lean):
    if number_of == 2:
        one = jax.random.randint(key, (), max(1, total - limit), min(limit, total - 1) + 1)
        return jnp.stack([one, total - one])
    sizes = jnp.asarray(split_up(number_of, total, limit, lean), jnp.int32)
    twos = (number_of - 1) // 2
    source_of, taker = sizes[1:1 + 2 * twos:2], sizes[2:2 + 2 * twos:2]
    margin = jnp.minimum(source_of - 1, limit - taker)
    moved = jax.random.randint(jax.random.fold_in(key, 1), (twos,), 0, 1 << 20) % (margin + 1)
    sizes = sizes.at[1:1 + 2 * twos:2].set(source_of - moved).at[2:2 + 2 * twos:2].set(taker + moved)
    return sizes[jax.random.permutation(jax.random.fold_in(key, 2), number_of)]


def gaussian(own_key, extent, spread, most, cuts=(), kind=jnp.bfloat16):
    level = steps_of(own_key, extent, cuts, -0.22, 0.18) if cuts else 1.0
    values = jax.random.normal(own_key, extent, jnp.float32) * spread * level
    return jnp.minimum(jnp.maximum(values, -most), most).astype(kind)


def setup_inputs(seed: int = 0) -> dict:
    key_list = jax.random.split(jax.random.key(seed), 18)
    media = gaussian(key_list[0], (BLOCKS, BLOCK_ROWS, D), 1.0, 6.0, ((0, 32),))
    latents = gaussian(key_list[1], (ITEMS, LATENTS, D), 1.0, 6.0, ((0, 32),))
    out_grad = gaussian(key_list[2], (ITEMS, LATENTS, D), 1.0, 6.0, ((0, 32),))
    frame_counts = jax.vmap(lambda own: ragged(own, ITEM_DEV, GROUP_BLOCKS // FRAME_BLOCKS, MOST_FRAMES, 1))(jax.random.split(key_list[3], GROUPS)).reshape((GROUPS, ITEM_DEV)).astype(jnp.int32)
    block_position = draw_block_position(jax.random.fold_in(key_list[17], 71), 0)
    w_query = gaussian(key_list[5], (D, D), (D // 4) ** -0.5, 0.3125, ((0, 32),))
    w_key = gaussian(key_list[6], (D, D), D ** -0.5, 0.15625, ((0, 32),))
    w_value = gaussian(key_list[7], (D, D), D ** -0.5, 0.15625, ((0, 32),))
    w_out = gaussian(key_list[8], (D, D), (D // 16) ** -0.5, 0.625, ((0, 32),))
    w_up = gaussian(key_list[9], (D, FF), D ** -0.5, 0.15625, ((0, 32),))
    w_down = gaussian(key_list[10], (FF, D), FF ** -0.5, 0.078125, ((0, 32),))
    gain_lat = jnp.clip(1.0 + 0.1 * jax.random.normal(key_list[11], (D,), jnp.float32), 0.5, 1.5).astype(jnp.bfloat16)
    shift_lat = gaussian(key_list[12], (D,), 0.5, 3.0, ((0, 32),))
    gain_media = jnp.clip(1.0 + 0.1 * jax.random.normal(key_list[13], (D,), jnp.float32), 0.5, 1.5).astype(jnp.bfloat16)
    shift_media = gaussian(key_list[14], (D,), 0.5, 3.0, ((0, 32),))
    gain_ffn = jnp.clip(1.0 + 0.1 * jax.random.normal(key_list[15], (D,), jnp.float32), 0.5, 1.5).astype(jnp.bfloat16)
    shift_ffn = gaussian(key_list[16], (D,), 0.5, 3.0, ((0, 32),))
    return {"media": media, "latents": latents, "out_grad": out_grad, "frame_counts": frame_counts, "block_position": block_position, "w_query": w_query, "w_key": w_key, "w_value": w_value, "w_out": w_out, "w_up": w_up, "w_down": w_down, "gain_lat": gain_lat, "shift_lat": shift_lat, "gain_media": gain_media, "shift_media": shift_media, "gain_ffn": gain_ffn, "shift_ffn": shift_ffn}


EPS = 1e-05
NEG = -1e+30
HIGH = lax.Precision.HIGHEST

@jax.custom_vjp
def low(v):
    return lax.optimization_barrier(v.astype(jnp.bfloat16)).astype(jnp.float32)

@jax.custom_vjp
def low_back(v):
    return v

def low_keep(v):
    return (low(v), None)

def low_pass(kept, grad):
    return (grad,)

def back_keep(v):
    return (v, None)

def back_low(kept, grad):
    return (low(grad),)
low.defvjp(low_keep, low_pass)
low_back.defvjp(back_keep, back_low)

def rounded_both(value):
    return low(low_back(value))

def layer_norm(rows, gain, shift):
    mean = lax.optimization_barrier(jnp.mean(rows, axis=-1, keepdims=True))
    centred = rows - mean
    variance = lax.optimization_barrier(jnp.mean(centred * centred, axis=-1, keepdims=True))
    return centred * lax.rsqrt(variance + EPS) * gain + shift

def swap_rows(stat):
    return jnp.swapaxes(stat, 1, 2)[..., None]

def group_forward(params, media_group, lat_group, item_of):
    w_query, w_key, w_value, w_out, w_up, w_down, gain_lat, shift_lat, gain_media, shift_media, gain_ffn, shift_ffn = params
    score_scale = HEAD_DIM ** (-0.5)
    lat_rows = lat_group.reshape(-1, D)
    norm_lat = low(layer_norm(lat_rows, gain_lat, shift_lat))
    query = rounded_both(jnp.dot(norm_lat, w_query, precision=HIGH)).reshape(ITEM_DEV, LATENTS, HEADS, HEAD_DIM)
    key_lat = rounded_both(jnp.dot(norm_lat, w_key, precision=HIGH)).reshape(ITEM_DEV, LATENTS, HEADS, HEAD_DIM)
    value_lat = rounded_both(jnp.dot(norm_lat, w_value, precision=HIGH)).reshape(ITEM_DEV, LATENTS, HEADS, HEAD_DIM)
    norm_media = low(layer_norm(media_group.reshape(-1, D), gain_media, shift_media))
    key_media = rounded_both(jnp.dot(norm_media, w_key, precision=HIGH)).reshape(GROUP_BLOCKS, BLOCK_ROWS, HEADS, HEAD_DIM)
    value_media = rounded_both(jnp.dot(norm_media, w_value, precision=HIGH)).reshape(GROUP_BLOCKS, BLOCK_ROWS, HEADS, HEAD_DIM)
    member = (item_of[:, None] == jnp.arange(ITEM_DEV, dtype=jnp.int32)[None, :]).astype(jnp.float32)
    query_blk = jnp.einsum('bi,iqhd->bqhd', member, query, precision=HIGH)
    scores_med = low_back(jnp.einsum('bqhd,bkhd->bhqk', query_blk, key_media, precision=HIGH) * score_scale)
    scores_lat = low_back(jnp.einsum('iqhd,ikhd->ihqk', query, key_lat, precision=HIGH) * score_scale)
    top_med = lax.optimization_barrier(jnp.max(scores_med, axis=-1))
    top_lat = lax.optimization_barrier(jnp.max(scores_lat, axis=-1))
    chosen = member.T[:, :, None, None] > 0
    top_item = jnp.maximum(lax.optimization_barrier(jnp.max(jnp.where(chosen, top_med[None], NEG), axis=1)), top_lat)
    expo_med = jnp.exp(scores_med - top_med[..., None])
    expo_lat = jnp.exp(scores_lat - top_lat[..., None])
    weight_med = jnp.exp(top_med - jnp.einsum('bi,ihq->bhq', member, top_item, precision=HIGH))
    weight_lat = jnp.exp(top_lat - top_item)
    total = jnp.einsum('bi,bhq->ihq', member, weight_med * lax.optimization_barrier(jnp.sum(expo_med, axis=-1)), precision=HIGH)
    total = total + weight_lat * lax.optimization_barrier(jnp.sum(expo_lat, axis=-1))
    accum_blk = jnp.einsum('bhqk,bkhd->bqhd', low(expo_med), value_media, precision=HIGH) * swap_rows(weight_med)
    accum = jnp.einsum('bi,bqhd->iqhd', member, accum_blk, precision=HIGH)
    accum = accum + jnp.einsum('ihqk,ikhd->iqhd', low(expo_lat), value_lat, precision=HIGH) * swap_rows(weight_lat)
    attended = rounded_both((accum / swap_rows(total)).reshape(-1, D))
    hidden = lat_rows + low_back(jnp.dot(attended, w_out, precision=HIGH))
    norm_ffn = low(layer_norm(hidden, gain_ffn, shift_ffn))
    pre = low_back(jnp.dot(norm_ffn, w_up, precision=HIGH))
    act = low(jax.nn.gelu(pre, approximate=False))
    result = hidden + low_back(jnp.dot(act, w_down, precision=HIGH))
    return result.reshape(ITEM_DEV, LATENTS, D)

def reference(media, latents, out_grad, frame_counts, block_position, w_query, w_key, w_value, w_out, w_up, w_down, gain_lat, shift_lat, gain_media, shift_media, gain_ffn, shift_ffn):
    params = tuple((weight.astype(jnp.float32) for weight in (w_query, w_key, w_value, w_out, w_up, w_down, gain_lat, shift_lat, gain_media, shift_media, gain_ffn, shift_ffn)))
    media_groups = media.astype(jnp.float32).reshape(GROUPS, GROUP_BLOCKS, BLOCK_ROWS, D)
    lat_groups = latents.astype(jnp.float32).reshape(GROUPS, ITEM_DEV, LATENTS, D)
    ends = FRAME_BLOCKS * jnp.cumsum(frame_counts, axis=1)
    items = lax.optimization_barrier(jnp.sum((ends[:, None, :] <= block_position[:, :, None]).astype(jnp.int32), axis=2))

    def run(weights, media_all, lat_all):

        def single(pieces):
            return group_forward(weights, pieces[0], pieces[1], pieces[2])
        return lax.map(jax.checkpoint(single), (media_all, lat_all, items))
    result, pullback = jax.vjp(run, params, media_groups, lat_groups)
    cotangent = out_grad.astype(jnp.float32).reshape(GROUPS, ITEM_DEV, LATENTS, D)
    grad_params, grad_media, grad_lat = pullback(cotangent)
    return (result.reshape(ITEMS, LATENTS, D).astype(jnp.bfloat16), grad_lat.reshape(ITEMS, LATENTS, D), grad_media.reshape(BLOCKS, BLOCK_ROWS, D), grad_params[0], grad_params[1], grad_params[2], grad_params[3], grad_params[4], grad_params[5], grad_params[6], grad_params[7], grad_params[8], grad_params[9], grad_params[10], grad_params[11])
```

```python
from functools import partial
from jax.sharding import PartitionSpec as P
import functools
import jax
import jax.numpy as jnp
from jax import lax
from jax.experimental import pallas as pl
from jax.experimental.pallas import tpu as pltpu

MESH = pl.DeviceIdType.MESH
ANY = pl.BlockSpec(memory_space=pl.ANY)
VMEM = pl.BlockSpec(memory_space=pltpu.VMEM)
DMA = pltpu.SemaphoreType.DMA


class Here:
    def __init__(self, dp_count):
        dp, seq = lax.axis_index("dp"), lax.axis_index("seq")
        self.nz = dp_count // 2
        self.z, self.x, self.y, self.c = dp // 2, dp % 2, seq // 2, seq % 2
        self.dp, self.seq = dp, seq

    def at(self, z=None, x=None, y=None, c=None):
        z = self.z if z is None else z
        x = self.x if x is None else x
        y = self.y if y is None else y
        c = self.c if c is None else c
        return (z * 2 + x, y * 2 + c)


def send(src, dst, ss, rs, to):
    copy = pltpu.make_async_remote_copy(
        src_ref=src, dst_ref=dst, send_sem=ss, recv_sem=rs, device_id=to, device_id_type=MESH
    )
    copy.start()


def landed(dst, ss, rs, me):
    pltpu.make_async_remote_copy(
        src_ref=dst, dst_ref=dst, send_sem=ss, recv_sem=rs, device_id=me.at(c=1 - me.c), device_id_type=MESH
    ).wait_recv()


def sent(src, ss, rs, me):
    pltpu.make_async_remote_copy(
        src_ref=src, dst_ref=src, send_sem=ss, recv_sem=rs, device_id=me.at(c=1 - me.c), device_id_type=MESH
    ).wait_send()


def greet(devices):
    barrier = pltpu.get_barrier_semaphore()
    for device in devices:
        pl.semaphore_signal(barrier, inc=1, device_id=device, device_id_type=MESH)
    pl.semaphore_wait(barrier, len(devices))


COL, FROMX, FROMY, DIAGA, DIAGB = range(5)
TOUP, TODOWN, TOX, TOY, FWDY, FWDX, TOC = range(7)
RECV_KINDS, SEND_KINDS = 10, 12


class Gather:
    def __init__(self, me, src, dst, ss, rs, axes, halves):
        self.me, self.src, self.dst, self.ss, self.rs = me, src, dst, ss, rs
        self.axes, self.halves = axes, halves
        self.sends = []
        self.depth = me.nz if "z" in axes else 1

    def slot(self, z, x, y, c):
        if self.axes == "zxyc":
            return ((z * 2 + x) * 2 + y) * 2 + c
        if self.axes == "zx":
            return z * 2 + x
        return y * 2 + c

    def shard(self, z, x, y, c, half=None):
        ref = self.dst.at[self.slot(z, x, y, c)]
        if half is None or not self.halves:
            return ref
        width = self.halves
        return ref.at[:, pl.ds(0, width)] if half == 0 else ref.at[:, pl.ds(width, width)]

    def key(self, z):
        return z if "z" in self.axes else 0

    def start(self, src, dst, out_kind, in_kind, z, to):
        k = self.key(z)
        send(src, dst, self.ss.at[out_kind, k], self.rs.at[in_kind, k], to)

    def hand_over(self, ref, kind, z):
        if "c" in self.axes:
            self.start(ref, ref, TOC + kind, 5 + kind, z, self.me.at(c=1 - self.me.c))

    def spread(self, ref, z):
        me = self.me
        if "x" in self.axes:
            self.start(ref, ref, TOX, FROMX, z, me.at(x=1 - me.x))
        if "y" in self.axes:
            self.start(ref, ref, TOY, FROMY, z, me.at(y=1 - me.y))
        self.hand_over(ref, COL, z)

    def own(self):
        me = self.me
        ref = self.shard(me.z, me.x, me.y, me.c)
        if "z" in self.axes:
            @pl.when(me.z + 1 < me.nz)
            def _():
                self.start(self.src, ref, TOUP, COL, me.z, me.at(z=me.z + 1))

            @pl.when(me.z > 0)
            def _():
                self.start(self.src, ref, TODOWN, COL, me.z, me.at(z=me.z - 1))
        if "x" in self.axes:
            self.start(self.src, ref, TOX, FROMX, me.z, me.at(x=1 - me.x))
        if "y" in self.axes:
            self.start(self.src, ref, TOY, FROMY, me.z, me.at(y=1 - me.y))
        if "c" in self.axes:
            self.start(self.src, ref, TOC, 5, me.z, me.at(c=1 - me.c))

    def around(self, event):
        me = self.me
        event(me.z)
        for d in range(1, self.depth):
            pl.when(me.z >= d)(functools.partial(event, me.z - d))
            pl.when(me.z + d < me.nz)(functools.partial(event, me.z + d))

    def column(self):
        me = self.me
        for d in range(1, self.depth):
            for below in (True, False):
                there = me.z - d if below else me.z + d
                ahead = me.z + 1 if below else me.z - 1

                @pl.when(there >= 0 if below else there < me.nz)
                def _():
                    ref = self.shard(there, me.x, me.y, me.c)
                    landed(ref, self.ss.at[0, 0], self.rs.at[COL, there], me)

                    @pl.when(ahead < me.nz if below else ahead >= 0)
                    def _():
                        self.start(ref, ref, TOUP if below else TODOWN, COL, there, me.at(z=ahead))
                    self.spread(ref, there)

    def neighbours(self):
        me = self.me

        def event(z):
            if "x" in self.axes:
                ref = self.shard(z, 1 - me.x, me.y, me.c)
                landed(ref, self.ss.at[0, 0], self.rs.at[FROMX, self.key(z)], me)
                if "y" in self.axes:
                    half = self.shard(z, 1 - me.x, me.y, me.c, 0)
                    self.start(half, half, FWDY, DIAGA, z, me.at(y=1 - me.y))
                self.hand_over(ref, FROMX, z)
            if "y" in self.axes:
                ref = self.shard(z, me.x, 1 - me.y, me.c)
                landed(ref, self.ss.at[0, 0], self.rs.at[FROMY, self.key(z)], me)
                if "x" in self.axes and self.halves:
                    half = self.shard(z, me.x, 1 - me.y, me.c, 1)
                    self.start(half, half, FWDX, DIAGB, z, me.at(x=1 - me.x))
                self.hand_over(ref, FROMY, z)
        self.around(event)

    def diagonal(self):
        me = self.me
        if "x" not in self.axes or "y" not in self.axes:
            return

        def event(z):
            for half in range(2 if self.halves else 1):
                ref = self.shard(z, 1 - me.x, 1 - me.y, me.c, half)
                landed(ref, self.ss.at[0, 0], self.rs.at[DIAGA + half, z], me)
                self.hand_over(ref, DIAGA + half, z)
        self.around(event)

    def kinds(self):
        me = self.me
        found = [(COL, me.x, me.y, None)]
        if "x" in self.axes:
            found.append((FROMX, 1 - me.x, me.y, None))
        if "y" in self.axes:
            found.append((FROMY, me.x, 1 - me.y, None))
        if "x" in self.axes and "y" in self.axes:
            found.append((DIAGA, 1 - me.x, 1 - me.y, 0))
            if self.halves:
                found.append((DIAGB, 1 - me.x, 1 - me.y, 1))
        return found

    def sibling(self):
        if "c" not in self.axes:
            return
        me = self.me

        def event(z):
            for kind, x, y, half in self.kinds():
                ref = self.shard(z, x, y, 1 - me.c, half)
                landed(ref, self.ss.at[0, 0], self.rs.at[5 + kind, self.key(z)], me)
        self.around(event)

    def drain(self):
        me = self.me

        def wait(kind, z, half=None):
            sent(self.shard(z, me.x, me.y, me.c, half), self.ss.at[kind, self.key(z)], self.rs.at[0, 0], me)

        def event(z):
            if "x" in self.axes:
                wait(TOX, z)
            if "y" in self.axes:
                wait(TOY, z)
            if "x" in self.axes and "y" in self.axes:
                wait(FWDY, z, 0)
                if self.halves:
                    wait(FWDX, z, 1)
            if "c" in self.axes:
                for kind, x, y, half in self.kinds():
                    wait(TOC + kind, z, half)
            if "z" in self.axes:
                pl.when((z <= me.z) & (me.z + 1 < me.nz))(functools.partial(wait, TOUP, z))
                pl.when((z >= me.z) & (me.z > 0))(functools.partial(wait, TODOWN, z))
        self.around(event)

    def phases(self):
        return [self.own, self.column, self.neighbours, self.diagonal, self.sibling, self.drain]


def skewed(items):
    lists = [item.phases() for item in items]
    for step in range(len(lists) + max(map(len, lists)) - 1):
        for i, phases in enumerate(lists):
            if 0 <= step - i < len(phases):
                phases[step - i]()


class Regroup:
    def __init__(self, me, dp_count, src, dst, ss, rs, width):
        self.me, self.n, self.src, self.dst, self.ss, self.rs, self.width = me, dp_count, src, dst, ss, rs, width

    def piece(self, dp, y, c):
        return self.dst.at[dp * 4 + y * 2 + c]

    def columns(self, dp):
        return self.src.at[:, pl.ds(pl.multiple_of(dp * self.width, 128), self.width)]

    def own(self):
        me = self.me
        mine = self.piece(me.dp, me.y, me.c)
        for k in range(1, self.n):
            to = lax.rem(me.dp + k, self.n)
            send(self.columns(to), mine, self.ss.at[0, to], self.rs.at[0, me.dp], (to, me.seq))
        src = self.columns(me.dp)
        send(src, mine, self.ss.at[1, me.dp], self.rs.at[1, me.dp], me.at(y=1 - me.y))
        send(src, mine, self.ss.at[2, me.dp], self.rs.at[2, me.dp], me.at(c=1 - me.c))

    def column(self):
        me = self.me
        for k in range(1, self.n):
            dp = lax.rem(me.dp + k, self.n)
            ref = self.piece(dp, me.y, me.c)
            landed(ref, self.ss.at[0, 0], self.rs.at[0, dp], me)
            send(ref, ref, self.ss.at[1, dp], self.rs.at[1, dp], me.at(y=1 - me.y))
            send(ref, ref, self.ss.at[2, dp], self.rs.at[2, dp], me.at(c=1 - me.c))

    def neighbours(self):
        me = self.me
        for k in range(self.n):
            dp = lax.rem(me.dp + k, self.n)
            ref = self.piece(dp, 1 - me.y, me.c)
            landed(ref, self.ss.at[0, 0], self.rs.at[1, dp], me)
            send(ref, ref, self.ss.at[3, dp], self.rs.at[3, dp], me.at(c=1 - me.c))

    def sibling(self):
        me = self.me
        for dp in range(self.n):
            landed(self.piece(dp, me.y, 1 - me.c), self.ss.at[0, 0], self.rs.at[2, dp], me)
            landed(self.piece(dp, 1 - me.y, 1 - me.c), self.ss.at[0, 0], self.rs.at[3, dp], me)

    def drain(self):
        me = self.me
        for k in range(self.n):
            dp = lax.rem(me.dp + k, self.n)
            ref = self.piece(dp, me.y, me.c)
            for kind in range(1 if k else 1, 4):
                sent(ref, self.ss.at[kind, dp], self.rs.at[0, 0], me)
            if k:
                sent(ref, self.ss.at[0, dp], self.rs.at[0, 0], me)

    def phases(self):
        return [self.own, self.column, self.neighbours, self.sibling, self.drain]


def gather_kernel(dp_count, plan, *refs):
    n = len(plan)
    srcs, dsts = refs[:n], refs[n:2 * n]
    ss, rs, rss, rrs, local = refs[2 * n:]
    me = Here(dp_count)
    greet([me.at(y=1 - me.y), me.at(c=1 - me.c)] + [(lax.rem(me.dp + k, dp_count), me.seq) for k in range(1, dp_count)])
    items, copies = [], []
    for i, (axes, halves) in enumerate(plan):
        if axes == "regroup":
            item = Regroup(me, dp_count, srcs[i], dsts[i], rss, rrs, halves)
            copies.append(pltpu.make_async_copy(item.columns(me.dp), item.piece(me.dp, me.y, me.c), local.at[i]))
        else:
            item = Gather(me, srcs[i], dsts[i], ss.at[i], rs.at[i], axes, halves)
            copies.append(pltpu.make_async_copy(srcs[i], item.shard(me.z, me.x, me.y, me.c), local.at[i]))
        items.append(item)
    for copy in copies:
        copy.start()
    skewed(items)
    for copy in copies:
        copy.wait()


def gather_all(dp_count, plan, arrays):
    def out(array, axes, halves):
        if axes == "regroup":
            return jax.ShapeDtypeStruct((dp_count * 4, array.shape[0], halves), array.dtype)
        count = {"zxyc": dp_count * 4, "zx": dp_count, "yc": 4}[axes]
        return jax.ShapeDtypeStruct((count,) + array.shape, array.dtype)
    nz = dp_count // 2
    n = len(plan)
    return pl.pallas_call(
        functools.partial(gather_kernel, dp_count, plan),
        out_shape=tuple(out(a, *p) for a, p in zip(arrays, plan)),
        in_specs=[ANY] * n,
        out_specs=tuple([ANY] * n),
        scratch_shapes=[
            DMA((n, SEND_KINDS, nz)), DMA((n, RECV_KINDS, nz)),
            DMA((4, dp_count)), DMA((4, dp_count)), DMA((n,)),
        ],
        compiler_params=pltpu.CompilerParams(collective_id=0, has_side_effects=True),
    )(*arrays)


HEADS = 16
HEAD_DIM = 96
FRAME_BLOCKS = 2
EPS = 1e-05
NEG = -1e30
HIGH = lax.Precision.HIGHEST
F32, BF16 = jnp.float32, jnp.bfloat16
WIDE = 60 << 20
PART = 4
PCOLS = PART * HEAD_DIM
SCALE = HEAD_DIM ** (-0.5)


def dot(left, right):
    return jnp.dot(left, right, preferred_element_type=F32)


def dot_t(left, right):
    return lax.dot_general(left, right, (((1,), (1,)), ((), ())), preferred_element_type=F32)


def t_dot(left, right):
    return lax.dot_general(left, right, (((0,), (0,)), ((), ())), preferred_element_type=F32)


def scaled_rows(rows):
    mean = jnp.mean(rows, axis=-1, keepdims=True)
    centred = rows - mean
    inverse = lax.rsqrt(jnp.mean(centred * centred, axis=-1, keepdims=True) + EPS)
    return centred * inverse, inverse


def norm_back(incoming, scaled, inverse, gain):
    inner = incoming * gain
    first = jnp.mean(inner, axis=-1, keepdims=True)
    second = jnp.mean(inner * scaled, axis=-1, keepdims=True)
    return inverse * (inner - first - scaled * second)


def part_mask(rows):
    row = lax.broadcasted_iota(jnp.int32, (PART * rows, PCOLS), 0)
    column = lax.broadcasted_iota(jnp.int32, (PART * rows, PCOLS), 1)
    low = (row // rows) * HEAD_DIM
    return (column >= low) & (column < low + HEAD_DIM)


def stacked(rows, mask):
    return jnp.where(mask, jnp.concatenate([rows] * PART, axis=0), jnp.zeros((), rows.dtype))


def unstacked(rows, mask, count):
    kept = jnp.where(mask, rows, 0.0)
    return sum(kept[h * count:(h + 1) * count] for h in range(PART))


def blocks_of(media_rows, block_rows, lat_rows):
    found = [(b * block_rows, block_rows) for b in range(media_rows // block_rows)]
    return found + [(media_rows, lat_rows)]


def attend_kernel(block_rows, items, owner, media, lat_all, gains, wq, wk, wv,
                  acc, stats, n_out, nl_out, q_out, k_out, v_out, wbuf, a_ref, m_ref, l_ref, sems):
    width = media.shape[1]
    half = width // 2
    media_rows = media.shape[0]
    lat_rows = lat_all.shape[0] // items
    seq = lax.axis_index("seq")

    def fetch(step, slot):
        cols = pl.ds(pl.multiple_of(step * half, 128), half)
        return [pltpu.make_async_copy(w.at[:, cols], wbuf.at[slot, i], sems.at[slot, i]) for i, w in enumerate((wq, wk, wv))]
    for copy in fetch(0, 0):
        copy.start()

    @pl.loop(0, media_rows // block_rows)
    def _(b):
        rows = pl.ds(pl.multiple_of(b * block_rows, block_rows), block_rows)
        u, _ = scaled_rows(media[rows, :].astype(F32))
        n_out[rows, :] = (u * gains[2:3, :] + gains[3:4, :]).astype(BF16)

    @pl.loop(0, items)
    def _(i):
        rows = pl.ds(pl.multiple_of(i * lat_rows, lat_rows), lat_rows)
        u, _ = scaled_rows(lat_all[rows, :].astype(F32))
        nl_out[rows, :] = (u * gains[0:1, :] + gains[1:2, :]).astype(BF16)
    n_out[pl.ds(media_rows, lat_rows), :] = nl_out[pl.ds(pl.multiple_of(seq * lat_rows, lat_rows), lat_rows), :]
    stats[...] = jnp.zeros_like(stats)
    mask = part_mask(lat_rows)
    lane = lax.broadcasted_iota(jnp.int32, (lat_rows, 128), 1)

    @pl.loop(0, 2)
    def _(step):
        slot = lax.rem(step, 2)
        cols = pl.ds(pl.multiple_of(step * half, 128), half)
        for copy in fetch(step, slot):
            copy.wait()

        @pl.when(step == 0)
        def _():
            for copy in fetch(1, 1):
                copy.start()
        q_out[:, cols] = dot(nl_out[...], wbuf[slot, 0]).astype(BF16)
        k_out[:, cols] = dot(n_out[...], wbuf[slot, 1]).astype(BF16)
        v_out[:, cols] = dot(n_out[...], wbuf[slot, 2]).astype(BF16)

        @pl.loop(0, half // PCOLS)
        def _(inner):
            part = step * (half // PCOLS) + inner
            pcols = pl.ds(pl.multiple_of(part * PCOLS, 128), PCOLS)
            a_ref[...] = jnp.zeros_like(a_ref)
            l_ref[...] = jnp.zeros_like(l_ref)
            m_ref[...] = jnp.full_like(m_ref, NEG)

            def block(start, count, item):
                rows = q_out[pl.ds(pl.multiple_of(item * lat_rows, lat_rows), lat_rows), pcols]
                query = stacked(rows, mask)
                keys, values = k_out[pl.ds(start, count), pcols], v_out[pl.ds(start, count), pcols]
                scores = dot_t(query, keys) * SCALE
                old = m_ref[item]
                new = jnp.maximum(old, jnp.max(scores, axis=-1, keepdims=True))
                factor = jnp.exp(old - new)
                expo = jnp.exp(scores - new[:, :count])
                m_ref[item] = new
                l_ref[item] = l_ref[item] * factor + jnp.sum(expo, axis=-1, keepdims=True)
                wide = jnp.concatenate([factor] * (PCOLS // 128), axis=1)
                a_ref[item] = a_ref[item] * wide + dot(expo.astype(BF16), values)
            for b, (start, count) in enumerate(blocks_of(media_rows, block_rows, lat_rows)):
                block(start, count, seq if count == lat_rows and start == media_rows else owner[b])
            for item in range(items):
                acc[item, :, pcols] = unstacked(a_ref[item], mask, lat_rows).astype(BF16)
                for h in range(PART):
                    chosen = lane == part * PART + h
                    at = pl.ds(h * lat_rows, lat_rows)
                    stats[item, 0] = jnp.where(chosen, m_ref[item, at, :], stats[item, 0])
                    stats[item, 1] = jnp.where(chosen, l_ref[item, at, :], stats[item, 1])


def attend(owner, media, lat_all, gains, wq, wk, wv, block_rows, items):
    width = media.shape[1]
    lat_rows = lat_all.shape[0] // items
    rows = media.shape[0] + lat_rows
    shape = jax.ShapeDtypeStruct
    return pl.pallas_call(
        functools.partial(attend_kernel, block_rows, items),
        out_shape=(
            shape((items, lat_rows, width), BF16), shape((items, 2, lat_rows, 128), F32),
            shape((rows, width), BF16), shape((items * lat_rows, width), BF16),
            shape((items * lat_rows, width), BF16), shape((rows, width), BF16), shape((rows, width), BF16),
        ),
        in_specs=[pl.BlockSpec(memory_space=pltpu.SMEM), VMEM, VMEM, VMEM, ANY, ANY, ANY],
        out_specs=tuple([VMEM] * 7),
        scratch_shapes=[
            pltpu.VMEM((2, 3, width, width // 2), BF16),
            pltpu.VMEM((items, PART * lat_rows, PCOLS), F32),
            pltpu.VMEM((items, PART * lat_rows, 128), F32), pltpu.VMEM((items, PART * lat_rows, 128), F32),
            DMA((2, 3)),
        ],
        compiler_params=pltpu.CompilerParams(vmem_limit_bytes=WIDE),
    )(owner, media, lat_all, gains, wq, wk, wv)


def media_back_kernel(block_rows, items, owner, media, gains, n_ref, nl_ref, q_ref, k_ref, v_ref, do_ref, stats, wq, wk, wv,
                      gwq, gwk, gwv, media_grad, sums, g_lat,
                      wbuf, g_ref, gq_ref, dq_acc, dq_ref, dk_ref, dv_ref, sems, out_sem):
    width = media.shape[1]
    half = width // 2
    media_rows = media.shape[0]
    lat_rows = nl_ref.shape[0] // items
    seq = lax.axis_index("seq")

    def fetch(step):
        cols = pl.ds(pl.multiple_of(step * half, 128), half)
        return [pltpu.make_async_copy(w.at[:, cols], wbuf.at[i], sems.at[i]) for i, w in enumerate((wq, wk, wv))]
    for copy in fetch(0):
        copy.start()
    mask = part_mask(lat_rows)
    lane = lax.broadcasted_iota(jnp.int32, (lat_rows, 128), 1)

    def replicated(stat, part):
        pieces = []
        for h in range(PART):
            column = jnp.sum(jnp.where(lane == part * PART + h, stat, 0.0), axis=-1, keepdims=True)
            pieces.append(jnp.broadcast_to(column, (lat_rows, 128)))
        return jnp.concatenate(pieces, axis=0)

    @pl.loop(0, 2)
    def _(step):
        cols = pl.ds(pl.multiple_of(step * half, 128), half)

        @pl.loop(0, half // PCOLS)
        def _(inner):
            part = step * (half // PCOLS) + inner
            pcols = pl.ds(pl.multiple_of(part * PCOLS, 128), PCOLS)
            lcols = pl.ds(pl.multiple_of(inner * PCOLS, 128), PCOLS)
            dq_acc[...] = jnp.zeros_like(dq_acc)

            def block(start, count, item):
                at = pl.ds(pl.multiple_of(item * lat_rows, lat_rows), lat_rows)
                query, grad = stacked(q_ref[at, pcols], mask), stacked(do_ref[at, pcols], mask)
                keys, values = k_ref[pl.ds(start, count), pcols], v_ref[pl.ds(start, count), pcols]
                lse, delta = replicated(stats[item, 0], part), replicated(stats[item, 1], part)
                prob = jnp.exp(dot_t(query, keys) * SCALE - lse[:, :count])
                score = (prob * (dot_t(grad, values) - delta[:, :count])).astype(BF16)
                dq_acc[item] = dq_acc[item] + dot(score, keys)
                dk_ref[pl.ds(start, count), lcols] = (t_dot(score, query) * SCALE).astype(BF16)
                dv_ref[pl.ds(start, count), lcols] = t_dot(prob.astype(BF16), grad).astype(BF16)
            for b, (start, count) in enumerate(blocks_of(media_rows, block_rows, lat_rows)):
                block(start, count, seq if count == lat_rows and start == media_rows else owner[b])
            for item in range(items):
                dq_ref[pl.ds(item * lat_rows, lat_rows), lcols] = (unstacked(dq_acc[item], mask, lat_rows) * SCALE).astype(BF16)
        for copy in fetch(step):
            copy.wait()
        gwq[:, cols] = t_dot(nl_ref[...], dq_ref[...]).astype(BF16)
        gwk[:, cols] = t_dot(n_ref[...], dk_ref[...]).astype(BF16)
        gwv[:, cols] = t_dot(n_ref[...], dv_ref[...]).astype(BF16)

        @pl.loop(0, 2)
        def _(piece):
            out = pl.ds(pl.multiple_of(piece * half, 128), half)
            g = dot_t(dk_ref[...], wbuf[1, out, :]) + dot_t(dv_ref[...], wbuf[2, out, :])
            gq = dot_t(dq_ref[...], wbuf[0, out, :])

            @pl.when(step == 0)
            def _():
                g_ref[:, out] = g
                gq_ref[:, out] = gq

            @pl.when(step == 1)
            def _():
                g_ref[:, out] += g
                gq_ref[:, out] += gq

        @pl.when(step == 0)
        def _():
            for copy in fetch(1):
                copy.start()
    mine = pl.ds(pl.multiple_of(seq * lat_rows, lat_rows), lat_rows)
    gq_ref[mine, :] += g_ref[pl.ds(media_rows, lat_rows), :]
    g_lat[...] = gq_ref[...].astype(BF16)
    sums[...] = jnp.zeros_like(sums)

    @pl.loop(0, media_rows // block_rows)
    def _(b):
        rows = pl.ds(pl.multiple_of(b * block_rows, block_rows), block_rows)
        u, inverse = scaled_rows(media[rows, :].astype(F32))
        g = g_ref[rows, :]
        g_ref[rows, :] = norm_back(g, u, inverse, gains[2:3, :])
        pltpu.make_async_copy(g_ref.at[rows, :], media_grad.at[rows, :], out_sem).start()
        sums[0:1, :] += jnp.sum(g * u, axis=0, keepdims=True)
        sums[1:2, :] += jnp.sum(g, axis=0, keepdims=True)
    whole = pl.ds(0, media_rows)
    pltpu.make_async_copy(g_ref.at[whole, :], media_grad.at[whole, :], out_sem).wait()


def media_back(owner, media, gains, n, nl, q, k, v, do_all, stats, wq, wk, wv, block_rows, items):
    width = media.shape[1]
    half = width // 2
    lat_rows = nl.shape[0] // items
    rows = n.shape[0]
    shape = jax.ShapeDtypeStruct
    return pl.pallas_call(
        functools.partial(media_back_kernel, block_rows, items),
        out_shape=(
            shape((width, width), BF16), shape((width, width), BF16), shape((width, width), BF16),
            shape(media.shape, F32), shape((8, width), F32), shape((items * lat_rows, width), BF16),
        ),
        in_specs=[pl.BlockSpec(memory_space=pltpu.SMEM)] + [VMEM] * 9 + [ANY] * 3,
        out_specs=(VMEM, VMEM, VMEM, ANY, VMEM, VMEM),
        scratch_shapes=[
            pltpu.VMEM((3, width, half), BF16),
            pltpu.VMEM((rows, width), F32), pltpu.VMEM((items * lat_rows, width), F32),
            pltpu.VMEM((items, PART * lat_rows, PCOLS), F32),
            pltpu.VMEM((items * lat_rows, half), BF16), pltpu.VMEM((rows, half), BF16), pltpu.VMEM((rows, half), BF16),
            DMA((3,)), DMA,
        ],
        compiler_params=pltpu.CompilerParams(vmem_limit_bytes=WIDE),
    )(owner, media, gains, n, nl, q, k, v, do_all, stats, wq, wk, wv)


def dp_peers(me, dp_count):
    return [(lax.rem(me.dp + k, dp_count), me.seq) for k in range(1, dp_count)]


def far_first(me, event):
    for d in range(me.nz - 1, 0, -1):
        pl.when(me.z >= d)(functools.partial(event, me.z - d))
        pl.when(me.z + d < me.nz)(functools.partial(event, me.z + d))
    event(me.z)


def add(*refs):
    total = refs[0][...].astype(F32)
    for ref in refs[1:]:
        total = total + ref[...].astype(F32)
    return total


class Line:
    def __init__(self, me, column, from_below, from_above, ss, rs):
        self.me, self.column, self.zb, self.za, self.ss, self.rs = me, column, from_below, from_above, ss, rs

    def event(self, z):
        me = self.me
        for up in (True, False):
            buf, kind = (self.zb, 0) if up else (self.za, 1)
            first = me.z == 0 if up else me.z == me.nz - 1
            to = me.at(z=me.z + 1 if up else me.z - 1)

            @pl.when(z > me.z if up else z < me.z)
            def _():
                term = self.column(z)

                @pl.when(jnp.logical_not(first))
                def _():
                    landed(buf.at[z], self.ss.at[0, 0], self.rs.at[kind, z], me)
                    term[...] = add(term, buf.at[z]).astype(term.dtype)
                send(term, buf.at[z], self.ss.at[kind, z], self.rs.at[kind, z], to)

    def total(self, out):
        me = self.me
        out[...] = self.column(me.z)[...].astype(F32)
        for up in (True, False):
            buf, kind = (self.zb, 0) if up else (self.za, 1)

            @pl.when(me.z > 0 if up else me.z < me.nz - 1)
            def _():
                landed(buf.at[me.z], self.ss.at[0, 0], self.rs.at[kind, me.z], me)
                out[...] += buf.at[me.z][...].astype(F32)

    def drain(self):
        me = self.me

        def event(z):
            pl.when(z > me.z)(lambda: sent(self.zb.at[z], self.ss.at[0, z], self.rs.at[0, 0], me))
            pl.when(z < me.z)(lambda: sent(self.za.at[z], self.ss.at[1, z], self.rs.at[0, 0], me))
        far_first(me, event)


class DpScatter:
    def __init__(self, me, part, out, ox, zb, za, ss, rs):
        self.me, self.part, self.out, self.ox, self.ss, self.rs = me, part, out, ox, ss, rs
        self.line = Line(me, lambda z: part.at[z * 2 + me.x], zb, za, ss, rs)

    def start(self, z):
        me = self.me
        send(self.part.at[z * 2 + 1 - me.x], self.ox.at[z], self.ss.at[2, z], self.rs.at[2, z], me.at(x=1 - me.x))

    def fold(self, z):
        me = self.me
        landed(self.ox.at[z], self.ss.at[0, 0], self.rs.at[2, z], me)
        mine = self.part.at[z * 2 + me.x]
        mine[...] = add(mine, self.ox.at[z]).astype(mine.dtype)
        self.line.event(z)

    def finish(self):
        self.line.total(self.out)

    def drain(self):
        far_first(self.me, lambda z: sent(self.ox.at[z], self.ss.at[2, z], self.rs.at[0, 0], self.me))
        self.line.drain()


def head_columns(width):
    row = lax.broadcasted_iota(jnp.int32, (128, width), 0) * HEAD_DIM
    column = lax.broadcasted_iota(jnp.int32, (128, width), 1)
    return ((column >= row) & (column < row + HEAD_DIM)).astype(F32)


def exact(left, right):
    return jnp.dot(left, right, preferred_element_type=F32, precision=HIGH)


def exact_t(left, right):
    return lax.dot_general(left, right, (((1,), (1,)), ((), ())), preferred_element_type=F32, precision=HIGH)


def latent_kernel(dp_count, acc, stats, lat, gains, og_all, wo, wup, wdn,
                  lat_out, grad_hidden, do_all, stat_all, gwo, gwu, gwd, sums,
                  acc_in, stat_in, nf_all, og, wo_v, up_v, dn_v, ga, act, gp,
                  part_g, ox_g, zb_g, za_g, part_y, ox_y, zb_y, za_y, own_do, own_stat, row_a, row_b, do_in, st_in,
                  xs, xr, ls, gs, gr, gs2, gr2, gs3, gr3, ys, yr, ws, wr):
    me = Here(dp_count)
    seq_count = acc.shape[0]
    rows, width = lat.shape
    seq_peers = [lax.rem(me.seq + k, seq_count) for k in range(1, seq_count)]
    loads = [pltpu.make_async_copy(src, dst, ls.at[i]) for i, (src, dst) in enumerate(((wdn, dn_v), (og_all, og), (wo, wo_v), (wup, up_v)))]
    for load in loads:
        load.start()
    greet(dp_peers(me, dp_count) + [(me.dp, s) for s in seq_peers])
    for k, to in enumerate(seq_peers):
        send(acc.at[to], acc_in.at[me.seq], xs.at[0, k], xr.at[0, me.seq], (me.dp, to))
        send(stats.at[to], stat_in.at[me.seq], xs.at[1, k], xr.at[1, me.seq], (me.dp, to))
    acc_in[me.seq] = acc[me.seq]
    stat_in[me.seq] = stats[me.seq]
    loads[0].wait()
    loads[1].wait()
    hidden_cols = dn_v.shape[0]
    all_rows = dp_count * rows

    @pl.loop(0, hidden_cols // 256)
    def _(t):
        at = pl.ds(pl.multiple_of(t * 256, 256), 256)
        ga[:, at] = dot_t(og[...].reshape(all_rows, width), dn_v[at, :])
    for k, source in enumerate(seq_peers):
        landed(acc_in.at[source], xs.at[0, 0], xr.at[0, source], me)
        landed(stat_in.at[source], xs.at[0, 0], xr.at[1, source], me)
    tops = [stat_in[s, 0] for s in range(seq_count)]
    best = functools.reduce(jnp.maximum, tops)
    weights = [jnp.exp(top - best) for top in tops]
    total = sum(w * stat_in[s, 1] for s, w in enumerate(weights))
    lane = lax.broadcasted_iota(jnp.int32, total.shape, 1)
    total = jnp.where(lane < HEADS, total, 1.0)
    spread = head_columns(width)
    attended = sum(exact(w / total, spread) * acc_in[s].astype(F32) for s, w in enumerate(weights))
    row_a[...] = attended
    own_stat[0] = best + jnp.log(total)
    loads[2].wait()
    loads[3].wait()
    hidden = lat[...].astype(F32) + dot(attended.astype(BF16), wo_v[...])
    row_b[...] = hidden
    scaled, _ = scaled_rows(hidden)
    nf_all[me.dp] = (scaled * gains[4:5, :] + gains[5:6, :]).astype(BF16)
    spread_nf = Gather(me, nf_all.at[me.dp], nf_all, gs, gr, "zx", 0)
    spread_nf.own()
    spread_nf.column()
    spread_nf.neighbours()

    @pl.loop(0, hidden_cols // 256)
    def _(t):
        at = pl.ds(pl.multiple_of(t * 256, 256), 256)
        pre = dot(nf_all[...].reshape(all_rows, width), up_v[:, at])
        phi = 0.5 * (1.0 + lax.erf(pre * 0.7071067811865476))
        act[:, at] = (pre * phi).astype(BF16)
        slope = phi + pre * jnp.exp(pre * pre * -0.5) * 0.3989422804014327
        gp[:, at] = (ga[:, at] * slope).astype(BF16)

    @pl.loop(0, width // 512)
    def _(t):
        at = pl.ds(pl.multiple_of(t * 512, 512), 512)
        part_g[:, :, at] = dot_t(gp[...], up_v[at, :]).astype(BF16).reshape(dp_count, rows, 512)
    sum_g = DpScatter(me, part_g, own_do, ox_g, zb_g, za_g, gs2, gr2)
    far_first(me, sum_g.start)

    @pl.loop(0, width // 512)
    def _(t):
        at = pl.ds(pl.multiple_of(t * 512, 512), 512)
        part_y[:, :, at] = dot(act[...], dn_v[:, at]).astype(BF16).reshape(dp_count, rows, 512)
    far_first(me, sum_g.fold)
    sum_y = DpScatter(me, part_y, own_do, ox_y, zb_y, za_y, gs3, gr3)
    far_first(me, sum_y.start)
    gwd[...] = t_dot(act[...], og[...].reshape(all_rows, width)).astype(BF16)
    sum_g.finish()
    gathered = own_do[...]
    scaled, inverse = scaled_rows(row_b[...])
    sums[...] = jnp.zeros_like(sums)
    sums[0:1, :] = jnp.sum(gathered * scaled, axis=0, keepdims=True)
    sums[1:2, :] = jnp.sum(gathered, axis=0, keepdims=True)
    grad = og[me.dp].astype(F32) + norm_back(gathered, scaled, inverse, gains[4:5, :])
    grad_hidden[...] = grad
    low = grad.astype(BF16)
    grad_att = dot_t(low, wo_v[...]).astype(BF16)
    do_in[me.seq] = grad_att
    own_stat[1] = exact_t(grad_att.astype(F32) * row_a[...], spread)
    st_in[me.seq] = own_stat[...]
    spread_do = Gather(me, do_in.at[me.seq], do_in, ys, yr, "yc", 0)
    spread_st = Gather(me, st_in.at[me.seq], st_in, ws, wr, "yc", 0)
    spread_do.own()
    spread_st.own()
    far_first(me, sum_y.fold)
    gwo[...] = t_dot(row_a[...].astype(BF16), low).astype(BF16)
    spread_do.neighbours()
    spread_st.neighbours()
    gwu[...] = t_dot(nf_all[...].reshape(all_rows, width), gp[...]).astype(BF16)
    sum_y.finish()
    lat_out[...] = (row_b[...] + own_do[...]).astype(BF16)
    spread_do.sibling()
    spread_st.sibling()
    do_all[...] = do_in[...]
    stat_all[...] = st_in[...]
    for k, to in enumerate(seq_peers):
        sent(acc_in.at[0], xs.at[0, k], xr.at[0, 0], me)
        sent(stat_in.at[0], xs.at[1, k], xr.at[0, 0], me)
    for item in (spread_nf, sum_g, sum_y, spread_do, spread_st):
        item.drain()


def latent(dp_count, acc, stats, lat, gains, og_all, wo, wup, wdn):
    nz = dp_count // 2
    items, rows, width = acc.shape
    hidden = wdn.shape[0]
    shape = jax.ShapeDtypeStruct
    buf = lambda *s: pltpu.VMEM(s, BF16)
    all_rows = dp_count * rows
    gather_sems = [DMA((SEND_KINDS, nz)), DMA((RECV_KINDS, nz))]
    return pl.pallas_call(
        functools.partial(latent_kernel, dp_count),
        out_shape=(
            shape((rows, width), BF16), shape((rows, width), F32), shape((items, rows, width), BF16),
            shape((items, 2, rows, 128), F32), shape((width, width), BF16), shape((width, hidden), BF16),
            shape((hidden, width), BF16), shape((8, width), F32),
        ),
        in_specs=[VMEM] * 4 + [ANY] * 4,
        out_specs=tuple([VMEM] * 8),
        scratch_shapes=[
            buf(items, rows, width), pltpu.VMEM((items, 2, rows, 128), F32), buf(dp_count, rows, width), buf(dp_count, rows, width),
            buf(width, width), buf(width, hidden), buf(hidden, width),
            pltpu.VMEM((all_rows, hidden), F32), buf(all_rows, hidden), buf(all_rows, hidden),
            buf(dp_count, rows, width), buf(nz, rows, width), buf(nz, rows, width), buf(nz, rows, width),
            buf(dp_count, rows, width), buf(nz, rows, width), buf(nz, rows, width), buf(nz, rows, width),
            pltpu.VMEM((rows, width), F32), pltpu.VMEM((2, rows, 128), F32),
            pltpu.VMEM((rows, width), F32), pltpu.VMEM((rows, width), F32),
            buf(items, rows, width), pltpu.VMEM((items, 2, rows, 128), F32),
            DMA((2, items)), DMA((2, items)), DMA((4,)),
            *gather_sems, DMA((3, nz)), DMA((3, nz)), DMA((3, nz)), DMA((3, nz)), *gather_sems, *gather_sems,
        ],
        compiler_params=pltpu.CompilerParams(collective_id=1, has_side_effects=True, vmem_limit_bytes=WIDE),
    )(acc, stats, lat, gains, og_all, wo, wup, wdn)


class Scatter:
    def __init__(self, me, src, out, bufs, ss, rs, ls, lss, lrs):
        self.me, self.src, self.out, self.ss, self.rs, self.ls = me, src, out, ss, rs, ls
        self.acc, self.cbuf, self.x1, self.y1, self.ox, self.oy, zb, za = bufs
        self.half = src.shape[-1] // 2
        self.line = Line(me, lambda z: self.acc.at[z, me.x, me.y], zb, za, lss, lrs)

    def part(self, ref, half):
        return ref.at[:, pl.ds(half * self.half, self.half)]

    def load(self, z):
        return pltpu.make_async_copy(self.src.at[pl.ds(2 * z, 2), :, self.me.c], self.acc.at[z], self.ls.at[z])

    def begin(self):
        me = self.me

        def event(z):
            send(self.src.at[pl.ds(2 * z, 2), :, 1 - me.c], self.cbuf.at[z], self.ss.at[0, z], self.rs.at[0, z], me.at(c=1 - me.c))
            self.load(z).start()
        far_first(me, event)

    def core(self):
        me = self.me

        def event(z):
            self.load(z).wait()
            landed(self.cbuf.at[z], self.ss.at[0, 0], self.rs.at[0, z], me)
            mine = self.acc.at[z]

            @pl.loop(0, 4)
            def _(i):
                x, y = i // 2, i % 2
                mine[x, y] = (mine[x, y].astype(F32) + self.cbuf[z, x, y].astype(F32)).astype(BF16)
            x_to, y_to = me.at(x=1 - me.x), me.at(y=1 - me.y)
            diag = mine.at[1 - me.x, 1 - me.y]
            send(self.part(diag, 0), self.x1.at[z], self.ss.at[1, z], self.rs.at[1, z], x_to)
            send(self.part(diag, 1), self.y1.at[z], self.ss.at[2, z], self.rs.at[2, z], y_to)
            send(self.part(mine.at[1 - me.x, me.y], 0), self.part(self.ox.at[z], 0), self.ss.at[3, z], self.rs.at[3, z], x_to)
            send(self.part(mine.at[me.x, 1 - me.y], 1), self.part(self.oy.at[z], 1), self.ss.at[4, z], self.rs.at[4, z], y_to)
        far_first(me, event)

    def middle(self):
        me = self.me

        def event(z):
            landed(self.x1.at[z], self.ss.at[0, 0], self.rs.at[1, z], me)
            ref = self.part(self.acc.at[z, me.x, 1 - me.y], 0)
            ref[...] = add(ref, self.x1.at[z]).astype(BF16)
            send(ref, self.part(self.oy.at[z], 0), self.ss.at[5, z], self.rs.at[5, z], me.at(y=1 - me.y))
            landed(self.y1.at[z], self.ss.at[0, 0], self.rs.at[2, z], me)
            ref = self.part(self.acc.at[z, 1 - me.x, me.y], 1)
            ref[...] = add(ref, self.y1.at[z]).astype(BF16)
            send(ref, self.part(self.ox.at[z], 1), self.ss.at[6, z], self.rs.at[6, z], me.at(x=1 - me.x))
        far_first(me, event)

    def fold(self):
        me = self.me

        def event(z):
            for kind, ref in ((3, self.part(self.ox.at[z], 0)), (4, self.part(self.oy.at[z], 1)),
                              (5, self.part(self.oy.at[z], 0)), (6, self.part(self.ox.at[z], 1))):
                landed(ref, self.ss.at[0, 0], self.rs.at[kind, z], me)
            mine = self.acc.at[z, me.x, me.y]
            mine[...] = add(mine, self.ox.at[z], self.oy.at[z]).astype(BF16)
            self.line.event(z)
        far_first(me, event)

    def finish(self):
        self.line.total(self.out)

    def drain(self):
        me = self.me

        def event(z):
            sent(self.cbuf.at[z], self.ss.at[0, z], self.rs.at[0, 0], me)
            for kind in range(1, 7):
                sent(self.x1.at[z], self.ss.at[kind, z], self.rs.at[0, 0], me)
        far_first(me, event)
        self.line.drain()

    def phases(self):
        return [self.begin, self.core, self.middle, self.fold, self.finish, self.drain]

    @staticmethod
    def scratch(nz, rows, cols):
        buf = lambda *s: pltpu.VMEM(s + (rows, cols), BF16)
        half = pltpu.VMEM((nz, rows, cols // 2), BF16)
        return [buf(nz, 2, 2), buf(nz, 2, 2), half, half, buf(nz), buf(nz), buf(nz), buf(nz),
                DMA((7, nz)), DMA((7, nz)), DMA((nz,)), DMA((2, nz)), DMA((2, nz))]


class SeqScatter:
    def __init__(self, me, src, then, acc, cbuf, oy, ss, rs, ls):
        self.me, self.src, self.then, self.acc, self.cbuf, self.oy = me, src, then, acc, cbuf, oy
        self.ss, self.rs = ss, rs
        self.load = pltpu.make_async_copy(src.at[:, :, me.c], acc, ls.at[0])

    def begin(self):
        me = self.me
        send(self.src.at[:, :, 1 - me.c], self.cbuf, self.ss.at[0], self.rs.at[0], me.at(c=1 - me.c))
        self.load.start()

    def core(self):
        me = self.me
        self.load.wait()
        landed(self.cbuf, self.ss.at[0], self.rs.at[0], me)

        @pl.loop(0, self.acc.shape[0])
        def _(i):
            for y in (0, 1):
                self.acc[i, y] = (self.acc[i, y].astype(F32) + self.cbuf[i, y].astype(F32)).astype(BF16)
        send(self.acc.at[:, 1 - me.y], self.oy, self.ss.at[1], self.rs.at[1], me.at(y=1 - me.y))

    def fold(self):
        me = self.me
        landed(self.oy, self.ss.at[0], self.rs.at[1], me)

        @pl.loop(0, self.acc.shape[0])
        def _(i):
            self.oy[i] = (self.acc[i, me.y].astype(F32) + self.oy[i].astype(F32)).astype(BF16)

    def finish(self):
        self.then(self.oy)

    def drain(self):
        sent(self.cbuf, self.ss.at[0], self.rs.at[0], self.me)
        sent(self.oy, self.ss.at[1], self.rs.at[0], self.me)

    def phases(self):
        return [self.begin, self.core, self.fold, self.finish, self.drain]

    @staticmethod
    def scratch(count, rows, cols):
        buf = lambda *s: pltpu.VMEM(s + (rows, cols), BF16)
        return [buf(count, 2), buf(count, 2), buf(count), DMA((2,)), DMA((2,)), DMA((1,))]


class SumAll:
    def __init__(self, me, ref, inbox, ss, rs):
        self.me, self.ref, self.inbox, self.ss, self.rs = me, ref, inbox, ss, rs

    def step(self, i, to):
        def begin():
            send(self.ref.at[i], self.inbox.at[i], self.ss.at[i], self.rs.at[i], to)

        def end():
            landed(self.inbox.at[i], self.ss.at[0], self.rs.at[i], self.me)
            self.ref[i + 1] = self.ref[i] + self.inbox[i]
        return begin, end

    def phases(self):
        me = self.me
        n = me.nz

        def begin_z():
            for k in range(1, n):
                to = lax.rem(me.z + k, n)
                send(self.ref.at[3], self.inbox.at[2 + k], self.ss.at[2 + k], self.rs.at[2 + k], me.at(z=to))

        def end_z():
            total = self.ref[3]
            for k in range(1, n):
                landed(self.inbox.at[2 + k], self.ss.at[0], self.rs.at[2 + k], me)
                total = total + self.inbox[2 + k]
            self.ref[4] = total

        def drain():
            for i in range(2 + n):
                sent(self.ref.at[0], self.ss.at[i], self.rs.at[0], me)
        first = self.step(0, me.at(c=1 - me.c))
        second = self.step(1, me.at(x=1 - me.x))
        third = self.step(2, me.at(y=1 - me.y))
        both = lambda one, other: (lambda: (one(), other()))
        return [first[0], both(first[1], second[0]), both(second[1], third[0]), both(third[1], begin_z), end_z, drain]


def scatter_kernel(dp_count, *refs):
    me = Here(dp_count)
    (g_lat, lat, grad_hidden, gains, sums_media, sums_ffn, gwq, gwk, gwv, gwo, gwu, gwd) = refs[:12]
    (lat_grad, sums, out_q, out_k, out_v, out_o, out_up, out_dn) = refs[12:20]
    scratch = list(refs[20:])
    take = lambda n: [scratch.pop(0) for _ in range(n)]
    full = [take(13) for _ in range(4)]
    seqs = [take(6) for _ in range(3)]
    up_in, up_ss, up_rs = take(3)
    small = take(4)
    greet(dp_peers(me, dp_count) + [me.at(y=1 - me.y), me.at(c=1 - me.c)])
    all_sum = SumAll(me, *small)

    def latents(total):
        scaled, inverse = scaled_rows(lat[...].astype(F32))
        grad = total[0].astype(F32)
        lat_grad[...] = grad_hidden[...] + norm_back(grad, scaled, inverse, gains[0:1, :])
        first = small[0]
        first[0, 0:1, :] = jnp.sum(grad * scaled, axis=0, keepdims=True)
        first[0, 1:2, :] = jnp.sum(grad, axis=0, keepdims=True)
        first[0, 2:4, :] = sums_media[0:2, :]
        first[0, 4:6, :] = sums_ffn[0:2, :]
        first[0, 6:8, :] = jnp.zeros_like(sums_ffn[0:2, :])

    def down(total):
        out_dn[...] = total[0].astype(F32)

    def up(total):
        for k in range(1, dp_count):
            to = lax.rem(me.dp + k, dp_count)
            send(total.at[to], up_in.at[me.dp], up_ss.at[to], up_rs.at[me.dp], (to, me.seq))
        up_in[me.dp] = total[me.dp]

    class Up(SeqScatter):
        def collect(self):
            for dp in range(dp_count):
                pl.when(dp != me.dp)(lambda: landed(up_in.at[dp], up_ss.at[0], up_rs.at[dp], me))
                cols = up_in.shape[2]
                out_up[:, dp * cols:(dp + 1) * cols] = up_in[dp].astype(F32)

        def drain(self):
            super().drain()
            for k in range(1, dp_count):
                to = lax.rem(me.dp + k, dp_count)
                sent(up_in.at[0], up_ss.at[to], up_rs.at[0], me)

        def phases(self):
            return [self.begin, self.core, self.fold, self.finish, self.collect, self.drain]
    lat_item = SeqScatter(me, g_lat, latents, *seqs[0])
    up_item = Up(me, gwu, up, *seqs[1])
    down_item = SeqScatter(me, gwd, down, *seqs[2])
    fulls = [Scatter(me, src, out, f[:8], *f[8:]) for src, out, f in zip((gwo, gwv, gwk, gwq), (out_o, out_v, out_k, out_q), full)]

    class After:
        def phases(self):
            return all_sum.phases()
    skewed([lat_item, fulls[0], up_item, After(), fulls[1], down_item, fulls[2], fulls[3]])
    sums[...] = small[0][4]


def scatter_all(dp_count, g_lat, lat, grad_hidden, gains, sums_media, sums_ffn, gwq, gwk, gwv, gwo, gwu, gwd):
    nz = dp_count // 2
    rows, width = lat.shape
    hidden = gwu.shape[1]
    n = dp_count * 4
    shape = jax.ShapeDtypeStruct
    square = lambda g: g.reshape(dp_count, 2, 2, width // n, width)
    arrays = (
        g_lat.reshape(1, 2, 2, rows, width), lat, grad_hidden, gains, sums_media, sums_ffn,
        square(gwq), square(gwk), square(gwv), square(gwo),
        gwu.reshape(dp_count, 2, 2, width // n, hidden), gwd.reshape(1, 2, 2, hidden // 4, width),
    )
    return pl.pallas_call(
        functools.partial(scatter_kernel, dp_count),
        out_shape=(
            shape((rows, width), F32), shape((8, width), F32),
            *[shape((width // n, width), F32)] * 4, shape((width // n, hidden * dp_count), F32), shape((hidden // 4, width), F32),
        ),
        in_specs=[ANY] + [VMEM] * 5 + [ANY] * 6,
        out_specs=tuple([VMEM] * 8),
        scratch_shapes=[
            *(Scatter.scratch(nz, width // n, width) * 4),
            *SeqScatter.scratch(1, rows, width), *SeqScatter.scratch(dp_count, width // n, hidden), *SeqScatter.scratch(1, hidden // 4, width),
            pltpu.VMEM((dp_count, width // n, hidden), BF16), DMA((dp_count,)), DMA((dp_count,)),
            pltpu.VMEM((5, 8, width), F32), pltpu.VMEM((2 + nz, 8, width), F32), DMA((2 + nz,)), DMA((2 + nz,)),
        ],
        compiler_params=pltpu.CompilerParams(collective_id=2, has_side_effects=True, vmem_limit_bytes=WIDE),
    )(*arrays)


def local_fast(
    media, latents, out_grad, frame_counts, block_position, w_query, w_key, w_value, w_out, w_up, w_down,
    gain_lat, shift_lat, gain_media, shift_media, gain_ffn, shift_ffn,
):
    dp_count, seq_count = lax.axis_size("dp"), lax.axis_size("seq")
    seq = lax.axis_index("seq")
    blocks, block_rows, width = media.shape
    items, lat_rows = seq_count, latents.shape[1]
    own_cols = gain_lat.shape[0]
    ends = FRAME_BLOCKS * jnp.cumsum(frame_counts[0])
    position = lax.dynamic_slice_in_dim(block_position[0], seq * blocks, blocks)
    owner = jnp.sum((ends[None, :] <= position[:, None]).astype(jnp.int32), axis=1)
    vectors = jnp.stack([gain_lat, shift_lat, gain_media, shift_media, gain_ffn, shift_ffn]).astype(F32)
    pack = jnp.pad(vectors, ((0, 2), (0, 128 - own_cols)))
    lat, og = latents.reshape(lat_rows, width), out_grad.reshape(lat_rows, width)
    plan = [("zxyc", 0), ("yc", 0)] + [("zxyc", width // 2)] * 4 + [("zx", 0), ("yc", 0), ("regroup", w_up.shape[1] // dp_count)]
    packs, lat_all, wq, wk, wv, wo, og_all, wdn, wup = gather_all(
        dp_count, plan, (pack, lat, w_query, w_key, w_value, w_out, og, w_down, w_up))
    gains = jnp.swapaxes(packs[:, :, :own_cols], 0, 1).reshape(8, width)
    wq, wk, wv, wo = [w.reshape(width, width) for w in (wq, wk, wv, wo)]
    wdn, wup = wdn.reshape(-1, width), wup.reshape(width, -1)
    med = media.reshape(-1, width)
    acc, stats, n, nl, q, k, v = attend(owner, med, lat_all.reshape(-1, width), gains, wq, wk, wv, block_rows, items)
    lat_out, grad_hidden, do_all, stat_all, gwo, gwu, gwd, sums_ffn = latent(dp_count, acc, stats, lat, gains, og_all, wo, wup, wdn)
    gwq, gwk, gwv, media_grad, sums_media, g_lat = media_back(
        owner, med, gains, n, nl, q, k, v, do_all.reshape(-1, width), stat_all, wq, wk, wv, block_rows, items)
    lat_grad, sums, *grads = scatter_all(
        dp_count, g_lat, lat, grad_hidden, gains, sums_media, sums_ffn, gwq, gwk, gwv, gwo, gwu, gwd)
    place = (lax.axis_index("dp") * seq_count + seq) * own_cols
    own = lax.dynamic_slice_in_dim(sums, place, own_cols, axis=1)
    return (lat_out.reshape(latents.shape), lat_grad.reshape(latents.shape), media_grad.reshape(media.shape), *grads, *[own[i] for i in range(6)])


def fits(mesh):
    return mesh.shape["seq"] == 4 and mesh.shape["dp"] % 2 == 0 and 1536 % (mesh.shape["dp"] * 64) == 0


def norm_forward(rows, gain, shift):
    mean = jnp.mean(rows, axis=-1, keepdims=True)
    centred = rows - mean
    variance = jnp.mean(centred * centred, axis=-1, keepdims=True)
    inverse = lax.rsqrt(variance + EPS)
    scaled = centred * inverse
    return (scaled * gain + shift, scaled, inverse)


def norm_backward(incoming, scaled, inverse, gain):
    inner = incoming * gain
    first = jnp.mean(inner, axis=-1, keepdims=True)
    second = jnp.mean(inner * scaled, axis=-1, keepdims=True)
    return (
        inverse * (inner - first - scaled * second),
        jnp.sum(incoming * scaled, axis=0),
        jnp.sum(incoming, axis=0),
    )


def matmul(left, right):
    return jnp.dot(left, right, preferred_element_type=jnp.float32)


def matmul_left_t(left, right):
    return lax.dot_general(
        left, right, (((0,), (0,)), ((), ())), preferred_element_type=jnp.float32
    )


def matmul_right_t(left, right):
    return lax.dot_general(
        left, right, (((1,), (1,)), ((), ())), preferred_element_type=jnp.float32
    )


def swap_rows(stat):
    return jnp.swapaxes(stat, 1, 2)[..., None]


def fold_sources(tops, totals, accums):
    best = jnp.max(tops, axis=0)
    factor = jnp.exp(tops - best[None])
    total = jnp.sum(factor * totals, axis=0)
    width = accums.shape[-1]
    spread = jnp.repeat(jnp.swapaxes(factor, 2, 3), width // factor.shape[2], axis=3)
    return (best, total, jnp.sum(accums * spread, axis=0))


def local(
    media,
    latents,
    out_grad,
    frame_counts,
    block_position,
    w_query,
    w_key,
    w_value,
    w_out,
    w_up,
    w_down,
    gain_lat,
    shift_lat,
    gain_media,
    shift_media,
    gain_ffn,
    shift_ffn,
):
    gathered = (
        lax.all_gather(w_query, ("dp", "seq"), axis=0, tiled=True),
        lax.all_gather(w_key, ("dp", "seq"), axis=0, tiled=True),
        lax.all_gather(w_value, ("dp", "seq"), axis=0, tiled=True),
        lax.all_gather(w_out, ("dp", "seq"), axis=0, tiled=True),
        lax.all_gather(w_up, ("dp", "seq"), axis=0, tiled=True),
        lax.all_gather(w_down, ("dp", "seq"), axis=0, tiled=True),
        lax.all_gather(gain_lat, ("dp", "seq"), axis=0, tiled=True),
        lax.all_gather(shift_lat, ("dp", "seq"), axis=0, tiled=True),
        lax.all_gather(gain_media, ("dp", "seq"), axis=0, tiled=True),
        lax.all_gather(shift_media, ("dp", "seq"), axis=0, tiled=True),
        lax.all_gather(gain_ffn, ("dp", "seq"), axis=0, tiled=True),
        lax.all_gather(shift_ffn, ("dp", "seq"), axis=0, tiled=True),
    )
    full_query, full_key, full_value, full_out, full_up, full_down = gathered[:6]
    lat_gain, lat_shift, med_gain, med_shift, ffn_gain, ffn_shift = [
        piece.astype(jnp.float32) for piece in gathered[6:]
    ]
    seq_rank = lax.axis_index("seq")
    seq_count = lax.axis_size("seq")
    blocks, block_rows, width = media.shape
    local_items, lat_rows, _ = latents.shape
    group_items = frame_counts.shape[1]
    heads = HEADS
    head_size = HEAD_DIM
    score_scale = head_size ** (-0.5)
    ends = FRAME_BLOCKS * jnp.cumsum(frame_counts[0])
    position = lax.dynamic_slice_in_dim(block_position[0], seq_rank * blocks, blocks)
    owner_item = jnp.sum((ends[None, :] <= position[:, None]).astype(jnp.int32), axis=1)
    member = (owner_item[:, None] == jnp.arange(group_items, dtype=jnp.int32)[None, :]).astype(
        jnp.float32
    )
    lat_input = latents.astype(jnp.float32).reshape(-1, width)
    normed_lat, scaled_lat, inverse_lat = norm_forward(lat_input, lat_gain, lat_shift)
    normed_lat = normed_lat.astype(jnp.bfloat16)
    query = matmul(normed_lat, full_query).astype(jnp.bfloat16)
    key_lat = (
        matmul(normed_lat, full_key)
        .astype(jnp.bfloat16)
        .reshape(local_items, lat_rows, heads, head_size)
    )
    value_lat = (
        matmul(normed_lat, full_value)
        .astype(jnp.bfloat16)
        .reshape(local_items, lat_rows, heads, head_size)
    )
    query_all = lax.all_gather(
        query.reshape(local_items, lat_rows, width), "seq", axis=0, tiled=True
    )
    med_input = media.astype(jnp.float32).reshape(-1, width)
    normed_med, scaled_med, inverse_med = norm_forward(med_input, med_gain, med_shift)
    normed_med = normed_med.astype(jnp.bfloat16)

    def media_keys(weight_key, weight_value):
        keys_out = (
            matmul(normed_med, weight_key)
            .astype(jnp.bfloat16)
            .reshape(blocks, block_rows, heads, head_size)
        )
        values_out = (
            matmul(normed_med, weight_value)
            .astype(jnp.bfloat16)
            .reshape(blocks, block_rows, heads, head_size)
        )
        return (keys_out, values_out)

    key_med, value_med = media_keys(full_key, full_value)
    query_blk = query_all[owner_item].reshape(blocks, lat_rows, heads, head_size)
    scores_med = (
        jnp.einsum("bqhd,bkhd->bhqk", query_blk, key_med, preferred_element_type=jnp.float32)
        * score_scale
    )
    block_top = jnp.max(scores_med, axis=-1)
    expo_med = jnp.exp(scores_med - block_top[..., None])
    expo_med_low = expo_med.astype(jnp.bfloat16)
    local_top = jnp.max(jnp.where(member.T[:, :, None, None] > 0, block_top[None], NEG), axis=1)
    to_local = jnp.exp(block_top - local_top[owner_item])
    local_total = jnp.einsum(
        "bi,bhq->ihq", member, to_local * jnp.sum(expo_med, axis=-1), precision=HIGH
    )
    accum_blk = jnp.einsum(
        "bhqk,bkhd->bqhd", expo_med_low, value_med, preferred_element_type=jnp.float32
    ) * swap_rows(to_local)
    local_accum = jnp.einsum("bi,bqhd->iqhd", member, accum_blk, precision=HIGH).reshape(
        group_items, lat_rows, width
    )
    part_top, part_total, part_accum = (
        lax.all_to_all(local_top, "seq", split_axis=0, concat_axis=0, tiled=True),
        lax.all_to_all(local_total, "seq", split_axis=0, concat_axis=0, tiled=True),
        lax.all_to_all(local_accum, "seq", split_axis=0, concat_axis=0, tiled=True),
    )
    top_own, total_own, accum_flat = fold_sources(
        part_top.reshape(seq_count, local_items, heads, lat_rows),
        part_total.reshape(seq_count, local_items, heads, lat_rows),
        part_accum.reshape(seq_count, local_items, lat_rows, width),
    )
    med_top = lax.all_gather(top_own, "seq", axis=0, tiled=True)
    accum_own = accum_flat.reshape(local_items, lat_rows, heads, head_size)
    query_lat = query.reshape(local_items, lat_rows, heads, head_size)
    scores_lat = (
        jnp.einsum("iqhd,ikhd->ihqk", query_lat, key_lat, preferred_element_type=jnp.float32)
        * score_scale
    )
    lat_top = jnp.max(scores_lat, axis=-1)
    expo_lat = jnp.exp(scores_lat - lat_top[..., None])
    expo_lat_low = expo_lat.astype(jnp.bfloat16)
    item_top = jnp.maximum(top_own, lat_top)
    media_weight = jnp.exp(top_own - item_top)
    lat_weight = jnp.exp(lat_top - item_top)
    item_total = total_own * media_weight + lat_weight * jnp.sum(expo_lat, axis=-1)
    inverse_total = 1.0 / item_total
    accum_lat = jnp.einsum(
        "ihqk,ikhd->iqhd", expo_lat_low, value_lat, preferred_element_type=jnp.float32
    ) * swap_rows(lat_weight)
    attended = (accum_own * swap_rows(media_weight) + accum_lat) * swap_rows(inverse_total)
    attended_low = attended.reshape(-1, width).astype(jnp.bfloat16)
    hidden = lat_input + matmul(attended_low, full_out)
    normed_ffn, scaled_ffn, inverse_ffn = norm_forward(hidden, ffn_gain, ffn_shift)
    normed_ffn = normed_ffn.astype(jnp.bfloat16)
    pre_act = matmul(normed_ffn, full_up)
    activated, gelu_back = jax.vjp(partial(jax.nn.gelu, approximate=False), pre_act)
    activated = activated.astype(jnp.bfloat16)
    result = hidden + matmul(activated, full_down)
    latents_out = result.astype(jnp.bfloat16).reshape(latents.shape)
    again = (
        lax.all_gather(w_query, ("dp", "seq"), axis=0, tiled=True),
        lax.all_gather(w_key, ("dp", "seq"), axis=0, tiled=True),
        lax.all_gather(w_value, ("dp", "seq"), axis=0, tiled=True),
        lax.all_gather(w_out, ("dp", "seq"), axis=0, tiled=True),
        lax.all_gather(w_up, ("dp", "seq"), axis=0, tiled=True),
        lax.all_gather(w_down, ("dp", "seq"), axis=0, tiled=True),
        lax.all_gather(gain_lat, ("dp", "seq"), axis=0, tiled=True),
        lax.all_gather(shift_lat, ("dp", "seq"), axis=0, tiled=True),
        lax.all_gather(gain_media, ("dp", "seq"), axis=0, tiled=True),
        lax.all_gather(shift_media, ("dp", "seq"), axis=0, tiled=True),
        lax.all_gather(gain_ffn, ("dp", "seq"), axis=0, tiled=True),
        lax.all_gather(shift_ffn, ("dp", "seq"), axis=0, tiled=True),
    )
    back_query, back_key, back_value, back_out, back_up, back_down = again[:6]
    grad_rows = out_grad.reshape(-1, width)
    cotangent = grad_rows.astype(jnp.float32)
    grad_down = matmul_left_t(activated, grad_rows)
    grad_act = matmul_right_t(grad_rows, back_down)
    grad_pre = gelu_back(grad_act)[0].astype(jnp.bfloat16)
    grad_up = matmul_left_t(normed_ffn, grad_pre)
    grad_normed_ffn = matmul_right_t(grad_pre, back_up)
    grad_hidden_norm, grad_gain_ffn, grad_shift_ffn = norm_backward(
        grad_normed_ffn, scaled_ffn, inverse_ffn, ffn_gain
    )
    grad_hidden = cotangent + grad_hidden_norm
    grad_hidden_low = grad_hidden.astype(jnp.bfloat16)
    grad_out = matmul_left_t(attended_low, grad_hidden_low)
    grad_att = matmul_right_t(grad_hidden_low, back_out).astype(jnp.bfloat16)
    grad_att_heads = grad_att.reshape(local_items, lat_rows, heads, head_size)
    delta = jnp.einsum(
        "iqhd,iqhd->ihq", grad_att_heads.astype(jnp.float32), attended, precision=HIGH
    )
    media_factor = media_weight * inverse_total
    grad_att_all = lax.all_gather(
        grad_att.reshape(local_items, lat_rows, width), "seq", axis=0, tiled=True
    )
    factor_all, delta_all = (
        lax.all_gather(media_factor, "seq", axis=0, tiled=True),
        lax.all_gather(delta, "seq", axis=0, tiled=True),
    )
    key_med, value_med = media_keys(back_key, back_value)
    grad_blk = grad_att_all[owner_item].reshape(blocks, lat_rows, heads, head_size)
    factor_blk = jnp.exp(block_top - med_top[owner_item]) * factor_all[owner_item]
    delta_blk = delta_all[owner_item]
    grad_prob_med = jnp.einsum(
        "bqhd,bkhd->bhqk", grad_blk, value_med, preferred_element_type=jnp.float32
    )
    grad_score_med = (
        expo_med * factor_blk[..., None] * (grad_prob_med - delta_blk[..., None])
    ).astype(jnp.bfloat16)
    grad_query_blk = (
        jnp.einsum("bhqk,bkhd->bqhd", grad_score_med, key_med, preferred_element_type=jnp.float32)
        * score_scale
    )
    grad_query_part = jnp.einsum("bi,bqhd->iqhd", member, grad_query_blk, precision=HIGH).reshape(
        group_items, lat_rows, width
    )
    grad_key_med = (
        (
            jnp.einsum(
                "bhqk,bqhd->bkhd", grad_score_med, query_blk, preferred_element_type=jnp.float32
            )
            * score_scale
        )
        .astype(jnp.bfloat16)
        .reshape(-1, width)
    )
    grad_value_med = (
        jnp.einsum(
            "bhqk,bqhd->bkhd",
            expo_med_low.astype(jnp.float32) * factor_blk[..., None],
            grad_blk.astype(jnp.float32),
            precision=HIGH,
        )
        .astype(jnp.bfloat16)
        .reshape(-1, width)
    )
    grad_query_own = lax.psum_scatter(
        grad_query_part.astype(jnp.bfloat16), "seq", scatter_dimension=0, tiled=True
    ).astype(jnp.float32)
    grad_normed_med = matmul_right_t(grad_key_med, back_key) + matmul_right_t(
        grad_value_med, back_value
    )
    grad_key = matmul_left_t(normed_med, grad_key_med)
    grad_value = matmul_left_t(normed_med, grad_value_med)
    media_grad, grad_gain_media, grad_shift_media = norm_backward(
        grad_normed_med, scaled_med, inverse_med, med_gain
    )
    lat_factor = lat_weight * inverse_total
    grad_prob_lat = jnp.einsum(
        "iqhd,ikhd->ihqk", grad_att_heads, value_lat, preferred_element_type=jnp.float32
    )
    grad_score_lat = (expo_lat * lat_factor[..., None] * (grad_prob_lat - delta[..., None])).astype(
        jnp.bfloat16
    )
    grad_query_lat = (
        jnp.einsum("ihqk,ikhd->iqhd", grad_score_lat, key_lat, preferred_element_type=jnp.float32)
        * score_scale
    )
    grad_key_lat = (
        (
            jnp.einsum(
                "ihqk,iqhd->ikhd", grad_score_lat, query_lat, preferred_element_type=jnp.float32
            )
            * score_scale
        )
        .astype(jnp.bfloat16)
        .reshape(-1, width)
    )
    grad_value_lat = (
        jnp.einsum(
            "ihqk,iqhd->ikhd",
            expo_lat_low.astype(jnp.float32) * lat_factor[..., None],
            grad_att_heads.astype(jnp.float32),
            precision=HIGH,
        )
        .astype(jnp.bfloat16)
        .reshape(-1, width)
    )
    grad_query = (
        (grad_query_own + grad_query_lat.reshape(local_items, lat_rows, width))
        .astype(jnp.bfloat16)
        .reshape(-1, width)
    )
    grad_normed_lat = (
        matmul_right_t(grad_query, back_query)
        + matmul_right_t(grad_key_lat, back_key)
        + matmul_right_t(grad_value_lat, back_value)
    )
    grad_query_weight = matmul_left_t(normed_lat, grad_query)
    grad_key = grad_key + matmul_left_t(normed_lat, grad_key_lat)
    grad_value = grad_value + matmul_left_t(normed_lat, grad_value_lat)
    grad_lat_norm, grad_gain_lat, grad_shift_lat = norm_backward(
        grad_normed_lat, scaled_lat, inverse_lat, lat_gain
    )
    latents_grad = (grad_hidden + grad_lat_norm).reshape(latents.shape)
    sharded = (
        lax.psum_scatter(grad_query_weight, ("dp", "seq"), scatter_dimension=0, tiled=True),
        lax.psum_scatter(grad_key, ("dp", "seq"), scatter_dimension=0, tiled=True),
        lax.psum_scatter(grad_value, ("dp", "seq"), scatter_dimension=0, tiled=True),
        lax.psum_scatter(grad_out, ("dp", "seq"), scatter_dimension=0, tiled=True),
        lax.psum_scatter(grad_up, ("dp", "seq"), scatter_dimension=0, tiled=True),
        lax.psum_scatter(grad_down, ("dp", "seq"), scatter_dimension=0, tiled=True),
        lax.psum_scatter(grad_gain_lat, ("dp", "seq"), scatter_dimension=0, tiled=True),
        lax.psum_scatter(grad_shift_lat, ("dp", "seq"), scatter_dimension=0, tiled=True),
        lax.psum_scatter(grad_gain_media, ("dp", "seq"), scatter_dimension=0, tiled=True),
        lax.psum_scatter(grad_shift_media, ("dp", "seq"), scatter_dimension=0, tiled=True),
        lax.psum_scatter(grad_gain_ffn, ("dp", "seq"), scatter_dimension=0, tiled=True),
        lax.psum_scatter(grad_shift_ffn, ("dp", "seq"), scatter_dimension=0, tiled=True),
    )
    return (latents_out, latents_grad, media_grad.reshape(media.shape)) + tuple(sharded)


def solution(mesh):
    return jax.shard_map(
        local_fast if fits(mesh) else local,
        mesh=mesh,
        in_specs=(
            P(("dp", "seq"), None, None),
            P(("dp", "seq"), None, None),
            P(("dp", "seq"), None, None),
            P("dp", None),
            P("dp", None),
            P(("dp", "seq"), None),
            P(("dp", "seq"), None),
            P(("dp", "seq"), None),
            P(("dp", "seq"), None),
            P(("dp", "seq"), None),
            P(("dp", "seq"), None),
            P(("dp", "seq")),
            P(("dp", "seq")),
            P(("dp", "seq")),
            P(("dp", "seq")),
            P(("dp", "seq")),
            P(("dp", "seq")),
        ),
        out_specs=(
            P(("dp", "seq"), None, None),
            P(("dp", "seq"), None, None),
            P(("dp", "seq"), None, None),
            P(("dp", "seq"), None),
            P(("dp", "seq"), None),
            P(("dp", "seq"), None),
            P(("dp", "seq"), None),
            P(("dp", "seq"), None),
            P(("dp", "seq"), None),
            P(("dp", "seq")),
            P(("dp", "seq")),
            P(("dp", "seq")),
            P(("dp", "seq")),
            P(("dp", "seq")),
            P(("dp", "seq")),
        ),
        check_vma=False,
    )
```

```python
from functools import partial
from jax.sharding import PartitionSpec as P
import functools
import jax
import jax.numpy as jnp
from jax import lax
from jax.experimental import pallas as pl
from jax.experimental.pallas import tpu as pltpu

MESH = pl.DeviceIdType.MESH
ANY = pl.BlockSpec(memory_space=pl.ANY)
VMEM = pl.BlockSpec(memory_space=pltpu.VMEM)
DMA = pltpu.SemaphoreType.DMA


class Here:
    def __init__(self, dp_count):
        dp, seq = lax.axis_index("dp"), lax.axis_index("seq")
        self.nz = dp_count // 2
        self.z, self.x, self.y, self.c = dp // 2, dp % 2, seq // 2, seq % 2
        self.dp, self.seq = dp, seq

    def at(self, z=None, x=None, y=None, c=None):
        z = self.z if z is None else z
        x = self.x if x is None else x
        y = self.y if y is None else y
        c = self.c if c is None else c
        return (z * 2 + x, y * 2 + c)


def send(src, dst, ss, rs, to):
    copy = pltpu.make_async_remote_copy(
        src_ref=src, dst_ref=dst, send_sem=ss, recv_sem=rs, device_id=to, device_id_type=MESH
    )
    copy.start()


def landed(dst, ss, rs, me):
    pltpu.make_async_remote_copy(
        src_ref=dst, dst_ref=dst, send_sem=ss, recv_sem=rs, device_id=me.at(c=1 - me.c), device_id_type=MESH
    ).wait_recv()


def sent(src, ss, rs, me):
    pltpu.make_async_remote_copy(
        src_ref=src, dst_ref=src, send_sem=ss, recv_sem=rs, device_id=me.at(c=1 - me.c), device_id_type=MESH
    ).wait_send()


def greet(devices):
    barrier = pltpu.get_barrier_semaphore()
    for device in devices:
        pl.semaphore_signal(barrier, inc=1, device_id=device, device_id_type=MESH)
    pl.semaphore_wait(barrier, len(devices))


COL, FROMX, FROMY, DIAGA, DIAGB = range(5)
TOUP, TODOWN, TOX, TOY, FWDY, FWDX, TOC = range(7)
RECV_KINDS, SEND_KINDS = 10, 12


class Gather:
    def __init__(self, me, src, dst, ss, rs, axes, halves):
        self.me, self.src, self.dst, self.ss, self.rs = me, src, dst, ss, rs
        self.axes, self.halves = axes, halves
        self.sends = []
        self.depth = me.nz if "z" in axes else 1

    def slot(self, z, x, y, c):
        if self.axes == "zxyc":
            return ((z * 2 + x) * 2 + y) * 2 + c
        if self.axes == "zx":
            return z * 2 + x
        return y * 2 + c

    def shard(self, z, x, y, c, half=None):
        ref = self.dst.at[self.slot(z, x, y, c)]
        if half is None or not self.halves:
            return ref
        width = self.halves
        return ref.at[:, pl.ds(0, width)] if half == 0 else ref.at[:, pl.ds(width, width)]

    def key(self, z):
        return z if "z" in self.axes else 0

    def start(self, src, dst, out_kind, in_kind, z, to):
        k = self.key(z)
        send(src, dst, self.ss.at[out_kind, k], self.rs.at[in_kind, k], to)

    def hand_over(self, ref, kind, z):
        if "c" in self.axes:
            self.start(ref, ref, TOC + kind, 5 + kind, z, self.me.at(c=1 - self.me.c))

    def spread(self, ref, z):
        me = self.me
        if "x" in self.axes:
            self.start(ref, ref, TOX, FROMX, z, me.at(x=1 - me.x))
        if "y" in self.axes:
            self.start(ref, ref, TOY, FROMY, z, me.at(y=1 - me.y))
        self.hand_over(ref, COL, z)

    def own(self):
        return [self.send_own]

    def send_own(self):
        me = self.me
        ref = self.shard(me.z, me.x, me.y, me.c)
        if "z" in self.axes:
            @pl.when(me.z + 1 < me.nz)
            def _():
                self.start(self.src, ref, TOUP, COL, me.z, me.at(z=me.z + 1))

            @pl.when(me.z > 0)
            def _():
                self.start(self.src, ref, TODOWN, COL, me.z, me.at(z=me.z - 1))
        if "x" in self.axes:
            self.start(self.src, ref, TOX, FROMX, me.z, me.at(x=1 - me.x))
        if "y" in self.axes:
            self.start(self.src, ref, TOY, FROMY, me.z, me.at(y=1 - me.y))
        if "c" in self.axes:
            self.start(self.src, ref, TOC, 5, me.z, me.at(c=1 - me.c))

    def around(self, event):
        me = self.me
        found = [lambda: event(me.z)]
        for d in range(1, self.depth):
            found.append(lambda d=d: pl.when(me.z >= d)(lambda: event(me.z - d)))
            found.append(lambda d=d: pl.when(me.z + d < me.nz)(lambda: event(me.z + d)))
        return found

    def column(self):
        me = self.me

        def event(d, below):
            there = me.z - d if below else me.z + d
            ahead = me.z + 1 if below else me.z - 1

            @pl.when(there >= 0 if below else there < me.nz)
            def _():
                ref = self.shard(there, me.x, me.y, me.c)
                landed(ref, self.ss.at[0, 0], self.rs.at[COL, there], me)

                @pl.when(ahead < me.nz if below else ahead >= 0)
                def _():
                    self.start(ref, ref, TOUP if below else TODOWN, COL, there, me.at(z=ahead))
                self.spread(ref, there)
        return [functools.partial(event, d, below) for d in range(1, self.depth) for below in (True, False)]

    def neighbours(self):
        me = self.me

        def event(z):
            if "x" in self.axes:
                ref = self.shard(z, 1 - me.x, me.y, me.c)
                landed(ref, self.ss.at[0, 0], self.rs.at[FROMX, self.key(z)], me)
                if "y" in self.axes:
                    half = self.shard(z, 1 - me.x, me.y, me.c, 0)
                    self.start(half, half, FWDY, DIAGA, z, me.at(y=1 - me.y))
                self.hand_over(ref, FROMX, z)
            if "y" in self.axes:
                ref = self.shard(z, me.x, 1 - me.y, me.c)
                landed(ref, self.ss.at[0, 0], self.rs.at[FROMY, self.key(z)], me)
                if "x" in self.axes and self.halves:
                    half = self.shard(z, me.x, 1 - me.y, me.c, 1)
                    self.start(half, half, FWDX, DIAGB, z, me.at(x=1 - me.x))
                self.hand_over(ref, FROMY, z)
        return self.around(event)

    def diagonal(self):
        me = self.me
        if "x" not in self.axes or "y" not in self.axes:
            return []

        def event(z):
            for half in range(2 if self.halves else 1):
                ref = self.shard(z, 1 - me.x, 1 - me.y, me.c, half)
                landed(ref, self.ss.at[0, 0], self.rs.at[DIAGA + half, z], me)
                self.hand_over(ref, DIAGA + half, z)
        return self.around(event)

    def kinds(self):
        me = self.me
        found = [(COL, me.x, me.y, None)]
        if "x" in self.axes:
            found.append((FROMX, 1 - me.x, me.y, None))
        if "y" in self.axes:
            found.append((FROMY, me.x, 1 - me.y, None))
        if "x" in self.axes and "y" in self.axes:
            found.append((DIAGA, 1 - me.x, 1 - me.y, 0))
            if self.halves:
                found.append((DIAGB, 1 - me.x, 1 - me.y, 1))
        return found

    def sibling(self):
        if "c" not in self.axes:
            return []
        me = self.me

        def event(z):
            for kind, x, y, half in self.kinds():
                ref = self.shard(z, x, y, 1 - me.c, half)
                landed(ref, self.ss.at[0, 0], self.rs.at[5 + kind, self.key(z)], me)
        return self.around(event)

    def drain(self):
        me = self.me

        def wait(kind, z, half=None):
            sent(self.shard(z, me.x, me.y, me.c, half), self.ss.at[kind, self.key(z)], self.rs.at[0, 0], me)

        def event(z):
            if "x" in self.axes:
                wait(TOX, z)
            if "y" in self.axes:
                wait(TOY, z)
            if "x" in self.axes and "y" in self.axes:
                wait(FWDY, z, 0)
                if self.halves:
                    wait(FWDX, z, 1)
            if "c" in self.axes:
                for kind, x, y, half in self.kinds():
                    wait(TOC + kind, z, half)
            if "z" in self.axes:
                pl.when((z <= me.z) & (me.z + 1 < me.nz))(functools.partial(wait, TOUP, z))
                pl.when((z >= me.z) & (me.z > 0))(functools.partial(wait, TODOWN, z))
        return self.around(event)

    def phases(self):
        return [self.own(), self.column(), self.neighbours(), self.diagonal(), self.sibling(), self.drain()]


def skewed(items):
    lists = [item.phases() for item in items]
    found = []
    for step in range(len(lists) + max(map(len, lists)) - 1):
        for i, phases in enumerate(lists):
            if 0 <= step - i < len(phases):
                found += phases[step - i]
    return found


ORDER = skewed


def run(events):
    for event in events:
        event()


def share(events, count):
    cuts = [len(events) * i // count for i in range(count + 1)]
    return [events[a:b] for a, b in zip(cuts, cuts[1:])]


def run_at(step, lists):
    for i, events in enumerate(lists):
        if events:
            pl.when(step == i)(functools.partial(run, events))


class Regroup:
    def __init__(self, me, dp_count, src, dst, ss, rs, width):
        self.me, self.n, self.src, self.dst, self.ss, self.rs, self.width = me, dp_count, src, dst, ss, rs, width

    def piece(self, dp, y, c):
        return self.dst.at[dp * 4 + y * 2 + c]

    def columns(self, dp):
        return self.src.at[:, pl.ds(pl.multiple_of(dp * self.width, 128), self.width)]

    def own(self):
        me = self.me
        mine = self.piece(me.dp, me.y, me.c)
        for k in range(1, self.n):
            to = lax.rem(me.dp + k, self.n)
            send(self.columns(to), mine, self.ss.at[0, to], self.rs.at[0, me.dp], (to, me.seq))
        src = self.columns(me.dp)
        send(src, mine, self.ss.at[1, me.dp], self.rs.at[1, me.dp], me.at(y=1 - me.y))
        send(src, mine, self.ss.at[2, me.dp], self.rs.at[2, me.dp], me.at(c=1 - me.c))

    def column(self):
        me = self.me
        for k in range(1, self.n):
            dp = lax.rem(me.dp + k, self.n)
            ref = self.piece(dp, me.y, me.c)
            landed(ref, self.ss.at[0, 0], self.rs.at[0, dp], me)
            send(ref, ref, self.ss.at[1, dp], self.rs.at[1, dp], me.at(y=1 - me.y))
            send(ref, ref, self.ss.at[2, dp], self.rs.at[2, dp], me.at(c=1 - me.c))

    def neighbours(self):
        me = self.me
        for k in range(self.n):
            dp = lax.rem(me.dp + k, self.n)
            ref = self.piece(dp, 1 - me.y, me.c)
            landed(ref, self.ss.at[0, 0], self.rs.at[1, dp], me)
            send(ref, ref, self.ss.at[3, dp], self.rs.at[3, dp], me.at(c=1 - me.c))

    def sibling(self):
        me = self.me
        for dp in range(self.n):
            landed(self.piece(dp, me.y, 1 - me.c), self.ss.at[0, 0], self.rs.at[2, dp], me)
            landed(self.piece(dp, 1 - me.y, 1 - me.c), self.ss.at[0, 0], self.rs.at[3, dp], me)

    def drain(self):
        me = self.me
        for k in range(self.n):
            dp = lax.rem(me.dp + k, self.n)
            ref = self.piece(dp, me.y, me.c)
            for kind in range(1 if k else 1, 4):
                sent(ref, self.ss.at[kind, dp], self.rs.at[0, 0], me)
            if k:
                sent(ref, self.ss.at[0, dp], self.rs.at[0, 0], me)

    def phases(self):
        return [[self.own], [self.column], [self.neighbours], [self.sibling], [self.drain]]


class Everyone:
    def __init__(self, me, dp_count, src, dst, ss, rs):
        self.me, self.n, self.src, self.dst, self.ss, self.rs = me, dp_count * 4, src, dst, ss, rs
        self.index = me.dp * 4 + me.seq

    def own(self):
        def event():
            @pl.loop(1, self.n)
            def _(k):
                to = lax.rem(self.index + k, self.n)
                send(self.src, self.dst.at[self.index], self.ss.at[to], self.rs.at[self.index], (to // 4, to % 4))
        return [event]

    def arrive(self):
        def event():
            @pl.loop(1, self.n)
            def _(k):
                source = lax.rem(self.index + k, self.n)
                landed(self.dst.at[source], self.ss.at[0], self.rs.at[source], self.me)
        return [event]

    def drain(self):
        def event():
            @pl.loop(1, self.n)
            def _(k):
                sent(self.src, self.ss.at[lax.rem(self.index + k, self.n)], self.rs.at[0], self.me)
        return [event]

    def phases(self):
        return [self.own(), self.arrive(), self.drain()]


def greet_all(me, dp_count):
    barrier = pltpu.get_barrier_semaphore()
    count = dp_count * 4

    @pl.loop(1, count)
    def _(k):
        to = lax.rem(me.dp * 4 + me.seq + k, count)
        pl.semaphore_signal(barrier, inc=1, device_id=(to // 4, to % 4), device_id_type=MESH)
    pl.semaphore_wait(barrier, count - 1)


def gather_kernel(dp_count, plan, *refs):
    n = len(plan)
    srcs, dsts = refs[:n], refs[n:2 * n]
    ss, rs, rss, rrs, local, es, er = refs[2 * n:]
    me = Here(dp_count)
    greet_all(me, dp_count)
    items, copies = [], []
    for i, (axes, halves) in enumerate(plan):
        if axes == "all":
            item = Everyone(me, dp_count, srcs[i], dsts[i], es, er)
            copies.append(pltpu.make_async_copy(srcs[i], dsts[i].at[item.index], local.at[i]))
        elif axes == "regroup":
            item = Regroup(me, dp_count, srcs[i], dsts[i], rss, rrs, halves)
            copies.append(pltpu.make_async_copy(item.columns(me.dp), item.piece(me.dp, me.y, me.c), local.at[i]))
        else:
            item = Gather(me, srcs[i], dsts[i], ss.at[i], rs.at[i], axes, halves)
            copies.append(pltpu.make_async_copy(srcs[i], item.shard(me.z, me.x, me.y, me.c), local.at[i]))
        items.append(item)
    for copy in copies:
        copy.start()
    run(ORDER(items))
    for copy in copies:
        copy.wait()


def gather_all(dp_count, plan, arrays):
    def out(array, axes, halves):
        if axes == "regroup":
            return jax.ShapeDtypeStruct((dp_count * 4, array.shape[0], halves), array.dtype)
        count = {"all": dp_count * 4, "zxyc": dp_count * 4, "zx": dp_count, "yc": 4}[axes]
        return jax.ShapeDtypeStruct((count,) + array.shape, array.dtype)
    nz = dp_count // 2
    n = len(plan)
    return pl.pallas_call(
        functools.partial(gather_kernel, dp_count, plan),
        out_shape=tuple(out(a, *p) for a, p in zip(arrays, plan)),
        in_specs=[ANY] * n,
        out_specs=tuple([ANY] * n),
        scratch_shapes=[
            DMA((n, SEND_KINDS, nz)), DMA((n, RECV_KINDS, nz)),
            DMA((4, dp_count)), DMA((4, dp_count)), DMA((n,)), DMA((dp_count * 4,)), DMA((dp_count * 4,)),
        ],
        compiler_params=pltpu.CompilerParams(collective_id=0, has_side_effects=True),
    )(*arrays)


HEADS = 16
HEAD_DIM = 96
FRAME_BLOCKS = 2
EPS = 1e-05
NEG = -1e30
HIGH = lax.Precision.HIGHEST
F32, BF16 = jnp.float32, jnp.bfloat16
WIDE = 60 << 20
PART = 4
PCOLS = PART * HEAD_DIM
SCALE = HEAD_DIM ** (-0.5)


def dot(left, right):
    return jnp.dot(left, right, preferred_element_type=F32)


def dot_t(left, right):
    return lax.dot_general(left, right, (((1,), (1,)), ((), ())), preferred_element_type=F32)


def t_dot(left, right):
    return lax.dot_general(left, right, (((0,), (0,)), ((), ())), preferred_element_type=F32)


def scaled_rows(rows):
    mean = jnp.mean(rows, axis=-1, keepdims=True)
    centred = rows - mean
    inverse = lax.rsqrt(jnp.mean(centred * centred, axis=-1, keepdims=True) + EPS)
    return centred * inverse, inverse


def norm_back(incoming, scaled, inverse, gain):
    inner = incoming * gain
    first = jnp.mean(inner, axis=-1, keepdims=True)
    second = jnp.mean(inner * scaled, axis=-1, keepdims=True)
    return inverse * (inner - first - scaled * second)


def part_mask(rows):
    row = lax.broadcasted_iota(jnp.int32, (PART * rows, PCOLS), 0)
    column = lax.broadcasted_iota(jnp.int32, (PART * rows, PCOLS), 1)
    low = (row // rows) * HEAD_DIM
    return (column >= low) & (column < low + HEAD_DIM)


def stacked(rows, mask):
    return jnp.where(mask, jnp.concatenate([rows] * PART, axis=0), jnp.zeros((), rows.dtype))


def unstacked(rows, mask, count):
    kept = jnp.where(mask, rows, 0.0)
    return sum(kept[h * count:(h + 1) * count] for h in range(PART))


def blocks_of(media_rows, block_rows, lat_rows):
    found = [(b * block_rows, block_rows) for b in range(media_rows // block_rows)]
    return found + [(media_rows, lat_rows)]


def attend_kernel(block_rows, items, owner, media, lat_all, gains, wq, wk, wv,
                  acc, stats, n_out, nl_out, q_out, k_out, v_out, wbuf, a_ref, m_ref, l_ref, sems):
    width = media.shape[1]
    half = width // 2
    media_rows = media.shape[0]
    lat_rows = lat_all.shape[0] // items
    seq = lax.axis_index("seq")

    def fetch(step, slot):
        cols = pl.ds(pl.multiple_of(step * half, 128), half)
        return [pltpu.make_async_copy(w.at[:, cols], wbuf.at[slot, i], sems.at[slot, i]) for i, w in enumerate((wq, wk, wv))]
    for copy in fetch(0, 0):
        copy.start()

    @pl.loop(0, media_rows // block_rows)
    def _(b):
        rows = pl.ds(pl.multiple_of(b * block_rows, block_rows), block_rows)
        u, _ = scaled_rows(media[rows, :].astype(F32))
        n_out[rows, :] = (u * gains[2:3, :] + gains[3:4, :]).astype(BF16)

    @pl.loop(0, items)
    def _(i):
        rows = pl.ds(pl.multiple_of(i * lat_rows, lat_rows), lat_rows)
        u, _ = scaled_rows(lat_all[rows, :].astype(F32))
        nl_out[rows, :] = (u * gains[0:1, :] + gains[1:2, :]).astype(BF16)
    n_out[pl.ds(media_rows, lat_rows), :] = nl_out[pl.ds(pl.multiple_of(seq * lat_rows, lat_rows), lat_rows), :]
    padding = n_out.shape[0] - media_rows - lat_rows
    n_out[pl.ds(media_rows + lat_rows, padding), :] = jnp.zeros((padding, width), BF16)
    stats[...] = jnp.zeros_like(stats)
    mask = part_mask(lat_rows)
    lane = lax.broadcasted_iota(jnp.int32, (lat_rows, 128), 1)

    @pl.loop(0, 2)
    def _(step):
        slot = lax.rem(step, 2)
        cols = pl.ds(pl.multiple_of(step * half, 128), half)
        for copy in fetch(step, slot):
            copy.wait()

        @pl.when(step == 0)
        def _():
            for copy in fetch(1, 1):
                copy.start()
        q_out[:, cols] = dot(nl_out[...], wbuf[slot, 0]).astype(BF16)
        k_out[:, cols] = dot(n_out[...], wbuf[slot, 1]).astype(BF16)
        v_out[:, cols] = dot(n_out[...], wbuf[slot, 2]).astype(BF16)

        @pl.loop(0, half // PCOLS)
        def _(inner):
            part = step * (half // PCOLS) + inner
            pcols = pl.ds(pl.multiple_of(part * PCOLS, 128), PCOLS)
            a_ref[...] = jnp.zeros_like(a_ref)
            l_ref[...] = jnp.zeros_like(l_ref)
            m_ref[...] = jnp.full_like(m_ref, NEG)

            def block(start, count, item):
                rows = q_out[pl.ds(pl.multiple_of(item * lat_rows, lat_rows), lat_rows), pcols]
                query = stacked(rows, mask)
                keys, values = k_out[pl.ds(start, count), pcols], v_out[pl.ds(start, count), pcols]
                scores = dot_t(query, keys) * SCALE
                old = m_ref[item]
                new = jnp.maximum(old, jnp.max(scores, axis=-1, keepdims=True))
                factor = jnp.exp(old - new)
                expo = jnp.exp(scores - new[:, :count])
                m_ref[item] = new
                l_ref[item] = l_ref[item] * factor + jnp.sum(expo, axis=-1, keepdims=True)
                wide = jnp.concatenate([factor] * (PCOLS // 128), axis=1)
                a_ref[item] = a_ref[item] * wide + dot(expo.astype(BF16), values)
            for b, (start, count) in enumerate(blocks_of(media_rows, block_rows, lat_rows)):
                block(start, count, seq if count == lat_rows and start == media_rows else owner[b])
            for item in range(items):
                acc[item, :, pcols] = unstacked(a_ref[item], mask, lat_rows).astype(BF16)
                for h in range(PART):
                    chosen = lane == part * PART + h
                    at = pl.ds(h * lat_rows, lat_rows)
                    stats[item, 0] = jnp.where(chosen, m_ref[item, at, :], stats[item, 0])
                    stats[item, 1] = jnp.where(chosen, l_ref[item, at, :], stats[item, 1])


def attend(owner, media, lat_all, gains, wq, wk, wv, block_rows, items):
    width = media.shape[1]
    lat_rows = lat_all.shape[0] // items
    rows = media.shape[0] + block_rows
    shape = jax.ShapeDtypeStruct
    return pl.pallas_call(
        functools.partial(attend_kernel, block_rows, items),
        out_shape=(
            shape((items, lat_rows, width), BF16), shape((items, 2, lat_rows, 128), F32),
            shape((rows, width), BF16), shape((items * lat_rows, width), BF16),
            shape((items * lat_rows, width), BF16), shape((rows, width), BF16), shape((rows, width), BF16),
        ),
        in_specs=[pl.BlockSpec(memory_space=pltpu.SMEM), VMEM, VMEM, VMEM, ANY, ANY, ANY],
        out_specs=tuple([VMEM] * 7),
        scratch_shapes=[
            pltpu.VMEM((2, 3, width, width // 2), BF16),
            pltpu.VMEM((items, PART * lat_rows, PCOLS), F32),
            pltpu.VMEM((items, PART * lat_rows, 128), F32), pltpu.VMEM((items, PART * lat_rows, 128), F32),
            DMA((2, 3)),
        ],
        compiler_params=pltpu.CompilerParams(vmem_limit_bytes=WIDE),
    )(owner, media, lat_all, gains, wq, wk, wv)


def dp_peers(me, dp_count):
    return [(lax.rem(me.dp + k, dp_count), me.seq) for k in range(1, dp_count)]


def far_first(me, event):
    found = []
    for d in range(me.nz - 1, 0, -1):
        found.append(lambda d=d: pl.when(me.z >= d)(lambda: event(me.z - d)))
        found.append(lambda d=d: pl.when(me.z + d < me.nz)(lambda: event(me.z + d)))
    return found + [lambda: event(me.z)]


def add(*refs):
    total = refs[0][...].astype(F32)
    for ref in refs[1:]:
        total = total + ref[...].astype(F32)
    return total


class Line:
    def __init__(self, me, column, from_below, from_above, ss, rs):
        self.me, self.column, self.zb, self.za, self.ss, self.rs = me, column, from_below, from_above, ss, rs

    def event(self, z):
        me = self.me
        for up in (True, False):
            buf, kind = (self.zb, 0) if up else (self.za, 1)
            first = me.z == 0 if up else me.z == me.nz - 1
            to = me.at(z=me.z + 1 if up else me.z - 1)

            @pl.when(z > me.z if up else z < me.z)
            def _():
                term = self.column(z)

                @pl.when(jnp.logical_not(first))
                def _():
                    landed(buf.at[z], self.ss.at[0, 0], self.rs.at[kind, z], me)
                    term[...] = add(term, buf.at[z]).astype(term.dtype)
                send(term, buf.at[z], self.ss.at[kind, z], self.rs.at[kind, z], to)

    def total(self, out):
        me = self.me
        out[...] = self.column(me.z)[...].astype(F32)
        for up in (True, False):
            buf, kind = (self.zb, 0) if up else (self.za, 1)

            @pl.when(me.z > 0 if up else me.z < me.nz - 1)
            def _():
                landed(buf.at[me.z], self.ss.at[0, 0], self.rs.at[kind, me.z], me)
                out[...] += buf.at[me.z][...].astype(F32)

    def drain(self):
        me = self.me

        def event(z):
            pl.when(z > me.z)(lambda: sent(self.zb.at[z], self.ss.at[0, z], self.rs.at[0, 0], me))
            pl.when(z < me.z)(lambda: sent(self.za.at[z], self.ss.at[1, z], self.rs.at[0, 0], me))
        return far_first(me, event)


class DpScatter:
    def __init__(self, me, part, out, ox, zb, za, ss, rs):
        self.me, self.part, self.out, self.ox, self.ss, self.rs = me, part, out, ox, ss, rs
        self.line = Line(me, lambda z: part.at[z * 2 + me.x], zb, za, ss, rs)

    def start(self, z):
        me = self.me
        send(self.part.at[z * 2 + 1 - me.x], self.ox.at[z], self.ss.at[2, z], self.rs.at[2, z], me.at(x=1 - me.x))

    def fold(self, z):
        me = self.me
        landed(self.ox.at[z], self.ss.at[0, 0], self.rs.at[2, z], me)
        mine = self.part.at[z * 2 + me.x]
        mine[...] = add(mine, self.ox.at[z]).astype(mine.dtype)
        self.line.event(z)

    def finish(self):
        self.line.total(self.out)

    def drain(self):
        return far_first(self.me, lambda z: sent(self.ox.at[z], self.ss.at[2, z], self.rs.at[0, 0], self.me)) + self.line.drain()


def head_columns(width):
    row = lax.broadcasted_iota(jnp.int32, (128, width), 0) * HEAD_DIM
    column = lax.broadcasted_iota(jnp.int32, (128, width), 1)
    return ((column >= row) & (column < row + HEAD_DIM)).astype(F32)


def exact(left, right):
    return jnp.dot(left, right, preferred_element_type=F32, precision=HIGH)


def exact_t(left, right):
    return lax.dot_general(left, right, (((1,), (1,)), ((), ())), preferred_element_type=F32, precision=HIGH)


def latent_kernel(dp_count, acc, stats, lat, gains, og_all, wo, wup, wdn,
                  lat_out, grad_hidden, do_all, stat_all, gwo, gwu, gwd, sums,
                  acc_in, stat_in, nf_all, og, wo_v, up_v, dn_v, ga, act, gp,
                  part_g, ox_g, zb_g, za_g, part_y, ox_y, zb_y, za_y, own_do, own_stat, row_a, row_b, do_in, st_in,
                  xs, xr, ls, gs, gr, gs2, gr2, gs3, gr3, ys, yr, ws, wr):
    me = Here(dp_count)
    seq_count = acc.shape[0]
    rows, width = lat.shape
    seq_peers = [lax.rem(me.seq + k, seq_count) for k in range(1, seq_count)]
    loads = [pltpu.make_async_copy(src, dst, ls.at[i]) for i, (src, dst) in enumerate(((wdn, dn_v), (og_all, og), (wo, wo_v), (wup, up_v)))]
    for load in loads:
        load.start()
    greet(dp_peers(me, dp_count) + [(me.dp, s) for s in seq_peers])
    for k, to in enumerate(seq_peers):
        send(acc.at[to], acc_in.at[me.seq], xs.at[0, k], xr.at[0, me.seq], (me.dp, to))
        send(stats.at[to], stat_in.at[me.seq], xs.at[1, k], xr.at[1, me.seq], (me.dp, to))
    acc_in[me.seq] = acc[me.seq]
    stat_in[me.seq] = stats[me.seq]
    loads[0].wait()
    loads[1].wait()
    hidden_cols = dn_v.shape[0]
    all_rows = dp_count * rows

    @pl.loop(0, hidden_cols // 256)
    def _(t):
        at = pl.ds(pl.multiple_of(t * 256, 256), 256)
        ga[:, at] = dot_t(og[...].reshape(all_rows, width), dn_v[at, :])
    for k, source in enumerate(seq_peers):
        landed(acc_in.at[source], xs.at[0, 0], xr.at[0, source], me)
        landed(stat_in.at[source], xs.at[0, 0], xr.at[1, source], me)
    tops = [stat_in[s, 0] for s in range(seq_count)]
    best = functools.reduce(jnp.maximum, tops)
    weights = [jnp.exp(top - best) for top in tops]
    total = sum(w * stat_in[s, 1] for s, w in enumerate(weights))
    lane = lax.broadcasted_iota(jnp.int32, total.shape, 1)
    total = jnp.where(lane < HEADS, total, 1.0)
    spread = head_columns(width)
    attended = sum(exact(w / total, spread) * acc_in[s].astype(F32) for s, w in enumerate(weights))
    row_a[...] = attended
    own_stat[0] = best + jnp.log(total)
    loads[2].wait()
    loads[3].wait()
    hidden = lat[...].astype(F32) + dot(attended.astype(BF16), wo_v[...])
    row_b[...] = hidden
    scaled, _ = scaled_rows(hidden)
    nf_all[me.dp] = (scaled * gains[4:5, :] + gains[5:6, :]).astype(BF16)
    spread_nf = Gather(me, nf_all.at[me.dp], nf_all, gs, gr, "zx", 0)
    run(spread_nf.own())
    run(spread_nf.column())
    run(spread_nf.neighbours())

    @pl.loop(0, hidden_cols // 256)
    def _(t):
        at = pl.ds(pl.multiple_of(t * 256, 256), 256)
        pre = dot(nf_all[...].reshape(all_rows, width), up_v[:, at])
        phi = 0.5 * (1.0 + lax.erf(pre * 0.7071067811865476))
        act[:, at] = (pre * phi).astype(BF16)
        slope = phi + pre * jnp.exp(pre * pre * -0.5) * 0.3989422804014327
        gp[:, at] = (ga[:, at] * slope).astype(BF16)

    @pl.loop(0, width // 512)
    def _(t):
        at = pl.ds(pl.multiple_of(t * 512, 512), 512)
        part_g[:, :, at] = dot_t(gp[...], up_v[at, :]).astype(BF16).reshape(dp_count, rows, 512)
    sum_g = DpScatter(me, part_g, own_do, ox_g, zb_g, za_g, gs2, gr2)
    run(far_first(me, sum_g.start))

    @pl.loop(0, width // 512)
    def _(t):
        at = pl.ds(pl.multiple_of(t * 512, 512), 512)
        part_y[:, :, at] = dot(act[...], dn_v[:, at]).astype(BF16).reshape(dp_count, rows, 512)
    run(far_first(me, sum_g.fold))
    sum_y = DpScatter(me, part_y, own_do, ox_y, zb_y, za_y, gs3, gr3)
    run(far_first(me, sum_y.start))
    gwd[...] = t_dot(act[...], og[...].reshape(all_rows, width)).astype(BF16)
    sum_g.finish()
    gathered = own_do[...]
    scaled, inverse = scaled_rows(row_b[...])
    sums[...] = jnp.zeros_like(sums)
    sums[0:1, :] = jnp.sum(gathered * scaled, axis=0, keepdims=True)
    sums[1:2, :] = jnp.sum(gathered, axis=0, keepdims=True)
    grad = og[me.dp].astype(F32) + norm_back(gathered, scaled, inverse, gains[4:5, :])
    grad_hidden[...] = grad
    low = grad.astype(BF16)
    grad_att = dot_t(low, wo_v[...]).astype(BF16)
    do_in[me.seq] = grad_att
    own_stat[1] = exact_t(grad_att.astype(F32) * row_a[...], spread)
    st_in[me.seq] = own_stat[...]
    spread_do = Gather(me, do_in.at[me.seq], do_in, ys, yr, "yc", 0)
    spread_st = Gather(me, st_in.at[me.seq], st_in, ws, wr, "yc", 0)
    run(spread_do.own())
    run(spread_st.own())
    run(far_first(me, sum_y.fold))
    gwo[...] = t_dot(row_a[...].astype(BF16), low).astype(BF16)
    run(spread_do.neighbours())
    run(spread_st.neighbours())
    gwu[...] = t_dot(nf_all[...].reshape(all_rows, width), gp[...]).astype(BF16)
    sum_y.finish()
    lat_out[...] = (row_b[...] + own_do[...]).astype(BF16)
    run(spread_do.sibling())
    run(spread_st.sibling())
    do_all[...] = do_in[...]
    stat_all[...] = st_in[...]
    for k, to in enumerate(seq_peers):
        sent(acc_in.at[0], xs.at[0, k], xr.at[0, 0], me)
        sent(stat_in.at[0], xs.at[1, k], xr.at[0, 0], me)
    for item in (spread_nf, sum_g, sum_y, spread_do, spread_st):
        run(item.drain())


def latent(dp_count, acc, stats, lat, gains, og_all, wo, wup, wdn):
    nz = dp_count // 2
    items, rows, width = acc.shape
    hidden = wdn.shape[0]
    shape = jax.ShapeDtypeStruct
    buf = lambda *s: pltpu.VMEM(s, BF16)
    all_rows = dp_count * rows
    gather_sems = [DMA((SEND_KINDS, nz)), DMA((RECV_KINDS, nz))]
    return pl.pallas_call(
        functools.partial(latent_kernel, dp_count),
        out_shape=(
            shape((rows, width), BF16), shape((rows, width), F32), shape((items, rows, width), BF16),
            shape((items, 2, rows, 128), F32), shape((width, width), BF16), shape((width, hidden), BF16),
            shape((hidden, width), BF16), shape((8, width), F32),
        ),
        in_specs=[VMEM] * 4 + [ANY] * 4,
        out_specs=tuple([VMEM] * 8),
        scratch_shapes=[
            buf(items, rows, width), pltpu.VMEM((items, 2, rows, 128), F32), buf(dp_count, rows, width), buf(dp_count, rows, width),
            buf(width, width), buf(width, hidden), buf(hidden, width),
            pltpu.VMEM((all_rows, hidden), F32), buf(all_rows, hidden), buf(all_rows, hidden),
            buf(dp_count, rows, width), buf(nz, rows, width), buf(nz, rows, width), buf(nz, rows, width),
            buf(dp_count, rows, width), buf(nz, rows, width), buf(nz, rows, width), buf(nz, rows, width),
            pltpu.VMEM((rows, width), F32), pltpu.VMEM((2, rows, 128), F32),
            pltpu.VMEM((rows, width), F32), pltpu.VMEM((rows, width), F32),
            buf(items, rows, width), pltpu.VMEM((items, 2, rows, 128), F32),
            DMA((2, items)), DMA((2, items)), DMA((4,)),
            *gather_sems, DMA((3, nz)), DMA((3, nz)), DMA((3, nz)), DMA((3, nz)), *gather_sems, *gather_sems,
        ],
        compiler_params=pltpu.CompilerParams(collective_id=1, has_side_effects=True, vmem_limit_bytes=WIDE),
    )(acc, stats, lat, gains, og_all, wo, wup, wdn)


class Scatter:
    def __init__(self, me, src, out, bufs, ss, rs, ls, lss, lrs):
        self.me, self.src, self.out, self.ss, self.rs, self.ls = me, src, out, ss, rs, ls
        self.acc, self.cbuf, self.x1, self.y1, self.ox, self.oy, zb, za = bufs
        self.half = src.shape[-1] // 2
        self.line = Line(me, lambda z: self.acc.at[z, me.x, me.y], zb, za, lss, lrs)

    def part(self, ref, half):
        return ref.at[:, pl.ds(half * self.half, self.half)]

    def load(self, z):
        return pltpu.make_async_copy(self.src.at[pl.ds(2 * z, 2), :, self.me.c], self.acc.at[z], self.ls.at[z])

    def begin(self):
        me = self.me

        def event(z):
            send(self.src.at[pl.ds(2 * z, 2), :, 1 - me.c], self.cbuf.at[z], self.ss.at[0, z], self.rs.at[0, z], me.at(c=1 - me.c))
            self.load(z).start()
        return far_first(me, event)

    def core(self):
        me = self.me

        def event(z):
            self.load(z).wait()
            landed(self.cbuf.at[z], self.ss.at[0, 0], self.rs.at[0, z], me)
            mine = self.acc.at[z]

            @pl.loop(0, 4)
            def _(i):
                x, y = i // 2, i % 2
                mine[x, y] = (mine[x, y].astype(F32) + self.cbuf[z, x, y].astype(F32)).astype(BF16)
            x_to, y_to = me.at(x=1 - me.x), me.at(y=1 - me.y)
            diag = mine.at[1 - me.x, 1 - me.y]
            send(self.part(diag, 0), self.x1.at[z], self.ss.at[1, z], self.rs.at[1, z], x_to)
            send(self.part(diag, 1), self.y1.at[z], self.ss.at[2, z], self.rs.at[2, z], y_to)
            send(self.part(mine.at[1 - me.x, me.y], 0), self.part(self.ox.at[z], 0), self.ss.at[3, z], self.rs.at[3, z], x_to)
            send(self.part(mine.at[me.x, 1 - me.y], 1), self.part(self.oy.at[z], 1), self.ss.at[4, z], self.rs.at[4, z], y_to)
        return far_first(me, event)

    def middle(self):
        me = self.me

        def event(z):
            landed(self.x1.at[z], self.ss.at[0, 0], self.rs.at[1, z], me)
            ref = self.part(self.acc.at[z, me.x, 1 - me.y], 0)
            ref[...] = add(ref, self.x1.at[z]).astype(BF16)
            send(ref, self.part(self.oy.at[z], 0), self.ss.at[5, z], self.rs.at[5, z], me.at(y=1 - me.y))
            landed(self.y1.at[z], self.ss.at[0, 0], self.rs.at[2, z], me)
            ref = self.part(self.acc.at[z, 1 - me.x, me.y], 1)
            ref[...] = add(ref, self.y1.at[z]).astype(BF16)
            send(ref, self.part(self.ox.at[z], 1), self.ss.at[6, z], self.rs.at[6, z], me.at(x=1 - me.x))
        return far_first(me, event)

    def fold(self):
        me = self.me

        def event(z):
            for kind, ref in ((3, self.part(self.ox.at[z], 0)), (4, self.part(self.oy.at[z], 1)),
                              (5, self.part(self.oy.at[z], 0)), (6, self.part(self.ox.at[z], 1))):
                landed(ref, self.ss.at[0, 0], self.rs.at[kind, z], me)
            mine = self.acc.at[z, me.x, me.y]
            mine[...] = add(mine, self.ox.at[z], self.oy.at[z]).astype(BF16)
            self.line.event(z)
        return far_first(me, event)

    def finish(self):
        return [lambda: self.line.total(self.out)]

    def drain(self):
        me = self.me

        def event(z):
            sent(self.cbuf.at[z], self.ss.at[0, z], self.rs.at[0, 0], me)
            for kind in range(1, 7):
                sent(self.x1.at[z], self.ss.at[kind, z], self.rs.at[0, 0], me)
        return far_first(me, event) + self.line.drain()

    def phases(self):
        return [self.begin(), self.core(), self.middle(), self.fold(), self.finish(), self.drain()]

    @staticmethod
    def scratch(nz, rows, cols):
        buf = lambda *s: pltpu.VMEM(s + (rows, cols), BF16)
        half = pltpu.VMEM((nz, rows, cols // 2), BF16)
        return [buf(nz, 2, 2), buf(nz, 2, 2), half, half, buf(nz), buf(nz), buf(nz), buf(nz),
                DMA((7, nz)), DMA((7, nz)), DMA((nz,)), DMA((2, nz)), DMA((2, nz))]


class SeqScatter:
    def __init__(self, me, src, then, acc, cbuf, oy, ss, rs, ls):
        self.me, self.src, self.then, self.acc, self.cbuf, self.oy = me, src, then, acc, cbuf, oy
        self.ss, self.rs = ss, rs
        self.load = pltpu.make_async_copy(src.at[:, :, me.c], acc, ls.at[0])

    def begin(self):
        me = self.me
        send(self.src.at[:, :, 1 - me.c], self.cbuf, self.ss.at[0], self.rs.at[0], me.at(c=1 - me.c))
        self.load.start()

    def core(self):
        me = self.me
        self.load.wait()
        landed(self.cbuf, self.ss.at[0], self.rs.at[0], me)

        @pl.loop(0, self.acc.shape[0])
        def _(i):
            for y in (0, 1):
                self.acc[i, y] = (self.acc[i, y].astype(F32) + self.cbuf[i, y].astype(F32)).astype(BF16)
        send(self.acc.at[:, 1 - me.y], self.oy, self.ss.at[1], self.rs.at[1], me.at(y=1 - me.y))

    def fold(self):
        me = self.me
        landed(self.oy, self.ss.at[0], self.rs.at[1], me)

        @pl.loop(0, self.acc.shape[0])
        def _(i):
            self.oy[i] = (self.acc[i, me.y].astype(F32) + self.oy[i].astype(F32)).astype(BF16)

    def finish(self):
        self.then(self.oy)

    def drain(self):
        sent(self.cbuf, self.ss.at[0], self.rs.at[0], self.me)
        sent(self.oy, self.ss.at[1], self.rs.at[0], self.me)

    def phases(self):
        return [[self.begin], [self.core], [self.fold], [self.finish], [self.drain]]

    @staticmethod
    def scratch(count, rows, cols):
        buf = lambda *s: pltpu.VMEM(s + (rows, cols), BF16)
        return [buf(count, 2), buf(count, 2), buf(count), DMA((2,)), DMA((2,)), DMA((1,))]


class Regrouped(SeqScatter):
    def __init__(self, me, dp_count, src, out, inbox, up_ss, up_rs, *rest):
        super().__init__(me, src, self.pass_on, *rest)
        self.n, self.out, self.inbox, self.up_ss, self.up_rs = dp_count, out, inbox, up_ss, up_rs

    def pass_on(self, total):
        me = self.me
        for k in range(1, self.n):
            to = lax.rem(me.dp + k, self.n)
            send(total.at[to], self.inbox.at[me.dp], self.up_ss.at[to], self.up_rs.at[me.dp], (to, me.seq))
        self.inbox[me.dp] = total[me.dp]

    def collect(self):
        cols = self.inbox.shape[2]
        for dp in range(self.n):
            pl.when(dp != self.me.dp)(lambda: landed(self.inbox.at[dp], self.up_ss.at[0], self.up_rs.at[dp], self.me))
            self.out[:, dp * cols:(dp + 1) * cols] = self.inbox[dp].astype(F32)

    def drain(self):
        super().drain()
        for k in range(1, self.n):
            sent(self.inbox.at[0], self.up_ss.at[lax.rem(self.me.dp + k, self.n)], self.up_rs.at[0], self.me)

    def phases(self):
        return [[self.begin], [self.core], [self.fold], [self.finish], [self.collect], [self.drain]]

    @staticmethod
    def scratch(count, rows, cols):
        return [pltpu.VMEM((count, rows, cols), BF16), DMA((count,)), DMA((count,))] + SeqScatter.scratch(count, rows, cols)


class SumAll:
    def __init__(self, me, ref, inbox, ss, rs):
        self.me, self.ref, self.inbox, self.ss, self.rs = me, ref, inbox, ss, rs

    def step(self, i, to):
        def begin():
            send(self.ref.at[i], self.inbox.at[i], self.ss.at[i], self.rs.at[i], to)

        def end():
            landed(self.inbox.at[i], self.ss.at[0], self.rs.at[i], self.me)
            self.ref[i + 1] = self.ref[i] + self.inbox[i]
        return begin, end

    def phases(self):
        me = self.me
        n = me.nz

        def begin_z():
            for k in range(1, n):
                to = lax.rem(me.z + k, n)
                send(self.ref.at[3], self.inbox.at[2 + k], self.ss.at[2 + k], self.rs.at[2 + k], me.at(z=to))

        def end_z():
            total = self.ref[3]
            for k in range(1, n):
                landed(self.inbox.at[2 + k], self.ss.at[0], self.rs.at[2 + k], me)
                total = total + self.inbox[2 + k]
            self.ref[4] = total

        def drain():
            for i in range(2 + n):
                sent(self.ref.at[0], self.ss.at[i], self.rs.at[0], me)
        first = self.step(0, me.at(c=1 - me.c))
        second = self.step(1, me.at(x=1 - me.x))
        third = self.step(2, me.at(y=1 - me.y))
        both = lambda one, other: (lambda: (one(), other()))
        return [[e] for e in (first[0], both(first[1], second[0]), both(second[1], third[0]), both(third[1], begin_z), end_z, drain)]


def back_kernel(dp_count, block_rows, owner, n_ref, nl_ref, q_ref, k_ref, v_ref, do_ref, stats, gwo, gwu, gwd,
                gwq, gwk, gwv, dq, dk, dv, out_o, out_up, out_dn, gw_buf, dq_acc, *scratch):
    me = Here(dp_count)
    items, lat_rows, width = q_ref.shape
    rows = n_ref.shape[0]
    half = width // 2
    o_s, up_s, dn_s, gw_sem = scratch[:13], scratch[13:22], scratch[22:28], scratch[28]

    def down(total):
        out_dn[...] = total[0].astype(F32)
    events = skewed([
        Scatter(me, gwo, out_o, o_s[:8], *o_s[8:]), Regrouped(me, dp_count, gwu, out_up, *up_s), SeqScatter(me, gwd, down, *dn_s)])
    greet(dp_peers(me, dp_count) + [me.at(y=1 - me.y), me.at(c=1 - me.c)])
    mask = part_mask(lat_rows)
    lane = lax.broadcasted_iota(jnp.int32, (lat_rows, 128), 1)
    key = lax.broadcasted_iota(jnp.int32, (PART * lat_rows, block_rows), 1)
    blocks, parts = rows // block_rows, HEADS // PART
    dq_acc[...] = jnp.zeros_like(dq_acc)

    def replicated(stat, part):
        pieces = []
        for h in range(PART):
            column = jnp.sum(jnp.where(lane == part * PART + h, stat, 0.0), axis=-1, keepdims=True)
            pieces.append(jnp.broadcast_to(column, (lat_rows, 128)))
        return jnp.concatenate(pieces, axis=0)

    def block(b, part, item):
        cols = pl.ds(pl.multiple_of(part * PCOLS, 128), PCOLS)
        at = pl.ds(pl.multiple_of(b * block_rows, block_rows), block_rows)
        query, grad = stacked(q_ref[item, :, cols], mask), stacked(do_ref[item, :, cols], mask)
        keys, values = k_ref[at, cols], v_ref[at, cols]
        lse, delta = replicated(stats[item, 0], part), replicated(stats[item, 1], part)
        prob = jnp.exp(dot_t(query, keys) * SCALE - lse)
        prob = jnp.where(key < jnp.where(b == blocks - 1, lat_rows, block_rows), prob, 0.0)
        score = (prob * (dot_t(grad, values) - delta)).astype(BF16)
        dk[at, cols] = (t_dot(score, query) * SCALE).astype(BF16)
        dv[at, cols] = t_dot(prob.astype(BF16), grad).astype(BF16)
        term = unstacked(dot(score, keys), mask, lat_rows) * SCALE
        for i in range(items):
            dq_acc[i, :, cols] += jnp.where(item == i, term, 0.0)
    first, second = events[:len(events) * 2 // 3], events[len(events) * 2 // 3:]
    steps = blocks * parts // 2
    shares = share(first, steps)

    @pl.loop(0, steps)
    def _(i):
        b, pair = i // (parts // 2), i % (parts // 2)
        run_at(i, shares)
        item = owner[b]
        block(b, pair * 2, item)
        block(b, pair * 2 + 1, item)
    dq[...] = dq_acc[...].astype(BF16)
    tile = 512
    shares = share(second, 2 * width // tile)

    @pl.loop(0, 2 * width // tile)
    def _(i):
        run_at(i, shares)
        row = pl.ds(pl.multiple_of((i // 2) * tile, tile), tile)
        col = pl.ds(pl.multiple_of((i % 2) * half, 128), half)
        gw_buf[0, row, col] = t_dot(nl_ref[:, row], dq_flat(dq, col, items, lat_rows)).astype(BF16)
        gw_buf[1, row, col] = t_dot(n_ref[:, row], dk[:, col]).astype(BF16)
        gw_buf[2, row, col] = t_dot(n_ref[:, row], dv[:, col]).astype(BF16)
    copies = [pltpu.make_async_copy(gw_buf.at[w], out, gw_sem.at[w]) for w, out in enumerate((gwq, gwk, gwv))]
    for copy in copies:
        copy.start()
    for copy in copies:
        copy.wait()


def dq_flat(dq, cols, items, lat_rows):
    return dq[:, :, cols].reshape(items * lat_rows, dq.shape[2] // 2)


def back(dp_count, owner, n, nl, q, k, v, do_all, stats, gwo, gwu, gwd, block_rows):
    nz = dp_count // 2
    items, lat_rows, width = q.shape
    hidden = gwu.shape[1]
    count = dp_count * 4
    shape = jax.ShapeDtypeStruct
    arrays = (owner, n, nl, q, k, v, do_all, stats, gwo.reshape(dp_count, 2, 2, width // count, width),
              gwu.reshape(dp_count, 2, 2, width // count, hidden), gwd.reshape(1, 2, 2, hidden // 4, width))
    return pl.pallas_call(
        functools.partial(back_kernel, dp_count, block_rows),
        out_shape=(
            *[shape((width, width), BF16)] * 3, shape(q.shape, BF16), shape(n.shape, BF16), shape(n.shape, BF16),
            shape((width // count, width), F32), shape((width // count, hidden * dp_count), F32), shape((hidden // 4, width), F32),
        ),
        in_specs=[pl.BlockSpec(memory_space=pltpu.SMEM)] + [VMEM] * 7 + [ANY] * 3,
        out_specs=tuple([ANY] * 3 + [VMEM] * 6),
        scratch_shapes=[
            pltpu.VMEM((3, width, width), BF16), pltpu.VMEM(q.shape, F32),
            *Scatter.scratch(nz, width // count, width), *Regrouped.scratch(dp_count, width // count, hidden),
            *SeqScatter.scratch(1, hidden // 4, width), DMA((3,)),
        ],
        compiler_params=pltpu.CompilerParams(collective_id=2, has_side_effects=True, vmem_limit_bytes=WIDE),
    )(*arrays)


def close_kernel(dp_count, block_rows, media, lat, grad_hidden, gains, sums_ffn, dq, dk, dv, wq, wk, wv, gwq, gwk, gwv,
                 media_grad, lat_grad, sums, out_q, out_k, out_v, w_ref, g_ref, gq_ref, sums_ref, *scratch):
    me = Here(dp_count)
    items, lat_rows, width = dq.shape
    media_rows = media.shape[0]
    small, lat_s, load_sem, out_sem = scratch[39:43], scratch[43:49], scratch[49], scratch[50]
    fulls = [scratch[13 * i:13 * i + 13] for i in range(3)]
    loads = [pltpu.make_async_copy(w, w_ref.at[i], load_sem.at[i]) for i, w in enumerate((wq, wk, wv))]
    for load in loads:
        load.start()
    greet(dp_peers(me, dp_count) + [me.at(y=1 - me.y), me.at(c=1 - me.c)])
    all_sum = SumAll(me, *small)

    def latents(total):
        scaled, inverse = scaled_rows(lat[...].astype(F32))
        grad = total[0].astype(F32)
        lat_grad[...] = grad_hidden[...] + norm_back(grad, scaled, inverse, gains[0:1, :])
        first = small[0]
        first[0, 0:1, :] = jnp.sum(grad * scaled, axis=0, keepdims=True)
        first[0, 1:2, :] = jnp.sum(grad, axis=0, keepdims=True)
        first[0, 2:4, :] = sums_ref[0:2, :]
        first[0, 4:6, :] = sums_ffn[0:2, :]
        first[0, 6:8, :] = jnp.zeros_like(sums_ffn[0:2, :])
    lat_item = SeqScatter(me, gq_ref, latents, *lat_s)
    fulls = [Scatter(me, src, out, f[:8], *f[8:]) for src, out, f in zip((gwk, gwv, gwq), (out_k, out_v, out_q), fulls)]
    events = skewed(fulls)
    begins = [e for f in fulls for e in f.begin()]
    count = len(fulls[0].begin())
    run(begins[:count])
    events = events[count:]
    mine = [lat_item.begin, lat_item.core, lat_item.fold]
    end = [e for phase in all_sum.phases() for e in phase]
    tile = 256
    steps = width // tile
    early, late = events[:len(events) * 2 // 5], events[len(events) * 2 // 5:]
    for load in loads:
        load.wait()
    shares = share(early, steps)

    @pl.loop(0, steps)
    def _(t):
        run_at(t, shares)
        at = pl.ds(pl.multiple_of(t * tile, tile), tile)
        grad = dot_t(dk[...], w_ref[1, at, :]) + dot_t(dv[...], w_ref[2, at, :])
        g_ref[:, at] = grad[:media_rows]
        own = dot_t(dq[...].reshape(items * lat_rows, width), w_ref[0, at, :])
        for i in range(items):
            term = own[i * lat_rows:(i + 1) * lat_rows]
            gq_ref[0, i // 2, i % 2, :, at] = jnp.where(me.seq == i, term + grad[media_rows:media_rows + lat_rows], term).astype(BF16)
    lat_item.begin()
    sums_ref[...] = jnp.zeros_like(sums_ref)
    blocks = media_rows // block_rows
    shares = share(late[:len(late) // 3], blocks)

    def out_copy(rows):
        return pltpu.make_async_copy(g_ref.at[rows, :], media_grad.at[rows, :], out_sem)

    @pl.loop(0, blocks)
    def _(b):
        run_at(b, shares)
        rows = pl.ds(pl.multiple_of(b * block_rows, block_rows), block_rows)
        u, inverse = scaled_rows(media[rows, :].astype(F32))
        g = g_ref[rows, :]
        g_ref[rows, :] = norm_back(g, u, inverse, gains[2:3, :])
        out_copy(rows).start()
        sums_ref[0:1, :] += jnp.sum(g * u, axis=0, keepdims=True)
        sums_ref[1:2, :] += jnp.sum(g, axis=0, keepdims=True)
    lat_item.core()
    rest = late[len(late) // 3:]
    own = [lat_item.fold, lat_item.finish, lat_item.drain] + end
    for event, extra in zip(share(rest, len(own)), own):
        run(event)
        extra()
    sums[...] = small[0][4]
    out_copy(pl.ds(0, media_rows)).wait()


def close(dp_count, media, lat, grad_hidden, gains, sums_ffn, dq, dk, dv, wq, wk, wv, gwq, gwk, gwv, block_rows):
    nz = dp_count // 2
    items, lat_rows, width = dq.shape
    count = dp_count * 4
    shape = jax.ShapeDtypeStruct
    square = lambda g: g.reshape(dp_count, 2, 2, width // count, width)
    return pl.pallas_call(
        functools.partial(close_kernel, dp_count, block_rows),
        out_shape=(
            shape(media.shape, F32), shape((lat_rows, width), F32), shape((8, width), F32), *[shape((width // count, width), F32)] * 3,
        ),
        in_specs=[VMEM] * 8 + [ANY] * 6,
        out_specs=tuple([ANY] + [VMEM] * 5),
        scratch_shapes=[
            pltpu.VMEM((3, width, width), BF16), pltpu.VMEM(media.shape, F32), pltpu.VMEM((1, 2, 2, lat_rows, width), BF16), pltpu.VMEM((8, width), F32),
            *(Scatter.scratch(nz, width // count, width) * 3),
            pltpu.VMEM((5, 8, width), F32), pltpu.VMEM((2 + nz, 8, width), F32), DMA((2 + nz,)), DMA((2 + nz,)),
            *SeqScatter.scratch(1, lat_rows, width), DMA((3,)), DMA,
        ],
        compiler_params=pltpu.CompilerParams(collective_id=3, has_side_effects=True, vmem_limit_bytes=WIDE),
    )(media, lat, grad_hidden, gains, sums_ffn, dq, dk, dv, wq, wk, wv, square(gwq), square(gwk), square(gwv))


def copy_kernel(*refs):
    n = (len(refs) - 2) // 3
    arrays, outs, held, first, second = refs[:n], refs[n:2 * n], refs[2 * n:3 * n], refs[-2], refs[-1]
    ins = [pltpu.make_async_copy(arrays[i], held[i], first.at[i]) for i in range(n)]
    backs = [pltpu.make_async_copy(held[i], outs[i], second.at[i]) for i in range(n)]
    for copy in ins:
        copy.start()
    for copy, after in zip(ins, backs):
        copy.wait()
        after.start()
    for copy in backs:
        copy.wait()


def copied(*arrays):
    n = len(arrays)
    return pl.pallas_call(
        copy_kernel, out_shape=tuple(jax.ShapeDtypeStruct(a.shape, a.dtype) for a in arrays),
        in_specs=[ANY] * n, out_specs=tuple([ANY] * n),
        scratch_shapes=[*[pltpu.VMEM(a.shape, a.dtype) for a in arrays], DMA((n,)), DMA((n,))],
        compiler_params=pltpu.CompilerParams(vmem_limit_bytes=WIDE),
    )(*arrays)


def ordered(items, starts):
    lists = [item.phases() for item in items]
    found, ends, tails = [], [0] * len(items), []
    for step in range(max(s + len(p) for s, p in zip(starts, lists))):
        for i, (begin, phases) in enumerate(zip(starts, lists)):
            k = step - begin
            if 0 <= k < len(phases) - 1:
                found += phases[k]
                ends[i] = len(found)
    for phases in lists:
        tails += phases[-1]
    return found, ends, tails


class Cursor:
    def __init__(self, events):
        self.events, self.done = events, 0

    def upto(self, mark):
        run(self.events[self.done:mark])
        self.done = max(self.done, mark)

    def spread(self, mark, steps):
        mark = max(mark, self.done)
        lists = share(self.events[self.done:mark], steps)
        self.done = mark
        return lists


def unpacked(packs, own_cols):
    count = packs.shape[0]
    group = 8
    rows = []
    for g in range(count // group):
        left = jnp.concatenate([packs[g * group + i] for i in range(group)], axis=1).astype(BF16)
        row = lax.broadcasted_iota(jnp.int32, (group * 128, group * own_cols), 0)
        column = lax.broadcasted_iota(jnp.int32, (group * 128, group * own_cols), 1)
        piece, place = row // 128, row % 128
        chosen = (place < own_cols) & (column == piece * own_cols + place)
        rows.append(dot(left, jnp.where(chosen, 1.0, 0.0).astype(BF16)))
    return jnp.concatenate(rows, axis=1)


def forward_kernel(dp_count, block_rows, own_cols, owner, media, pack, lat, sq, sk, sv, so, sg, sd, su,
                   wq, wk, wv, n_out, nl_out, q_out, k_out, v_out, gwo, gwu, gwd,
                   gains, lat_out, grad_hidden, do_all, stat_all, sums,
                   packs, lat_all, wo, og, dn, up, med, n, nl, q, k, v, expo, acc_f, acc, tops, stats, wbuf,
                   acc_in, stat_in, nf_all, ga, act, gp, part_g, ox_g, zb_g, za_g, part_y, ox_y, zb_y, za_y,
                   own_sum, row_a, row_b, do_in, st_in, gwo_v, gwu_v, gwd_v,
                   ss, rs, rss, rrs, es, er, local, ws, ms, outs, xs, xr, gs, gr, gs2, gr2, gs3, gr3, ys, yr, zs, zr):
    me = Here(dp_count)
    seq_count, lat_rows, width = lat_all.shape
    half = width // 2
    seq_peers = [lax.rem(me.seq + i, seq_count) for i in range(1, seq_count)]
    blocks, parts = n.shape[0] // block_rows, HEADS // PART
    media_rows = media.shape[0]
    greet_all(me, dp_count)
    gather = lambda i, src, dst, axes, halves: Gather(me, src, dst, ss.at[i], rs.at[i], axes, halves)
    regroup = Regroup(me, dp_count, su, up, rss, rrs, up.shape[2])
    items = [
        Everyone(me, dp_count, pack, packs, es, er), gather(0, lat, lat_all, "yc", 0),
        gather(1, sk, wk, "zxyc", half), gather(2, sq, wq, "zxyc", half), gather(3, sv, wv, "zxyc", half),
        gather(4, so, wo, "zxyc", half), gather(5, sg, og, "zx", 0), gather(6, sd, dn, "yc", 0), regroup,
    ]
    own = [(pack, packs.at[items[0].index])]
    own += [(src, item.shard(me.z, me.x, me.y, me.c)) for src, item in zip((lat, sk, sq, sv, so, sg, sd), items[1:8])]
    own += [(regroup.columns(me.dp), regroup.piece(me.dp, me.y, me.c))]
    own = [pltpu.make_async_copy(src, dst, local.at[i]) for i, (src, dst) in enumerate(own)]
    for copy in own:
        copy.start()
    events, (m_pack, m_lat, m_k, m_q, m_v, m_o, m_g, m_d, m_u), drains = ordered(items, (0, 0, 0, 0, 1, 3, 5, 5, 5))
    cursor = Cursor(events)

    def media_load(b):
        rows = pl.ds(pl.multiple_of(b * block_rows, block_rows), block_rows)
        slot = lax.rem(b, 2)
        return pltpu.make_async_copy(media.at[rows, :], med.at[slot], ms.at[slot])
    media_load(0).start()
    cursor.upto(max(m_pack, m_lat))
    for copy in own:
        copy.wait()
    gains[...] = unpacked(packs, own_cols)

    shares = cursor.spread(cursor.done + (m_k - cursor.done) * 2 // 3, blocks - 1)

    @pl.loop(0, blocks - 1)
    def _(b):
        run_at(b, shares)
        pl.when(b + 1 < blocks - 1)(lambda: media_load(b + 1).start())
        media_load(b).wait()
        u, _ = scaled_rows(med[lax.rem(b, 2)].astype(F32))
        n[pl.ds(pl.multiple_of(b * block_rows, block_rows), block_rows), :] = (u * gains[2:3, :] + gains[3:4, :]).astype(BF16)
    u, _ = scaled_rows(lat_all[...].reshape(seq_count * lat_rows, width).astype(F32))
    nl[...] = (u * gains[0:1, :] + gains[1:2, :]).astype(BF16).reshape(nl.shape)
    n[pl.ds(media_rows, lat_rows), :] = nl[me.seq]
    n[pl.ds(media_rows + lat_rows, block_rows - lat_rows), :] = jnp.zeros((block_rows - lat_rows, width), BF16)

    def weight(w, i):
        return pltpu.make_async_copy(w.at[:, :, pl.ds(pl.multiple_of(i * half, 128), half)], wbuf.at[i], ws.at[i])

    def project(rows, w, out, mark):
        for i in range(2):
            weight(w, i).start()
        shares = cursor.spread(mark, 2)

        @pl.loop(0, 2)
        def _(i):
            run_at(i, shares)
            weight(w, i).wait()
            cols = pl.ds(pl.multiple_of(i * half, 128), half)
            out[:, cols] = dot(rows[...], wbuf[i].reshape(width, half)).astype(BF16)
    cursor.upto(m_k)
    project(n, wk, k, cursor.done + (m_q - cursor.done) * 2 // 3)
    cursor.upto(m_q)
    project(nl.reshape(seq_count * lat_rows, width), wq, q.reshape(seq_count * lat_rows, width), cursor.done + 2)
    mask = part_mask(lat_rows)
    lane = lax.broadcasted_iota(jnp.int32, (lat_rows, 128), 1)
    key = lax.broadcasted_iota(jnp.int32, (PART * lat_rows, block_rows), 1)

    def scores(b, part, item):
        cols = pl.ds(pl.multiple_of(part * PCOLS, 128), PCOLS)
        at = pl.ds(pl.multiple_of(b * block_rows, block_rows), block_rows)
        found = dot_t(stacked(q[item, :, cols], mask), k[at, cols]) * SCALE
        return jnp.where(key < jnp.where(b == blocks - 1, lat_rows, block_rows), found, NEG)

    def replicated(stat, part):
        pieces = []
        for h in range(PART):
            column = jnp.sum(jnp.where(lane == part * PART + h, stat, 0.0), axis=-1, keepdims=True)
            pieces.append(jnp.broadcast_to(column, (lat_rows, 128)))
        return jnp.concatenate(pieces, axis=0)

    def place(stat, column, part):
        for h in range(PART):
            stat = jnp.where(lane == part * PART + h, column[h * lat_rows:(h + 1) * lat_rows], stat)
        return stat
    steps = blocks * parts // 2
    tops[...] = jnp.zeros_like(tops)
    shares = cursor.spread(cursor.done + (m_v - cursor.done) // 2, steps)

    @pl.loop(0, steps)
    def _(i):
        b, pair = i // (parts // 2), i % (parts // 2)
        run_at(i, shares)
        item = owner[b]
        for part in (pair * 2, pair * 2 + 1):
            tops[b, 0] = place(tops[b, 0], jnp.max(scores(b, part, item), axis=-1, keepdims=True), part)
    for i in range(seq_count):
        best = jnp.full((lat_rows, 128), NEG, F32)
        for b in range(blocks):
            best = jnp.maximum(best, jnp.where(owner[b] == i, tops[b, 0], NEG))
        stats[i, 0] = best
    shares = cursor.spread(cursor.done + (m_v - cursor.done) // 2, steps)

    @pl.loop(0, steps)
    def _(i):
        b, pair = i // (parts // 2), i % (parts // 2)
        run_at(i, shares)
        item = owner[b]
        for part in (pair * 2, pair * 2 + 1):
            e = jnp.exp(scores(b, part, item) - replicated(stats[item, 0], part))
            expo[b, part] = e.astype(BF16)
            tops[b, 1] = place(tops[b, 1], jnp.sum(e, axis=-1, keepdims=True), part)
    for i in range(seq_count):
        stats[i, 1] = sum(jnp.where(owner[b] == i, tops[b, 1], 0.0) for b in range(blocks))
    acc_f[...] = jnp.zeros_like(acc_f)
    cursor.upto(m_v)
    project(n, wv, v, cursor.done + 4)
    saves = [(n, n_out), (nl, nl_out), (q, q_out), (k, k_out), (v, v_out)]
    saves = [pltpu.make_async_copy(src, dst, outs.at[i]) for i, (src, dst) in enumerate(saves)]
    for copy in saves:
        copy.start()
    shares = cursor.spread(cursor.done + (m_o - cursor.done) // 2, steps)

    @pl.loop(0, steps)
    def _(i):
        b, pair = i // (parts // 2), i % (parts // 2)
        run_at(i, shares)
        item = owner[b]
        for part in (pair * 2, pair * 2 + 1):
            cols = pl.ds(pl.multiple_of(part * PCOLS, 128), PCOLS)
            at = pl.ds(pl.multiple_of(b * block_rows, block_rows), block_rows)
            term = unstacked(dot(expo[b, part], v[at, cols]), mask, lat_rows)
            for j in range(seq_count):
                acc_f[j, :, cols] += jnp.where(item == j, term, 0.0)
    acc[...] = acc_f[...].astype(BF16)
    for i, to in enumerate(seq_peers):
        send(acc.at[to], acc_in.at[me.seq], xs.at[0, i], xr.at[0, me.seq], (me.dp, to))
        send(stats.at[to], stat_in.at[me.seq], xs.at[1, i], xr.at[1, me.seq], (me.dp, to))
    acc_in[me.seq] = acc[me.seq]
    stat_in[me.seq] = stats[me.seq]
    cursor.upto(m_o)
    for source in seq_peers:
        landed(acc_in.at[source], xs.at[0, 0], xr.at[0, source], me)
        landed(stat_in.at[source], xs.at[0, 0], xr.at[1, source], me)
    best = functools.reduce(jnp.maximum, [stat_in[s, 0] for s in range(seq_count)])
    weights = [jnp.exp(stat_in[s, 0] - best) for s in range(seq_count)]
    total = sum(w * stat_in[s, 1] for s, w in enumerate(weights))
    total = jnp.where(lane < HEADS, total, 1.0)
    spread = head_columns(width)
    attended = sum(exact(w / total, spread) * acc_in[s].astype(F32) for s, w in enumerate(weights))
    row_a[...] = attended
    st_in[me.seq, 0] = best + jnp.log(total)
    hidden = lat_all[me.seq].astype(F32) + dot(attended.astype(BF16), wo[...].reshape(width, width))
    row_b[...] = hidden
    scaled, _ = scaled_rows(hidden)
    nf_all[me.dp] = (scaled * gains[4:5, :] + gains[5:6, :]).astype(BF16)
    spread_nf = Gather(me, nf_all.at[me.dp], nf_all, gs, gr, "zx", 0)
    run(spread_nf.own())
    cursor.upto(max(m_g, m_d))
    all_rows = dp_count * lat_rows
    hidden_cols = gp.shape[1]
    og_all = lambda: og[...].reshape(all_rows, width)
    tile = hidden_cols // 2
    per = seq_count // 2

    @pl.loop(0, 2)
    def _(t):
        at = pl.ds(pl.multiple_of(t * tile, 128), tile)
        ga[:, at] = dot_t(og_all(), dn[pl.ds(t * per, per)].reshape(tile, width))
    run(spread_nf.column())
    cursor.upto(len(events))
    run(spread_nf.neighbours())

    @pl.loop(0, 2)
    def _(t):
        at = pl.ds(pl.multiple_of(t * tile, 128), tile)
        pre = dot(nf_all[...].reshape(all_rows, width), up[:, :, at].reshape(width, tile))
        phi = 0.5 * (1.0 + lax.erf(pre * 0.7071067811865476))
        act[:, at] = (pre * phi).astype(BF16)
        slope = phi + pre * jnp.exp(pre * pre * -0.5) * 0.3989422804014327
        gp[:, at] = (ga[:, at] * slope).astype(BF16)
    group = up.shape[0] // 4
    wide = width // 4

    @pl.loop(0, 4)
    def _(t):
        at = pl.ds(pl.multiple_of(t * wide, 128), wide)
        part_g[:, :, at] = dot_t(gp[...], up[pl.ds(t * group, group)].reshape(wide, hidden_cols)).astype(BF16).reshape(dp_count, lat_rows, wide)
    sum_g = DpScatter(me, part_g, own_sum, ox_g, zb_g, za_g, gs2, gr2)
    run(far_first(me, sum_g.start))

    @pl.loop(0, 3)
    def _(t):
        at = pl.ds(pl.multiple_of(t * 512, 512), 512)
        part_y[:, :, at] = dot(act[...], dn[:, :, at].reshape(hidden_cols, 512)).astype(BF16).reshape(dp_count, lat_rows, 512)
    run(far_first(me, sum_g.fold))
    sum_y = DpScatter(me, part_y, own_sum, ox_y, zb_y, za_y, gs3, gr3)
    run(far_first(me, sum_y.start))
    gwd_v[...] = t_dot(act[...], og_all()).astype(BF16)
    save_d = pltpu.make_async_copy(gwd_v, gwd, outs.at[5])
    save_d.start()
    sum_g.finish()
    gathered = own_sum[...]
    scaled, inverse = scaled_rows(row_b[...])
    sums[...] = jnp.zeros_like(sums)
    sums[0:1, :] = jnp.sum(gathered * scaled, axis=0, keepdims=True)
    sums[1:2, :] = jnp.sum(gathered, axis=0, keepdims=True)
    grad = og[me.dp].astype(F32) + norm_back(gathered, scaled, inverse, gains[4:5, :])
    grad_hidden[...] = grad
    low = grad.astype(BF16)
    grad_att = dot_t(low, wo[...].reshape(width, width)).astype(BF16)
    do_in[me.seq] = grad_att
    st_in[me.seq, 1] = exact_t(grad_att.astype(F32) * row_a[...], spread)
    spread_do = Gather(me, do_in.at[me.seq], do_in, ys, yr, "yc", 0)
    spread_st = Gather(me, st_in.at[me.seq], st_in, zs, zr, "yc", 0)
    run(spread_do.own())
    run(spread_st.own())
    run(far_first(me, sum_y.fold))
    save_o = []
    for i in range(2):
        cols = pl.ds(i * half, half)
        if i:
            save_o[0].wait()
        gwo_v[...] = t_dot(row_a[...].astype(BF16), low[:, i * half:(i + 1) * half]).astype(BF16)
        save_o.append(pltpu.make_async_copy(gwo_v, gwo.at[:, cols], outs.at[6 + i]))
        save_o[-1].start()
    run(spread_do.neighbours())
    run(spread_st.neighbours())
    gwu_v[...] = t_dot(nf_all[...].reshape(all_rows, width), gp[...]).astype(BF16)
    save_u = pltpu.make_async_copy(gwu_v, gwu, outs.at[8])
    save_u.start()
    sum_y.finish()
    lat_out[...] = (row_b[...] + own_sum[...]).astype(BF16)
    run(spread_do.sibling())
    run(spread_st.sibling())
    do_all[...] = do_in[...]
    stat_all[...] = st_in[...]
    for i in range(len(seq_peers)):
        sent(acc_in.at[0], xs.at[0, i], xr.at[0, 0], me)
        sent(stat_in.at[0], xs.at[1, i], xr.at[0, 0], me)
    run(drains)
    for item in (spread_nf, sum_g, sum_y, spread_do, spread_st):
        run(item.drain())
    for copy in saves + save_o[1:] + [save_d, save_u]:
        copy.wait()


def forward(dp_count, owner, media, pack, lat, sq, sk, sv, so, sg, sd, su, block_rows, own_cols):
    nz = dp_count // 2
    rows, width = lat.shape
    items, count = 4, dp_count * 4
    hidden = su.shape[1] // dp_count
    total = media.shape[0] + block_rows
    blocks = total // block_rows
    parts = HEADS // PART
    all_rows = dp_count * rows
    shape = jax.ShapeDtypeStruct
    buf = lambda *s: pltpu.VMEM(s, BF16)
    flt = lambda *s: pltpu.VMEM(s, F32)
    square = shape((count, width // count, width), BF16)
    sems = [DMA((SEND_KINDS, nz)), DMA((RECV_KINDS, nz))]
    stat = (items, 2, rows, 128)
    line = [buf(nz, rows, width)] * 3
    return pl.pallas_call(
        functools.partial(forward_kernel, dp_count, block_rows, own_cols),
        out_shape=(
            square, square, square, shape((total, width), BF16), shape((items, rows, width), BF16), shape((items, rows, width), BF16),
            shape((total, width), BF16), shape((total, width), BF16),
            shape((width, width), BF16), shape((width, hidden), BF16), shape((hidden, width), BF16),
            shape((8, width), F32), shape((rows, width), BF16), shape((rows, width), F32),
            shape((items, rows, width), BF16), shape(stat, F32), shape((8, width), F32),
        ),
        in_specs=[pl.BlockSpec(memory_space=pltpu.SMEM)] + [ANY] * 10,
        out_specs=tuple([ANY] * 11 + [VMEM] * 6),
        scratch_shapes=[
            flt(count, 8, 128), buf(items, rows, width), buf(count, width // count, width), buf(dp_count, rows, width),
            buf(items, hidden // items, width), buf(count, width // count, hidden), buf(2, block_rows, width),
            buf(total, width), buf(items, rows, width), buf(items, rows, width), buf(total, width), buf(total, width),
            buf(blocks, parts, PART * rows, block_rows), flt(items, rows, width), buf(items, rows, width),
            flt(blocks, 2, rows, 128), flt(*stat), buf(2, count, width // count, width // 2),
            buf(items, rows, width), flt(*stat), buf(dp_count, rows, width), flt(all_rows, hidden), buf(all_rows, hidden), buf(all_rows, hidden),
            buf(dp_count, rows, width), *line, buf(dp_count, rows, width), *line,
            flt(rows, width), flt(rows, width), flt(rows, width), buf(items, rows, width), flt(*stat),
            buf(width, width // 2), buf(width, hidden), buf(hidden, width),
            DMA((7, SEND_KINDS, nz)), DMA((7, RECV_KINDS, nz)), DMA((4, dp_count)), DMA((4, dp_count)), DMA((count,)), DMA((count,)),
            DMA((9,)), DMA((2,)), DMA((2,)), DMA((9,)), DMA((2, items)), DMA((2, items)),
            *sems, DMA((3, nz)), DMA((3, nz)), DMA((3, nz)), DMA((3, nz)), *sems, *sems,
        ],
        compiler_params=pltpu.CompilerParams(collective_id=1, has_side_effects=True, vmem_limit_bytes=WIDE),
    )(owner, media, pack, lat, sq, sk, sv, so, sg, sd, su)


def local_fast(
    media, latents, out_grad, frame_counts, block_position, w_query, w_key, w_value, w_out, w_up, w_down,
    gain_lat, shift_lat, gain_media, shift_media, gain_ffn, shift_ffn,
):
    dp_count, seq_count = lax.axis_size("dp"), lax.axis_size("seq")
    seq = lax.axis_index("seq")
    blocks, block_rows, width = media.shape
    items, lat_rows = seq_count, latents.shape[1]
    own_cols = gain_lat.shape[0]
    ends = FRAME_BLOCKS * jnp.cumsum(frame_counts[0])
    position = lax.dynamic_slice_in_dim(block_position[0], seq * blocks, blocks)
    owner = jnp.sum((ends[None, :] <= position[:, None]).astype(jnp.int32), axis=1)
    owner = jnp.concatenate([owner, seq[None]])
    vectors = jnp.stack([gain_lat, shift_lat, gain_media, shift_media, gain_ffn, shift_ffn]).astype(F32)
    pack = jnp.pad(vectors, ((0, 2), (0, 128 - own_cols)))
    lat, og = latents.reshape(lat_rows, width), out_grad.reshape(lat_rows, width)
    med = media.reshape(-1, width)
    (wq, wk, wv, n, nl, q, k, v, gwo, gwu, gwd, gains, lat_out, grad_hidden, do_all, stat_all, sums_ffn) = forward(
        dp_count, owner, med, pack, lat, w_query, w_key, w_value, w_out, og, w_down, w_up, block_rows, own_cols)
    wq, wk, wv = [w.reshape(width, width) for w in (wq, wk, wv)]
    gwq, gwk, gwv, dq, dk, dv, out_o, out_up, out_dn = back(
        dp_count, owner, n, nl.reshape(-1, width), q, k, v, do_all, stat_all, gwo, gwu, gwd, block_rows)
    media_grad, lat_grad, sums, out_q, out_k, out_v = close(
        dp_count, med, lat, grad_hidden, gains, sums_ffn, dq, dk, dv, wq, wk, wv, gwq, gwk, gwv, block_rows)
    place = (lax.axis_index("dp") * seq_count + seq) * own_cols
    own = lax.dynamic_slice_in_dim(sums, place, own_cols, axis=1)
    lat_out, lat_grad, media_grad, *grads = copied(lat_out, lat_grad, media_grad, out_q, out_k, out_v, out_o, out_up, out_dn)
    return (lat_out.reshape(latents.shape), lat_grad.reshape(latents.shape), media_grad.reshape(media.shape), *grads, *[own[i] for i in range(6)])


def fits(mesh):
    return mesh.shape["seq"] == 4 and mesh.shape["dp"] % 2 == 0 and 1536 % (mesh.shape["dp"] * 64) == 0


def norm_forward(rows, gain, shift):
    mean = jnp.mean(rows, axis=-1, keepdims=True)
    centred = rows - mean
    variance = jnp.mean(centred * centred, axis=-1, keepdims=True)
    inverse = lax.rsqrt(variance + EPS)
    scaled = centred * inverse
    return (scaled * gain + shift, scaled, inverse)


def norm_backward(incoming, scaled, inverse, gain):
    inner = incoming * gain
    first = jnp.mean(inner, axis=-1, keepdims=True)
    second = jnp.mean(inner * scaled, axis=-1, keepdims=True)
    return (
        inverse * (inner - first - scaled * second),
        jnp.sum(incoming * scaled, axis=0),
        jnp.sum(incoming, axis=0),
    )


def matmul(left, right):
    return jnp.dot(left, right, preferred_element_type=jnp.float32)


def matmul_left_t(left, right):
    return lax.dot_general(
        left, right, (((0,), (0,)), ((), ())), preferred_element_type=jnp.float32
    )


def matmul_right_t(left, right):
    return lax.dot_general(
        left, right, (((1,), (1,)), ((), ())), preferred_element_type=jnp.float32
    )


def swap_rows(stat):
    return jnp.swapaxes(stat, 1, 2)[..., None]


def fold_sources(tops, totals, accums):
    best = jnp.max(tops, axis=0)
    factor = jnp.exp(tops - best[None])
    total = jnp.sum(factor * totals, axis=0)
    width = accums.shape[-1]
    spread = jnp.repeat(jnp.swapaxes(factor, 2, 3), width // factor.shape[2], axis=3)
    return (best, total, jnp.sum(accums * spread, axis=0))


def local(
    media,
    latents,
    out_grad,
    frame_counts,
    block_position,
    w_query,
    w_key,
    w_value,
    w_out,
    w_up,
    w_down,
    gain_lat,
    shift_lat,
    gain_media,
    shift_media,
    gain_ffn,
    shift_ffn,
):
    gathered = (
        lax.all_gather(w_query, ("dp", "seq"), axis=0, tiled=True),
        lax.all_gather(w_key, ("dp", "seq"), axis=0, tiled=True),
        lax.all_gather(w_value, ("dp", "seq"), axis=0, tiled=True),
        lax.all_gather(w_out, ("dp", "seq"), axis=0, tiled=True),
        lax.all_gather(w_up, ("dp", "seq"), axis=0, tiled=True),
        lax.all_gather(w_down, ("dp", "seq"), axis=0, tiled=True),
        lax.all_gather(gain_lat, ("dp", "seq"), axis=0, tiled=True),
        lax.all_gather(shift_lat, ("dp", "seq"), axis=0, tiled=True),
        lax.all_gather(gain_media, ("dp", "seq"), axis=0, tiled=True),
        lax.all_gather(shift_media, ("dp", "seq"), axis=0, tiled=True),
        lax.all_gather(gain_ffn, ("dp", "seq"), axis=0, tiled=True),
        lax.all_gather(shift_ffn, ("dp", "seq"), axis=0, tiled=True),
    )
    full_query, full_key, full_value, full_out, full_up, full_down = gathered[:6]
    lat_gain, lat_shift, med_gain, med_shift, ffn_gain, ffn_shift = [
        piece.astype(jnp.float32) for piece in gathered[6:]
    ]
    seq_rank = lax.axis_index("seq")
    seq_count = lax.axis_size("seq")
    blocks, block_rows, width = media.shape
    local_items, lat_rows, _ = latents.shape
    group_items = frame_counts.shape[1]
    heads = HEADS
    head_size = HEAD_DIM
    score_scale = head_size ** (-0.5)
    ends = FRAME_BLOCKS * jnp.cumsum(frame_counts[0])
    position = lax.dynamic_slice_in_dim(block_position[0], seq_rank * blocks, blocks)
    owner_item = jnp.sum((ends[None, :] <= position[:, None]).astype(jnp.int32), axis=1)
    member = (owner_item[:, None] == jnp.arange(group_items, dtype=jnp.int32)[None, :]).astype(
        jnp.float32
    )
    lat_input = latents.astype(jnp.float32).reshape(-1, width)
    normed_lat, scaled_lat, inverse_lat = norm_forward(lat_input, lat_gain, lat_shift)
    normed_lat = normed_lat.astype(jnp.bfloat16)
    query = matmul(normed_lat, full_query).astype(jnp.bfloat16)
    key_lat = (
        matmul(normed_lat, full_key)
        .astype(jnp.bfloat16)
        .reshape(local_items, lat_rows, heads, head_size)
    )
    value_lat = (
        matmul(normed_lat, full_value)
        .astype(jnp.bfloat16)
        .reshape(local_items, lat_rows, heads, head_size)
    )
    query_all = lax.all_gather(
        query.reshape(local_items, lat_rows, width), "seq", axis=0, tiled=True
    )
    med_input = media.astype(jnp.float32).reshape(-1, width)
    normed_med, scaled_med, inverse_med = norm_forward(med_input, med_gain, med_shift)
    normed_med = normed_med.astype(jnp.bfloat16)

    def media_keys(weight_key, weight_value):
        keys_out = (
            matmul(normed_med, weight_key)
            .astype(jnp.bfloat16)
            .reshape(blocks, block_rows, heads, head_size)
        )
        values_out = (
            matmul(normed_med, weight_value)
            .astype(jnp.bfloat16)
            .reshape(blocks, block_rows, heads, head_size)
        )
        return (keys_out, values_out)

    key_med, value_med = media_keys(full_key, full_value)
    query_blk = query_all[owner_item].reshape(blocks, lat_rows, heads, head_size)
    scores_med = (
        jnp.einsum("bqhd,bkhd->bhqk", query_blk, key_med, preferred_element_type=jnp.float32)
        * score_scale
    )
    block_top = jnp.max(scores_med, axis=-1)
    expo_med = jnp.exp(scores_med - block_top[..., None])
    expo_med_low = expo_med.astype(jnp.bfloat16)
    local_top = jnp.max(jnp.where(member.T[:, :, None, None] > 0, block_top[None], NEG), axis=1)
    to_local = jnp.exp(block_top - local_top[owner_item])
    local_total = jnp.einsum(
        "bi,bhq->ihq", member, to_local * jnp.sum(expo_med, axis=-1), precision=HIGH
    )
    accum_blk = jnp.einsum(
        "bhqk,bkhd->bqhd", expo_med_low, value_med, preferred_element_type=jnp.float32
    ) * swap_rows(to_local)
    local_accum = jnp.einsum("bi,bqhd->iqhd", member, accum_blk, precision=HIGH).reshape(
        group_items, lat_rows, width
    )
    part_top, part_total, part_accum = (
        lax.all_to_all(local_top, "seq", split_axis=0, concat_axis=0, tiled=True),
        lax.all_to_all(local_total, "seq", split_axis=0, concat_axis=0, tiled=True),
        lax.all_to_all(local_accum, "seq", split_axis=0, concat_axis=0, tiled=True),
    )
    top_own, total_own, accum_flat = fold_sources(
        part_top.reshape(seq_count, local_items, heads, lat_rows),
        part_total.reshape(seq_count, local_items, heads, lat_rows),
        part_accum.reshape(seq_count, local_items, lat_rows, width),
    )
    med_top = lax.all_gather(top_own, "seq", axis=0, tiled=True)
    accum_own = accum_flat.reshape(local_items, lat_rows, heads, head_size)
    query_lat = query.reshape(local_items, lat_rows, heads, head_size)
    scores_lat = (
        jnp.einsum("iqhd,ikhd->ihqk", query_lat, key_lat, preferred_element_type=jnp.float32)
        * score_scale
    )
    lat_top = jnp.max(scores_lat, axis=-1)
    expo_lat = jnp.exp(scores_lat - lat_top[..., None])
    expo_lat_low = expo_lat.astype(jnp.bfloat16)
    item_top = jnp.maximum(top_own, lat_top)
    media_weight = jnp.exp(top_own - item_top)
    lat_weight = jnp.exp(lat_top - item_top)
    item_total = total_own * media_weight + lat_weight * jnp.sum(expo_lat, axis=-1)
    inverse_total = 1.0 / item_total
    accum_lat = jnp.einsum(
        "ihqk,ikhd->iqhd", expo_lat_low, value_lat, preferred_element_type=jnp.float32
    ) * swap_rows(lat_weight)
    attended = (accum_own * swap_rows(media_weight) + accum_lat) * swap_rows(inverse_total)
    attended_low = attended.reshape(-1, width).astype(jnp.bfloat16)
    hidden = lat_input + matmul(attended_low, full_out)
    normed_ffn, scaled_ffn, inverse_ffn = norm_forward(hidden, ffn_gain, ffn_shift)
    normed_ffn = normed_ffn.astype(jnp.bfloat16)
    pre_act = matmul(normed_ffn, full_up)
    activated, gelu_back = jax.vjp(partial(jax.nn.gelu, approximate=False), pre_act)
    activated = activated.astype(jnp.bfloat16)
    result = hidden + matmul(activated, full_down)
    latents_out = result.astype(jnp.bfloat16).reshape(latents.shape)
    again = (
        lax.all_gather(w_query, ("dp", "seq"), axis=0, tiled=True),
        lax.all_gather(w_key, ("dp", "seq"), axis=0, tiled=True),
        lax.all_gather(w_value, ("dp", "seq"), axis=0, tiled=True),
        lax.all_gather(w_out, ("dp", "seq"), axis=0, tiled=True),
        lax.all_gather(w_up, ("dp", "seq"), axis=0, tiled=True),
        lax.all_gather(w_down, ("dp", "seq"), axis=0, tiled=True),
        lax.all_gather(gain_lat, ("dp", "seq"), axis=0, tiled=True),
        lax.all_gather(shift_lat, ("dp", "seq"), axis=0, tiled=True),
        lax.all_gather(gain_media, ("dp", "seq"), axis=0, tiled=True),
        lax.all_gather(shift_media, ("dp", "seq"), axis=0, tiled=True),
        lax.all_gather(gain_ffn, ("dp", "seq"), axis=0, tiled=True),
        lax.all_gather(shift_ffn, ("dp", "seq"), axis=0, tiled=True),
    )
    back_query, back_key, back_value, back_out, back_up, back_down = again[:6]
    grad_rows = out_grad.reshape(-1, width)
    cotangent = grad_rows.astype(jnp.float32)
    grad_down = matmul_left_t(activated, grad_rows)
    grad_act = matmul_right_t(grad_rows, back_down)
    grad_pre = gelu_back(grad_act)[0].astype(jnp.bfloat16)
    grad_up = matmul_left_t(normed_ffn, grad_pre)
    grad_normed_ffn = matmul_right_t(grad_pre, back_up)
    grad_hidden_norm, grad_gain_ffn, grad_shift_ffn = norm_backward(
        grad_normed_ffn, scaled_ffn, inverse_ffn, ffn_gain
    )
    grad_hidden = cotangent + grad_hidden_norm
    grad_hidden_low = grad_hidden.astype(jnp.bfloat16)
    grad_out = matmul_left_t(attended_low, grad_hidden_low)
    grad_att = matmul_right_t(grad_hidden_low, back_out).astype(jnp.bfloat16)
    grad_att_heads = grad_att.reshape(local_items, lat_rows, heads, head_size)
    delta = jnp.einsum(
        "iqhd,iqhd->ihq", grad_att_heads.astype(jnp.float32), attended, precision=HIGH
    )
    media_factor = media_weight * inverse_total
    grad_att_all = lax.all_gather(
        grad_att.reshape(local_items, lat_rows, width), "seq", axis=0, tiled=True
    )
    factor_all, delta_all = (
        lax.all_gather(media_factor, "seq", axis=0, tiled=True),
        lax.all_gather(delta, "seq", axis=0, tiled=True),
    )
    key_med, value_med = media_keys(back_key, back_value)
    grad_blk = grad_att_all[owner_item].reshape(blocks, lat_rows, heads, head_size)
    factor_blk = jnp.exp(block_top - med_top[owner_item]) * factor_all[owner_item]
    delta_blk = delta_all[owner_item]
    grad_prob_med = jnp.einsum(
        "bqhd,bkhd->bhqk", grad_blk, value_med, preferred_element_type=jnp.float32
    )
    grad_score_med = (
        expo_med * factor_blk[..., None] * (grad_prob_med - delta_blk[..., None])
    ).astype(jnp.bfloat16)
    grad_query_blk = (
        jnp.einsum("bhqk,bkhd->bqhd", grad_score_med, key_med, preferred_element_type=jnp.float32)
        * score_scale
    )
    grad_query_part = jnp.einsum("bi,bqhd->iqhd", member, grad_query_blk, precision=HIGH).reshape(
        group_items, lat_rows, width
    )
    grad_key_med = (
        (
            jnp.einsum(
                "bhqk,bqhd->bkhd", grad_score_med, query_blk, preferred_element_type=jnp.float32
            )
            * score_scale
        )
        .astype(jnp.bfloat16)
        .reshape(-1, width)
    )
    grad_value_med = (
        jnp.einsum(
            "bhqk,bqhd->bkhd",
            expo_med_low.astype(jnp.float32) * factor_blk[..., None],
            grad_blk.astype(jnp.float32),
            precision=HIGH,
        )
        .astype(jnp.bfloat16)
        .reshape(-1, width)
    )
    grad_query_own = lax.psum_scatter(
        grad_query_part.astype(jnp.bfloat16), "seq", scatter_dimension=0, tiled=True
    ).astype(jnp.float32)
    grad_normed_med = matmul_right_t(grad_key_med, back_key) + matmul_right_t(
        grad_value_med, back_value
    )
    grad_key = matmul_left_t(normed_med, grad_key_med)
    grad_value = matmul_left_t(normed_med, grad_value_med)
    media_grad, grad_gain_media, grad_shift_media = norm_backward(
        grad_normed_med, scaled_med, inverse_med, med_gain
    )
    lat_factor = lat_weight * inverse_total
    grad_prob_lat = jnp.einsum(
        "iqhd,ikhd->ihqk", grad_att_heads, value_lat, preferred_element_type=jnp.float32
    )
    grad_score_lat = (expo_lat * lat_factor[..., None] * (grad_prob_lat - delta[..., None])).astype(
        jnp.bfloat16
    )
    grad_query_lat = (
        jnp.einsum("ihqk,ikhd->iqhd", grad_score_lat, key_lat, preferred_element_type=jnp.float32)
        * score_scale
    )
    grad_key_lat = (
        (
            jnp.einsum(
                "ihqk,iqhd->ikhd", grad_score_lat, query_lat, preferred_element_type=jnp.float32
            )
            * score_scale
        )
        .astype(jnp.bfloat16)
        .reshape(-1, width)
    )
    grad_value_lat = (
        jnp.einsum(
            "ihqk,iqhd->ikhd",
            expo_lat_low.astype(jnp.float32) * lat_factor[..., None],
            grad_att_heads.astype(jnp.float32),
            precision=HIGH,
        )
        .astype(jnp.bfloat16)
        .reshape(-1, width)
    )
    grad_query = (
        (grad_query_own + grad_query_lat.reshape(local_items, lat_rows, width))
        .astype(jnp.bfloat16)
        .reshape(-1, width)
    )
    grad_normed_lat = (
        matmul_right_t(grad_query, back_query)
        + matmul_right_t(grad_key_lat, back_key)
        + matmul_right_t(grad_value_lat, back_value)
    )
    grad_query_weight = matmul_left_t(normed_lat, grad_query)
    grad_key = grad_key + matmul_left_t(normed_lat, grad_key_lat)
    grad_value = grad_value + matmul_left_t(normed_lat, grad_value_lat)
    grad_lat_norm, grad_gain_lat, grad_shift_lat = norm_backward(
        grad_normed_lat, scaled_lat, inverse_lat, lat_gain
    )
    latents_grad = (grad_hidden + grad_lat_norm).reshape(latents.shape)
    sharded = (
        lax.psum_scatter(grad_query_weight, ("dp", "seq"), scatter_dimension=0, tiled=True),
        lax.psum_scatter(grad_key, ("dp", "seq"), scatter_dimension=0, tiled=True),
        lax.psum_scatter(grad_value, ("dp", "seq"), scatter_dimension=0, tiled=True),
        lax.psum_scatter(grad_out, ("dp", "seq"), scatter_dimension=0, tiled=True),
        lax.psum_scatter(grad_up, ("dp", "seq"), scatter_dimension=0, tiled=True),
        lax.psum_scatter(grad_down, ("dp", "seq"), scatter_dimension=0, tiled=True),
        lax.psum_scatter(grad_gain_lat, ("dp", "seq"), scatter_dimension=0, tiled=True),
        lax.psum_scatter(grad_shift_lat, ("dp", "seq"), scatter_dimension=0, tiled=True),
        lax.psum_scatter(grad_gain_media, ("dp", "seq"), scatter_dimension=0, tiled=True),
        lax.psum_scatter(grad_shift_media, ("dp", "seq"), scatter_dimension=0, tiled=True),
        lax.psum_scatter(grad_gain_ffn, ("dp", "seq"), scatter_dimension=0, tiled=True),
        lax.psum_scatter(grad_shift_ffn, ("dp", "seq"), scatter_dimension=0, tiled=True),
    )
    return (latents_out, latents_grad, media_grad.reshape(media.shape)) + tuple(sharded)


def solution(mesh):
    return jax.shard_map(
        local_fast if fits(mesh) else local,
        mesh=mesh,
        in_specs=(
            P(("dp", "seq"), None, None),
            P(("dp", "seq"), None, None),
            P(("dp", "seq"), None, None),
            P("dp", None),
            P("dp", None),
            P(("dp", "seq"), None),
            P(("dp", "seq"), None),
            P(("dp", "seq"), None),
            P(("dp", "seq"), None),
            P(("dp", "seq"), None),
            P(("dp", "seq"), None),
            P(("dp", "seq")),
            P(("dp", "seq")),
            P(("dp", "seq")),
            P(("dp", "seq")),
            P(("dp", "seq")),
            P(("dp", "seq")),
        ),
        out_specs=(
            P(("dp", "seq"), None, None),
            P(("dp", "seq"), None, None),
            P(("dp", "seq"), None, None),
            P(("dp", "seq"), None),
            P(("dp", "seq"), None),
            P(("dp", "seq"), None),
            P(("dp", "seq"), None),
            P(("dp", "seq"), None),
            P(("dp", "seq"), None),
            P(("dp", "seq")),
            P(("dp", "seq")),
            P(("dp", "seq")),
            P(("dp", "seq")),
            P(("dp", "seq")),
            P(("dp", "seq")),
        ),
        check_vma=False,
    )
```

```python
from functools import partial
from jax.sharding import PartitionSpec as P
import functools
import jax
import jax.numpy as jnp
from jax import lax
from jax.experimental import pallas as pl
from jax.experimental.pallas import tpu as pltpu

MESH = pl.DeviceIdType.MESH
ANY = pl.BlockSpec(memory_space=pl.ANY)
VMEM = pl.BlockSpec(memory_space=pltpu.VMEM)
DMA = pltpu.SemaphoreType.DMA


class Here:
    def __init__(self, dp_count):
        dp, seq = lax.axis_index("dp"), lax.axis_index("seq")
        self.nz = dp_count // 2
        self.z, self.x, self.y, self.c = dp // 2, dp % 2, seq // 2, seq % 2
        self.dp, self.seq = dp, seq

    def at(self, z=None, x=None, y=None, c=None):
        z = self.z if z is None else z
        x = self.x if x is None else x
        y = self.y if y is None else y
        c = self.c if c is None else c
        return (z * 2 + x, y * 2 + c)


def send(src, dst, ss, rs, to):
    copy = pltpu.make_async_remote_copy(
        src_ref=src, dst_ref=dst, send_sem=ss, recv_sem=rs, device_id=to, device_id_type=MESH
    )
    copy.start()


def landed(dst, ss, rs, me):
    pltpu.make_async_remote_copy(
        src_ref=dst, dst_ref=dst, send_sem=ss, recv_sem=rs, device_id=me.at(c=1 - me.c), device_id_type=MESH
    ).wait_recv()


def sent(src, ss, rs, me):
    pltpu.make_async_remote_copy(
        src_ref=src, dst_ref=src, send_sem=ss, recv_sem=rs, device_id=me.at(c=1 - me.c), device_id_type=MESH
    ).wait_send()


def greet(devices):
    barrier = pltpu.get_barrier_semaphore()
    for device in devices:
        pl.semaphore_signal(barrier, inc=1, device_id=device, device_id_type=MESH)
    pl.semaphore_wait(barrier, len(devices))


COL, FROMX, FROMY, DIAGA, DIAGB = range(5)
TOUP, TODOWN, TOX, TOY, FWDY, FWDX, TOC = range(7)


class Gather:
    def __init__(self, me, src, dst, ss, rs, axes, halves):
        self.me, self.src, self.dst, self.ss, self.rs = me, src, dst, ss, rs
        self.axes, self.halves = axes, halves
        self.sends = []
        self.depth = me.nz if "z" in axes else 1

    def slot(self, z, x, y, c):
        if self.axes == "zxyc":
            return ((z * 2 + x) * 2 + y) * 2 + c
        if self.axes == "zx":
            return z * 2 + x
        return y * 2 + c

    def shard(self, z, x, y, c, half=None):
        ref = self.dst.at[self.slot(z, x, y, c)]
        if half is None or not self.halves:
            return ref
        width = self.halves
        return ref.at[:, pl.ds(0, width)] if half == 0 else ref.at[:, pl.ds(width, width)]

    def key(self, z):
        return z if "z" in self.axes else 0

    def start(self, src, dst, out_kind, in_kind, z, to):
        send(src, dst, self.leaves(out_kind, z), self.arrives(in_kind, z), to)

    def leaves(self, kind, z):
        return self.ss.at[1 + kind * self.depth + z] if kind in (TOUP, TODOWN) else self.ss.at[0]

    def arrives(self, kind, z):
        return self.rs.at[5 * self.depth if kind >= 5 else kind * self.depth + self.key(z)]

    def whole(self, count):
        return self.dst.at[pl.ds(0, count)]

    def gone(self, ref, kind, z):
        sent(ref, self.leaves(kind, z), self.rs.at[0], self.me)

    def here(self, ref, kind, z):
        landed(ref, self.ss.at[0], self.arrives(kind, z), self.me)

    @staticmethod
    def semaphores(axes, nz):
        depth = nz if "z" in axes else 1
        return [DMA((1 + 2 * depth,)), DMA((5 * depth + 1,))]

    def hand_over(self, ref, kind, z):
        if "c" in self.axes:
            self.start(ref, ref, TOC + kind, 5 + kind, z, self.me.at(c=1 - self.me.c))

    def spread(self, ref, z):
        me = self.me
        if "x" in self.axes:
            self.start(ref, ref, TOX, FROMX, z, me.at(x=1 - me.x))
        if "y" in self.axes:
            self.start(ref, ref, TOY, FROMY, z, me.at(y=1 - me.y))
        self.hand_over(ref, COL, z)

    def own(self):
        return [self.send_own]

    def send_own(self):
        me = self.me
        ref = self.shard(me.z, me.x, me.y, me.c)
        if "z" in self.axes:
            @pl.when(me.z + 1 < me.nz)
            def _():
                self.start(self.src, ref, TOUP, COL, me.z, me.at(z=me.z + 1))

            @pl.when(me.z > 0)
            def _():
                self.start(self.src, ref, TODOWN, COL, me.z, me.at(z=me.z - 1))
        if "x" in self.axes:
            self.start(self.src, ref, TOX, FROMX, me.z, me.at(x=1 - me.x))
        if "y" in self.axes:
            self.start(self.src, ref, TOY, FROMY, me.z, me.at(y=1 - me.y))
        if "c" in self.axes:
            self.start(self.src, ref, TOC, 5, me.z, me.at(c=1 - me.c))

    def around(self, event):
        me = self.me
        found = [lambda: event(me.z)]
        for d in range(1, self.depth):
            found.append(lambda d=d: pl.when(me.z >= d)(lambda: event(me.z - d)))
            found.append(lambda d=d: pl.when(me.z + d < me.nz)(lambda: event(me.z + d)))
        return found

    def column(self):
        me = self.me

        def event(d, below):
            there = me.z - d if below else me.z + d
            ahead = me.z + 1 if below else me.z - 1

            @pl.when(there >= 0 if below else there < me.nz)
            def _():
                ref = self.shard(there, me.x, me.y, me.c)
                self.here(ref, COL, there)

                @pl.when(ahead < me.nz if below else ahead >= 0)
                def _():
                    self.start(ref, ref, TOUP if below else TODOWN, COL, there, me.at(z=ahead))
                self.spread(ref, there)
        return [functools.partial(event, d, below) for d in range(1, self.depth) for below in (True, False)]

    def neighbours(self):
        me = self.me

        def event(z):
            if "x" in self.axes:
                ref = self.shard(z, 1 - me.x, me.y, me.c)
                self.here(ref, FROMX, z)
                if "y" in self.axes:
                    half = self.shard(z, 1 - me.x, me.y, me.c, 0)
                    self.start(half, half, FWDY, DIAGA, z, me.at(y=1 - me.y))
                self.hand_over(ref, FROMX, z)
            if "y" in self.axes:
                ref = self.shard(z, me.x, 1 - me.y, me.c)
                self.here(ref, FROMY, z)
                if "x" in self.axes and self.halves:
                    half = self.shard(z, me.x, 1 - me.y, me.c, 1)
                    self.start(half, half, FWDX, DIAGB, z, me.at(x=1 - me.x))
                self.hand_over(ref, FROMY, z)
        return self.around(event)

    def diagonal(self):
        me = self.me
        if "x" not in self.axes or "y" not in self.axes:
            return []

        def event(z):
            for half in range(2 if self.halves else 1):
                ref = self.shard(z, 1 - me.x, 1 - me.y, me.c, half)
                self.here(ref, DIAGA + half, z)
                self.hand_over(ref, DIAGA + half, z)
        return self.around(event)

    def kinds(self):
        me = self.me
        found = [(COL, me.x, me.y, None)]
        if "x" in self.axes:
            found.append((FROMX, 1 - me.x, me.y, None))
        if "y" in self.axes:
            found.append((FROMY, me.x, 1 - me.y, None))
        if "x" in self.axes and "y" in self.axes:
            found.append((DIAGA, 1 - me.x, 1 - me.y, 0))
            if self.halves:
                found.append((DIAGB, 1 - me.x, 1 - me.y, 1))
        return found

    def sibling(self):
        if "c" not in self.axes:
            return []
        count = self.depth * (1 + ("x" in self.axes)) * (1 + ("y" in self.axes))
        return [lambda: self.here(self.whole(count), 5, 0)]

    def drain(self):
        me = self.me
        x, y, c = ["xyc".index(a) >= 0 and a in self.axes for a in "xyc"]
        count = self.depth * (x + y + (x and y) + c * (1 + x) * (1 + y))
        found = [lambda: self.gone(self.whole(count), TOC, 0)]
        if "z" in self.axes:
            shard = self.shard(me.z, me.x, me.y, me.c)

            def event(z):
                pl.when((z <= me.z) & (me.z + 1 < me.nz))(lambda: self.gone(shard, TOUP, z))
                pl.when((z >= me.z) & (me.z > 0))(lambda: self.gone(shard, TODOWN, z))
            found += self.around(event)
        return found

    def phases(self):
        return [self.own(), self.column(), self.neighbours(), self.diagonal(), self.sibling(), self.drain()]


def skewed(items):
    lists = [item.phases() for item in items]
    found = []
    for step in range(len(lists) + max(map(len, lists)) - 1):
        for i, phases in enumerate(lists):
            if 0 <= step - i < len(phases):
                found += phases[step - i]
    return found


def run(events):
    for event in events:
        event()


def share(events, count):
    cuts = [len(events) * i // count for i in range(count + 1)]
    return [events[a:b] for a, b in zip(cuts, cuts[1:])]


def run_at(step, lists):
    for i, events in enumerate(lists):
        if events:
            pl.when(step == i)(functools.partial(run, events))


class Regroup:
    def __init__(self, me, dp_count, src, dst, ss, rs, width):
        self.me, self.n, self.src, self.dst, self.ss, self.rs, self.width = me, dp_count, src, dst, ss, rs, width

    def piece(self, dp, y, c):
        return self.dst.at[dp * 4 + y * 2 + c]

    def columns(self, dp):
        return self.src.at[:, pl.ds(pl.multiple_of(dp * self.width, 128), self.width)]

    def hand(self, src, dp, y, place, to):
        send(src, self.piece(dp, y, self.me.c), self.ss.at[0], self.rs.at[place], to)

    def own(self):
        me = self.me
        for k in range(1, self.n):
            to = lax.rem(me.dp + k, self.n)
            self.hand(self.columns(to), me.dp, me.y, me.dp, (to, me.seq))
        self.share(self.columns(me.dp), me.dp)

    def share(self, src, dp):
        me = self.me
        self.hand(src, dp, me.y, self.n + dp, me.at(y=1 - me.y))
        self.hand(src, dp, me.y, 2 * self.n, me.at(c=1 - me.c))

    def here(self, ref, place):
        landed(ref, self.ss.at[0], self.rs.at[place], self.me)

    def column(self):
        me = self.me
        for k in range(1, self.n):
            dp = lax.rem(me.dp + k, self.n)
            ref = self.piece(dp, me.y, me.c)
            self.here(ref, dp)
            self.share(ref, dp)

    def neighbours(self):
        me = self.me
        for k in range(self.n):
            dp = lax.rem(me.dp + k, self.n)
            ref = self.piece(dp, 1 - me.y, me.c)
            self.here(ref, self.n + dp)
            self.hand(ref, dp, 1 - me.y, 2 * self.n, me.at(c=1 - me.c))

    def sibling(self):
        self.here(self.dst.at[pl.ds(0, 2 * self.n)], 2 * self.n)

    def drain(self):
        sent(self.dst.at[pl.ds(0, 4 * self.n - 1)], self.ss.at[0], self.rs.at[0], self.me)

    def phases(self):
        return [[self.own], [self.column], [self.neighbours], [self.sibling], [self.drain]]

    @staticmethod
    def semaphores(dp_count):
        return [DMA((1,)), DMA((2 * dp_count + 1,))]


class Everyone:
    def __init__(self, me, dp_count, src, dst, ss, rs):
        self.me, self.n, self.src, self.dst, self.ss, self.rs = me, dp_count * 4, src, dst, ss, rs
        self.index = me.dp * 4 + me.seq

    def own(self):
        def event():
            @pl.loop(1, self.n)
            def _(k):
                to = lax.rem(self.index + k, self.n)
                send(self.src, self.dst.at[self.index], self.ss.at[0], self.rs.at[0], (to // 4, to % 4))
        return [event]

    def arrive(self):
        return [lambda: landed(self.dst.at[pl.ds(0, self.n - 1)], self.ss.at[0], self.rs.at[0], self.me)]

    def drain(self):
        return [lambda: sent(self.dst.at[pl.ds(0, self.n - 1)], self.ss.at[0], self.rs.at[0], self.me)]

    def phases(self):
        return [self.own(), self.arrive(), self.drain()]


def greet_all(me, dp_count):
    barrier = pltpu.get_barrier_semaphore()
    count = dp_count * 4

    @pl.loop(1, count)
    def _(k):
        to = lax.rem(me.dp * 4 + me.seq + k, count)
        pl.semaphore_signal(barrier, inc=1, device_id=(to // 4, to % 4), device_id_type=MESH)
    pl.semaphore_wait(barrier, count - 1)


HEADS = 16
HEAD_DIM = 96
FRAME_BLOCKS = 2
EPS = 1e-05
NEG = -1e30
HIGH = lax.Precision.HIGHEST
F32, BF16 = jnp.float32, jnp.bfloat16
WIDE = 62 << 20
PART = 4
PCOLS = PART * HEAD_DIM
SCALE = HEAD_DIM ** (-0.5)


def dot(left, right):
    return jnp.dot(left, right, preferred_element_type=F32)


def dot_t(left, right):
    return lax.dot_general(left, right, (((1,), (1,)), ((), ())), preferred_element_type=F32)


def t_dot(left, right):
    return lax.dot_general(left, right, (((0,), (0,)), ((), ())), preferred_element_type=F32)


def scaled_rows(rows):
    mean = jnp.mean(rows, axis=-1, keepdims=True)
    centred = rows - mean
    inverse = lax.rsqrt(jnp.mean(centred * centred, axis=-1, keepdims=True) + EPS)
    return centred * inverse, inverse


def norm_back(incoming, scaled, inverse, gain):
    inner = incoming * gain
    first = jnp.mean(inner, axis=-1, keepdims=True)
    second = jnp.mean(inner * scaled, axis=-1, keepdims=True)
    return inverse * (inner - first - scaled * second)


def part_mask(rows):
    row = lax.broadcasted_iota(jnp.int32, (PART * rows, PCOLS), 0)
    column = lax.broadcasted_iota(jnp.int32, (PART * rows, PCOLS), 1)
    low = (row // rows) * HEAD_DIM
    return (column >= low) & (column < low + HEAD_DIM)


def stacked(rows, mask):
    return jnp.where(mask, jnp.concatenate([rows] * PART, axis=0), jnp.zeros((), rows.dtype))


def unstacked(rows, mask, count):
    kept = jnp.where(mask, rows, 0.0)
    return sum(kept[h * count:(h + 1) * count] for h in range(PART))


def blocks_of(media_rows, block_rows, lat_rows):
    found = [(b * block_rows, block_rows) for b in range(media_rows // block_rows)]
    return found + [(media_rows, lat_rows)]


def attend_kernel(block_rows, items, owner, media, lat_all, gains, wq, wk, wv,
                  acc, stats, n_out, nl_out, q_out, k_out, v_out, wbuf, a_ref, m_ref, l_ref, sems):
    width = media.shape[1]
    half = width // 2
    media_rows = media.shape[0]
    lat_rows = lat_all.shape[0] // items
    seq = lax.axis_index("seq")

    def fetch(step, slot):
        cols = pl.ds(pl.multiple_of(step * half, 128), half)
        return [pltpu.make_async_copy(w.at[:, cols], wbuf.at[slot, i], sems.at[slot, i]) for i, w in enumerate((wq, wk, wv))]
    for copy in fetch(0, 0):
        copy.start()

    @pl.loop(0, media_rows // block_rows)
    def _(b):
        rows = pl.ds(pl.multiple_of(b * block_rows, block_rows), block_rows)
        u, _ = scaled_rows(media[rows, :].astype(F32))
        n_out[rows, :] = (u * gains[2:3, :] + gains[3:4, :]).astype(BF16)

    @pl.loop(0, items)
    def _(i):
        rows = pl.ds(pl.multiple_of(i * lat_rows, lat_rows), lat_rows)
        u, _ = scaled_rows(lat_all[rows, :].astype(F32))
        nl_out[rows, :] = (u * gains[0:1, :] + gains[1:2, :]).astype(BF16)
    n_out[pl.ds(media_rows, lat_rows), :] = nl_out[pl.ds(pl.multiple_of(seq * lat_rows, lat_rows), lat_rows), :]
    padding = n_out.shape[0] - media_rows - lat_rows
    n_out[pl.ds(media_rows + lat_rows, padding), :] = jnp.zeros((padding, width), BF16)
    stats[...] = jnp.zeros_like(stats)
    mask = part_mask(lat_rows)
    lane = lax.broadcasted_iota(jnp.int32, (lat_rows, 128), 1)

    @pl.loop(0, 2)
    def _(step):
        slot = lax.rem(step, 2)
        cols = pl.ds(pl.multiple_of(step * half, 128), half)
        for copy in fetch(step, slot):
            copy.wait()

        @pl.when(step == 0)
        def _():
            for copy in fetch(1, 1):
                copy.start()
        q_out[:, cols] = dot(nl_out[...], wbuf[slot, 0]).astype(BF16)
        k_out[:, cols] = dot(n_out[...], wbuf[slot, 1]).astype(BF16)
        v_out[:, cols] = dot(n_out[...], wbuf[slot, 2]).astype(BF16)

        @pl.loop(0, half // PCOLS)
        def _(inner):
            part = step * (half // PCOLS) + inner
            pcols = pl.ds(pl.multiple_of(part * PCOLS, 128), PCOLS)
            a_ref[...] = jnp.zeros_like(a_ref)
            l_ref[...] = jnp.zeros_like(l_ref)
            m_ref[...] = jnp.full_like(m_ref, NEG)

            def block(start, count, item):
                rows = q_out[pl.ds(pl.multiple_of(item * lat_rows, lat_rows), lat_rows), pcols]
                query = stacked(rows, mask)
                keys, values = k_out[pl.ds(start, count), pcols], v_out[pl.ds(start, count), pcols]
                scores = dot_t(query, keys) * SCALE
                old = m_ref[item]
                new = jnp.maximum(old, jnp.max(scores, axis=-1, keepdims=True))
                factor = jnp.exp(old - new)
                expo = jnp.exp(scores - new[:, :count])
                m_ref[item] = new
                l_ref[item] = l_ref[item] * factor + jnp.sum(expo, axis=-1, keepdims=True)
                wide = jnp.concatenate([factor] * (PCOLS // 128), axis=1)
                a_ref[item] = a_ref[item] * wide + dot(expo.astype(BF16), values)
            for b, (start, count) in enumerate(blocks_of(media_rows, block_rows, lat_rows)):
                block(start, count, seq if count == lat_rows and start == media_rows else owner[b])
            for item in range(items):
                acc[item, :, pcols] = unstacked(a_ref[item], mask, lat_rows).astype(BF16)
                for h in range(PART):
                    chosen = lane == part * PART + h
                    at = pl.ds(h * lat_rows, lat_rows)
                    stats[item, 0] = jnp.where(chosen, m_ref[item, at, :], stats[item, 0])
                    stats[item, 1] = jnp.where(chosen, l_ref[item, at, :], stats[item, 1])


def attend(owner, media, lat_all, gains, wq, wk, wv, block_rows, items):
    width = media.shape[1]
    lat_rows = lat_all.shape[0] // items
    rows = media.shape[0] + block_rows
    shape = jax.ShapeDtypeStruct
    return pl.pallas_call(
        functools.partial(attend_kernel, block_rows, items),
        out_shape=(
            shape((items, lat_rows, width), BF16), shape((items, 2, lat_rows, 128), F32),
            shape((rows, width), BF16), shape((items * lat_rows, width), BF16),
            shape((items * lat_rows, width), BF16), shape((rows, width), BF16), shape((rows, width), BF16),
        ),
        in_specs=[pl.BlockSpec(memory_space=pltpu.SMEM), VMEM, VMEM, VMEM, ANY, ANY, ANY],
        out_specs=tuple([VMEM] * 7),
        scratch_shapes=[
            pltpu.VMEM((2, 3, width, width // 2), BF16),
            pltpu.VMEM((items, PART * lat_rows, PCOLS), F32),
            pltpu.VMEM((items, PART * lat_rows, 128), F32), pltpu.VMEM((items, PART * lat_rows, 128), F32),
            DMA((2, 3)),
        ],
        compiler_params=pltpu.CompilerParams(vmem_limit_bytes=WIDE),
    )(owner, media, lat_all, gains, wq, wk, wv)


def dp_peers(me, dp_count):
    return [(lax.rem(me.dp + k, dp_count), me.seq) for k in range(1, dp_count)]


def far_first(me, event):
    found = []
    for d in range(me.nz - 1, 0, -1):
        found.append(lambda d=d: pl.when(me.z >= d)(lambda: event(me.z - d)))
        found.append(lambda d=d: pl.when(me.z + d < me.nz)(lambda: event(me.z + d)))
    return found + [lambda: event(me.z)]


def add(*refs):
    total = refs[0][...].astype(F32)
    for ref in refs[1:]:
        total = total + ref[...].astype(F32)
    return total


class Line:
    def __init__(self, me, column, boxes, ss, rs):
        self.me, self.column, self.boxes, self.ss, self.rs = me, column, boxes, ss, rs

    def event(self, z):
        me = self.me

        @pl.when(z != me.z)
        def _():
            send(self.column(z), self.boxes.at[me.z], self.ss.at[0], self.rs.at[0], me.at(z=z))

    def total(self, out):
        me = self.me
        landed(self.boxes.at[pl.ds(0, me.nz - 1)], self.ss.at[0], self.rs.at[0], me)
        out[...] = self.column(me.z)[...].astype(F32)
        for z in range(me.nz):
            @pl.when(z != me.z)
            def _():
                out[...] += self.boxes.at[z][...].astype(F32)

    def drain(self):
        return [lambda: sent(self.boxes.at[pl.ds(0, self.me.nz - 1)], self.ss.at[0], self.rs.at[0], self.me)]


class DpScatter:
    def __init__(self, me, part, out, ox, boxes, ss, rs, lss, lrs):
        self.me, self.part, self.out, self.ox, self.ss, self.rs = me, part, out, ox, ss, rs
        self.line = Line(me, lambda z: part.at[z * 2 + me.x], boxes, lss, lrs)

    def start(self, z):
        me = self.me
        send(self.part.at[z * 2 + 1 - me.x], self.ox.at[z], self.ss.at[0], self.rs.at[z], me.at(x=1 - me.x))

    def fold(self, z):
        me = self.me
        landed(self.ox.at[z], self.ss.at[0], self.rs.at[z], me)
        mine = self.part.at[z * 2 + me.x]
        mine[...] = add(mine, self.ox.at[z]).astype(mine.dtype)
        self.line.event(z)

    def finish(self):
        self.line.total(self.out)

    def drain(self):
        return [lambda: sent(self.ox, self.ss.at[0], self.rs.at[0], self.me)] + self.line.drain()

    @staticmethod
    def semaphores(nz):
        return [DMA((1,)), DMA((nz,)), DMA((1,)), DMA((1,))]


def head_columns(width):
    row = lax.broadcasted_iota(jnp.int32, (128, width), 0) * HEAD_DIM
    column = lax.broadcasted_iota(jnp.int32, (128, width), 1)
    return ((column >= row) & (column < row + HEAD_DIM)).astype(F32)


def exact(left, right):
    return jnp.dot(left, right, preferred_element_type=F32, precision=HIGH)


def exact_t(left, right):
    return lax.dot_general(left, right, (((1,), (1,)), ((), ())), preferred_element_type=F32, precision=HIGH)


class Scatter:
    def __init__(self, me, src, out, bufs, ss, rs, ls, lss, lrs):
        self.me, self.src, self.out, self.ss, self.rs, self.ls = me, src, out, ss, rs, ls
        self.acc, self.cbuf, self.x1, self.y1, self.ox, self.oy, boxes = bufs
        self.cut = self.x1.shape[-1]
        self.line = Line(me, lambda z: self.acc.at[z, me.x, me.y], boxes, lss, lrs)

    def part(self, ref, half):
        width = self.acc.shape[-1]
        return ref.at[:, pl.ds(self.cut, width - self.cut)] if half else ref.at[:, pl.ds(0, self.cut)]

    def load(self, z):
        return pltpu.make_async_copy(self.src.at[pl.ds(2 * z, 2), :, self.me.c], self.acc.at[z], self.ls.at[z])

    def feed(self, stage, z):
        me = self.me
        send(stage.at[:, :, 1 - me.c], self.cbuf.at[z], self.ss.at[1 + z], self.rs.at[z], me.at(c=1 - me.c))
        for i in range(4):
            self.acc[z, i // 2, i % 2] = stage[i // 2, i % 2, me.c]

    def fed(self, z):
        sent(self.cbuf.at[z], self.ss.at[1 + z], self.rs.at[0], self.me)

    def begin(self):
        me = self.me

        def event(z):
            send(self.src.at[pl.ds(2 * z, 2), :, 1 - me.c], self.cbuf.at[z], self.ss.at[1 + z], self.rs.at[z], me.at(c=1 - me.c))
            self.load(z).start()
        return far_first(me, event)

    def core(self):
        me = self.me

        def event(z):
            if self.src is not None:
                self.load(z).wait()
            landed(self.cbuf.at[z], self.ss.at[0], self.rs.at[z], me)
            mine = self.acc.at[z]

            @pl.loop(0, 4)
            def _(i):
                x, y = i // 2, i % 2
                mine[x, y] = (mine[x, y].astype(F32) + self.cbuf[z, x, y].astype(F32)).astype(BF16)
            x_to, y_to = me.at(x=1 - me.x), me.at(y=1 - me.y)
            diag = mine.at[1 - me.x, 1 - me.y]
            send(self.part(diag, 0), self.x1.at[z], self.ss.at[0], self.rs.at[1 * me.nz + z], x_to)
            send(self.part(diag, 1), self.y1.at[z], self.ss.at[0], self.rs.at[2 * me.nz + z], y_to)
            send(self.part(mine.at[1 - me.x, me.y], 0), self.part(self.ox.at[z], 0), self.ss.at[0], self.rs.at[3 * me.nz + z], x_to)
            send(self.part(mine.at[me.x, 1 - me.y], 1), self.part(self.oy.at[z], 1), self.ss.at[0], self.rs.at[3 * me.nz + z], y_to)
        return far_first(me, event)

    def middle(self):
        me = self.me

        def event(z):
            landed(self.x1.at[z], self.ss.at[0], self.rs.at[me.nz + z], me)
            ref = self.part(self.acc.at[z, me.x, 1 - me.y], 0)
            ref[...] = add(ref, self.x1.at[z]).astype(BF16)
            send(ref, self.part(self.oy.at[z], 0), self.ss.at[0], self.rs.at[3 * me.nz + z], me.at(y=1 - me.y))
            landed(self.y1.at[z], self.ss.at[0], self.rs.at[2 * me.nz + z], me)
            ref = self.part(self.acc.at[z, 1 - me.x, me.y], 1)
            ref[...] = add(ref, self.y1.at[z]).astype(BF16)
            send(ref, self.part(self.ox.at[z], 1), self.ss.at[0], self.rs.at[3 * me.nz + z], me.at(x=1 - me.x))
        return far_first(me, event)

    def fold(self):
        me = self.me

        def event(z):
            landed(self.acc.at[z, 0], self.ss.at[0], self.rs.at[3 * me.nz + z], me)
            mine = self.acc.at[z, me.x, me.y]
            mine[...] = add(mine, self.ox.at[z], self.oy.at[z]).astype(BF16)
            self.line.event(z)
        return far_first(me, event)

    def finish(self):
        return [lambda: self.line.total(self.out)]

    def drain(self):
        me = self.me
        found = far_first(me, self.fed) if self.src is not None else []
        found.append(lambda: sent(self.acc.at[pl.ds(0, me.nz * 3 // 4)], self.ss.at[0], self.rs.at[0], me))
        return found + self.line.drain()

    def phases(self):
        return [self.begin(), self.core(), self.middle(), self.fold(), self.finish(), self.drain()]

    @staticmethod
    def scratch(nz, rows, cols):
        buf = lambda *s: pltpu.VMEM(s + (rows, cols), BF16)
        cut = cols * 2 // 3 // 128 * 128
        return [buf(nz, 2, 2), buf(nz, 2, 2), pltpu.VMEM((nz, rows, cut), BF16), pltpu.VMEM((nz, rows, cols - cut), BF16), buf(nz), buf(nz), buf(nz),
                DMA((1 + nz,)), DMA((4 * nz,)), DMA((nz,)), DMA((1,)), DMA((1,))]


class SeqScatter:
    def __init__(self, me, src, then, acc, cbuf, oy, ss, rs, ls):
        self.me, self.src, self.then, self.acc, self.cbuf, self.oy = me, src, then, acc, cbuf, oy
        self.ss, self.rs = ss, rs
        self.load = pltpu.make_async_copy(src.at[:, :, me.c], acc, ls.at[0])

    def begin(self):
        me = self.me
        send(self.src.at[:, :, 1 - me.c], self.cbuf, self.ss.at[0], self.rs.at[0], me.at(c=1 - me.c))
        self.load.start()

    def core(self):
        me = self.me
        self.load.wait()
        landed(self.cbuf, self.ss.at[0], self.rs.at[0], me)

        @pl.loop(0, self.acc.shape[0])
        def _(i):
            for y in (0, 1):
                self.acc[i, y] = (self.acc[i, y].astype(F32) + self.cbuf[i, y].astype(F32)).astype(BF16)
        send(self.acc.at[:, 1 - me.y], self.oy, self.ss.at[1], self.rs.at[1], me.at(y=1 - me.y))

    def fold(self):
        me = self.me
        landed(self.oy, self.ss.at[0], self.rs.at[1], me)

        @pl.loop(0, self.acc.shape[0])
        def _(i):
            self.oy[i] = (self.acc[i, me.y].astype(F32) + self.oy[i].astype(F32)).astype(BF16)

    def finish(self):
        self.then(self.oy)

    def drain(self):
        sent(self.cbuf, self.ss.at[0], self.rs.at[0], self.me)
        sent(self.oy, self.ss.at[1], self.rs.at[0], self.me)

    def phases(self):
        return [[self.begin], [self.core], [self.fold], [self.finish], [self.drain]]

    @staticmethod
    def scratch(count, rows, cols):
        buf = lambda *s: pltpu.VMEM(s + (rows, cols), BF16)
        return [buf(count, 2), buf(count, 2), buf(count), DMA((2,)), DMA((2,)), DMA((1,))]


class Regrouped(SeqScatter):
    def __init__(self, me, dp_count, src, out, inbox, up_ss, up_rs, *rest):
        super().__init__(me, src, self.pass_on, *rest)
        self.n, self.out, self.inbox, self.up_ss, self.up_rs = dp_count, out, inbox, up_ss, up_rs

    def pass_on(self, total):
        me = self.me
        for k in range(1, self.n):
            to = lax.rem(me.dp + k, self.n)
            send(total.at[to], self.inbox.at[me.dp], self.up_ss.at[to], self.up_rs.at[me.dp], (to, me.seq))
        self.inbox[me.dp] = total[me.dp]

    def collect(self):
        cols = self.inbox.shape[2]
        for dp in range(self.n):
            pl.when(dp != self.me.dp)(lambda: landed(self.inbox.at[dp], self.up_ss.at[0], self.up_rs.at[dp], self.me))
            self.out[:, dp * cols:(dp + 1) * cols] = self.inbox[dp].astype(F32)

    def drain(self):
        super().drain()
        for k in range(1, self.n):
            sent(self.inbox.at[0], self.up_ss.at[lax.rem(self.me.dp + k, self.n)], self.up_rs.at[0], self.me)

    def phases(self):
        return [[self.begin], [self.core], [self.fold], [self.finish], [self.collect], [self.drain]]

    @staticmethod
    def scratch(count, rows, cols):
        return [pltpu.VMEM((count, rows, cols), BF16), DMA((count,)), DMA((count,))] + SeqScatter.scratch(count, rows, cols)


class SumAll:
    def __init__(self, me, ref, inbox, ss, rs):
        self.me, self.ref, self.inbox, self.ss, self.rs = me, ref, inbox, ss, rs

    def step(self, i, to):
        def begin():
            send(self.ref.at[i], self.inbox.at[i], self.ss.at[i], self.rs.at[i], to)

        def end():
            landed(self.inbox.at[i], self.ss.at[0], self.rs.at[i], self.me)
            self.ref[i + 1] = self.ref[i] + self.inbox[i]
        return begin, end

    def phases(self):
        me = self.me
        n = me.nz

        def begin_z():
            for k in range(1, n):
                to = lax.rem(me.z + k, n)
                send(self.ref.at[3], self.inbox.at[2 + k], self.ss.at[2 + k], self.rs.at[2 + k], me.at(z=to))

        def end_z():
            total = self.ref[3]
            for k in range(1, n):
                landed(self.inbox.at[2 + k], self.ss.at[0], self.rs.at[2 + k], me)
                total = total + self.inbox[2 + k]
            self.ref[4] = total

        def drain():
            for i in range(2 + n):
                sent(self.ref.at[0], self.ss.at[i], self.rs.at[0], me)
        first = self.step(0, me.at(c=1 - me.c))
        second = self.step(1, me.at(x=1 - me.x))
        third = self.step(2, me.at(y=1 - me.y))
        both = lambda one, other: (lambda: (one(), other()))
        return [[e] for e in (first[0], both(first[1], second[0]), both(second[1], third[0]), both(third[1], begin_z), end_z, drain)]


def backward_kernel(dp_count, block_rows, owner, lat, grad_hidden, gains, sums_ffn,
                    n_in, nl_in, q_in, k_in, v_in, do_in, stat_in, gwo, gwu, gwd, media, wq, wk, wv,
                    media_grad, lat_grad, sums, out_q, out_k, out_v, out_o, out_up, out_dn,
                    n, nl, q, do, k, v, stats, dq, g, gq, med, stage, sums_ref, *scratch):
    me = Here(dp_count)
    items, lat_rows, width = q.shape
    rows = k.shape[0]
    media_rows = media.shape[0]
    blocks, parts = rows // block_rows, HEADS // PART
    scratch = list(scratch)
    take = lambda count: [scratch.pop(0) for _ in range(count)]
    o_s, fulls, up_s, dn_s, lat_s, small = take(12), [take(12) for _ in range(3)], take(9), take(6), take(6), take(4)
    in_sem, tile_sem, med_sem, out_sem = scratch
    loads = [(stat_in, stats), (q_in, q), (do_in, do), (k_in, k), (v_in, v), (n_in, n), (nl_in, nl)]
    loads = [pltpu.make_async_copy(src, dst, in_sem.at[i]) for i, (src, dst) in enumerate(loads)]
    for load in loads:
        load.start()
    all_sum = SumAll(me, *small)

    def latents(total):
        scaled, inverse = scaled_rows(lat[...].astype(F32))
        grad = total[0].astype(F32)
        lat_grad[...] = grad_hidden[...] + norm_back(grad, scaled, inverse, gains[0:1, :])
        first = small[0]
        first[0, 0:1, :] = jnp.sum(grad * scaled, axis=0, keepdims=True)
        first[0, 1:2, :] = jnp.sum(grad, axis=0, keepdims=True)
        first[0, 2:4, :] = sums_ref[0:2, :]
        first[0, 4:6, :] = sums_ffn[0:2, :]
        first[0, 6:8, :] = jnp.zeros_like(sums_ffn[0:2, :])

    def down(total):
        out_dn[...] = total[0].astype(F32)
    f_o = Scatter(me, gwo, out_o, o_s[:7], *o_s[7:])
    f_k, f_v, f_q = [Scatter(me, None, out, f[:7], *f[7:]) for out, f in zip((out_k, out_v, out_q), fulls)]
    up, dn = Regrouped(me, dp_count, gwu, out_up, *up_s), SeqScatter(me, gwd, down, *dn_s)
    lat_item = SeqScatter(me, gq, latents, *lat_s)
    greet(dp_peers(me, dp_count) + [me.at(y=1 - me.y), me.at(c=1 - me.c)])
    mask = part_mask(lat_rows)
    lane = lax.broadcasted_iota(jnp.int32, (lat_rows, 128), 1)
    key = lax.broadcasted_iota(jnp.int32, (PART * lat_rows, block_rows), 1)
    held = pl.ds(0, items * lat_rows)
    g[held, :] = jnp.zeros((items * lat_rows, width), F32)

    def replicated(stat, part):
        pieces = []
        for h in range(PART):
            column = jnp.sum(jnp.where(lane == part * PART + h, stat, 0.0), axis=-1, keepdims=True)
            pieces.append(jnp.broadcast_to(column, (lat_rows, 128)))
        return jnp.concatenate(pieces, axis=0)

    def block(b, part, item):
        cols = pl.ds(pl.multiple_of(part * PCOLS, 128), PCOLS)
        at = pl.ds(pl.multiple_of(b * block_rows, block_rows), block_rows)
        query, grad = stacked(q[item, :, cols], mask), stacked(do[item, :, cols], mask)
        keys, values = k[at, cols], v[at, cols]
        lse, delta = replicated(stats[item, 0], part), replicated(stats[item, 1], part)
        prob = jnp.exp(dot_t(query, keys) * SCALE - lse)
        prob = jnp.where(key < jnp.where(b == blocks - 1, lat_rows, block_rows), prob, 0.0)
        score = (prob * (dot_t(grad, values) - delta)).astype(BF16)
        term = unstacked(dot(score, keys), mask, lat_rows) * SCALE
        k[at, cols] = (t_dot(score, query) * SCALE).astype(BF16)
        v[at, cols] = t_dot(prob.astype(BF16), grad).astype(BF16)
        for i in range(items):
            g[i * lat_rows:(i + 1) * lat_rows, cols] += jnp.where(item == i, term, 0.0)
    steps = blocks * parts // 2
    shares = share(f_o.begin() + [up.begin, dn.begin] + f_o.core() + [up.core, dn.core], steps // 2)
    for load in loads[:5]:
        load.wait()

    @pl.loop(0, steps)
    def _(i):
        b, pair = i // (parts // 2), i % (parts // 2)
        run_at(i, shares)
        item = owner[b]
        block(b, pair * 2, item)
        block(b, pair * 2 + 1, item)
    dq[...] = g[held, :].astype(BF16)
    for load in loads[5:]:
        load.wait()
    layer = width // me.nz

    def produce(full, left, right, events):
        shares = share(events, me.nz)

        @pl.loop(0, me.nz)
        def _(t):
            run_at(t, shares)
            slot = lax.rem(t, 2)
            z = lax.rem(me.z + 1 + t, me.nz)
            pl.when(t >= 2)(lambda: full.fed(lax.rem(me.z + t - 1, me.nz)))
            cols = pl.ds(pl.multiple_of(z * layer, 128), layer)
            found = t_dot(left(cols), right()).astype(BF16)
            stage[slot] = found.reshape(stage.shape[1:])
            full.feed(stage.at[slot], z)
        full.fed(lax.rem(me.z + me.nz - 1, me.nz))
        full.fed(me.z)
    n_cols = lambda cols: n[:, :, cols].reshape(rows, layer)
    produce(f_k, n_cols, lambda: k[...], f_o.middle())
    produce(f_v, n_cols, lambda: v[...], f_k.core() + f_o.fold())
    produce(f_q, lambda cols: nl[:, :, cols].reshape(items * lat_rows, layer), lambda: dq[...],
            f_v.core() + [up.fold, up.finish, dn.fold, dn.finish] + f_k.middle())
    span = rows // 2
    per, tile = items, items * lat_rows
    tiles = width // tile
    slots = ((n.at[pl.ds(0, per)], n.at[pl.ds(per, per)], n.at[pl.ds(2 * per, per)]), (q, nl, do))

    def fetch(t, slot):
        return [pltpu.make_async_copy(w.at[pl.ds(t * per, per)], dst, tile_sem.at[slot, i]) for i, (w, dst) in enumerate(zip((wk, wv, wq), slots[slot]))]

    def media_load(i, start):
        at = pl.ds(pl.multiple_of(start + i * lat_rows, lat_rows), lat_rows)
        slot = lax.rem(i, 2)
        return pltpu.make_async_copy(media.at[at, :], med.at[slot], med_sem.at[slot])
    rest = [f_o.finish(), f_q.core(), f_k.fold(), f_v.middle(), f_k.finish(), f_q.middle(), f_v.fold(), f_v.finish(), f_q.fold()]
    cursor = Cursor([e for events in rest for e in events])
    total = len(cursor.events)
    sums_ref[...] = jnp.zeros_like(sums_ref)
    for turn, start in enumerate((span, 0)):
        shares = cursor.spread(total * (1 + 2 * turn) // 4, tiles)
        for copy in fetch(0, 0) + fetch(1, 1):
            copy.start()

        @pl.loop(0, tiles // 2)
        def _(pair):
            for slot in (0, 1):
                t = pair * 2 + slot
                run_at(t, shares)
                for copy in fetch(t, slot):
                    copy.wait()
                at = pl.ds(pl.multiple_of(t * tile, 128), tile)
                w_k, w_v, w_q = [ref[...].reshape(tile, width) for ref in slots[slot]]
                grad = dot_t(k[pl.ds(start, span), :], w_k) + dot_t(v[pl.ds(start, span), :], w_v)
                g[:, at] = grad
                if turn == 0:
                    own = dot_t(dq[...], w_q)
                    extra = grad[media_rows - start:media_rows - start + lat_rows]
                    for i in range(items):
                        term = own[i * lat_rows:(i + 1) * lat_rows]
                        gq[0, i // 2, i % 2, :, at] = jnp.where(me.seq == i, term + extra, term).astype(BF16)

                @pl.when(t + 2 < tiles)
                def _():
                    for copy in fetch(t + 2, slot):
                        copy.start()
        if turn == 0:
            lat_item.begin()
        count = (min(media_rows, start + span) - start) // lat_rows
        shares = cursor.spread(total * (2 + 2 * turn) // 4, count)
        media_load(0, start).start()

        def out_copy(first, length):
            at = pl.ds(pl.multiple_of(start + first, lat_rows), length)
            return pltpu.make_async_copy(g.at[pl.ds(pl.multiple_of(first, lat_rows), length), :], media_grad.at[at, :], out_sem)

        @pl.loop(0, count)
        def _(i):
            run_at(i, shares)
            pl.when(i + 1 < count)(lambda: media_load(i + 1, start).start())
            media_load(i, start).wait()
            at = pl.ds(pl.multiple_of(i * lat_rows, lat_rows), lat_rows)
            u, inverse = scaled_rows(med[lax.rem(i, 2)].astype(F32))
            grad = g[at, :]
            g[at, :] = norm_back(grad, u, inverse, gains[2:3, :])
            out_copy(i * lat_rows, lat_rows).start()
            sums_ref[0:1, :] += jnp.sum(grad * u, axis=0, keepdims=True)
            sums_ref[1:2, :] += jnp.sum(grad, axis=0, keepdims=True)
        if turn == 0:
            lat_item.core()
        out_copy(0, count * lat_rows).wait()
    lat_item.fold()
    lat_item.finish()
    for phase in all_sum.phases():
        run(phase)
    run(f_q.finish())
    up.collect()
    sums[...] = small[0][4]
    for item in (f_o, f_k, f_v, f_q):
        run(item.drain())
    for item in (up, dn, lat_item):
        item.drain()


def backward(dp_count, owner, lat, grad_hidden, gains, sums_ffn, n, nl, q, k, v, do_all, stats, gwo, gwu, gwd, media, wq, wk, wv, block_rows):
    nz = dp_count // 2
    items, lat_rows, width = q.shape
    rows = n.shape[0]
    hidden = gwu.shape[1]
    count = dp_count * 4
    shape = jax.ShapeDtypeStruct
    buf = lambda *s: pltpu.VMEM(s, BF16)
    flt = lambda *s: pltpu.VMEM(s, F32)
    pieces = lambda w: w.reshape(width // lat_rows, lat_rows, width)
    arrays = (owner, lat, grad_hidden, gains, sums_ffn, n.reshape(rows // lat_rows, lat_rows, width), nl, q, k, v, do_all, stats,
              gwo.reshape(dp_count, 2, 2, width // count, width),
              gwu.reshape(dp_count, 2, 2, width // count, hidden), gwd.reshape(1, 2, 2, hidden // 4, width),
              media, pieces(wq), pieces(wk), pieces(wv))
    return pl.pallas_call(
        functools.partial(backward_kernel, dp_count, block_rows),
        out_shape=(
            shape(media.shape, F32), shape((lat_rows, width), F32), shape((8, width), F32), *[shape((width // count, width), F32)] * 4,
            shape((width // count, hidden * dp_count), F32), shape((hidden // 4, width), F32),
        ),
        in_specs=[pl.BlockSpec(memory_space=pltpu.SMEM)] + [VMEM] * 4 + [ANY] * 14,
        out_specs=tuple([ANY] + [VMEM] * 8),
        scratch_shapes=[
            buf(rows // lat_rows, lat_rows, width), buf(items, lat_rows, width), buf(items, lat_rows, width), buf(items, lat_rows, width),
            buf(rows, width), buf(rows, width), flt(*stats.shape), buf(items * lat_rows, width), flt(rows // 2, width),
            buf(1, 2, 2, lat_rows, width), buf(2, lat_rows, width), buf(2, 2, 2, 2, width // count, width), flt(8, width),
            *Scatter.scratch(nz, width // count, width), *(Scatter.scratch(nz, width // count, width) * 3), *Regrouped.scratch(dp_count, width // count, hidden),
            *SeqScatter.scratch(1, hidden // 4, width), *SeqScatter.scratch(1, lat_rows, width),
            flt(5, 8, width), flt(2 + nz, 8, width), DMA((2 + nz,)), DMA((2 + nz,)),
            DMA((7,)), DMA((2, 3)), DMA((2,)), DMA,
        ],
        compiler_params=pltpu.CompilerParams(collective_id=2, has_side_effects=True, vmem_limit_bytes=WIDE),
    )(*arrays)


def copy_kernel(*refs):
    n = (len(refs) - 2) // 3
    arrays, outs, held, first, second = refs[:n], refs[n:2 * n], refs[2 * n:3 * n], refs[-2], refs[-1]
    ins = [pltpu.make_async_copy(arrays[i], held[i], first.at[i]) for i in range(n)]
    backs = [pltpu.make_async_copy(held[i], outs[i], second.at[i]) for i in range(n)]
    for copy in ins:
        copy.start()
    for copy, after in zip(ins, backs):
        copy.wait()
        after.start()
    for copy in backs:
        copy.wait()


def copied(*arrays):
    n = len(arrays)
    return pl.pallas_call(
        copy_kernel, out_shape=tuple(jax.ShapeDtypeStruct(a.shape, a.dtype) for a in arrays),
        in_specs=[ANY] * n, out_specs=tuple([ANY] * n),
        scratch_shapes=[*[pltpu.VMEM(a.shape, a.dtype) for a in arrays], DMA((n,)), DMA((n,))],
        compiler_params=pltpu.CompilerParams(vmem_limit_bytes=WIDE),
    )(*arrays)


def ordered(items, starts):
    lists = [item.phases() for item in items]
    found, ends, tails = [], [0] * len(items), []
    for step in range(max(s + len(p) for s, p in zip(starts, lists))):
        for i, (begin, phases) in enumerate(zip(starts, lists)):
            k = step - begin
            if 0 <= k < len(phases) - 1:
                found += phases[k]
                ends[i] = len(found)
    for phases in lists:
        tails += phases[-1]
    return found, ends, tails


class Cursor:
    def __init__(self, events):
        self.events, self.done = events, 0

    def upto(self, mark):
        run(self.events[self.done:mark])
        self.done = max(self.done, mark)

    def spread(self, mark, steps):
        mark = max(mark, self.done)
        lists = share(self.events[self.done:mark], steps)
        self.done = mark
        return lists


def unpacked(packs, own_cols):
    count = packs.shape[0]
    group = 8
    rows = []
    for g in range(count // group):
        left = jnp.concatenate([packs[g * group + i] for i in range(group)], axis=1).astype(BF16)
        row = lax.broadcasted_iota(jnp.int32, (group * 128, group * own_cols), 0)
        column = lax.broadcasted_iota(jnp.int32, (group * 128, group * own_cols), 1)
        piece, place = row // 128, row % 128
        chosen = (place < own_cols) & (column == piece * own_cols + place)
        rows.append(dot(left, jnp.where(chosen, 1.0, 0.0).astype(BF16)))
    return jnp.concatenate(rows, axis=1)


def forward_kernel(dp_count, block_rows, own_cols, owner, media, pack, lat, sq, sk, sv, so, sg, sd, su,
                   wq, wk, wv, n_out, nl_out, q_out, k_out, v_out, gwo, gwu, gwd,
                   gains, lat_out, grad_hidden, do_all, stat_all, sums,
                   packs, lat_all, wo, og, dn, up, med, n, nl, q, k, v, expo, acc_f, acc, tops, stats, wbuf,
                   acc_in, stat_in, nf_all, ga, act, gp, part_g, ox_g, zz_g, part_y, ox_y, zz_y,
                   own_sum, row_a, row_b, do_in, st_in, gwo_v, gwu_v, gwd_v,
                   local, ws, ms, outs, xs, xr, *sems):
    me = Here(dp_count)
    (rss, rrs, es, er), g_sems, y_sems, sems = sems[:4], sems[4:8], sems[8:12], sems[12:]
    nf_sems, do_sems, st_sems = sems[14:16], sems[16:18], sems[18:20]
    seq_count, lat_rows, width = lat_all.shape
    half = width // 2
    seq_peers = [lax.rem(me.seq + i, seq_count) for i in range(1, seq_count)]
    blocks, parts = n.shape[0] // block_rows, HEADS // PART
    media_rows = media.shape[0]
    greet_all(me, dp_count)
    gather = lambda i, src, dst, axes, halves: Gather(me, src, dst, *sems[2 * i:2 * i + 2], axes, halves)
    regroup = Regroup(me, dp_count, su, up, rss, rrs, up.shape[2])
    items = [
        Everyone(me, dp_count, pack, packs, es, er), gather(0, lat, lat_all, "yc", 0),
        gather(1, sk, wk, "zxyc", half), gather(2, sq, wq, "zxyc", half), gather(3, sv, wv, "zxyc", half),
        gather(4, so, wo, "zxyc", half), gather(5, sg, og, "zx", 0), gather(6, sd, dn, "yc", 0), regroup,
    ]
    own = [(pack, packs.at[items[0].index])]
    own += [(src, item.shard(me.z, me.x, me.y, me.c)) for src, item in zip((lat, sk, sq, sv, so, sg, sd), items[1:8])]
    own += [(regroup.columns(me.dp), regroup.piece(me.dp, me.y, me.c))]
    own = [pltpu.make_async_copy(src, dst, local.at[i]) for i, (src, dst) in enumerate(own)]
    for copy in own:
        copy.start()
    events, (m_pack, m_lat, m_k, m_q, m_v, m_o, m_g, m_d, m_u), drains = ordered(items, (0, 0, 0, 1, 2, 3, 4, 4, 4))
    cursor = Cursor(events)

    def media_load(b):
        rows = pl.ds(pl.multiple_of(b * block_rows, block_rows), block_rows)
        slot = lax.rem(b, 2)
        return pltpu.make_async_copy(media.at[rows, :], med.at[slot], ms.at[slot])
    media_load(0).start()
    cursor.upto(max(m_pack, m_lat))
    for copy in own:
        copy.wait()
    gains[...] = unpacked(packs, own_cols)

    shares = cursor.spread(cursor.done + (m_k - cursor.done) * 2 // 3, blocks - 1)

    @pl.loop(0, blocks - 1)
    def _(b):
        run_at(b, shares)
        pl.when(b + 1 < blocks - 1)(lambda: media_load(b + 1).start())
        media_load(b).wait()
        u, _ = scaled_rows(med[lax.rem(b, 2)].astype(F32))
        n[pl.ds(pl.multiple_of(b * block_rows, block_rows), block_rows), :] = (u * gains[2:3, :] + gains[3:4, :]).astype(BF16)
    u, _ = scaled_rows(lat_all[...].reshape(seq_count * lat_rows, width).astype(F32))
    nl[...] = (u * gains[0:1, :] + gains[1:2, :]).astype(BF16).reshape(nl.shape)
    n[pl.ds(media_rows, lat_rows), :] = nl[me.seq]
    n[pl.ds(media_rows + lat_rows, block_rows - lat_rows), :] = jnp.zeros((block_rows - lat_rows, width), BF16)

    def weight(w, i):
        return pltpu.make_async_copy(w.at[:, :, pl.ds(pl.multiple_of(i * half, 128), half)], wbuf.at[i], ws.at[i])

    def project(rows, w, out, mark):
        for i in range(2):
            weight(w, i).start()
        shares = cursor.spread(mark, 2)

        @pl.loop(0, 2)
        def _(i):
            run_at(i, shares)
            weight(w, i).wait()
            cols = pl.ds(pl.multiple_of(i * half, 128), half)
            out[:, cols] = dot(rows[...], wbuf[i].reshape(width, half)).astype(BF16)
    cursor.upto(m_k)
    project(n, wk, k, cursor.done + (m_q - cursor.done) * 2 // 3)
    cursor.upto(m_q)
    project(nl.reshape(seq_count * lat_rows, width), wq, q.reshape(seq_count * lat_rows, width), cursor.done + 2)
    mask = part_mask(lat_rows)
    lane = lax.broadcasted_iota(jnp.int32, (lat_rows, 128), 1)
    key = lax.broadcasted_iota(jnp.int32, (PART * lat_rows, block_rows), 1)

    def scores(b, part, item):
        cols = pl.ds(pl.multiple_of(part * PCOLS, 128), PCOLS)
        at = pl.ds(pl.multiple_of(b * block_rows, block_rows), block_rows)
        found = dot_t(stacked(q[item, :, cols], mask), k[at, cols]) * SCALE
        return jnp.where(key < jnp.where(b == blocks - 1, lat_rows, block_rows), found, NEG)

    def replicated(stat, part):
        pieces = []
        for h in range(PART):
            column = jnp.sum(jnp.where(lane == part * PART + h, stat, 0.0), axis=-1, keepdims=True)
            pieces.append(jnp.broadcast_to(column, (lat_rows, 128)))
        return jnp.concatenate(pieces, axis=0)

    def place(stat, column, part):
        for h in range(PART):
            stat = jnp.where(lane == part * PART + h, column[h * lat_rows:(h + 1) * lat_rows], stat)
        return stat
    steps = blocks * parts // 2
    tops[...] = jnp.zeros_like(tops)
    shares = cursor.spread(cursor.done + (m_v - cursor.done) // 2, steps)

    @pl.loop(0, steps)
    def _(i):
        b, pair = i // (parts // 2), i % (parts // 2)
        run_at(i, shares)
        item = owner[b]
        for part in (pair * 2, pair * 2 + 1):
            tops[b, 0] = place(tops[b, 0], jnp.max(scores(b, part, item), axis=-1, keepdims=True), part)
    for i in range(seq_count):
        best = jnp.full((lat_rows, 128), NEG, F32)
        for b in range(blocks):
            best = jnp.maximum(best, jnp.where(owner[b] == i, tops[b, 0], NEG))
        stats[i, 0] = best
    shares = cursor.spread(cursor.done + (m_v - cursor.done) // 2, steps)

    @pl.loop(0, steps)
    def _(i):
        b, pair = i // (parts // 2), i % (parts // 2)
        run_at(i, shares)
        item = owner[b]
        for part in (pair * 2, pair * 2 + 1):
            e = jnp.exp(scores(b, part, item) - replicated(stats[item, 0], part))
            expo[b, part] = e.astype(BF16)
            tops[b, 1] = place(tops[b, 1], jnp.sum(e, axis=-1, keepdims=True), part)
    for i in range(seq_count):
        stats[i, 1] = sum(jnp.where(owner[b] == i, tops[b, 1], 0.0) for b in range(blocks))
    acc_f[...] = jnp.zeros_like(acc_f)
    cursor.upto(m_v)
    project(n, wv, v, cursor.done + 4)
    saves = [(n, n_out), (nl, nl_out), (q, q_out), (k, k_out), (v, v_out)]
    saves = [pltpu.make_async_copy(src, dst, outs.at[i]) for i, (src, dst) in enumerate(saves)]
    for copy in saves:
        copy.start()
    shares = cursor.spread(cursor.done + (m_o - cursor.done) // 2, steps)

    @pl.loop(0, steps)
    def _(i):
        b, pair = i // (parts // 2), i % (parts // 2)
        run_at(i, shares)
        item = owner[b]
        for part in (pair * 2, pair * 2 + 1):
            cols = pl.ds(pl.multiple_of(part * PCOLS, 128), PCOLS)
            at = pl.ds(pl.multiple_of(b * block_rows, block_rows), block_rows)
            term = unstacked(dot(expo[b, part], v[at, cols]), mask, lat_rows)
            for j in range(seq_count):
                acc_f[j, :, cols] += jnp.where(item == j, term, 0.0)
    acc[...] = acc_f[...].astype(BF16)
    for i, to in enumerate(seq_peers):
        send(acc.at[to], acc_in.at[me.seq], xs.at[0, i], xr.at[0, me.seq], (me.dp, to))
        send(stats.at[to], stat_in.at[me.seq], xs.at[1, i], xr.at[1, me.seq], (me.dp, to))
    acc_in[me.seq] = acc[me.seq]
    stat_in[me.seq] = stats[me.seq]
    cursor.upto(m_o)
    for source in seq_peers:
        landed(acc_in.at[source], xs.at[0, 0], xr.at[0, source], me)
        landed(stat_in.at[source], xs.at[0, 0], xr.at[1, source], me)
    best = functools.reduce(jnp.maximum, [stat_in[s, 0] for s in range(seq_count)])
    weights = [jnp.exp(stat_in[s, 0] - best) for s in range(seq_count)]
    total = sum(w * stat_in[s, 1] for s, w in enumerate(weights))
    total = jnp.where(lane < HEADS, total, 1.0)
    spread = head_columns(width)
    attended = sum(exact(w / total, spread) * acc_in[s].astype(F32) for s, w in enumerate(weights))
    row_a[...] = attended
    st_in[me.seq, 0] = best + jnp.log(total)
    hidden = lat_all[me.seq].astype(F32) + dot(attended.astype(BF16), wo[...].reshape(width, width))
    row_b[...] = hidden
    scaled, _ = scaled_rows(hidden)
    nf_all[me.dp] = (scaled * gains[4:5, :] + gains[5:6, :]).astype(BF16)
    spread_nf = Gather(me, nf_all.at[me.dp], nf_all, *nf_sems, "zx", 0)
    run(spread_nf.own())
    cursor.upto(max(m_g, m_d))
    all_rows = dp_count * lat_rows
    hidden_cols = gp.shape[1]
    og_all = lambda: og[...].reshape(all_rows, width)
    tile = hidden_cols // 2
    per = seq_count // 2

    @pl.loop(0, 2)
    def _(t):
        at = pl.ds(pl.multiple_of(t * tile, 128), tile)
        ga[:, at] = dot_t(og_all(), dn[pl.ds(t * per, per)].reshape(tile, width))
    run(spread_nf.column())
    cursor.upto(len(events))
    run(spread_nf.neighbours())

    @pl.loop(0, 2)
    def _(t):
        at = pl.ds(pl.multiple_of(t * tile, 128), tile)
        pre = dot(nf_all[...].reshape(all_rows, width), up[:, :, at].reshape(width, tile))
        phi = 0.5 * (1.0 + lax.erf(pre * 0.7071067811865476))
        act[:, at] = (pre * phi).astype(BF16)
        slope = phi + pre * jnp.exp(pre * pre * -0.5) * 0.3989422804014327
        gp[:, at] = (ga[:, at] * slope).astype(BF16)
    group = up.shape[0] // 4
    wide = width // 4

    @pl.loop(0, 4)
    def _(t):
        at = pl.ds(pl.multiple_of(t * wide, 128), wide)
        part_g[:, :, at] = dot_t(gp[...], up[pl.ds(t * group, group)].reshape(wide, hidden_cols)).astype(BF16).reshape(dp_count, lat_rows, wide)
    sum_g = DpScatter(me, part_g, own_sum, ox_g, zz_g, *g_sems)
    run(far_first(me, sum_g.start))

    @pl.loop(0, 3)
    def _(t):
        at = pl.ds(pl.multiple_of(t * 512, 512), 512)
        part_y[:, :, at] = dot(act[...], dn[:, :, at].reshape(hidden_cols, 512)).astype(BF16).reshape(dp_count, lat_rows, 512)
    run(far_first(me, sum_g.fold))
    sum_y = DpScatter(me, part_y, own_sum, ox_y, zz_y, *y_sems)
    run(far_first(me, sum_y.start))
    gwd_v[...] = t_dot(act[...], og_all()).astype(BF16)
    save_d = pltpu.make_async_copy(gwd_v, gwd, outs.at[5])
    save_d.start()
    sum_g.finish()
    gathered = own_sum[...]
    scaled, inverse = scaled_rows(row_b[...])
    sums[...] = jnp.zeros_like(sums)
    sums[0:1, :] = jnp.sum(gathered * scaled, axis=0, keepdims=True)
    sums[1:2, :] = jnp.sum(gathered, axis=0, keepdims=True)
    grad = og[me.dp].astype(F32) + norm_back(gathered, scaled, inverse, gains[4:5, :])
    grad_hidden[...] = grad
    low = grad.astype(BF16)
    grad_att = dot_t(low, wo[...].reshape(width, width)).astype(BF16)
    do_in[me.seq] = grad_att
    st_in[me.seq, 1] = exact_t(grad_att.astype(F32) * row_a[...], spread)
    spread_do = Gather(me, do_in.at[me.seq], do_in, *do_sems, "yc", 0)
    spread_st = Gather(me, st_in.at[me.seq], st_in, *st_sems, "yc", 0)
    run(spread_do.own())
    run(spread_st.own())
    run(far_first(me, sum_y.fold))
    save_o = []
    for i in range(2):
        cols = pl.ds(i * half, half)
        if i:
            save_o[0].wait()
        gwo_v[...] = t_dot(row_a[...].astype(BF16), low[:, i * half:(i + 1) * half]).astype(BF16)
        save_o.append(pltpu.make_async_copy(gwo_v, gwo.at[:, cols], outs.at[6 + i]))
        save_o[-1].start()
    run(spread_do.neighbours())
    run(spread_st.neighbours())
    gwu_v[...] = t_dot(nf_all[...].reshape(all_rows, width), gp[...]).astype(BF16)
    save_u = pltpu.make_async_copy(gwu_v, gwu, outs.at[8])
    save_u.start()
    sum_y.finish()
    lat_out[...] = (row_b[...] + own_sum[...]).astype(BF16)
    run(spread_do.sibling())
    run(spread_st.sibling())
    do_all[...] = do_in[...]
    stat_all[...] = st_in[...]
    for i in range(len(seq_peers)):
        sent(acc_in.at[0], xs.at[0, i], xr.at[0, 0], me)
        sent(stat_in.at[0], xs.at[1, i], xr.at[0, 0], me)
    run(drains)
    for item in (spread_nf, sum_g, sum_y, spread_do, spread_st):
        run(item.drain())
    for copy in saves + save_o[1:] + [save_d, save_u]:
        copy.wait()


def forward(dp_count, owner, media, pack, lat, sq, sk, sv, so, sg, sd, su, block_rows, own_cols):
    nz = dp_count // 2
    rows, width = lat.shape
    items, count = 4, dp_count * 4
    hidden = su.shape[1] // dp_count
    total = media.shape[0] + block_rows
    blocks = total // block_rows
    parts = HEADS // PART
    all_rows = dp_count * rows
    shape = jax.ShapeDtypeStruct
    buf = lambda *s: pltpu.VMEM(s, BF16)
    flt = lambda *s: pltpu.VMEM(s, F32)
    square = shape((count, width // count, width), BF16)
    stat = (items, 2, rows, 128)
    line = [buf(nz, rows, width), buf(nz, rows, width)]
    return pl.pallas_call(
        functools.partial(forward_kernel, dp_count, block_rows, own_cols),
        out_shape=(
            square, square, square, shape((total, width), BF16), shape((items, rows, width), BF16), shape((items, rows, width), BF16),
            shape((total, width), BF16), shape((total, width), BF16),
            shape((width, width), BF16), shape((width, hidden), BF16), shape((hidden, width), BF16),
            shape((8, width), F32), shape((rows, width), BF16), shape((rows, width), F32),
            shape((items, rows, width), BF16), shape(stat, F32), shape((8, width), F32),
        ),
        in_specs=[pl.BlockSpec(memory_space=pltpu.SMEM)] + [ANY] * 10,
        out_specs=tuple([ANY] * 11 + [VMEM] * 6),
        scratch_shapes=[
            flt(count, 8, 128), buf(items, rows, width), buf(count, width // count, width), buf(dp_count, rows, width),
            buf(items, hidden // items, width), buf(count, width // count, hidden), buf(2, block_rows, width),
            buf(total, width), buf(items, rows, width), buf(items, rows, width), buf(total, width), buf(total, width),
            buf(blocks, parts, PART * rows, block_rows), flt(items, rows, width), buf(items, rows, width),
            flt(blocks, 2, rows, 128), flt(*stat), buf(2, count, width // count, width // 2),
            buf(items, rows, width), flt(*stat), buf(dp_count, rows, width), flt(all_rows, hidden), buf(all_rows, hidden), buf(all_rows, hidden),
            buf(dp_count, rows, width), *line, buf(dp_count, rows, width), *line,
            flt(rows, width), flt(rows, width), flt(rows, width), buf(items, rows, width), flt(*stat),
            buf(width, width // 2), buf(width, hidden), buf(hidden, width),
            DMA((9,)), DMA((2,)), DMA((2,)), DMA((9,)), DMA((2, items)), DMA((2, items)),
            *Regroup.semaphores(dp_count), DMA((1,)), DMA((1,)), *DpScatter.semaphores(nz), *DpScatter.semaphores(nz),
            *[sem for axes in ("yc", "zxyc", "zxyc", "zxyc", "zxyc", "zx", "yc", "zx", "yc", "yc") for sem in Gather.semaphores(axes, nz)],
        ],
        compiler_params=pltpu.CompilerParams(collective_id=1, has_side_effects=True, vmem_limit_bytes=WIDE),
    )(owner, media, pack, lat, sq, sk, sv, so, sg, sd, su)


def local_fast(
    media, latents, out_grad, frame_counts, block_position, w_query, w_key, w_value, w_out, w_up, w_down,
    gain_lat, shift_lat, gain_media, shift_media, gain_ffn, shift_ffn,
):
    dp_count, seq_count = lax.axis_size("dp"), lax.axis_size("seq")
    seq = lax.axis_index("seq")
    blocks, block_rows, width = media.shape
    items, lat_rows = seq_count, latents.shape[1]
    own_cols = gain_lat.shape[0]
    ends = FRAME_BLOCKS * jnp.cumsum(frame_counts[0])
    position = lax.dynamic_slice_in_dim(block_position[0], seq * blocks, blocks)
    owner = jnp.sum((ends[None, :] <= position[:, None]).astype(jnp.int32), axis=1)
    owner = jnp.concatenate([owner, seq[None]])
    vectors = jnp.stack([gain_lat, shift_lat, gain_media, shift_media, gain_ffn, shift_ffn]).astype(F32)
    pack = jnp.pad(vectors, ((0, 2), (0, 128 - own_cols)))
    lat, og = latents.reshape(lat_rows, width), out_grad.reshape(lat_rows, width)
    med = media.reshape(-1, width)
    (wq, wk, wv, n, nl, q, k, v, gwo, gwu, gwd, gains, lat_out, grad_hidden, do_all, stat_all, sums_ffn) = forward(
        dp_count, owner, med, pack, lat, w_query, w_key, w_value, w_out, og, w_down, w_up, block_rows, own_cols)
    wq, wk, wv = [w.reshape(width, width) for w in (wq, wk, wv)]
    media_grad, lat_grad, sums, out_q, out_k, out_v, out_o, out_up, out_dn = backward(
        dp_count, owner, lat, grad_hidden, gains, sums_ffn, n, nl, q, k, v, do_all, stat_all, gwo, gwu, gwd, med, wq, wk, wv, block_rows)
    place = (lax.axis_index("dp") * seq_count + seq) * own_cols
    own = lax.dynamic_slice_in_dim(sums, place, own_cols, axis=1)
    lat_out, lat_grad, media_grad, *grads = copied(lat_out, lat_grad, media_grad, out_q, out_k, out_v, out_o, out_up, out_dn)
    return (lat_out.reshape(latents.shape), lat_grad.reshape(latents.shape), media_grad.reshape(media.shape), *grads, *[own[i] for i in range(6)])


def fits(mesh):
    return mesh.shape["seq"] == 4 and mesh.shape["dp"] % 2 == 0 and 1536 % (mesh.shape["dp"] * 64) == 0


def norm_forward(rows, gain, shift):
    mean = jnp.mean(rows, axis=-1, keepdims=True)
    centred = rows - mean
    variance = jnp.mean(centred * centred, axis=-1, keepdims=True)
    inverse = lax.rsqrt(variance + EPS)
    scaled = centred * inverse
    return (scaled * gain + shift, scaled, inverse)


def norm_backward(incoming, scaled, inverse, gain):
    inner = incoming * gain
    first = jnp.mean(inner, axis=-1, keepdims=True)
    second = jnp.mean(inner * scaled, axis=-1, keepdims=True)
    return (
        inverse * (inner - first - scaled * second),
        jnp.sum(incoming * scaled, axis=0),
        jnp.sum(incoming, axis=0),
    )


def matmul(left, right):
    return jnp.dot(left, right, preferred_element_type=jnp.float32)


def matmul_left_t(left, right):
    return lax.dot_general(
        left, right, (((0,), (0,)), ((), ())), preferred_element_type=jnp.float32
    )


def matmul_right_t(left, right):
    return lax.dot_general(
        left, right, (((1,), (1,)), ((), ())), preferred_element_type=jnp.float32
    )


def swap_rows(stat):
    return jnp.swapaxes(stat, 1, 2)[..., None]


def fold_sources(tops, totals, accums):
    best = jnp.max(tops, axis=0)
    factor = jnp.exp(tops - best[None])
    total = jnp.sum(factor * totals, axis=0)
    width = accums.shape[-1]
    spread = jnp.repeat(jnp.swapaxes(factor, 2, 3), width // factor.shape[2], axis=3)
    return (best, total, jnp.sum(accums * spread, axis=0))


def local(
    media,
    latents,
    out_grad,
    frame_counts,
    block_position,
    w_query,
    w_key,
    w_value,
    w_out,
    w_up,
    w_down,
    gain_lat,
    shift_lat,
    gain_media,
    shift_media,
    gain_ffn,
    shift_ffn,
):
    gathered = (
        lax.all_gather(w_query, ("dp", "seq"), axis=0, tiled=True),
        lax.all_gather(w_key, ("dp", "seq"), axis=0, tiled=True),
        lax.all_gather(w_value, ("dp", "seq"), axis=0, tiled=True),
        lax.all_gather(w_out, ("dp", "seq"), axis=0, tiled=True),
        lax.all_gather(w_up, ("dp", "seq"), axis=0, tiled=True),
        lax.all_gather(w_down, ("dp", "seq"), axis=0, tiled=True),
        lax.all_gather(gain_lat, ("dp", "seq"), axis=0, tiled=True),
        lax.all_gather(shift_lat, ("dp", "seq"), axis=0, tiled=True),
        lax.all_gather(gain_media, ("dp", "seq"), axis=0, tiled=True),
        lax.all_gather(shift_media, ("dp", "seq"), axis=0, tiled=True),
        lax.all_gather(gain_ffn, ("dp", "seq"), axis=0, tiled=True),
        lax.all_gather(shift_ffn, ("dp", "seq"), axis=0, tiled=True),
    )
    full_query, full_key, full_value, full_out, full_up, full_down = gathered[:6]
    lat_gain, lat_shift, med_gain, med_shift, ffn_gain, ffn_shift = [
        piece.astype(jnp.float32) for piece in gathered[6:]
    ]
    seq_rank = lax.axis_index("seq")
    seq_count = lax.axis_size("seq")
    blocks, block_rows, width = media.shape
    local_items, lat_rows, _ = latents.shape
    group_items = frame_counts.shape[1]
    heads = HEADS
    head_size = HEAD_DIM
    score_scale = head_size ** (-0.5)
    ends = FRAME_BLOCKS * jnp.cumsum(frame_counts[0])
    position = lax.dynamic_slice_in_dim(block_position[0], seq_rank * blocks, blocks)
    owner_item = jnp.sum((ends[None, :] <= position[:, None]).astype(jnp.int32), axis=1)
    member = (owner_item[:, None] == jnp.arange(group_items, dtype=jnp.int32)[None, :]).astype(
        jnp.float32
    )
    lat_input = latents.astype(jnp.float32).reshape(-1, width)
    normed_lat, scaled_lat, inverse_lat = norm_forward(lat_input, lat_gain, lat_shift)
    normed_lat = normed_lat.astype(jnp.bfloat16)
    query = matmul(normed_lat, full_query).astype(jnp.bfloat16)
    key_lat = (
        matmul(normed_lat, full_key)
        .astype(jnp.bfloat16)
        .reshape(local_items, lat_rows, heads, head_size)
    )
    value_lat = (
        matmul(normed_lat, full_value)
        .astype(jnp.bfloat16)
        .reshape(local_items, lat_rows, heads, head_size)
    )
    query_all = lax.all_gather(
        query.reshape(local_items, lat_rows, width), "seq", axis=0, tiled=True
    )
    med_input = media.astype(jnp.float32).reshape(-1, width)
    normed_med, scaled_med, inverse_med = norm_forward(med_input, med_gain, med_shift)
    normed_med = normed_med.astype(jnp.bfloat16)

    def media_keys(weight_key, weight_value):
        keys_out = (
            matmul(normed_med, weight_key)
            .astype(jnp.bfloat16)
            .reshape(blocks, block_rows, heads, head_size)
        )
        values_out = (
            matmul(normed_med, weight_value)
            .astype(jnp.bfloat16)
            .reshape(blocks, block_rows, heads, head_size)
        )
        return (keys_out, values_out)

    key_med, value_med = media_keys(full_key, full_value)
    query_blk = query_all[owner_item].reshape(blocks, lat_rows, heads, head_size)
    scores_med = (
        jnp.einsum("bqhd,bkhd->bhqk", query_blk, key_med, preferred_element_type=jnp.float32)
        * score_scale
    )
    block_top = jnp.max(scores_med, axis=-1)
    expo_med = jnp.exp(scores_med - block_top[..., None])
    expo_med_low = expo_med.astype(jnp.bfloat16)
    local_top = jnp.max(jnp.where(member.T[:, :, None, None] > 0, block_top[None], NEG), axis=1)
    to_local = jnp.exp(block_top - local_top[owner_item])
    local_total = jnp.einsum(
        "bi,bhq->ihq", member, to_local * jnp.sum(expo_med, axis=-1), precision=HIGH
    )
    accum_blk = jnp.einsum(
        "bhqk,bkhd->bqhd", expo_med_low, value_med, preferred_element_type=jnp.float32
    ) * swap_rows(to_local)
    local_accum = jnp.einsum("bi,bqhd->iqhd", member, accum_blk, precision=HIGH).reshape(
        group_items, lat_rows, width
    )
    part_top, part_total, part_accum = (
        lax.all_to_all(local_top, "seq", split_axis=0, concat_axis=0, tiled=True),
        lax.all_to_all(local_total, "seq", split_axis=0, concat_axis=0, tiled=True),
        lax.all_to_all(local_accum, "seq", split_axis=0, concat_axis=0, tiled=True),
    )
    top_own, total_own, accum_flat = fold_sources(
        part_top.reshape(seq_count, local_items, heads, lat_rows),
        part_total.reshape(seq_count, local_items, heads, lat_rows),
        part_accum.reshape(seq_count, local_items, lat_rows, width),
    )
    med_top = lax.all_gather(top_own, "seq", axis=0, tiled=True)
    accum_own = accum_flat.reshape(local_items, lat_rows, heads, head_size)
    query_lat = query.reshape(local_items, lat_rows, heads, head_size)
    scores_lat = (
        jnp.einsum("iqhd,ikhd->ihqk", query_lat, key_lat, preferred_element_type=jnp.float32)
        * score_scale
    )
    lat_top = jnp.max(scores_lat, axis=-1)
    expo_lat = jnp.exp(scores_lat - lat_top[..., None])
    expo_lat_low = expo_lat.astype(jnp.bfloat16)
    item_top = jnp.maximum(top_own, lat_top)
    media_weight = jnp.exp(top_own - item_top)
    lat_weight = jnp.exp(lat_top - item_top)
    item_total = total_own * media_weight + lat_weight * jnp.sum(expo_lat, axis=-1)
    inverse_total = 1.0 / item_total
    accum_lat = jnp.einsum(
        "ihqk,ikhd->iqhd", expo_lat_low, value_lat, preferred_element_type=jnp.float32
    ) * swap_rows(lat_weight)
    attended = (accum_own * swap_rows(media_weight) + accum_lat) * swap_rows(inverse_total)
    attended_low = attended.reshape(-1, width).astype(jnp.bfloat16)
    hidden = lat_input + matmul(attended_low, full_out)
    normed_ffn, scaled_ffn, inverse_ffn = norm_forward(hidden, ffn_gain, ffn_shift)
    normed_ffn = normed_ffn.astype(jnp.bfloat16)
    pre_act = matmul(normed_ffn, full_up)
    activated, gelu_back = jax.vjp(partial(jax.nn.gelu, approximate=False), pre_act)
    activated = activated.astype(jnp.bfloat16)
    result = hidden + matmul(activated, full_down)
    latents_out = result.astype(jnp.bfloat16).reshape(latents.shape)
    again = (
        lax.all_gather(w_query, ("dp", "seq"), axis=0, tiled=True),
        lax.all_gather(w_key, ("dp", "seq"), axis=0, tiled=True),
        lax.all_gather(w_value, ("dp", "seq"), axis=0, tiled=True),
        lax.all_gather(w_out, ("dp", "seq"), axis=0, tiled=True),
        lax.all_gather(w_up, ("dp", "seq"), axis=0, tiled=True),
        lax.all_gather(w_down, ("dp", "seq"), axis=0, tiled=True),
        lax.all_gather(gain_lat, ("dp", "seq"), axis=0, tiled=True),
        lax.all_gather(shift_lat, ("dp", "seq"), axis=0, tiled=True),
        lax.all_gather(gain_media, ("dp", "seq"), axis=0, tiled=True),
        lax.all_gather(shift_media, ("dp", "seq"), axis=0, tiled=True),
        lax.all_gather(gain_ffn, ("dp", "seq"), axis=0, tiled=True),
        lax.all_gather(shift_ffn, ("dp", "seq"), axis=0, tiled=True),
    )
    back_query, back_key, back_value, back_out, back_up, back_down = again[:6]
    grad_rows = out_grad.reshape(-1, width)
    cotangent = grad_rows.astype(jnp.float32)
    grad_down = matmul_left_t(activated, grad_rows)
    grad_act = matmul_right_t(grad_rows, back_down)
    grad_pre = gelu_back(grad_act)[0].astype(jnp.bfloat16)
    grad_up = matmul_left_t(normed_ffn, grad_pre)
    grad_normed_ffn = matmul_right_t(grad_pre, back_up)
    grad_hidden_norm, grad_gain_ffn, grad_shift_ffn = norm_backward(
        grad_normed_ffn, scaled_ffn, inverse_ffn, ffn_gain
    )
    grad_hidden = cotangent + grad_hidden_norm
    grad_hidden_low = grad_hidden.astype(jnp.bfloat16)
    grad_out = matmul_left_t(attended_low, grad_hidden_low)
    grad_att = matmul_right_t(grad_hidden_low, back_out).astype(jnp.bfloat16)
    grad_att_heads = grad_att.reshape(local_items, lat_rows, heads, head_size)
    delta = jnp.einsum(
        "iqhd,iqhd->ihq", grad_att_heads.astype(jnp.float32), attended, precision=HIGH
    )
    media_factor = media_weight * inverse_total
    grad_att_all = lax.all_gather(
        grad_att.reshape(local_items, lat_rows, width), "seq", axis=0, tiled=True
    )
    factor_all, delta_all = (
        lax.all_gather(media_factor, "seq", axis=0, tiled=True),
        lax.all_gather(delta, "seq", axis=0, tiled=True),
    )
    key_med, value_med = media_keys(back_key, back_value)
    grad_blk = grad_att_all[owner_item].reshape(blocks, lat_rows, heads, head_size)
    factor_blk = jnp.exp(block_top - med_top[owner_item]) * factor_all[owner_item]
    delta_blk = delta_all[owner_item]
    grad_prob_med = jnp.einsum(
        "bqhd,bkhd->bhqk", grad_blk, value_med, preferred_element_type=jnp.float32
    )
    grad_score_med = (
        expo_med * factor_blk[..., None] * (grad_prob_med - delta_blk[..., None])
    ).astype(jnp.bfloat16)
    grad_query_blk = (
        jnp.einsum("bhqk,bkhd->bqhd", grad_score_med, key_med, preferred_element_type=jnp.float32)
        * score_scale
    )
    grad_query_part = jnp.einsum("bi,bqhd->iqhd", member, grad_query_blk, precision=HIGH).reshape(
        group_items, lat_rows, width
    )
    grad_key_med = (
        (
            jnp.einsum(
                "bhqk,bqhd->bkhd", grad_score_med, query_blk, preferred_element_type=jnp.float32
            )
            * score_scale
        )
        .astype(jnp.bfloat16)
        .reshape(-1, width)
    )
    grad_value_med = (
        jnp.einsum(
            "bhqk,bqhd->bkhd",
            expo_med_low.astype(jnp.float32) * factor_blk[..., None],
            grad_blk.astype(jnp.float32),
            precision=HIGH,
        )
        .astype(jnp.bfloat16)
        .reshape(-1, width)
    )
    grad_query_own = lax.psum_scatter(
        grad_query_part.astype(jnp.bfloat16), "seq", scatter_dimension=0, tiled=True
    ).astype(jnp.float32)
    grad_normed_med = matmul_right_t(grad_key_med, back_key) + matmul_right_t(
        grad_value_med, back_value
    )
    grad_key = matmul_left_t(normed_med, grad_key_med)
    grad_value = matmul_left_t(normed_med, grad_value_med)
    media_grad, grad_gain_media, grad_shift_media = norm_backward(
        grad_normed_med, scaled_med, inverse_med, med_gain
    )
    lat_factor = lat_weight * inverse_total
    grad_prob_lat = jnp.einsum(
        "iqhd,ikhd->ihqk", grad_att_heads, value_lat, preferred_element_type=jnp.float32
    )
    grad_score_lat = (expo_lat * lat_factor[..., None] * (grad_prob_lat - delta[..., None])).astype(
        jnp.bfloat16
    )
    grad_query_lat = (
        jnp.einsum("ihqk,ikhd->iqhd", grad_score_lat, key_lat, preferred_element_type=jnp.float32)
        * score_scale
    )
    grad_key_lat = (
        (
            jnp.einsum(
                "ihqk,iqhd->ikhd", grad_score_lat, query_lat, preferred_element_type=jnp.float32
            )
            * score_scale
        )
        .astype(jnp.bfloat16)
        .reshape(-1, width)
    )
    grad_value_lat = (
        jnp.einsum(
            "ihqk,iqhd->ikhd",
            expo_lat_low.astype(jnp.float32) * lat_factor[..., None],
            grad_att_heads.astype(jnp.float32),
            precision=HIGH,
        )
        .astype(jnp.bfloat16)
        .reshape(-1, width)
    )
    grad_query = (
        (grad_query_own + grad_query_lat.reshape(local_items, lat_rows, width))
        .astype(jnp.bfloat16)
        .reshape(-1, width)
    )
    grad_normed_lat = (
        matmul_right_t(grad_query, back_query)
        + matmul_right_t(grad_key_lat, back_key)
        + matmul_right_t(grad_value_lat, back_value)
    )
    grad_query_weight = matmul_left_t(normed_lat, grad_query)
    grad_key = grad_key + matmul_left_t(normed_lat, grad_key_lat)
    grad_value = grad_value + matmul_left_t(normed_lat, grad_value_lat)
    grad_lat_norm, grad_gain_lat, grad_shift_lat = norm_backward(
        grad_normed_lat, scaled_lat, inverse_lat, lat_gain
    )
    latents_grad = (grad_hidden + grad_lat_norm).reshape(latents.shape)
    sharded = (
        lax.psum_scatter(grad_query_weight, ("dp", "seq"), scatter_dimension=0, tiled=True),
        lax.psum_scatter(grad_key, ("dp", "seq"), scatter_dimension=0, tiled=True),
        lax.psum_scatter(grad_value, ("dp", "seq"), scatter_dimension=0, tiled=True),
        lax.psum_scatter(grad_out, ("dp", "seq"), scatter_dimension=0, tiled=True),
        lax.psum_scatter(grad_up, ("dp", "seq"), scatter_dimension=0, tiled=True),
        lax.psum_scatter(grad_down, ("dp", "seq"), scatter_dimension=0, tiled=True),
        lax.psum_scatter(grad_gain_lat, ("dp", "seq"), scatter_dimension=0, tiled=True),
        lax.psum_scatter(grad_shift_lat, ("dp", "seq"), scatter_dimension=0, tiled=True),
        lax.psum_scatter(grad_gain_media, ("dp", "seq"), scatter_dimension=0, tiled=True),
        lax.psum_scatter(grad_shift_media, ("dp", "seq"), scatter_dimension=0, tiled=True),
        lax.psum_scatter(grad_gain_ffn, ("dp", "seq"), scatter_dimension=0, tiled=True),
        lax.psum_scatter(grad_shift_ffn, ("dp", "seq"), scatter_dimension=0, tiled=True),
    )
    return (latents_out, latents_grad, media_grad.reshape(media.shape)) + tuple(sharded)


def solution(mesh):
    return jax.shard_map(
        local_fast if fits(mesh) else local,
        mesh=mesh,
        in_specs=(
            P(("dp", "seq"), None, None),
            P(("dp", "seq"), None, None),
            P(("dp", "seq"), None, None),
            P("dp", None),
            P("dp", None),
            P(("dp", "seq"), None),
            P(("dp", "seq"), None),
            P(("dp", "seq"), None),
            P(("dp", "seq"), None),
            P(("dp", "seq"), None),
            P(("dp", "seq"), None),
            P(("dp", "seq")),
            P(("dp", "seq")),
            P(("dp", "seq")),
            P(("dp", "seq")),
            P(("dp", "seq")),
            P(("dp", "seq")),
        ),
        out_specs=(
            P(("dp", "seq"), None, None),
            P(("dp", "seq"), None, None),
            P(("dp", "seq"), None, None),
            P(("dp", "seq"), None),
            P(("dp", "seq"), None),
            P(("dp", "seq"), None),
            P(("dp", "seq"), None),
            P(("dp", "seq"), None),
            P(("dp", "seq"), None),
            P(("dp", "seq")),
            P(("dp", "seq")),
            P(("dp", "seq")),
            P(("dp", "seq")),
            P(("dp", "seq")),
            P(("dp", "seq")),
        ),
        check_vma=False,
    )
```

```python
import math
from functools import partial
from jax.sharding import PartitionSpec as P
import functools
import jax
import jax.numpy as jnp
from jax import lax
from jax.experimental import pallas as pl
from jax.experimental.pallas import tpu as pltpu

MESH = pl.DeviceIdType.MESH
ANY = pl.BlockSpec(memory_space=pl.ANY)
VMEM = pl.BlockSpec(memory_space=pltpu.VMEM)
DMA = pltpu.SemaphoreType.DMA


class Here:
    def __init__(self, dp_count):
        dp, seq = lax.axis_index("dp"), lax.axis_index("seq")
        self.nz = dp_count // 2
        self.z, self.x, self.y, self.c = dp // 2, dp % 2, seq // 2, seq % 2
        self.dp, self.seq = dp, seq

    def at(self, z=None, x=None, y=None, c=None):
        z = self.z if z is None else z
        x = self.x if x is None else x
        y = self.y if y is None else y
        c = self.c if c is None else c
        return (z * 2 + x, y * 2 + c)


def send(src, dst, ss, rs, to):
    copy = pltpu.make_async_remote_copy(
        src_ref=src, dst_ref=dst, send_sem=ss, recv_sem=rs, device_id=to, device_id_type=MESH
    )
    copy.start()


def landed(dst, ss, rs, me):
    pltpu.make_async_remote_copy(
        src_ref=dst, dst_ref=dst, send_sem=ss, recv_sem=rs, device_id=me.at(c=1 - me.c), device_id_type=MESH
    ).wait_recv()


def sent(src, ss, rs, me):
    pltpu.make_async_remote_copy(
        src_ref=src, dst_ref=src, send_sem=ss, recv_sem=rs, device_id=me.at(c=1 - me.c), device_id_type=MESH
    ).wait_send()


def greet(devices):
    barrier = pltpu.get_barrier_semaphore()
    for device in devices:
        pl.semaphore_signal(barrier, inc=1, device_id=device, device_id_type=MESH)
    pl.semaphore_wait(barrier, len(devices))


COL, FROMX, FROMY, DIAGA, DIAGB = range(5)
TOUP, TODOWN, TOX, TOY, FWDY, FWDX, TOC = range(7)


class Gather:
    def __init__(self, me, src, dst, ss, rs, axes, halves):
        self.me, self.src, self.dst, self.ss, self.rs = me, src, dst, ss, rs
        self.axes, self.halves = axes, halves
        self.sends = []
        self.depth = me.nz if "z" in axes else 1

    def slot(self, z, x, y, c):
        if self.axes == "zxyc":
            return ((z * 2 + x) * 2 + y) * 2 + c
        if self.axes == "zx":
            return z * 2 + x
        return y * 2 + c

    def shard(self, z, x, y, c, half=None):
        ref = self.dst.at[self.slot(z, x, y, c)]
        if half is None or not self.halves:
            return ref
        cut, width = self.halves, self.dst.shape[-1]
        return ref.at[:, pl.ds(0, cut)] if half == 0 else ref.at[:, pl.ds(cut, width - cut)]

    def key(self, z):
        return z if "z" in self.axes else 0

    def start(self, src, dst, out_kind, in_kind, z, to):
        send(src, dst, self.leaves(out_kind, z), self.arrives(in_kind, z), to)

    def leaves(self, kind, z):
        return self.ss.at[1 + kind * self.depth + z] if kind in (TOUP, TODOWN) else self.ss.at[0]

    def arrives(self, kind, z):
        return self.rs.at[5 * self.depth if kind >= 5 else kind * self.depth + self.key(z)]

    def whole(self, count):
        return self.dst.at[pl.ds(0, count)]

    def gone(self, ref, kind, z):
        sent(ref, self.leaves(kind, z), self.rs.at[0], self.me)

    def here(self, ref, kind, z):
        landed(ref, self.ss.at[0], self.arrives(kind, z), self.me)

    def groups(self):
        return dict(own=self.own(), column=self.column(), neighbours=self.neighbours(), diagonal=self.diagonal(), sibling=self.sibling())

    @staticmethod
    def semaphores(axes, nz):
        depth = nz if "z" in axes else 1
        return [DMA((1 + 2 * depth,)), DMA((5 * depth + 1,))]

    def hand_over(self, ref, kind, z):
        if "c" in self.axes:
            self.start(ref, ref, TOC + kind, 5 + kind, z, self.me.at(c=1 - self.me.c))

    def spread(self, ref, z):
        me = self.me
        if "x" in self.axes:
            self.start(ref, ref, TOX, FROMX, z, me.at(x=1 - me.x))
        if "y" in self.axes:
            self.start(ref, ref, TOY, FROMY, z, me.at(y=1 - me.y))
        self.hand_over(ref, COL, z)

    def own(self):
        return [self.send_own]

    def send_own(self):
        me = self.me
        ref = self.shard(me.z, me.x, me.y, me.c)
        if "z" in self.axes:
            @pl.when(me.z + 1 < me.nz)
            def _():
                self.start(self.src, ref, TOUP, COL, me.z, me.at(z=me.z + 1))

            @pl.when(me.z > 0)
            def _():
                self.start(self.src, ref, TODOWN, COL, me.z, me.at(z=me.z - 1))
        if "x" in self.axes:
            self.start(self.src, ref, TOX, FROMX, me.z, me.at(x=1 - me.x))
        if "y" in self.axes:
            self.start(self.src, ref, TOY, FROMY, me.z, me.at(y=1 - me.y))
        if "c" in self.axes:
            self.start(self.src, ref, TOC, 5, me.z, me.at(c=1 - me.c))

    def around(self, event):
        me = self.me
        found = [lambda: event(me.z)]
        for d in range(1, self.depth):
            found.append(lambda d=d: pl.when(me.z >= d)(lambda: event(me.z - d)))
            found.append(lambda d=d: pl.when(me.z + d < me.nz)(lambda: event(me.z + d)))
        return found

    def column(self):
        me = self.me

        def event(d, below):
            there = me.z - d if below else me.z + d
            ahead = me.z + 1 if below else me.z - 1

            @pl.when(there >= 0 if below else there < me.nz)
            def _():
                ref = self.shard(there, me.x, me.y, me.c)
                self.here(ref, COL, there)

                @pl.when(ahead < me.nz if below else ahead >= 0)
                def _():
                    self.start(ref, ref, TOUP if below else TODOWN, COL, there, me.at(z=ahead))
                self.spread(ref, there)
        return [functools.partial(event, d, below) for d in range(1, self.depth) for below in (True, False)]

    def neighbours(self):
        me = self.me

        def event(z):
            if "x" in self.axes:
                ref = self.shard(z, 1 - me.x, me.y, me.c)
                self.here(ref, FROMX, z)
                if "y" in self.axes:
                    half = self.shard(z, 1 - me.x, me.y, me.c, 0)
                    self.start(half, half, FWDY, DIAGA, z, me.at(y=1 - me.y))
                self.hand_over(ref, FROMX, z)
            if "y" in self.axes:
                ref = self.shard(z, me.x, 1 - me.y, me.c)
                self.here(ref, FROMY, z)
                if "x" in self.axes and self.halves:
                    half = self.shard(z, me.x, 1 - me.y, me.c, 1)
                    self.start(half, half, FWDX, DIAGB, z, me.at(x=1 - me.x))
                self.hand_over(ref, FROMY, z)
        return self.around(event)

    def diagonal(self):
        me = self.me
        if "x" not in self.axes or "y" not in self.axes:
            return []

        def event(z):
            for half in range(2 if self.halves else 1):
                ref = self.shard(z, 1 - me.x, 1 - me.y, me.c, half)
                self.here(ref, DIAGA + half, z)
                self.hand_over(ref, DIAGA + half, z)
        return self.around(event)

    def kinds(self):
        me = self.me
        found = [(COL, me.x, me.y, None)]
        if "x" in self.axes:
            found.append((FROMX, 1 - me.x, me.y, None))
        if "y" in self.axes:
            found.append((FROMY, me.x, 1 - me.y, None))
        if "x" in self.axes and "y" in self.axes:
            found.append((DIAGA, 1 - me.x, 1 - me.y, 0))
            if self.halves:
                found.append((DIAGB, 1 - me.x, 1 - me.y, 1))
        return found

    def sibling(self):
        if "c" not in self.axes:
            return []
        count = self.depth * (1 + ("x" in self.axes)) * (1 + ("y" in self.axes))
        return [lambda: self.here(self.whole(count), 5, 0)]

    def drain(self):
        me = self.me
        x, y, c = ["xyc".index(a) >= 0 and a in self.axes for a in "xyc"]
        count = self.depth * (x + y + (x and y) + c * (1 + x) * (1 + y))
        found = [lambda: self.gone(self.whole(count), TOC, 0)]
        if "z" in self.axes:
            shard = self.shard(me.z, me.x, me.y, me.c)

            def event(z):
                pl.when((z <= me.z) & (me.z + 1 < me.nz))(lambda: self.gone(shard, TOUP, z))
                pl.when((z >= me.z) & (me.z > 0))(lambda: self.gone(shard, TODOWN, z))
            found += self.around(event)
        return found

    def phases(self):
        return [self.own(), self.column(), self.neighbours(), self.diagonal(), self.sibling(), self.drain()]


def skewed(items):
    lists = [item.phases() for item in items]
    found = []
    for step in range(len(lists) + max(map(len, lists)) - 1):
        for i, phases in enumerate(lists):
            if 0 <= step - i < len(phases):
                found += phases[step - i]
    return found


def run(events):
    for event in events:
        event()


def share(events, count):
    cuts = [len(events) * i // count for i in range(count + 1)]
    return [events[a:b] for a, b in zip(cuts, cuts[1:])]


def run_at(step, lists):
    for i, events in enumerate(lists):
        if events:
            pl.when(step == i)(functools.partial(run, events))


class Regroup:
    def __init__(self, me, dp_count, src, dst, ss, rs, width):
        self.me, self.n, self.src, self.dst, self.ss, self.rs, self.width = me, dp_count, src, dst, ss, rs, width

    def piece(self, dp, y, c):
        return self.dst.at[dp * 4 + y * 2 + c]

    def columns(self, dp):
        return self.src.at[:, pl.ds(pl.multiple_of(dp * self.width, 128), self.width)]

    def hand(self, src, dp, y, place, to):
        send(src, self.piece(dp, y, self.me.c), self.ss.at[0], self.rs.at[place], to)

    def own(self):
        me = self.me
        for k in range(1, self.n):
            to = lax.rem(me.dp + k, self.n)
            self.hand(self.columns(to), me.dp, me.y, me.dp, (to, me.seq))
        self.share(self.columns(me.dp), me.dp)

    def share(self, src, dp):
        me = self.me
        self.hand(src, dp, me.y, self.n + dp, me.at(y=1 - me.y))
        self.hand(src, dp, me.y, 2 * self.n, me.at(c=1 - me.c))

    def here(self, ref, place):
        landed(ref, self.ss.at[0], self.rs.at[place], self.me)

    def column(self):
        me = self.me
        for k in range(1, self.n):
            dp = lax.rem(me.dp + k, self.n)
            ref = self.piece(dp, me.y, me.c)
            self.here(ref, dp)
            self.share(ref, dp)

    def neighbours(self):
        me = self.me
        for k in range(self.n):
            dp = lax.rem(me.dp + k, self.n)
            ref = self.piece(dp, 1 - me.y, me.c)
            self.here(ref, self.n + dp)
            self.hand(ref, dp, 1 - me.y, 2 * self.n, me.at(c=1 - me.c))

    def sibling(self):
        self.here(self.dst.at[pl.ds(0, 2 * self.n)], 2 * self.n)

    def drain(self):
        sent(self.dst.at[pl.ds(0, 4 * self.n - 1)], self.ss.at[0], self.rs.at[0], self.me)

    def phases(self):
        return [[self.own], [self.column], [self.neighbours], [self.sibling], [self.drain]]

    @staticmethod
    def semaphores(dp_count):
        return [DMA((1,)), DMA((2 * dp_count + 1,))]


class Everyone:
    def __init__(self, me, dp_count, src, dst, ss, rs):
        self.me, self.n, self.src, self.dst, self.ss, self.rs = me, dp_count * 4, src, dst, ss, rs
        self.index = me.dp * 4 + me.seq

    def own(self):
        def event():
            @pl.loop(1, self.n)
            def _(k):
                to = lax.rem(self.index + k, self.n)
                send(self.src, self.dst.at[self.index], self.ss.at[0], self.rs.at[0], (to // 4, to % 4))
        return [event]

    def arrive(self):
        return [lambda: landed(self.dst.at[pl.ds(0, self.n - 1)], self.ss.at[0], self.rs.at[0], self.me)]

    def drain(self):
        return [lambda: sent(self.dst.at[pl.ds(0, self.n - 1)], self.ss.at[0], self.rs.at[0], self.me)]

    def phases(self):
        return [self.own(), self.arrive(), self.drain()]


def greet_all(me, dp_count):
    barrier = pltpu.get_barrier_semaphore()
    count = dp_count * 4

    @pl.loop(1, count)
    def _(k):
        to = lax.rem(me.dp * 4 + me.seq + k, count)
        pl.semaphore_signal(barrier, inc=1, device_id=(to // 4, to % 4), device_id_type=MESH)
    pl.semaphore_wait(barrier, count - 1)


FORWARD_ORDER = dict(
    q=dict(own=-1.671, column=-0.997, neighbours=2.973, diagonal=8.049, sibling=9.285),
    pack=dict(own=-1.0, arrive=-0.731),
    lat=dict(own=-0.999, neighbours=-0.917, sibling=-0.732),
    k=dict(own=-0.998, column=-0.996, neighbours=2.5, diagonal=4.61, sibling=7.657),
    v=dict(own=-0.336, column=3.046, neighbours=14.914, diagonal=28.532, sibling=40.12),
    o=dict(own=8.048, column=23.68, neighbours=44.275, diagonal=59.459, sibling=59.943),
    og=dict(own=27.572, column=59.273, neighbours=61.672),
    up=dict(own=28.241, column=59.555, neighbours=61.854, sibling=62.713),
    dn=dict(own=28.533, neighbours=58.926, sibling=59.917),
    x=dict(send0=50.963, send1=59.241, wait=59.918),
    nf=dict(own=61.183, a1=61.853, a2=62.093, b0=62.272, b1=64.105, b2=65.251, a3=65.818, b3=66.796),
    g=dict(a0=64.191, a1=66.009, a2=66.274, a3=67.798, b0=69.586, b1=70.423, b2=71.005, b3=71.804, finish=71.853),
    y=dict(start=71.382, fold=72.623, finish=76.92),
    st=dict(own=73.217, neighbours=74.655, sibling=76.353),
    do=dict(own=73.218, neighbours=76.825, sibling=78.0),
)
BACK_ORDER = dict(
    o=dict(begin=-1.0, core=0.257, middle=14.163, fold=21.903, finish=28.444),
    up=dict(begin=1.335, core=6.978, fold=24.753, finish=24.894, collect=50.506),
    k=dict(core=18.955, middle=28.229, fold=40.734, finish=48.103),
    v=dict(core=24.416, middle=37.863, fold=48.42, finish=51.002),
    dn=dict(begin=24.67, core=37.79, fold=50.639, finish=51.001),
    lat=dict(begin=34.007, core=37.914, fold=48.961, finish=50.002),
    q=dict(core=40.466, middle=50.058, fold=50.129, finish=51.003),
    sum=dict(s0=50.057, s1=50.128, s2=50.64, s3=51.0, s4=450.823),
)


HEADS = 16
HEAD_DIM = 96
FRAME_BLOCKS = 2
EPS = 1e-05
NEG = -1e30
HIGH = lax.Precision.HIGHEST
F32, BF16 = jnp.float32, jnp.bfloat16
WIDE = 62 << 20
PART = 4
PCOLS = PART * HEAD_DIM
SCALE = HEAD_DIM ** (-0.5)


def dot(left, right):
    return jnp.dot(left, right, preferred_element_type=F32)


def dot_t(left, right):
    return lax.dot_general(left, right, (((1,), (1,)), ((), ())), preferred_element_type=F32)


def t_dot(left, right):
    return lax.dot_general(left, right, (((0,), (0,)), ((), ())), preferred_element_type=F32)


def scaled_rows(rows):
    mean = jnp.mean(rows, axis=-1, keepdims=True)
    centred = rows - mean
    inverse = lax.rsqrt(jnp.mean(centred * centred, axis=-1, keepdims=True) + EPS)
    return centred * inverse, inverse


def norm_back(incoming, scaled, inverse, gain):
    inner = incoming * gain
    first = jnp.mean(inner, axis=-1, keepdims=True)
    second = jnp.mean(inner * scaled, axis=-1, keepdims=True)
    return inverse * (inner - first - scaled * second)


def part_mask(rows):
    row = lax.broadcasted_iota(jnp.int32, (PART * rows, PCOLS), 0)
    column = lax.broadcasted_iota(jnp.int32, (PART * rows, PCOLS), 1)
    low = (row // rows) * HEAD_DIM
    return (column >= low) & (column < low + HEAD_DIM)


def stacked(rows, mask):
    return jnp.where(mask, jnp.concatenate([rows] * PART, axis=0), jnp.zeros((), rows.dtype))


def unstacked(rows, mask, count):
    kept = jnp.where(mask, rows, 0.0)
    return sum(kept[h * count:(h + 1) * count] for h in range(PART))


def blocks_of(media_rows, block_rows, lat_rows):
    found = [(b * block_rows, block_rows) for b in range(media_rows // block_rows)]
    return found + [(media_rows, lat_rows)]


def attend_kernel(block_rows, items, owner, media, lat_all, gains, wq, wk, wv,
                  acc, stats, n_out, nl_out, q_out, k_out, v_out, wbuf, a_ref, m_ref, l_ref, sems):
    width = media.shape[1]
    half = width // 2
    media_rows = media.shape[0]
    lat_rows = lat_all.shape[0] // items
    seq = lax.axis_index("seq")

    def fetch(step, slot):
        cols = pl.ds(pl.multiple_of(step * half, 128), half)
        return [pltpu.make_async_copy(w.at[:, cols], wbuf.at[slot, i], sems.at[slot, i]) for i, w in enumerate((wq, wk, wv))]
    for copy in fetch(0, 0):
        copy.start()

    @pl.loop(0, media_rows // block_rows)
    def _(b):
        rows = pl.ds(pl.multiple_of(b * block_rows, block_rows), block_rows)
        u, _ = scaled_rows(media[rows, :].astype(F32))
        n_out[rows, :] = (u * gains[2:3, :] + gains[3:4, :]).astype(BF16)

    @pl.loop(0, items)
    def _(i):
        rows = pl.ds(pl.multiple_of(i * lat_rows, lat_rows), lat_rows)
        u, _ = scaled_rows(lat_all[rows, :].astype(F32))
        nl_out[rows, :] = (u * gains[0:1, :] + gains[1:2, :]).astype(BF16)
    n_out[pl.ds(media_rows, lat_rows), :] = nl_out[pl.ds(pl.multiple_of(seq * lat_rows, lat_rows), lat_rows), :]
    padding = n_out.shape[0] - media_rows - lat_rows
    n_out[pl.ds(media_rows + lat_rows, padding), :] = jnp.zeros((padding, width), BF16)
    stats[...] = jnp.zeros_like(stats)
    mask = part_mask(lat_rows)
    lane = lax.broadcasted_iota(jnp.int32, (lat_rows, 128), 1)

    @pl.loop(0, 2)
    def _(step):
        slot = lax.rem(step, 2)
        cols = pl.ds(pl.multiple_of(step * half, 128), half)
        for copy in fetch(step, slot):
            copy.wait()

        @pl.when(step == 0)
        def _():
            for copy in fetch(1, 1):
                copy.start()
        q_out[:, cols] = dot(nl_out[...], wbuf[slot, 0]).astype(BF16)
        k_out[:, cols] = dot(n_out[...], wbuf[slot, 1]).astype(BF16)
        v_out[:, cols] = dot(n_out[...], wbuf[slot, 2]).astype(BF16)

        @pl.loop(0, half // PCOLS)
        def _(inner):
            part = step * (half // PCOLS) + inner
            pcols = pl.ds(pl.multiple_of(part * PCOLS, 128), PCOLS)
            a_ref[...] = jnp.zeros_like(a_ref)
            l_ref[...] = jnp.zeros_like(l_ref)
            m_ref[...] = jnp.full_like(m_ref, NEG)

            def block(start, count, item):
                rows = q_out[pl.ds(pl.multiple_of(item * lat_rows, lat_rows), lat_rows), pcols]
                query = stacked(rows, mask)
                keys, values = k_out[pl.ds(start, count), pcols], v_out[pl.ds(start, count), pcols]
                scores = dot_t(query, keys) * SCALE
                old = m_ref[item]
                new = jnp.maximum(old, jnp.max(scores, axis=-1, keepdims=True))
                factor = jnp.exp(old - new)
                expo = jnp.exp(scores - new[:, :count])
                m_ref[item] = new
                l_ref[item] = l_ref[item] * factor + jnp.sum(expo, axis=-1, keepdims=True)
                wide = jnp.concatenate([factor] * (PCOLS // 128), axis=1)
                a_ref[item] = a_ref[item] * wide + dot(expo.astype(BF16), values)
            for b, (start, count) in enumerate(blocks_of(media_rows, block_rows, lat_rows)):
                block(start, count, seq if count == lat_rows and start == media_rows else owner[b])
            for item in range(items):
                acc[item, :, pcols] = unstacked(a_ref[item], mask, lat_rows).astype(BF16)
                for h in range(PART):
                    chosen = lane == part * PART + h
                    at = pl.ds(h * lat_rows, lat_rows)
                    stats[item, 0] = jnp.where(chosen, m_ref[item, at, :], stats[item, 0])
                    stats[item, 1] = jnp.where(chosen, l_ref[item, at, :], stats[item, 1])


def attend(owner, media, lat_all, gains, wq, wk, wv, block_rows, items):
    width = media.shape[1]
    lat_rows = lat_all.shape[0] // items
    rows = media.shape[0] + block_rows
    shape = jax.ShapeDtypeStruct
    return pl.pallas_call(
        functools.partial(attend_kernel, block_rows, items),
        out_shape=(
            shape((items, lat_rows, width), BF16), shape((items, 2, lat_rows, 128), F32),
            shape((rows, width), BF16), shape((items * lat_rows, width), BF16),
            shape((items * lat_rows, width), BF16), shape((rows, width), BF16), shape((rows, width), BF16),
        ),
        in_specs=[pl.BlockSpec(memory_space=pltpu.SMEM), VMEM, VMEM, VMEM, ANY, ANY, ANY],
        out_specs=tuple([VMEM] * 7),
        scratch_shapes=[
            pltpu.VMEM((2, 3, width, width // 2), BF16),
            pltpu.VMEM((items, PART * lat_rows, PCOLS), F32),
            pltpu.VMEM((items, PART * lat_rows, 128), F32), pltpu.VMEM((items, PART * lat_rows, 128), F32),
            DMA((2, 3)),
        ],
        compiler_params=pltpu.CompilerParams(vmem_limit_bytes=WIDE),
    )(owner, media, lat_all, gains, wq, wk, wv)


def dp_peers(me, dp_count):
    return [(lax.rem(me.dp + k, dp_count), me.seq) for k in range(1, dp_count)]


def far_first(me, event):
    found = []
    for d in range(me.nz - 1, 0, -1):
        found.append(lambda d=d: pl.when(me.z >= d)(lambda: event(me.z - d)))
        found.append(lambda d=d: pl.when(me.z + d < me.nz)(lambda: event(me.z + d)))
    return found + [lambda: event(me.z)]


def add(*refs):
    total = refs[0][...].astype(F32)
    for ref in refs[1:]:
        total = total + ref[...].astype(F32)
    return total


class Line:
    def __init__(self, me, column, boxes, ss, rs):
        self.me, self.column, self.boxes, self.ss, self.rs = me, column, boxes, ss, rs

    def event(self, z):
        me = self.me

        @pl.when(z != me.z)
        def _():
            send(self.column(z), self.boxes.at[me.z], self.ss.at[0], self.rs.at[0], me.at(z=z))

    def total(self, out):
        me = self.me
        landed(self.boxes.at[pl.ds(0, me.nz - 1)], self.ss.at[0], self.rs.at[0], me)
        out[...] = self.column(me.z)[...].astype(F32)
        for z in range(me.nz):
            @pl.when(z != me.z)
            def _():
                out[...] += self.boxes.at[z][...].astype(F32)

    def drain(self):
        return [lambda: sent(self.boxes.at[pl.ds(0, self.me.nz - 1)], self.ss.at[0], self.rs.at[0], self.me)]


class DpScatter:
    def __init__(self, me, part, out, ox, boxes, ss, rs, lss, lrs):
        self.me, self.part, self.out, self.ox, self.ss, self.rs = me, part, out, ox, ss, rs
        self.line = Line(me, lambda z: part.at[z * 2 + me.x], boxes, lss, lrs)

    def order(self):
        n = self.me.nz
        return [lax.rem(self.me.z + k, n) for k in sorted(range(1, n), key=lambda k: -min(k, n - k))] + [self.me.z]

    def send_x(self, z):
        me = self.me
        send(self.part.at[z * 2 + 1 - me.x], self.ox.at[z], self.ss.at[0], self.rs.at[z], me.at(x=1 - me.x))

    def start(self):
        return [functools.partial(self.send_x, z) for z in self.order()]

    def fold_in(self, z):
        landed(self.ox.at[z], self.ss.at[0], self.rs.at[z], self.me)
        mine = self.part.at[z * 2 + self.me.x]
        mine[...] = add(mine, self.ox.at[z]).astype(mine.dtype)
        self.line.event(z)

    def fold(self):
        return [functools.partial(self.fold_in, z) for z in self.order()]

    def finish(self):
        self.line.total(self.out)

    def groups(self):
        return dict(start=self.start(), fold=self.fold(), finish=[self.finish])

    def drain(self):
        return [lambda: sent(self.ox, self.ss.at[0], self.rs.at[0], self.me)] + self.line.drain()

    @staticmethod
    def semaphores(nz):
        return [DMA((1,)), DMA((nz,)), DMA((1,)), DMA((1,))]


def head_columns(width):
    row = lax.broadcasted_iota(jnp.int32, (128, width), 0) * HEAD_DIM
    column = lax.broadcasted_iota(jnp.int32, (128, width), 1)
    return ((column >= row) & (column < row + HEAD_DIM)).astype(F32)


def exact(left, right):
    return jnp.dot(left, right, preferred_element_type=F32, precision=HIGH)


def exact_t(left, right):
    return lax.dot_general(left, right, (((1,), (1,)), ((), ())), preferred_element_type=F32, precision=HIGH)


class Scatter:
    def __init__(self, me, src, out, bufs, ss, rs, ls, lss, lrs):
        self.me, self.src, self.out, self.ss, self.rs, self.ls = me, src, out, ss, rs, ls
        self.acc, self.cbuf, self.x1, self.y1, self.ox, self.oy, boxes = bufs
        self.cut = self.x1.shape[-1]
        self.line = Line(me, lambda z: self.acc.at[z, me.x, me.y], boxes, lss, lrs)

    def part(self, ref, half):
        width = self.acc.shape[-1]
        return ref.at[:, pl.ds(self.cut, width - self.cut)] if half else ref.at[:, pl.ds(0, self.cut)]

    def load(self, z):
        return pltpu.make_async_copy(self.src.at[pl.ds(2 * z, 2), :, self.me.c], self.acc.at[z], self.ls.at[z])

    def feed(self, stage, z):
        me = self.me
        send(stage.at[:, :, 1 - me.c], self.cbuf.at[z], self.ss.at[1 + z], self.rs.at[z], me.at(c=1 - me.c))
        for i in range(4):
            self.acc[z, i // 2, i % 2] = stage[i // 2, i % 2, me.c]

    def fed(self, z):
        sent(self.cbuf.at[z], self.ss.at[1 + z], self.rs.at[0], self.me)

    def begin(self):
        me = self.me

        def event(z):
            send(self.src.at[pl.ds(2 * z, 2), :, 1 - me.c], self.cbuf.at[z], self.ss.at[1 + z], self.rs.at[z], me.at(c=1 - me.c))
            self.load(z).start()
        return far_first(me, event)

    def core(self):
        me = self.me

        def event(z):
            if self.src is not None:
                self.load(z).wait()
            landed(self.cbuf.at[z], self.ss.at[0], self.rs.at[z], me)
            mine = self.acc.at[z]

            @pl.loop(0, 4)
            def _(i):
                x, y = i // 2, i % 2
                mine[x, y] = (mine[x, y].astype(F32) + self.cbuf[z, x, y].astype(F32)).astype(BF16)
            x_to, y_to = me.at(x=1 - me.x), me.at(y=1 - me.y)
            diag = mine.at[1 - me.x, 1 - me.y]
            send(self.part(diag, 0), self.x1.at[z], self.ss.at[0], self.rs.at[1 * me.nz + z], x_to)
            send(self.part(diag, 1), self.y1.at[z], self.ss.at[0], self.rs.at[2 * me.nz + z], y_to)
            send(self.part(mine.at[1 - me.x, me.y], 0), self.part(self.ox.at[z], 0), self.ss.at[0], self.rs.at[3 * me.nz + z], x_to)
            send(self.part(mine.at[me.x, 1 - me.y], 1), self.part(self.oy.at[z], 1), self.ss.at[0], self.rs.at[3 * me.nz + z], y_to)
        return far_first(me, event)

    def middle(self):
        me = self.me

        def event(z):
            landed(self.x1.at[z], self.ss.at[0], self.rs.at[me.nz + z], me)
            ref = self.part(self.acc.at[z, me.x, 1 - me.y], 0)
            ref[...] = add(ref, self.x1.at[z]).astype(BF16)
            send(ref, self.part(self.oy.at[z], 0), self.ss.at[0], self.rs.at[3 * me.nz + z], me.at(y=1 - me.y))
            landed(self.y1.at[z], self.ss.at[0], self.rs.at[2 * me.nz + z], me)
            ref = self.part(self.acc.at[z, 1 - me.x, me.y], 1)
            ref[...] = add(ref, self.y1.at[z]).astype(BF16)
            send(ref, self.part(self.ox.at[z], 1), self.ss.at[0], self.rs.at[3 * me.nz + z], me.at(x=1 - me.x))
        return far_first(me, event)

    def fold(self):
        me = self.me

        def event(z):
            landed(self.acc.at[z, 0], self.ss.at[0], self.rs.at[3 * me.nz + z], me)
            mine = self.acc.at[z, me.x, me.y]
            mine[...] = add(mine, self.ox.at[z], self.oy.at[z]).astype(BF16)
            self.line.event(z)
        return far_first(me, event)

    def finish(self):
        return [lambda: self.line.total(self.out)]

    def drain(self):
        me = self.me
        found = far_first(me, self.fed) if self.src is not None else []
        found.append(lambda: sent(self.acc.at[pl.ds(0, me.nz * 3 // 4)], self.ss.at[0], self.rs.at[0], me))
        return found + self.line.drain()

    def groups(self):
        begin = self.begin() if self.src is not None else []
        return dict(begin=begin, core=self.core(), middle=self.middle(), fold=self.fold(), finish=self.finish())

    @staticmethod
    def scratch(nz, rows, cols):
        buf = lambda *s: pltpu.VMEM(s + (rows, cols), BF16)
        cut = cols * 2 // 3 // 128 * 128
        return [buf(nz, 2, 2), buf(nz, 2, 2), pltpu.VMEM((nz, rows, cut), BF16), pltpu.VMEM((nz, rows, cols - cut), BF16), buf(nz), buf(nz), buf(nz),
                DMA((1 + nz,)), DMA((4 * nz,)), DMA((nz,)), DMA((1,)), DMA((1,))]


class SeqScatter:
    def __init__(self, me, src, then, acc, cbuf, oy, ss, rs, ls):
        self.me, self.src, self.then, self.acc, self.cbuf, self.oy = me, src, then, acc, cbuf, oy
        self.ss, self.rs = ss, rs
        self.load = pltpu.make_async_copy(src.at[:, :, me.c], acc, ls.at[0])

    def begin(self):
        me = self.me
        send(self.src.at[:, :, 1 - me.c], self.cbuf, self.ss.at[0], self.rs.at[0], me.at(c=1 - me.c))
        self.load.start()

    def core(self):
        me = self.me
        self.load.wait()
        landed(self.cbuf, self.ss.at[0], self.rs.at[0], me)

        @pl.loop(0, self.acc.shape[0])
        def _(i):
            for y in (0, 1):
                self.acc[i, y] = (self.acc[i, y].astype(F32) + self.cbuf[i, y].astype(F32)).astype(BF16)
        send(self.acc.at[:, 1 - me.y], self.oy, self.ss.at[1], self.rs.at[1], me.at(y=1 - me.y))

    def fold(self):
        me = self.me
        landed(self.oy, self.ss.at[0], self.rs.at[1], me)

        @pl.loop(0, self.acc.shape[0])
        def _(i):
            self.oy[i] = (self.acc[i, me.y].astype(F32) + self.oy[i].astype(F32)).astype(BF16)

    def finish(self):
        self.then(self.oy)

    def drain(self):
        sent(self.cbuf, self.ss.at[0], self.rs.at[0], self.me)
        sent(self.oy, self.ss.at[1], self.rs.at[0], self.me)

    def groups(self):
        return dict(begin=[self.begin], core=[self.core], fold=[self.fold], finish=[self.finish])

    @staticmethod
    def scratch(count, rows, cols):
        buf = lambda *s: pltpu.VMEM(s + (rows, cols), BF16)
        return [buf(count, 2), buf(count, 2), buf(count), DMA((2,)), DMA((2,)), DMA((1,))]


class Regrouped(SeqScatter):
    def __init__(self, me, dp_count, src, out, inbox, up_ss, up_rs, *rest):
        super().__init__(me, src, self.pass_on, *rest)
        self.n, self.out, self.inbox, self.up_ss, self.up_rs = dp_count, out, inbox, up_ss, up_rs

    def pass_on(self, total):
        me = self.me
        for k in range(1, self.n):
            to = lax.rem(me.dp + k, self.n)
            send(total.at[to], self.inbox.at[me.dp], self.up_ss.at[to], self.up_rs.at[me.dp], (to, me.seq))
        self.inbox[me.dp] = total[me.dp]

    def collect(self):
        cols = self.inbox.shape[2]
        for dp in range(self.n):
            pl.when(dp != self.me.dp)(lambda: landed(self.inbox.at[dp], self.up_ss.at[0], self.up_rs.at[dp], self.me))
            self.out[:, dp * cols:(dp + 1) * cols] = self.inbox[dp].astype(F32)

    def drain(self):
        super().drain()
        for k in range(1, self.n):
            sent(self.inbox.at[0], self.up_ss.at[lax.rem(self.me.dp + k, self.n)], self.up_rs.at[0], self.me)

    @staticmethod
    def scratch(count, rows, cols):
        return [pltpu.VMEM((count, rows, cols), BF16), DMA((count,)), DMA((count,))] + SeqScatter.scratch(count, rows, cols)


class SumAll:
    def __init__(self, me, ref, inbox, ss, rs):
        self.me, self.ref, self.inbox, self.ss, self.rs = me, ref, inbox, ss, rs

    def step(self, i, to):
        def begin():
            send(self.ref.at[i], self.inbox.at[i], self.ss.at[i], self.rs.at[i], to)

        def end():
            landed(self.inbox.at[i], self.ss.at[0], self.rs.at[i], self.me)
            self.ref[i + 1] = self.ref[i] + self.inbox[i]
        return begin, end

    def phases(self):
        me = self.me
        n = me.nz

        def begin_z():
            for k in range(1, n):
                to = lax.rem(me.z + k, n)
                send(self.ref.at[3], self.inbox.at[2 + k], self.ss.at[2 + k], self.rs.at[2 + k], me.at(z=to))

        def end_z():
            total = self.ref[3]
            for k in range(1, n):
                landed(self.inbox.at[2 + k], self.ss.at[0], self.rs.at[2 + k], me)
                total = total + self.inbox[2 + k]
            self.ref[4] = total

        def drain():
            for i in range(2 + n):
                sent(self.ref.at[0], self.ss.at[i], self.rs.at[0], me)
        first = self.step(0, me.at(c=1 - me.c))
        second = self.step(1, me.at(x=1 - me.x))
        third = self.step(2, me.at(y=1 - me.y))
        both = lambda one, other: (lambda: (one(), other()))
        return [[e] for e in (first[0], both(first[1], second[0]), both(second[1], third[0]), both(third[1], begin_z), end_z, drain)]


CUT, LATE_CUT = 640, 384


def laid_out(order, groups, steps):
    places, count = {}, 0
    for name, number in steps.items():
        places[name] = (count, number)
        count += number
    ahead = [[] for _ in range(count)]
    placed = [(position, name, phase) for name, phases in order.items() for phase, position in phases.items()]
    for position, name, phase in sorted(placed):
        ahead[min(count - 1, max(0, math.ceil(position)))] += groups[name][phase]
    return lambda name: ahead[places[name][0]:places[name][0] + places[name][1]]


def unpacked(packs, own_cols):
    count = packs.shape[0]
    group = 8
    rows = []
    for g in range(count // group):
        left = jnp.concatenate([packs[g * group + i] for i in range(group)], axis=1).astype(BF16)
        row = lax.broadcasted_iota(jnp.int32, (group * 128, group * own_cols), 0)
        column = lax.broadcasted_iota(jnp.int32, (group * 128, group * own_cols), 1)
        piece, place = row // 128, row % 128
        chosen = (place < own_cols) & (column == piece * own_cols + place)
        rows.append(dot(left, jnp.where(chosen, 1.0, 0.0).astype(BF16)))
    return jnp.concatenate(rows, axis=1)


def forward_kernel(dp_count, block_rows, own_cols, owner, media, pack, lat, sq, sk, sv, so, sg, sd, su,
                   wq, wk, wv, n_out, nl_out, q_out, k_out, v_out, gwo, gwu, gwd,
                   gains, lat_out, grad_hidden, do_all, stat_all, sums,
                   packs, lat_all, wo, og, dn, up, med, n, nl, q, k, v, expo, acc_f, acc, tops, stats, wbuf,
                   acc_in, stat_in, nf_all, ga, act, gp, part_g, ox_g, zz_g, part_y, ox_y, zz_y,
                   own_sum, row_a, row_b, do_in, st_in, gwo_v, gwu_v, gwd_v,
                   local, ws, ms, outs, xs, xr, *sems):
    me = Here(dp_count)
    (rss, rrs, es, er), g_sems, y_sems, sems = sems[:4], sems[4:8], sems[8:12], sems[12:]
    nf_sems, do_sems, st_sems = sems[14:16], sems[16:18], sems[18:20]
    seq_count, lat_rows, width = lat_all.shape
    half = width // 2
    seq_peers = [lax.rem(me.seq + i, seq_count) for i in range(1, seq_count)]
    blocks, parts = n.shape[0] // block_rows, HEADS // PART
    media_rows = media.shape[0]
    greet_all(me, dp_count)
    gather = lambda i, src, dst, axes, halves: Gather(me, src, dst, *sems[2 * i:2 * i + 2], axes, halves)
    regroup = Regroup(me, dp_count, su, up, rss, rrs, up.shape[2])
    items = [
        Everyone(me, dp_count, pack, packs, es, er), gather(0, lat, lat_all, "yc", 0),
        gather(1, sk, wk, "zxyc", CUT), gather(2, sq, wq, "zxyc", CUT), gather(3, sv, wv, "zxyc", CUT),
        gather(4, so, wo, "zxyc", LATE_CUT), gather(5, sg, og, "zx", 0), gather(6, sd, dn, "yc", 0), regroup,
    ]
    own = [(pack, packs.at[items[0].index])]
    own += [(src, item.shard(me.z, me.x, me.y, me.c)) for src, item in zip((lat, sk, sq, sv, so, sg, sd), items[1:8])]
    own += [(regroup.columns(me.dp), regroup.piece(me.dp, me.y, me.c))]
    own = [pltpu.make_async_copy(src, dst, local.at[i]) for i, (src, dst) in enumerate(own)]
    for copy in own:
        copy.start()
    spread_nf = Gather(me, nf_all.at[me.dp], nf_all, *nf_sems, "zx", 0)
    sum_g = DpScatter(me, part_g, own_sum, ox_g, zz_g, *g_sems)
    sum_y = DpScatter(me, part_y, own_sum, ox_y, zz_y, *y_sems)
    spread_do = Gather(me, do_in.at[me.seq], do_in, *do_sems, "yc", 0)
    spread_st = Gather(me, st_in.at[me.seq], st_in, *st_sems, "yc", 0)

    def exchange(part):
        cols = pl.ds(part * half, half)
        for i, to in enumerate(seq_peers):
            send(acc.at[to, :, cols], acc_in.at[me.seq, :, cols], xs.at[part, i], xr.at[part, me.seq], (me.dp, to))
            if part == 0:
                send(stats.at[to], stat_in.at[me.seq], xs.at[2, i], xr.at[2, me.seq], (me.dp, to))

    def exchanged():
        for source in seq_peers:
            landed(stat_in.at[source], xs.at[0, 0], xr.at[2, source], me)
            for part in range(2):
                landed(acc_in.at[source, :, pl.ds(part * half, half)], xs.at[0, 0], xr.at[part, source], me)
    column = spread_nf.column()
    way = 1 - 2 * (me.z // (me.nz // 2))

    def layer(k):
        return lax.rem(me.z + way * k + me.nz, me.nz)

    def arrived(z):
        spread_nf.here(spread_nf.shard(z, 1 - me.x, me.y, me.c), FROMX, z)

    def steps_of(first, second):
        return {**{"a%d" % k: first(k) for k in range(me.nz)}, **{"b%d" % k: second(k) for k in range(me.nz)}}
    groups = dict(
        pack=dict(own=items[0].own(), arrive=items[0].arrive()),
        x=dict(send0=[lambda: exchange(0)], send1=[lambda: exchange(1)], wait=[exchanged]),
        up=dict(own=[regroup.own], column=[regroup.column], neighbours=[regroup.neighbours], sibling=[regroup.sibling]),
        g=dict(**steps_of(lambda k: [lambda: sum_g.send_x(layer(k))], lambda k: [lambda: sum_g.fold_in(layer(k))]), finish=[sum_g.finish]),
        nf=dict(own=spread_nf.own(), **steps_of(lambda k: column[2 * k - 2:2 * k], lambda k: [lambda: arrived(layer(k))])),
        y=sum_y.groups(), do=spread_do.groups(), st=spread_st.groups(),
        **dict(zip(("lat", "k", "q", "v", "o", "og", "dn"), [item.groups() for item in items[1:8]])))
    steps = blocks * parts // 2
    ahead_of = laid_out(FORWARD_ORDER, groups, dict(
        gains=1, norm=blocks - 1, latnorm=1, kproj=2, qproj=2, tops=steps, best=1, expo=steps, sums=1,
        vproj0=1, acc0=steps // 2, cast0=1, vproj1=1, acc1=steps // 2, cast1=1, fold=1, hidden=1, ga=2, ffn=me.nz, ypart=me.nz, gwd=1,
        grad=1, gwo=2, gwu=1, latout=1, end=1))

    def ahead(name):
        run(ahead_of(name)[0])

    def media_load(b):
        rows = pl.ds(pl.multiple_of(b * block_rows, block_rows), block_rows)
        slot = lax.rem(b, 2)
        return pltpu.make_async_copy(media.at[rows, :], med.at[slot], ms.at[slot])
    media_load(0).start()
    ahead("gains")
    for copy in own:
        copy.wait()
    gains[...] = unpacked(packs, own_cols)

    norm_events = ahead_of("norm")

    @pl.loop(0, blocks - 1)
    def _(b):
        run_at(b, norm_events)
        pl.when(b + 1 < blocks - 1)(lambda: media_load(b + 1).start())
        media_load(b).wait()
        u, _ = scaled_rows(med[lax.rem(b, 2)].astype(F32))
        n[pl.ds(pl.multiple_of(b * block_rows, block_rows), block_rows), :] = (u * gains[2:3, :] + gains[3:4, :]).astype(BF16)
    ahead("latnorm")
    u, _ = scaled_rows(lat_all[...].reshape(seq_count * lat_rows, width).astype(F32))
    nl[...] = (u * gains[0:1, :] + gains[1:2, :]).astype(BF16).reshape(nl.shape)
    n[pl.ds(media_rows, lat_rows), :] = nl[me.seq]
    n[pl.ds(media_rows + lat_rows, block_rows - lat_rows), :] = jnp.zeros((block_rows - lat_rows, width), BF16)

    def weight(w, i):
        return pltpu.make_async_copy(w.at[:, :, pl.ds(pl.multiple_of(i * half, 128), half)], wbuf.at[i], ws.at[i])

    def project(rows, w, out, name):
        events = ahead_of(name)
        run(events[0])
        for i in range(2):
            weight(w, i).start()

        @pl.loop(0, 2)
        def _(i):
            run_at(i, [[], events[1]])
            weight(w, i).wait()
            cols = pl.ds(pl.multiple_of(i * half, 128), half)
            out[:, cols] = dot(rows[...], wbuf[i].reshape(width, half)).astype(BF16)
    project(n, wk, k, "kproj")
    project(nl.reshape(seq_count * lat_rows, width), wq, q.reshape(seq_count * lat_rows, width), "qproj")
    mask = part_mask(lat_rows)
    lane = lax.broadcasted_iota(jnp.int32, (lat_rows, 128), 1)
    key = lax.broadcasted_iota(jnp.int32, (PART * lat_rows, block_rows), 1)

    def scores(b, part, item):
        cols = pl.ds(pl.multiple_of(part * PCOLS, 128), PCOLS)
        at = pl.ds(pl.multiple_of(b * block_rows, block_rows), block_rows)
        found = dot_t(stacked(q[item, :, cols], mask), k[at, cols]) * SCALE
        return jnp.where(key < jnp.where(b == blocks - 1, lat_rows, block_rows), found, NEG)

    def replicated(stat, part):
        pieces = []
        for h in range(PART):
            column = jnp.sum(jnp.where(lane == part * PART + h, stat, 0.0), axis=-1, keepdims=True)
            pieces.append(jnp.broadcast_to(column, (lat_rows, 128)))
        return jnp.concatenate(pieces, axis=0)

    def place(stat, column, part):
        for h in range(PART):
            stat = jnp.where(lane == part * PART + h, column[h * lat_rows:(h + 1) * lat_rows], stat)
        return stat
    tops[...] = jnp.zeros_like(tops)
    top_events = ahead_of("tops")

    @pl.loop(0, steps)
    def _(i):
        b, pair = i // (parts // 2), i % (parts // 2)
        run_at(i, top_events)
        item = owner[b]
        for part in (pair * 2, pair * 2 + 1):
            tops[b, 0] = place(tops[b, 0], jnp.max(scores(b, part, item), axis=-1, keepdims=True), part)
    ahead("best")
    for i in range(seq_count):
        best = jnp.full((lat_rows, 128), NEG, F32)
        for b in range(blocks):
            best = jnp.maximum(best, jnp.where(owner[b] == i, tops[b, 0], NEG))
        stats[i, 0] = best
    expo_events = ahead_of("expo")

    @pl.loop(0, steps)
    def _(i):
        b, pair = i // (parts // 2), i % (parts // 2)
        run_at(i, expo_events)
        item = owner[b]
        for part in (pair * 2, pair * 2 + 1):
            e = jnp.exp(scores(b, part, item) - replicated(stats[item, 0], part))
            expo[b, part] = e.astype(BF16)
            tops[b, 1] = place(tops[b, 1], jnp.sum(e, axis=-1, keepdims=True), part)
    ahead("sums")
    for i in range(seq_count):
        stats[i, 1] = sum(jnp.where(owner[b] == i, tops[b, 1], 0.0) for b in range(blocks))
    acc_f[...] = jnp.zeros_like(acc_f)
    for part in range(2):
        ahead("vproj%d" % part)
        if part == 0:
            for i in range(2):
                weight(wv, i).start()
        weight(wv, part).wait()
        cols = pl.ds(part * half, half)
        v[:, cols] = dot(n[...], wbuf[part].reshape(width, half)).astype(BF16)
        acc_events = ahead_of("acc%d" % part)

        @pl.loop(0, steps // 2)
        def _(b):
            run_at(b, acc_events)
            item = owner[b]
            for head_part in range(part * parts // 2, (part + 1) * parts // 2):
                pcols = pl.ds(head_part * PCOLS, PCOLS)
                at = pl.ds(pl.multiple_of(b * block_rows, block_rows), block_rows)
                term = unstacked(dot(expo[b, head_part], v[at, pcols]), mask, lat_rows)
                for j in range(seq_count):
                    acc_f[j, :, pcols] += jnp.where(item == j, term, 0.0)
        ahead("cast%d" % part)
        acc[:, :, cols] = acc_f[:, :, cols].astype(BF16)
        acc_in[me.seq, :, cols] = acc[me.seq, :, cols]
    stat_in[me.seq] = stats[me.seq]
    saves = [(n, n_out), (nl, nl_out), (q, q_out), (k, k_out), (v, v_out)]
    saves = [pltpu.make_async_copy(src, dst, outs.at[i]) for i, (src, dst) in enumerate(saves)]
    for copy in saves:
        copy.start()
    ahead("fold")
    best = functools.reduce(jnp.maximum, [stat_in[s, 0] for s in range(seq_count)])
    weights = [jnp.exp(stat_in[s, 0] - best) for s in range(seq_count)]
    total = sum(w * stat_in[s, 1] for s, w in enumerate(weights))
    total = jnp.where(lane < HEADS, total, 1.0)
    spread = head_columns(width)
    attended = sum(exact(w / total, spread) * acc_in[s].astype(F32) for s, w in enumerate(weights))
    row_a[...] = attended
    st_in[me.seq, 0] = best + jnp.log(total)
    ahead("hidden")
    hidden = lat_all[me.seq].astype(F32) + dot(attended.astype(BF16), wo[...].reshape(width, width))
    row_b[...] = hidden
    scaled, _ = scaled_rows(hidden)
    nf_all[me.dp] = (scaled * gains[4:5, :] + gains[5:6, :]).astype(BF16)
    all_rows = dp_count * lat_rows
    hidden_cols = gp.shape[1]
    og_all = lambda: og[...].reshape(all_rows, width)
    tile = hidden_cols // 2
    per = seq_count // 2
    ga_events = ahead_of("ga")

    @pl.loop(0, 2)
    def _(t):
        run_at(t, ga_events)
        at = pl.ds(pl.multiple_of(t * tile, 128), tile)
        ga[:, at] = dot_t(og_all(), dn[pl.ds(t * per, per)].reshape(tile, width))
    ffn_events = ahead_of("ffn")
    pair_rows = 2 * lat_rows

    def pair(z):
        return pl.ds(2 * z, 2), pl.ds(pl.multiple_of(z * pair_rows, pair_rows), pair_rows)

    @pl.loop(0, me.nz)
    def _(k):
        run_at(k, ffn_events)
        both, at = pair(layer(k))
        pre = dot(nf_all[both].reshape(pair_rows, width), up[...].reshape(width, hidden_cols))
        phi = 0.5 * (1.0 + lax.erf(pre * 0.7071067811865476))
        act[at, :] = (pre * phi).astype(BF16)
        slope = phi + pre * jnp.exp(pre * pre * -0.5) * 0.3989422804014327
        gp[at, :] = (ga[at, :] * slope).astype(BF16)
        part_g[both] = dot_t(gp[at, :], up[...].reshape(width, hidden_cols)).astype(BF16).reshape(2, lat_rows, width)
    y_events = ahead_of("ypart")

    @pl.loop(0, me.nz)
    def _(k):
        run_at(k, y_events)
        both, at = pair(layer(k))
        part_y[both] = dot(act[at, :], dn[...].reshape(hidden_cols, width)).astype(BF16).reshape(2, lat_rows, width)
    ahead("gwd")
    gwd_v[...] = t_dot(act[...], og_all()).astype(BF16)
    save_d = pltpu.make_async_copy(gwd_v, gwd, outs.at[5])
    save_d.start()
    ahead("grad")
    gathered = own_sum[...]
    scaled, inverse = scaled_rows(row_b[...])
    sums[...] = jnp.zeros_like(sums)
    sums[0:1, :] = jnp.sum(gathered * scaled, axis=0, keepdims=True)
    sums[1:2, :] = jnp.sum(gathered, axis=0, keepdims=True)
    grad = og[me.dp].astype(F32) + norm_back(gathered, scaled, inverse, gains[4:5, :])
    grad_hidden[...] = grad
    low = grad.astype(BF16)
    grad_att = dot_t(low, wo[...].reshape(width, width)).astype(BF16)
    do_in[me.seq] = grad_att
    st_in[me.seq, 1] = exact_t(grad_att.astype(F32) * row_a[...], spread)
    save_o = []
    for i in range(2):
        cols = pl.ds(i * half, half)
        run(ahead_of("gwo")[i])
        if i:
            save_o[0].wait()
        gwo_v[...] = t_dot(row_a[...].astype(BF16), low[:, i * half:(i + 1) * half]).astype(BF16)
        save_o.append(pltpu.make_async_copy(gwo_v, gwo.at[:, cols], outs.at[6 + i]))
        save_o[-1].start()
    ahead("gwu")
    gwu_v[...] = t_dot(nf_all[...].reshape(all_rows, width), gp[...]).astype(BF16)
    save_u = pltpu.make_async_copy(gwu_v, gwu, outs.at[8])
    save_u.start()
    ahead("latout")
    lat_out[...] = (row_b[...] + own_sum[...]).astype(BF16)
    ahead("end")
    do_all[...] = do_in[...]
    stat_all[...] = st_in[...]
    for i in range(len(seq_peers)):
        for part in range(2):
            sent(acc_in.at[0, :, pl.ds(part * half, half)], xs.at[part, i], xr.at[0, 0], me)
        sent(stat_in.at[0], xs.at[2, i], xr.at[0, 0], me)
    for item in items[:8]:
        run(item.drain())
    regroup.drain()
    for item in (spread_nf, sum_g, sum_y, spread_do, spread_st):
        run(item.drain())
    for copy in saves + save_o[1:] + [save_d, save_u]:
        copy.wait()


def forward(dp_count, owner, media, pack, lat, sq, sk, sv, so, sg, sd, su, block_rows, own_cols):
    nz = dp_count // 2
    rows, width = lat.shape
    items, count = 4, dp_count * 4
    hidden = su.shape[1] // dp_count
    total = media.shape[0] + block_rows
    blocks = total // block_rows
    parts = HEADS // PART
    all_rows = dp_count * rows
    shape = jax.ShapeDtypeStruct
    buf = lambda *s: pltpu.VMEM(s, BF16)
    flt = lambda *s: pltpu.VMEM(s, F32)
    square = shape((count, width // count, width), BF16)
    stat = (items, 2, rows, 128)
    line = [buf(nz, rows, width), buf(nz, rows, width)]
    return pl.pallas_call(
        functools.partial(forward_kernel, dp_count, block_rows, own_cols),
        out_shape=(
            square, square, square, shape((total, width), BF16), shape((items, rows, width), BF16), shape((items, rows, width), BF16),
            shape((total, width), BF16), shape((total, width), BF16),
            shape((width, width), BF16), shape((width, hidden), BF16), shape((hidden, width), BF16),
            shape((8, width), F32), shape((rows, width), BF16), shape((rows, width), F32),
            shape((items, rows, width), BF16), shape(stat, F32), shape((8, width), F32),
        ),
        in_specs=[pl.BlockSpec(memory_space=pltpu.SMEM)] + [ANY] * 10,
        out_specs=tuple([ANY] * 11 + [VMEM] * 6),
        scratch_shapes=[
            flt(count, 8, 128), buf(items, rows, width), buf(count, width // count, width), buf(dp_count, rows, width),
            buf(items, hidden // items, width), buf(count, width // count, hidden), buf(2, block_rows, width),
            buf(total, width), buf(items, rows, width), buf(items, rows, width), buf(total, width), buf(total, width),
            buf(blocks, parts, PART * rows, block_rows), flt(items, rows, width), buf(items, rows, width),
            flt(blocks, 2, rows, 128), flt(*stat), buf(2, count, width // count, width // 2),
            buf(items, rows, width), flt(*stat), buf(dp_count, rows, width), flt(all_rows, hidden), buf(all_rows, hidden), buf(all_rows, hidden),
            buf(dp_count, rows, width), *line, buf(dp_count, rows, width), *line,
            flt(rows, width), flt(rows, width), flt(rows, width), buf(items, rows, width), flt(*stat),
            buf(width, width // 2), buf(width, hidden), buf(hidden, width),
            DMA((9,)), DMA((2,)), DMA((2,)), DMA((9,)), DMA((3, items)), DMA((3, items)),
            *Regroup.semaphores(dp_count), DMA((1,)), DMA((1,)), *DpScatter.semaphores(nz), *DpScatter.semaphores(nz),
            *[sem for axes in ("yc", "zxyc", "zxyc", "zxyc", "zxyc", "zx", "yc", "zx", "yc", "yc") for sem in Gather.semaphores(axes, nz)],
        ],
        compiler_params=pltpu.CompilerParams(collective_id=1, has_side_effects=True, vmem_limit_bytes=WIDE),
    )(owner, media, pack, lat, sq, sk, sv, so, sg, sd, su)


def backward_kernel(dp_count, block_rows, owner, lat, grad_hidden, gains, sums_ffn,
                    n_in, nl_in, q_in, k_in, v_in, do_in, stat_in, gwo, gwu, gwd, media, wq, wk, wv,
                    media_grad, lat_grad, sums, out_q, out_k, out_v, out_o, out_up, out_dn,
                    n, nl, q, do, k, v, stats, dq, g, gq, med, stage, sums_ref, *scratch):
    me = Here(dp_count)
    items, lat_rows, width = q.shape
    rows = k.shape[0]
    media_rows = media.shape[0]
    blocks, parts = rows // block_rows, HEADS // PART
    scratch = list(scratch)
    take = lambda count: [scratch.pop(0) for _ in range(count)]
    o_s, fulls, up_s, dn_s, lat_s, small = take(12), [take(12) for _ in range(3)], take(9), take(6), take(6), take(4)
    in_sem, tile_sem, med_sem, out_sem = scratch
    loads = [(stat_in, stats), (q_in, q), (do_in, do), (k_in, k), (v_in, v), (n_in, n), (nl_in, nl)]
    loads = [pltpu.make_async_copy(src, dst, in_sem.at[i]) for i, (src, dst) in enumerate(loads)]
    for load in loads:
        load.start()
    all_sum = SumAll(me, *small)

    def latents(total):
        scaled, inverse = scaled_rows(lat[...].astype(F32))
        grad = total[0].astype(F32)
        lat_grad[...] = grad_hidden[...] + norm_back(grad, scaled, inverse, gains[0:1, :])
        first = small[0]
        first[0, 0:1, :] = jnp.sum(grad * scaled, axis=0, keepdims=True)
        first[0, 1:2, :] = jnp.sum(grad, axis=0, keepdims=True)
        first[0, 2:4, :] = sums_ref[0:2, :]
        first[0, 4:6, :] = sums_ffn[0:2, :]
        first[0, 6:8, :] = jnp.zeros_like(sums_ffn[0:2, :])

    def down(total):
        out_dn[...] = total[0].astype(F32)
    f_o = Scatter(me, gwo, out_o, o_s[:7], *o_s[7:])
    f_k, f_v, f_q = [Scatter(me, None, out, f[:7], *f[7:]) for out, f in zip((out_k, out_v, out_q), fulls)]
    up, dn = Regrouped(me, dp_count, gwu, out_up, *up_s), SeqScatter(me, gwd, down, *dn_s)
    lat_item = SeqScatter(me, gq, latents, *lat_s)
    greet(dp_peers(me, dp_count) + [me.at(y=1 - me.y), me.at(c=1 - me.c)])
    mask = part_mask(lat_rows)
    lane = lax.broadcasted_iota(jnp.int32, (lat_rows, 128), 1)
    key = lax.broadcasted_iota(jnp.int32, (PART * lat_rows, block_rows), 1)
    held = pl.ds(0, items * lat_rows)
    g[held, :] = jnp.zeros((items * lat_rows, width), F32)

    def replicated(stat, part):
        pieces = []
        for h in range(PART):
            column = jnp.sum(jnp.where(lane == part * PART + h, stat, 0.0), axis=-1, keepdims=True)
            pieces.append(jnp.broadcast_to(column, (lat_rows, 128)))
        return jnp.concatenate(pieces, axis=0)

    def block(b, part, item):
        cols = pl.ds(pl.multiple_of(part * PCOLS, 128), PCOLS)
        at = pl.ds(pl.multiple_of(b * block_rows, block_rows), block_rows)
        query, grad = stacked(q[item, :, cols], mask), stacked(do[item, :, cols], mask)
        keys, values = k[at, cols], v[at, cols]
        lse, delta = replicated(stats[item, 0], part), replicated(stats[item, 1], part)
        prob = jnp.exp(dot_t(query, keys) * SCALE - lse)
        prob = jnp.where(key < jnp.where(b == blocks - 1, lat_rows, block_rows), prob, 0.0)
        score = (prob * (dot_t(grad, values) - delta)).astype(BF16)
        term = unstacked(dot(score, keys), mask, lat_rows) * SCALE
        k[at, cols] = (t_dot(score, query) * SCALE).astype(BF16)
        v[at, cols] = t_dot(prob.astype(BF16), grad).astype(BF16)
        for i in range(items):
            g[i * lat_rows:(i + 1) * lat_rows, cols] += jnp.where(item == i, term, 0.0)
    steps = blocks * parts // 2
    span = rows // 2
    turns = (span, 0)
    tile = items * lat_rows
    tiles = width // tile
    norms = [(min(media_rows, start + span) - start) // lat_rows for start in turns]
    groups = dict(
        o=f_o.groups(), k=f_k.groups(), v=f_v.groups(), q=f_q.groups(), lat=lat_item.groups(), dn=dn.groups(),
        up=dict(collect=[up.collect], **up.groups()), sum=dict(zip(("s0", "s1", "s2", "s3", "s4"), all_sum.phases())))
    ahead_of = laid_out(BACK_ORDER, groups, dict(
        attention=steps, dq=1, gwk=me.nz, gwv=me.nz, gwq=me.nz, tiles0=tiles, norms0=norms[0], tiles1=tiles, norms1=norms[1], end=1))
    for load in loads[:5]:
        load.wait()

    shares = ahead_of("attention")

    @pl.loop(0, steps)
    def _(i):
        b, pair = i // (parts // 2), i % (parts // 2)
        run_at(i, shares)
        item = owner[b]
        block(b, pair * 2, item)
        block(b, pair * 2 + 1, item)
    run(ahead_of("dq")[0])
    dq[...] = g[held, :].astype(BF16)
    for load in loads[5:]:
        load.wait()
    layer = width // me.nz

    def produce(full, left, right, name):
        shares = ahead_of(name)

        @pl.loop(0, me.nz)
        def _(t):
            run_at(t, shares)
            slot = lax.rem(t, 2)
            z = lax.rem(me.z + 1 + t, me.nz)
            pl.when(t >= 2)(lambda: full.fed(lax.rem(me.z + t - 1, me.nz)))
            cols = pl.ds(pl.multiple_of(z * layer, 128), layer)
            found = t_dot(left(cols), right()).astype(BF16)
            stage[slot] = found.reshape(stage.shape[1:])
            full.feed(stage.at[slot], z)
        full.fed(lax.rem(me.z + me.nz - 1, me.nz))
        full.fed(me.z)
    n_cols = lambda cols: n[:, :, cols].reshape(rows, layer)
    produce(f_k, n_cols, lambda: k[...], "gwk")
    produce(f_v, n_cols, lambda: v[...], "gwv")
    produce(f_q, lambda cols: nl[:, :, cols].reshape(items * lat_rows, layer), lambda: dq[...], "gwq")
    per = items
    slots = ((n.at[pl.ds(0, per)], n.at[pl.ds(per, per)], n.at[pl.ds(2 * per, per)]), (q, nl, do))

    def fetch(t, slot):
        return [pltpu.make_async_copy(w.at[pl.ds(t * per, per)], dst, tile_sem.at[slot, i]) for i, (w, dst) in enumerate(zip((wk, wv, wq), slots[slot]))]

    def media_load(i, start):
        at = pl.ds(pl.multiple_of(start + i * lat_rows, lat_rows), lat_rows)
        slot = lax.rem(i, 2)
        return pltpu.make_async_copy(media.at[at, :], med.at[slot], med_sem.at[slot])
    sums_ref[...] = jnp.zeros_like(sums_ref)
    for turn, start in enumerate(turns):
        shares = ahead_of("tiles%d" % turn)
        for copy in fetch(0, 0) + fetch(1, 1):
            copy.start()

        @pl.loop(0, tiles // 2)
        def _(pair):
            for slot in (0, 1):
                t = pair * 2 + slot
                run_at(t, shares)
                for copy in fetch(t, slot):
                    copy.wait()
                at = pl.ds(pl.multiple_of(t * tile, 128), tile)
                w_k, w_v, w_q = [ref[...].reshape(tile, width) for ref in slots[slot]]
                grad = dot_t(k[pl.ds(start, span), :], w_k) + dot_t(v[pl.ds(start, span), :], w_v)
                g[:, at] = grad
                if turn == 0:
                    own = dot_t(dq[...], w_q)
                    extra = grad[media_rows - start:media_rows - start + lat_rows]
                    for i in range(items):
                        term = own[i * lat_rows:(i + 1) * lat_rows]
                        gq[0, i // 2, i % 2, :, at] = jnp.where(me.seq == i, term + extra, term).astype(BF16)

                @pl.when(t + 2 < tiles)
                def _():
                    for copy in fetch(t + 2, slot):
                        copy.start()
        count = norms[turn]
        norm_shares = ahead_of("norms%d" % turn)
        media_load(0, start).start()

        def out_copy(first, length):
            at = pl.ds(pl.multiple_of(start + first, lat_rows), length)
            return pltpu.make_async_copy(g.at[pl.ds(pl.multiple_of(first, lat_rows), length), :], media_grad.at[at, :], out_sem)

        @pl.loop(0, count)
        def _(i):
            run_at(i, norm_shares)
            pl.when(i + 1 < count)(lambda: media_load(i + 1, start).start())
            media_load(i, start).wait()
            at = pl.ds(pl.multiple_of(i * lat_rows, lat_rows), lat_rows)
            u, inverse = scaled_rows(med[lax.rem(i, 2)].astype(F32))
            grad = g[at, :]
            g[at, :] = norm_back(grad, u, inverse, gains[2:3, :])
            out_copy(i * lat_rows, lat_rows).start()
            sums_ref[0:1, :] += jnp.sum(grad * u, axis=0, keepdims=True)
            sums_ref[1:2, :] += jnp.sum(grad, axis=0, keepdims=True)
        out_copy(0, count * lat_rows).wait()
    run(ahead_of("end")[0])
    sums[...] = small[0][4]
    for item in (f_o, f_k, f_v, f_q):
        run(item.drain())
    for item in (up, dn, lat_item):
        item.drain()
    run(all_sum.phases()[-1])


def backward(dp_count, owner, lat, grad_hidden, gains, sums_ffn, n, nl, q, k, v, do_all, stats, gwo, gwu, gwd, media, wq, wk, wv, block_rows):
    nz = dp_count // 2
    items, lat_rows, width = q.shape
    rows = n.shape[0]
    hidden = gwu.shape[1]
    count = dp_count * 4
    shape = jax.ShapeDtypeStruct
    buf = lambda *s: pltpu.VMEM(s, BF16)
    flt = lambda *s: pltpu.VMEM(s, F32)
    pieces = lambda w: w.reshape(width // lat_rows, lat_rows, width)
    arrays = (owner, lat, grad_hidden, gains, sums_ffn, n.reshape(rows // lat_rows, lat_rows, width), nl, q, k, v, do_all, stats,
              gwo.reshape(dp_count, 2, 2, width // count, width),
              gwu.reshape(dp_count, 2, 2, width // count, hidden), gwd.reshape(1, 2, 2, hidden // 4, width),
              media, pieces(wq), pieces(wk), pieces(wv))
    return pl.pallas_call(
        functools.partial(backward_kernel, dp_count, block_rows),
        out_shape=(
            shape(media.shape, F32), shape((lat_rows, width), F32), shape((8, width), F32), *[shape((width // count, width), F32)] * 4,
            shape((width // count, hidden * dp_count), F32), shape((hidden // 4, width), F32),
        ),
        in_specs=[pl.BlockSpec(memory_space=pltpu.SMEM)] + [VMEM] * 4 + [ANY] * 14,
        out_specs=tuple([ANY] + [VMEM] * 8),
        scratch_shapes=[
            buf(rows // lat_rows, lat_rows, width), buf(items, lat_rows, width), buf(items, lat_rows, width), buf(items, lat_rows, width),
            buf(rows, width), buf(rows, width), flt(*stats.shape), buf(items * lat_rows, width), flt(rows // 2, width),
            buf(1, 2, 2, lat_rows, width), buf(2, lat_rows, width), buf(2, 2, 2, 2, width // count, width), flt(8, width),
            *Scatter.scratch(nz, width // count, width), *(Scatter.scratch(nz, width // count, width) * 3), *Regrouped.scratch(dp_count, width // count, hidden),
            *SeqScatter.scratch(1, hidden // 4, width), *SeqScatter.scratch(1, lat_rows, width),
            flt(5, 8, width), flt(2 + nz, 8, width), DMA((2 + nz,)), DMA((2 + nz,)),
            DMA((7,)), DMA((2, 3)), DMA((2,)), DMA,
        ],
        compiler_params=pltpu.CompilerParams(collective_id=2, has_side_effects=True, vmem_limit_bytes=WIDE),
    )(*arrays)


def copy_kernel(*refs):
    n = (len(refs) - 2) // 3
    arrays, outs, held, first, second = refs[:n], refs[n:2 * n], refs[2 * n:3 * n], refs[-2], refs[-1]
    ins = [pltpu.make_async_copy(arrays[i], held[i], first.at[i]) for i in range(n)]
    backs = [pltpu.make_async_copy(held[i], outs[i], second.at[i]) for i in range(n)]
    for copy in ins:
        copy.start()
    for copy, after in zip(ins, backs):
        copy.wait()
        after.start()
    for copy in backs:
        copy.wait()


def copied(*arrays):
    n = len(arrays)
    return pl.pallas_call(
        copy_kernel, out_shape=tuple(jax.ShapeDtypeStruct(a.shape, a.dtype) for a in arrays),
        in_specs=[ANY] * n, out_specs=tuple([ANY] * n),
        scratch_shapes=[*[pltpu.VMEM(a.shape, a.dtype) for a in arrays], DMA((n,)), DMA((n,))],
        compiler_params=pltpu.CompilerParams(vmem_limit_bytes=WIDE),
    )(*arrays)


def local_fast(
    media, latents, out_grad, frame_counts, block_position, w_query, w_key, w_value, w_out, w_up, w_down,
    gain_lat, shift_lat, gain_media, shift_media, gain_ffn, shift_ffn,
):
    dp_count, seq_count = lax.axis_size("dp"), lax.axis_size("seq")
    seq = lax.axis_index("seq")
    blocks, block_rows, width = media.shape
    items, lat_rows = seq_count, latents.shape[1]
    own_cols = gain_lat.shape[0]
    ends = FRAME_BLOCKS * jnp.cumsum(frame_counts[0])
    position = lax.dynamic_slice_in_dim(block_position[0], seq * blocks, blocks)
    owner = jnp.sum((ends[None, :] <= position[:, None]).astype(jnp.int32), axis=1)
    owner = jnp.concatenate([owner, seq[None]])
    vectors = jnp.stack([gain_lat, shift_lat, gain_media, shift_media, gain_ffn, shift_ffn]).astype(F32)
    pack = jnp.pad(vectors, ((0, 2), (0, 128 - own_cols)))
    lat, og = latents.reshape(lat_rows, width), out_grad.reshape(lat_rows, width)
    med = media.reshape(-1, width)
    (wq, wk, wv, n, nl, q, k, v, gwo, gwu, gwd, gains, lat_out, grad_hidden, do_all, stat_all, sums_ffn) = forward(
        dp_count, owner, med, pack, lat, w_query, w_key, w_value, w_out, og, w_down, w_up, block_rows, own_cols)
    wq, wk, wv = [w.reshape(width, width) for w in (wq, wk, wv)]
    media_grad, lat_grad, sums, out_q, out_k, out_v, out_o, out_up, out_dn = backward(
        dp_count, owner, lat, grad_hidden, gains, sums_ffn, n, nl, q, k, v, do_all, stat_all, gwo, gwu, gwd, med, wq, wk, wv, block_rows)
    place = (lax.axis_index("dp") * seq_count + seq) * own_cols
    own = lax.dynamic_slice_in_dim(sums, place, own_cols, axis=1)
    lat_out, lat_grad, media_grad, *grads = copied(lat_out, lat_grad, media_grad, out_q, out_k, out_v, out_o, out_up, out_dn)
    return (lat_out.reshape(latents.shape), lat_grad.reshape(latents.shape), media_grad.reshape(media.shape), *grads, *[own[i] for i in range(6)])


def fits(mesh):
    return mesh.shape["seq"] == 4 and mesh.shape["dp"] % 2 == 0 and 1536 % (mesh.shape["dp"] * 64) == 0


def norm_forward(rows, gain, shift):
    mean = jnp.mean(rows, axis=-1, keepdims=True)
    centred = rows - mean
    variance = jnp.mean(centred * centred, axis=-1, keepdims=True)
    inverse = lax.rsqrt(variance + EPS)
    scaled = centred * inverse
    return (scaled * gain + shift, scaled, inverse)


def norm_backward(incoming, scaled, inverse, gain):
    inner = incoming * gain
    first = jnp.mean(inner, axis=-1, keepdims=True)
    second = jnp.mean(inner * scaled, axis=-1, keepdims=True)
    return (
        inverse * (inner - first - scaled * second),
        jnp.sum(incoming * scaled, axis=0),
        jnp.sum(incoming, axis=0),
    )


def matmul(left, right):
    return jnp.dot(left, right, preferred_element_type=jnp.float32)


def matmul_left_t(left, right):
    return lax.dot_general(
        left, right, (((0,), (0,)), ((), ())), preferred_element_type=jnp.float32
    )


def matmul_right_t(left, right):
    return lax.dot_general(
        left, right, (((1,), (1,)), ((), ())), preferred_element_type=jnp.float32
    )


def swap_rows(stat):
    return jnp.swapaxes(stat, 1, 2)[..., None]


def fold_sources(tops, totals, accums):
    best = jnp.max(tops, axis=0)
    factor = jnp.exp(tops - best[None])
    total = jnp.sum(factor * totals, axis=0)
    width = accums.shape[-1]
    spread = jnp.repeat(jnp.swapaxes(factor, 2, 3), width // factor.shape[2], axis=3)
    return (best, total, jnp.sum(accums * spread, axis=0))


def local(
    media,
    latents,
    out_grad,
    frame_counts,
    block_position,
    w_query,
    w_key,
    w_value,
    w_out,
    w_up,
    w_down,
    gain_lat,
    shift_lat,
    gain_media,
    shift_media,
    gain_ffn,
    shift_ffn,
):
    gathered = (
        lax.all_gather(w_query, ("dp", "seq"), axis=0, tiled=True),
        lax.all_gather(w_key, ("dp", "seq"), axis=0, tiled=True),
        lax.all_gather(w_value, ("dp", "seq"), axis=0, tiled=True),
        lax.all_gather(w_out, ("dp", "seq"), axis=0, tiled=True),
        lax.all_gather(w_up, ("dp", "seq"), axis=0, tiled=True),
        lax.all_gather(w_down, ("dp", "seq"), axis=0, tiled=True),
        lax.all_gather(gain_lat, ("dp", "seq"), axis=0, tiled=True),
        lax.all_gather(shift_lat, ("dp", "seq"), axis=0, tiled=True),
        lax.all_gather(gain_media, ("dp", "seq"), axis=0, tiled=True),
        lax.all_gather(shift_media, ("dp", "seq"), axis=0, tiled=True),
        lax.all_gather(gain_ffn, ("dp", "seq"), axis=0, tiled=True),
        lax.all_gather(shift_ffn, ("dp", "seq"), axis=0, tiled=True),
    )
    full_query, full_key, full_value, full_out, full_up, full_down = gathered[:6]
    lat_gain, lat_shift, med_gain, med_shift, ffn_gain, ffn_shift = [
        piece.astype(jnp.float32) for piece in gathered[6:]
    ]
    seq_rank = lax.axis_index("seq")
    seq_count = lax.axis_size("seq")
    blocks, block_rows, width = media.shape
    local_items, lat_rows, _ = latents.shape
    group_items = frame_counts.shape[1]
    heads = HEADS
    head_size = HEAD_DIM
    score_scale = head_size ** (-0.5)
    ends = FRAME_BLOCKS * jnp.cumsum(frame_counts[0])
    position = lax.dynamic_slice_in_dim(block_position[0], seq_rank * blocks, blocks)
    owner_item = jnp.sum((ends[None, :] <= position[:, None]).astype(jnp.int32), axis=1)
    member = (owner_item[:, None] == jnp.arange(group_items, dtype=jnp.int32)[None, :]).astype(
        jnp.float32
    )
    lat_input = latents.astype(jnp.float32).reshape(-1, width)
    normed_lat, scaled_lat, inverse_lat = norm_forward(lat_input, lat_gain, lat_shift)
    normed_lat = normed_lat.astype(jnp.bfloat16)
    query = matmul(normed_lat, full_query).astype(jnp.bfloat16)
    key_lat = (
        matmul(normed_lat, full_key)
        .astype(jnp.bfloat16)
        .reshape(local_items, lat_rows, heads, head_size)
    )
    value_lat = (
        matmul(normed_lat, full_value)
        .astype(jnp.bfloat16)
        .reshape(local_items, lat_rows, heads, head_size)
    )
    query_all = lax.all_gather(
        query.reshape(local_items, lat_rows, width), "seq", axis=0, tiled=True
    )
    med_input = media.astype(jnp.float32).reshape(-1, width)
    normed_med, scaled_med, inverse_med = norm_forward(med_input, med_gain, med_shift)
    normed_med = normed_med.astype(jnp.bfloat16)

    def media_keys(weight_key, weight_value):
        keys_out = (
            matmul(normed_med, weight_key)
            .astype(jnp.bfloat16)
            .reshape(blocks, block_rows, heads, head_size)
        )
        values_out = (
            matmul(normed_med, weight_value)
            .astype(jnp.bfloat16)
            .reshape(blocks, block_rows, heads, head_size)
        )
        return (keys_out, values_out)

    key_med, value_med = media_keys(full_key, full_value)
    query_blk = query_all[owner_item].reshape(blocks, lat_rows, heads, head_size)
    scores_med = (
        jnp.einsum("bqhd,bkhd->bhqk", query_blk, key_med, preferred_element_type=jnp.float32)
        * score_scale
    )
    block_top = jnp.max(scores_med, axis=-1)
    expo_med = jnp.exp(scores_med - block_top[..., None])
    expo_med_low = expo_med.astype(jnp.bfloat16)
    local_top = jnp.max(jnp.where(member.T[:, :, None, None] > 0, block_top[None], NEG), axis=1)
    to_local = jnp.exp(block_top - local_top[owner_item])
    local_total = jnp.einsum(
        "bi,bhq->ihq", member, to_local * jnp.sum(expo_med, axis=-1), precision=HIGH
    )
    accum_blk = jnp.einsum(
        "bhqk,bkhd->bqhd", expo_med_low, value_med, preferred_element_type=jnp.float32
    ) * swap_rows(to_local)
    local_accum = jnp.einsum("bi,bqhd->iqhd", member, accum_blk, precision=HIGH).reshape(
        group_items, lat_rows, width
    )
    part_top, part_total, part_accum = (
        lax.all_to_all(local_top, "seq", split_axis=0, concat_axis=0, tiled=True),
        lax.all_to_all(local_total, "seq", split_axis=0, concat_axis=0, tiled=True),
        lax.all_to_all(local_accum, "seq", split_axis=0, concat_axis=0, tiled=True),
    )
    top_own, total_own, accum_flat = fold_sources(
        part_top.reshape(seq_count, local_items, heads, lat_rows),
        part_total.reshape(seq_count, local_items, heads, lat_rows),
        part_accum.reshape(seq_count, local_items, lat_rows, width),
    )
    med_top = lax.all_gather(top_own, "seq", axis=0, tiled=True)
    accum_own = accum_flat.reshape(local_items, lat_rows, heads, head_size)
    query_lat = query.reshape(local_items, lat_rows, heads, head_size)
    scores_lat = (
        jnp.einsum("iqhd,ikhd->ihqk", query_lat, key_lat, preferred_element_type=jnp.float32)
        * score_scale
    )
    lat_top = jnp.max(scores_lat, axis=-1)
    expo_lat = jnp.exp(scores_lat - lat_top[..., None])
    expo_lat_low = expo_lat.astype(jnp.bfloat16)
    item_top = jnp.maximum(top_own, lat_top)
    media_weight = jnp.exp(top_own - item_top)
    lat_weight = jnp.exp(lat_top - item_top)
    item_total = total_own * media_weight + lat_weight * jnp.sum(expo_lat, axis=-1)
    inverse_total = 1.0 / item_total
    accum_lat = jnp.einsum(
        "ihqk,ikhd->iqhd", expo_lat_low, value_lat, preferred_element_type=jnp.float32
    ) * swap_rows(lat_weight)
    attended = (accum_own * swap_rows(media_weight) + accum_lat) * swap_rows(inverse_total)
    attended_low = attended.reshape(-1, width).astype(jnp.bfloat16)
    hidden = lat_input + matmul(attended_low, full_out)
    normed_ffn, scaled_ffn, inverse_ffn = norm_forward(hidden, ffn_gain, ffn_shift)
    normed_ffn = normed_ffn.astype(jnp.bfloat16)
    pre_act = matmul(normed_ffn, full_up)
    activated, gelu_back = jax.vjp(partial(jax.nn.gelu, approximate=False), pre_act)
    activated = activated.astype(jnp.bfloat16)
    result = hidden + matmul(activated, full_down)
    latents_out = result.astype(jnp.bfloat16).reshape(latents.shape)
    again = (
        lax.all_gather(w_query, ("dp", "seq"), axis=0, tiled=True),
        lax.all_gather(w_key, ("dp", "seq"), axis=0, tiled=True),
        lax.all_gather(w_value, ("dp", "seq"), axis=0, tiled=True),
        lax.all_gather(w_out, ("dp", "seq"), axis=0, tiled=True),
        lax.all_gather(w_up, ("dp", "seq"), axis=0, tiled=True),
        lax.all_gather(w_down, ("dp", "seq"), axis=0, tiled=True),
        lax.all_gather(gain_lat, ("dp", "seq"), axis=0, tiled=True),
        lax.all_gather(shift_lat, ("dp", "seq"), axis=0, tiled=True),
        lax.all_gather(gain_media, ("dp", "seq"), axis=0, tiled=True),
        lax.all_gather(shift_media, ("dp", "seq"), axis=0, tiled=True),
        lax.all_gather(gain_ffn, ("dp", "seq"), axis=0, tiled=True),
        lax.all_gather(shift_ffn, ("dp", "seq"), axis=0, tiled=True),
    )
    back_query, back_key, back_value, back_out, back_up, back_down = again[:6]
    grad_rows = out_grad.reshape(-1, width)
    cotangent = grad_rows.astype(jnp.float32)
    grad_down = matmul_left_t(activated, grad_rows)
    grad_act = matmul_right_t(grad_rows, back_down)
    grad_pre = gelu_back(grad_act)[0].astype(jnp.bfloat16)
    grad_up = matmul_left_t(normed_ffn, grad_pre)
    grad_normed_ffn = matmul_right_t(grad_pre, back_up)
    grad_hidden_norm, grad_gain_ffn, grad_shift_ffn = norm_backward(
        grad_normed_ffn, scaled_ffn, inverse_ffn, ffn_gain
    )
    grad_hidden = cotangent + grad_hidden_norm
    grad_hidden_low = grad_hidden.astype(jnp.bfloat16)
    grad_out = matmul_left_t(attended_low, grad_hidden_low)
    grad_att = matmul_right_t(grad_hidden_low, back_out).astype(jnp.bfloat16)
    grad_att_heads = grad_att.reshape(local_items, lat_rows, heads, head_size)
    delta = jnp.einsum(
        "iqhd,iqhd->ihq", grad_att_heads.astype(jnp.float32), attended, precision=HIGH
    )
    media_factor = media_weight * inverse_total
    grad_att_all = lax.all_gather(
        grad_att.reshape(local_items, lat_rows, width), "seq", axis=0, tiled=True
    )
    factor_all, delta_all = (
        lax.all_gather(media_factor, "seq", axis=0, tiled=True),
        lax.all_gather(delta, "seq", axis=0, tiled=True),
    )
    key_med, value_med = media_keys(back_key, back_value)
    grad_blk = grad_att_all[owner_item].reshape(blocks, lat_rows, heads, head_size)
    factor_blk = jnp.exp(block_top - med_top[owner_item]) * factor_all[owner_item]
    delta_blk = delta_all[owner_item]
    grad_prob_med = jnp.einsum(
        "bqhd,bkhd->bhqk", grad_blk, value_med, preferred_element_type=jnp.float32
    )
    grad_score_med = (
        expo_med * factor_blk[..., None] * (grad_prob_med - delta_blk[..., None])
    ).astype(jnp.bfloat16)
    grad_query_blk = (
        jnp.einsum("bhqk,bkhd->bqhd", grad_score_med, key_med, preferred_element_type=jnp.float32)
        * score_scale
    )
    grad_query_part = jnp.einsum("bi,bqhd->iqhd", member, grad_query_blk, precision=HIGH).reshape(
        group_items, lat_rows, width
    )
    grad_key_med = (
        (
            jnp.einsum(
                "bhqk,bqhd->bkhd", grad_score_med, query_blk, preferred_element_type=jnp.float32
            )
            * score_scale
        )
        .astype(jnp.bfloat16)
        .reshape(-1, width)
    )
    grad_value_med = (
        jnp.einsum(
            "bhqk,bqhd->bkhd",
            expo_med_low.astype(jnp.float32) * factor_blk[..., None],
            grad_blk.astype(jnp.float32),
            precision=HIGH,
        )
        .astype(jnp.bfloat16)
        .reshape(-1, width)
    )
    grad_query_own = lax.psum_scatter(
        grad_query_part.astype(jnp.bfloat16), "seq", scatter_dimension=0, tiled=True
    ).astype(jnp.float32)
    grad_normed_med = matmul_right_t(grad_key_med, back_key) + matmul_right_t(
        grad_value_med, back_value
    )
    grad_key = matmul_left_t(normed_med, grad_key_med)
    grad_value = matmul_left_t(normed_med, grad_value_med)
    media_grad, grad_gain_media, grad_shift_media = norm_backward(
        grad_normed_med, scaled_med, inverse_med, med_gain
    )
    lat_factor = lat_weight * inverse_total
    grad_prob_lat = jnp.einsum(
        "iqhd,ikhd->ihqk", grad_att_heads, value_lat, preferred_element_type=jnp.float32
    )
    grad_score_lat = (expo_lat * lat_factor[..., None] * (grad_prob_lat - delta[..., None])).astype(
        jnp.bfloat16
    )
    grad_query_lat = (
        jnp.einsum("ihqk,ikhd->iqhd", grad_score_lat, key_lat, preferred_element_type=jnp.float32)
        * score_scale
    )
    grad_key_lat = (
        (
            jnp.einsum(
                "ihqk,iqhd->ikhd", grad_score_lat, query_lat, preferred_element_type=jnp.float32
            )
            * score_scale
        )
        .astype(jnp.bfloat16)
        .reshape(-1, width)
    )
    grad_value_lat = (
        jnp.einsum(
            "ihqk,iqhd->ikhd",
            expo_lat_low.astype(jnp.float32) * lat_factor[..., None],
            grad_att_heads.astype(jnp.float32),
            precision=HIGH,
        )
        .astype(jnp.bfloat16)
        .reshape(-1, width)
    )
    grad_query = (
        (grad_query_own + grad_query_lat.reshape(local_items, lat_rows, width))
        .astype(jnp.bfloat16)
        .reshape(-1, width)
    )
    grad_normed_lat = (
        matmul_right_t(grad_query, back_query)
        + matmul_right_t(grad_key_lat, back_key)
        + matmul_right_t(grad_value_lat, back_value)
    )
    grad_query_weight = matmul_left_t(normed_lat, grad_query)
    grad_key = grad_key + matmul_left_t(normed_lat, grad_key_lat)
    grad_value = grad_value + matmul_left_t(normed_lat, grad_value_lat)
    grad_lat_norm, grad_gain_lat, grad_shift_lat = norm_backward(
        grad_normed_lat, scaled_lat, inverse_lat, lat_gain
    )
    latents_grad = (grad_hidden + grad_lat_norm).reshape(latents.shape)
    sharded = (
        lax.psum_scatter(grad_query_weight, ("dp", "seq"), scatter_dimension=0, tiled=True),
        lax.psum_scatter(grad_key, ("dp", "seq"), scatter_dimension=0, tiled=True),
        lax.psum_scatter(grad_value, ("dp", "seq"), scatter_dimension=0, tiled=True),
        lax.psum_scatter(grad_out, ("dp", "seq"), scatter_dimension=0, tiled=True),
        lax.psum_scatter(grad_up, ("dp", "seq"), scatter_dimension=0, tiled=True),
        lax.psum_scatter(grad_down, ("dp", "seq"), scatter_dimension=0, tiled=True),
        lax.psum_scatter(grad_gain_lat, ("dp", "seq"), scatter_dimension=0, tiled=True),
        lax.psum_scatter(grad_shift_lat, ("dp", "seq"), scatter_dimension=0, tiled=True),
        lax.psum_scatter(grad_gain_media, ("dp", "seq"), scatter_dimension=0, tiled=True),
        lax.psum_scatter(grad_shift_media, ("dp", "seq"), scatter_dimension=0, tiled=True),
        lax.psum_scatter(grad_gain_ffn, ("dp", "seq"), scatter_dimension=0, tiled=True),
        lax.psum_scatter(grad_shift_ffn, ("dp", "seq"), scatter_dimension=0, tiled=True),
    )
    return (latents_out, latents_grad, media_grad.reshape(media.shape)) + tuple(sharded)


def solution(mesh):
    return jax.shard_map(
        local_fast if fits(mesh) else local,
        mesh=mesh,
        in_specs=(
            P(("dp", "seq"), None, None),
            P(("dp", "seq"), None, None),
            P(("dp", "seq"), None, None),
            P("dp", None),
            P("dp", None),
            P(("dp", "seq"), None),
            P(("dp", "seq"), None),
            P(("dp", "seq"), None),
            P(("dp", "seq"), None),
            P(("dp", "seq"), None),
            P(("dp", "seq"), None),
            P(("dp", "seq")),
            P(("dp", "seq")),
            P(("dp", "seq")),
            P(("dp", "seq")),
            P(("dp", "seq")),
            P(("dp", "seq")),
        ),
        out_specs=(
            P(("dp", "seq"), None, None),
            P(("dp", "seq"), None, None),
            P(("dp", "seq"), None, None),
            P(("dp", "seq"), None),
            P(("dp", "seq"), None),
            P(("dp", "seq"), None),
            P(("dp", "seq"), None),
            P(("dp", "seq"), None),
            P(("dp", "seq"), None),
            P(("dp", "seq")),
            P(("dp", "seq")),
            P(("dp", "seq")),
            P(("dp", "seq")),
            P(("dp", "seq")),
            P(("dp", "seq")),
        ),
        check_vma=False,
    )
```

```python
import math
from functools import partial
from jax.sharding import PartitionSpec as P
import functools
import jax
import jax.numpy as jnp
from jax import lax
from jax.experimental import pallas as pl
from jax.experimental.pallas import tpu as pltpu

MESH = pl.DeviceIdType.MESH
ANY = pl.BlockSpec(memory_space=pl.ANY)
VMEM = pl.BlockSpec(memory_space=pltpu.VMEM)
DMA = pltpu.SemaphoreType.DMA


class Here:
    def __init__(self, dp_count):
        dp, seq = lax.axis_index("dp"), lax.axis_index("seq")
        self.nz = dp_count // 2
        self.z, self.x, self.y, self.c = dp // 2, dp % 2, seq // 2, seq % 2
        self.dp, self.seq = dp, seq

    def at(self, z=None, x=None, y=None, c=None):
        z = self.z if z is None else z
        x = self.x if x is None else x
        y = self.y if y is None else y
        c = self.c if c is None else c
        return (z * 2 + x, y * 2 + c)


def send(src, dst, ss, rs, to):
    copy = pltpu.make_async_remote_copy(
        src_ref=src, dst_ref=dst, send_sem=ss, recv_sem=rs, device_id=to, device_id_type=MESH
    )
    copy.start()


def landed(dst, ss, rs, me):
    pltpu.make_async_remote_copy(
        src_ref=dst, dst_ref=dst, send_sem=ss, recv_sem=rs, device_id=me.at(c=1 - me.c), device_id_type=MESH
    ).wait_recv()


def sent(src, ss, rs, me):
    pltpu.make_async_remote_copy(
        src_ref=src, dst_ref=src, send_sem=ss, recv_sem=rs, device_id=me.at(c=1 - me.c), device_id_type=MESH
    ).wait_send()


def greet(devices):
    barrier = pltpu.get_barrier_semaphore()
    for device in devices:
        pl.semaphore_signal(barrier, inc=1, device_id=device, device_id_type=MESH)
    pl.semaphore_wait(barrier, len(devices))


COL, FROMX, FROMY, DIAGA, DIAGB = range(5)
TOUP, TODOWN, TOX, TOY, FWDY, FWDX, TOC = range(7)


class Gather:
    def __init__(self, me, src, dst, ss, rs, axes, halves):
        self.me, self.src, self.dst, self.ss, self.rs = me, src, dst, ss, rs
        self.axes, self.halves = axes, halves
        self.sends = []
        self.depth = me.nz if "z" in axes else 1

    def slot(self, z, x, y, c):
        if self.axes == "zxyc":
            return ((z * 2 + x) * 2 + y) * 2 + c
        if self.axes == "zx":
            return z * 2 + x
        return y * 2 + c

    def shard(self, z, x, y, c, half=None):
        ref = self.dst.at[self.slot(z, x, y, c)]
        if half is None or not self.halves:
            return ref
        cut, width = self.halves, self.dst.shape[-1]
        return ref.at[:, pl.ds(0, cut)] if half == 0 else ref.at[:, pl.ds(cut, width - cut)]

    def key(self, z):
        return z if "z" in self.axes else 0

    def start(self, src, dst, out_kind, in_kind, z, to):
        send(src, dst, self.leaves(out_kind, z), self.arrives(in_kind, z), to)

    def leaves(self, kind, z):
        return self.ss.at[1 + kind * self.depth + z] if kind in (TOUP, TODOWN) else self.ss.at[0]

    def arrives(self, kind, z):
        return self.rs.at[5 * self.depth if kind >= 5 else kind * self.depth + self.key(z)]

    def whole(self, count):
        return self.dst.at[pl.ds(0, count)]

    def gone(self, ref, kind, z):
        sent(ref, self.leaves(kind, z), self.rs.at[0], self.me)

    def here(self, ref, kind, z):
        landed(ref, self.ss.at[0], self.arrives(kind, z), self.me)

    def groups(self):
        return dict(own=self.own(), column=self.column(), neighbours=self.neighbours(), diagonal=self.diagonal(), sibling=self.sibling())

    @staticmethod
    def semaphores(axes, nz):
        depth = nz if "z" in axes else 1
        return [DMA((1 + 2 * depth,)), DMA((5 * depth + 1,))]

    def hand_over(self, ref, kind, z):
        if "c" in self.axes:
            self.start(ref, ref, TOC + kind, 5 + kind, z, self.me.at(c=1 - self.me.c))

    def spread(self, ref, z):
        me = self.me
        if "x" in self.axes:
            self.start(ref, ref, TOX, FROMX, z, me.at(x=1 - me.x))
        if "y" in self.axes:
            self.start(ref, ref, TOY, FROMY, z, me.at(y=1 - me.y))
        self.hand_over(ref, COL, z)

    def own(self):
        return [self.send_own]

    def send_own(self):
        me = self.me
        ref = self.shard(me.z, me.x, me.y, me.c)
        if "z" in self.axes:
            @pl.when(me.z + 1 < me.nz)
            def _():
                self.start(self.src, ref, TOUP, COL, me.z, me.at(z=me.z + 1))

            @pl.when(me.z > 0)
            def _():
                self.start(self.src, ref, TODOWN, COL, me.z, me.at(z=me.z - 1))
        if "x" in self.axes:
            self.start(self.src, ref, TOX, FROMX, me.z, me.at(x=1 - me.x))
        if "y" in self.axes:
            self.start(self.src, ref, TOY, FROMY, me.z, me.at(y=1 - me.y))
        if "c" in self.axes:
            self.start(self.src, ref, TOC, 5, me.z, me.at(c=1 - me.c))

    def around(self, event):
        me = self.me
        found = [lambda: event(me.z)]
        for d in range(1, self.depth):
            found.append(lambda d=d: pl.when(me.z >= d)(lambda: event(me.z - d)))
            found.append(lambda d=d: pl.when(me.z + d < me.nz)(lambda: event(me.z + d)))
        return found

    def column(self):
        me = self.me

        def event(d, below):
            there = me.z - d if below else me.z + d
            ahead = me.z + 1 if below else me.z - 1

            @pl.when(there >= 0 if below else there < me.nz)
            def _():
                ref = self.shard(there, me.x, me.y, me.c)
                self.here(ref, COL, there)

                @pl.when(ahead < me.nz if below else ahead >= 0)
                def _():
                    self.start(ref, ref, TOUP if below else TODOWN, COL, there, me.at(z=ahead))
                self.spread(ref, there)
        return [functools.partial(event, d, below) for d in range(1, self.depth) for below in (True, False)]

    def neighbours(self):
        me = self.me

        def event(z):
            if "x" in self.axes:
                ref = self.shard(z, 1 - me.x, me.y, me.c)
                self.here(ref, FROMX, z)
                if "y" in self.axes:
                    half = self.shard(z, 1 - me.x, me.y, me.c, 0)
                    self.start(half, half, FWDY, DIAGA, z, me.at(y=1 - me.y))
                self.hand_over(ref, FROMX, z)
            if "y" in self.axes:
                ref = self.shard(z, me.x, 1 - me.y, me.c)
                self.here(ref, FROMY, z)
                if "x" in self.axes and self.halves:
                    half = self.shard(z, me.x, 1 - me.y, me.c, 1)
                    self.start(half, half, FWDX, DIAGB, z, me.at(x=1 - me.x))
                self.hand_over(ref, FROMY, z)
        return self.around(event)

    def diagonal(self):
        me = self.me
        if "x" not in self.axes or "y" not in self.axes:
            return []

        def event(z):
            for half in range(2 if self.halves else 1):
                ref = self.shard(z, 1 - me.x, 1 - me.y, me.c, half)
                self.here(ref, DIAGA + half, z)
                self.hand_over(ref, DIAGA + half, z)
        return self.around(event)

    def kinds(self):
        me = self.me
        found = [(COL, me.x, me.y, None)]
        if "x" in self.axes:
            found.append((FROMX, 1 - me.x, me.y, None))
        if "y" in self.axes:
            found.append((FROMY, me.x, 1 - me.y, None))
        if "x" in self.axes and "y" in self.axes:
            found.append((DIAGA, 1 - me.x, 1 - me.y, 0))
            if self.halves:
                found.append((DIAGB, 1 - me.x, 1 - me.y, 1))
        return found

    def sibling(self):
        if "c" not in self.axes:
            return []
        count = self.depth * (1 + ("x" in self.axes)) * (1 + ("y" in self.axes))
        return [lambda: self.here(self.whole(count), 5, 0)]

    def drain(self):
        me = self.me
        x, y, c = ["xyc".index(a) >= 0 and a in self.axes for a in "xyc"]
        count = self.depth * (x + y + (x and y) + c * (1 + x) * (1 + y))
        found = [lambda: self.gone(self.whole(count), TOC, 0)]
        if "z" in self.axes:
            shard = self.shard(me.z, me.x, me.y, me.c)

            def event(z):
                pl.when((z <= me.z) & (me.z + 1 < me.nz))(lambda: self.gone(shard, TOUP, z))
                pl.when((z >= me.z) & (me.z > 0))(lambda: self.gone(shard, TODOWN, z))
            found += self.around(event)
        return found

    def phases(self):
        return [self.own(), self.column(), self.neighbours(), self.diagonal(), self.sibling(), self.drain()]


def skewed(items):
    lists = [item.phases() for item in items]
    found = []
    for step in range(len(lists) + max(map(len, lists)) - 1):
        for i, phases in enumerate(lists):
            if 0 <= step - i < len(phases):
                found += phases[step - i]
    return found


def run(events):
    for event in events:
        event()


def share(events, count):
    cuts = [len(events) * i // count for i in range(count + 1)]
    return [events[a:b] for a, b in zip(cuts, cuts[1:])]


def run_at(step, lists):
    for i, events in enumerate(lists):
        if events:
            pl.when(step == i)(functools.partial(run, events))


class Regroup:
    def __init__(self, me, dp_count, src, dst, ss, rs, width):
        self.me, self.n, self.src, self.dst, self.ss, self.rs, self.width = me, dp_count, src, dst, ss, rs, width

    def piece(self, dp, y, c):
        return self.dst.at[dp * 4 + y * 2 + c]

    def columns(self, dp):
        return self.src.at[:, pl.ds(pl.multiple_of(dp * self.width, 128), self.width)]

    def hand(self, src, dp, y, place, to):
        send(src, self.piece(dp, y, self.me.c), self.ss.at[0], self.rs.at[place], to)

    def own(self):
        me = self.me
        for k in range(1, self.n):
            to = lax.rem(me.dp + k, self.n)
            self.hand(self.columns(to), me.dp, me.y, me.dp, (to, me.seq))
        self.share(self.columns(me.dp), me.dp)

    def share(self, src, dp):
        me = self.me
        self.hand(src, dp, me.y, self.n + dp, me.at(y=1 - me.y))
        self.hand(src, dp, me.y, 2 * self.n, me.at(c=1 - me.c))

    def here(self, ref, place):
        landed(ref, self.ss.at[0], self.rs.at[place], self.me)

    def column(self):
        me = self.me
        for k in range(1, self.n):
            dp = lax.rem(me.dp + k, self.n)
            ref = self.piece(dp, me.y, me.c)
            self.here(ref, dp)
            self.share(ref, dp)

    def neighbours(self):
        me = self.me
        for k in range(self.n):
            dp = lax.rem(me.dp + k, self.n)
            ref = self.piece(dp, 1 - me.y, me.c)
            self.here(ref, self.n + dp)
            self.hand(ref, dp, 1 - me.y, 2 * self.n, me.at(c=1 - me.c))

    def sibling(self):
        self.here(self.dst.at[pl.ds(0, 2 * self.n)], 2 * self.n)

    def drain(self):
        sent(self.dst.at[pl.ds(0, 4 * self.n - 1)], self.ss.at[0], self.rs.at[0], self.me)

    def phases(self):
        return [[self.own], [self.column], [self.neighbours], [self.sibling], [self.drain]]

    @staticmethod
    def semaphores(dp_count):
        return [DMA((1,)), DMA((2 * dp_count + 1,))]


class Everyone:
    def __init__(self, me, dp_count, src, dst, ss, rs):
        self.me, self.n, self.src, self.dst, self.ss, self.rs = me, dp_count * 4, src, dst, ss, rs
        self.index = me.dp * 4 + me.seq

    def own(self):
        def event():
            @pl.loop(1, self.n)
            def _(k):
                to = lax.rem(self.index + k, self.n)
                send(self.src, self.dst.at[self.index], self.ss.at[0], self.rs.at[0], (to // 4, to % 4))
        return [event]

    def arrive(self):
        return [lambda: landed(self.dst.at[pl.ds(0, self.n - 1)], self.ss.at[0], self.rs.at[0], self.me)]

    def drain(self):
        return [lambda: sent(self.dst.at[pl.ds(0, self.n - 1)], self.ss.at[0], self.rs.at[0], self.me)]

    def phases(self):
        return [self.own(), self.arrive(), self.drain()]


def greet_all(me, dp_count):
    barrier = pltpu.get_barrier_semaphore()
    count = dp_count * 4

    @pl.loop(1, count)
    def _(k):
        to = lax.rem(me.dp * 4 + me.seq + k, count)
        pl.semaphore_signal(barrier, inc=1, device_id=(to // 4, to % 4), device_id_type=MESH)
    pl.semaphore_wait(barrier, count - 1)


FORWARD_ORDER = dict(
    q=dict(own=-1.671, column=-0.997, neighbours=2.973, diagonal=8.049, sibling=9.285),
    pack=dict(own=-1.0, arrive=-0.731),
    lat=dict(own=-0.999, neighbours=-0.917, sibling=-0.732),
    k=dict(own=-0.998, column=-0.996, neighbours=2.5, diagonal=4.61, sibling=7.657),
    v=dict(own=-0.336, column=3.046, neighbours=14.914, diagonal=28.532, sibling=40.12),
    o=dict(own=8.048, column=23.68, neighbours=44.275, diagonal=59.459, sibling=59.943),
    og=dict(own=27.572, column=59.273, neighbours=61.672),
    up=dict(own=28.241, column=59.555, neighbours=61.854, sibling=62.713),
    dn=dict(own=28.533, neighbours=58.926, sibling=59.917),
    x=dict(send0=50.963, send1=59.241, wait=59.918),
    nf=dict(own=61.183, a1=61.853, a2=62.093, b0=62.272, b1=64.105, b2=65.251, a3=65.818, b3=66.796),
    g=dict(a0=64.191, a1=66.009, a2=66.274, a3=67.798, b0=69.586, b1=70.423, b2=71.005, b3=71.804, finish=71.853),
    y=dict(start=71.382, fold=72.623, finish=76.92),
    st=dict(own=73.217, neighbours=74.655, sibling=76.353),
    do=dict(own=73.218, neighbours=76.825, sibling=78.0),
)
BACK_ORDER = dict(
    o=dict(begin=-1.0, core=0.257, middle=14.163, fold=21.903, finish=28.444),
    up=dict(begin=1.335, core=6.978, fold=24.753, finish=24.894, collect=50.506),
    k=dict(core=18.955, middle=28.229, fold=40.734, finish=48.103),
    v=dict(core=24.416, middle=37.863, fold=48.42, finish=51.002),
    dn=dict(begin=24.67, core=37.79, fold=50.639, finish=51.001),
    lat=dict(begin=34.007, core=37.914, fold=48.961, finish=50.002),
    q=dict(core=40.466, middle=50.058, fold=50.129, finish=51.003),
    sum=dict(s0=50.057, s1=50.128, s2=50.64, s3=51.0, s4=450.823),
)


HEADS = 16
HEAD_DIM = 96
FRAME_BLOCKS = 2
EPS = 1e-05
NEG = -1e30
HIGH = lax.Precision.HIGHEST
F32, BF16 = jnp.float32, jnp.bfloat16
WIDE = 62 << 20
PART = 4
PCOLS = PART * HEAD_DIM
SCALE = HEAD_DIM ** (-0.5)


def dot(left, right):
    return jnp.dot(left, right, preferred_element_type=F32)


def dot_t(left, right):
    return lax.dot_general(left, right, (((1,), (1,)), ((), ())), preferred_element_type=F32)


def t_dot(left, right):
    return lax.dot_general(left, right, (((0,), (0,)), ((), ())), preferred_element_type=F32)


def scaled_rows(rows):
    mean = jnp.mean(rows, axis=-1, keepdims=True)
    centred = rows - mean
    inverse = lax.rsqrt(jnp.mean(centred * centred, axis=-1, keepdims=True) + EPS)
    return centred * inverse, inverse


def norm_back(incoming, scaled, inverse, gain):
    inner = incoming * gain
    first = jnp.mean(inner, axis=-1, keepdims=True)
    second = jnp.mean(inner * scaled, axis=-1, keepdims=True)
    return inverse * (inner - first - scaled * second)


def part_mask(rows):
    row = lax.broadcasted_iota(jnp.int32, (PART * rows, PCOLS), 0)
    column = lax.broadcasted_iota(jnp.int32, (PART * rows, PCOLS), 1)
    low = (row // rows) * HEAD_DIM
    return (column >= low) & (column < low + HEAD_DIM)


def stacked(rows, mask):
    return jnp.where(mask, jnp.concatenate([rows] * PART, axis=0), jnp.zeros((), rows.dtype))


def unstacked(rows, mask, count):
    kept = jnp.where(mask, rows, 0.0)
    return sum(kept[h * count:(h + 1) * count] for h in range(PART))


def blocks_of(media_rows, block_rows, lat_rows):
    found = [(b * block_rows, block_rows) for b in range(media_rows // block_rows)]
    return found + [(media_rows, lat_rows)]


def attend_kernel(block_rows, items, owner, media, lat_all, gains, wq, wk, wv,
                  acc, stats, n_out, nl_out, q_out, k_out, v_out, wbuf, a_ref, m_ref, l_ref, sems):
    width = media.shape[1]
    half = width // 2
    media_rows = media.shape[0]
    lat_rows = lat_all.shape[0] // items
    seq = lax.axis_index("seq")

    def fetch(step, slot):
        cols = pl.ds(pl.multiple_of(step * half, 128), half)
        return [pltpu.make_async_copy(w.at[:, cols], wbuf.at[slot, i], sems.at[slot, i]) for i, w in enumerate((wq, wk, wv))]
    for copy in fetch(0, 0):
        copy.start()

    @pl.loop(0, media_rows // block_rows)
    def _(b):
        rows = pl.ds(pl.multiple_of(b * block_rows, block_rows), block_rows)
        u, _ = scaled_rows(media[rows, :].astype(F32))
        n_out[rows, :] = (u * gains[2:3, :] + gains[3:4, :]).astype(BF16)

    @pl.loop(0, items)
    def _(i):
        rows = pl.ds(pl.multiple_of(i * lat_rows, lat_rows), lat_rows)
        u, _ = scaled_rows(lat_all[rows, :].astype(F32))
        nl_out[rows, :] = (u * gains[0:1, :] + gains[1:2, :]).astype(BF16)
    n_out[pl.ds(media_rows, lat_rows), :] = nl_out[pl.ds(pl.multiple_of(seq * lat_rows, lat_rows), lat_rows), :]
    padding = n_out.shape[0] - media_rows - lat_rows
    n_out[pl.ds(media_rows + lat_rows, padding), :] = jnp.zeros((padding, width), BF16)
    stats[...] = jnp.zeros_like(stats)
    mask = part_mask(lat_rows)
    lane = lax.broadcasted_iota(jnp.int32, (lat_rows, 128), 1)

    @pl.loop(0, 2)
    def _(step):
        slot = lax.rem(step, 2)
        cols = pl.ds(pl.multiple_of(step * half, 128), half)
        for copy in fetch(step, slot):
            copy.wait()

        @pl.when(step == 0)
        def _():
            for copy in fetch(1, 1):
                copy.start()
        q_out[:, cols] = dot(nl_out[...], wbuf[slot, 0]).astype(BF16)
        k_out[:, cols] = dot(n_out[...], wbuf[slot, 1]).astype(BF16)
        v_out[:, cols] = dot(n_out[...], wbuf[slot, 2]).astype(BF16)

        @pl.loop(0, half // PCOLS)
        def _(inner):
            part = step * (half // PCOLS) + inner
            pcols = pl.ds(pl.multiple_of(part * PCOLS, 128), PCOLS)
            a_ref[...] = jnp.zeros_like(a_ref)
            l_ref[...] = jnp.zeros_like(l_ref)
            m_ref[...] = jnp.full_like(m_ref, NEG)

            def block(start, count, item):
                rows = q_out[pl.ds(pl.multiple_of(item * lat_rows, lat_rows), lat_rows), pcols]
                query = stacked(rows, mask)
                keys, values = k_out[pl.ds(start, count), pcols], v_out[pl.ds(start, count), pcols]
                scores = dot_t(query, keys) * SCALE
                old = m_ref[item]
                new = jnp.maximum(old, jnp.max(scores, axis=-1, keepdims=True))
                factor = jnp.exp(old - new)
                expo = jnp.exp(scores - new[:, :count])
                m_ref[item] = new
                l_ref[item] = l_ref[item] * factor + jnp.sum(expo, axis=-1, keepdims=True)
                wide = jnp.concatenate([factor] * (PCOLS // 128), axis=1)
                a_ref[item] = a_ref[item] * wide + dot(expo.astype(BF16), values)
            for b, (start, count) in enumerate(blocks_of(media_rows, block_rows, lat_rows)):
                block(start, count, seq if count == lat_rows and start == media_rows else owner[b])
            for item in range(items):
                acc[item, :, pcols] = unstacked(a_ref[item], mask, lat_rows).astype(BF16)
                for h in range(PART):
                    chosen = lane == part * PART + h
                    at = pl.ds(h * lat_rows, lat_rows)
                    stats[item, 0] = jnp.where(chosen, m_ref[item, at, :], stats[item, 0])
                    stats[item, 1] = jnp.where(chosen, l_ref[item, at, :], stats[item, 1])


def attend(owner, media, lat_all, gains, wq, wk, wv, block_rows, items):
    width = media.shape[1]
    lat_rows = lat_all.shape[0] // items
    rows = media.shape[0] + block_rows
    shape = jax.ShapeDtypeStruct
    return pl.pallas_call(
        functools.partial(attend_kernel, block_rows, items),
        out_shape=(
            shape((items, lat_rows, width), BF16), shape((items, 2, lat_rows, 128), F32),
            shape((rows, width), BF16), shape((items * lat_rows, width), BF16),
            shape((items * lat_rows, width), BF16), shape((rows, width), BF16), shape((rows, width), BF16),
        ),
        in_specs=[pl.BlockSpec(memory_space=pltpu.SMEM), VMEM, VMEM, VMEM, ANY, ANY, ANY],
        out_specs=tuple([VMEM] * 7),
        scratch_shapes=[
            pltpu.VMEM((2, 3, width, width // 2), BF16),
            pltpu.VMEM((items, PART * lat_rows, PCOLS), F32),
            pltpu.VMEM((items, PART * lat_rows, 128), F32), pltpu.VMEM((items, PART * lat_rows, 128), F32),
            DMA((2, 3)),
        ],
        compiler_params=pltpu.CompilerParams(vmem_limit_bytes=WIDE),
    )(owner, media, lat_all, gains, wq, wk, wv)


def dp_peers(me, dp_count):
    return [(lax.rem(me.dp + k, dp_count), me.seq) for k in range(1, dp_count)]


def far_first(me, event):
    found = []
    for d in range(me.nz - 1, 0, -1):
        found.append(lambda d=d: pl.when(me.z >= d)(lambda: event(me.z - d)))
        found.append(lambda d=d: pl.when(me.z + d < me.nz)(lambda: event(me.z + d)))
    return found + [lambda: event(me.z)]


def add(*refs):
    total = refs[0][...].astype(F32)
    for ref in refs[1:]:
        total = total + ref[...].astype(F32)
    return total


class Line:
    def __init__(self, me, column, boxes, ss, rs):
        self.me, self.column, self.boxes, self.ss, self.rs = me, column, boxes, ss, rs

    def event(self, z):
        me = self.me

        @pl.when(z != me.z)
        def _():
            send(self.column(z), self.boxes.at[me.z], self.ss.at[0], self.rs.at[0], me.at(z=z))

    def total(self, out):
        me = self.me
        landed(self.boxes.at[pl.ds(0, me.nz - 1)], self.ss.at[0], self.rs.at[0], me)
        out[...] = self.column(me.z)[...].astype(F32)
        for z in range(me.nz):
            @pl.when(z != me.z)
            def _():
                out[...] += self.boxes.at[z][...].astype(F32)

    def drain(self):
        return [lambda: sent(self.boxes.at[pl.ds(0, self.me.nz - 1)], self.ss.at[0], self.rs.at[0], self.me)]


class DpScatter:
    def __init__(self, me, part, out, ox, boxes, ss, rs, lss, lrs):
        self.me, self.part, self.out, self.ox, self.ss, self.rs = me, part, out, ox, ss, rs
        self.line = Line(me, lambda z: part.at[z * 2 + me.x], boxes, lss, lrs)

    def order(self):
        n = self.me.nz
        return [lax.rem(self.me.z + k, n) for k in sorted(range(1, n), key=lambda k: -min(k, n - k))] + [self.me.z]

    def send_x(self, z):
        me = self.me
        send(self.part.at[z * 2 + 1 - me.x], self.ox.at[z], self.ss.at[0], self.rs.at[z], me.at(x=1 - me.x))

    def start(self):
        return [functools.partial(self.send_x, z) for z in self.order()]

    def fold_in(self, z):
        landed(self.ox.at[z], self.ss.at[0], self.rs.at[z], self.me)
        mine = self.part.at[z * 2 + self.me.x]
        mine[...] = add(mine, self.ox.at[z]).astype(mine.dtype)
        self.line.event(z)

    def fold(self):
        return [functools.partial(self.fold_in, z) for z in self.order()]

    def finish(self):
        self.line.total(self.out)

    def groups(self):
        return dict(start=self.start(), fold=self.fold(), finish=[self.finish])

    def drain(self):
        return [lambda: sent(self.ox, self.ss.at[0], self.rs.at[0], self.me)] + self.line.drain()

    @staticmethod
    def semaphores(nz):
        return [DMA((1,)), DMA((nz,)), DMA((1,)), DMA((1,))]


def head_columns(width):
    row = lax.broadcasted_iota(jnp.int32, (128, width), 0) * HEAD_DIM
    column = lax.broadcasted_iota(jnp.int32, (128, width), 1)
    return ((column >= row) & (column < row + HEAD_DIM)).astype(F32)


def exact(left, right):
    return jnp.dot(left, right, preferred_element_type=F32, precision=HIGH)


def exact_t(left, right):
    return lax.dot_general(left, right, (((1,), (1,)), ((), ())), preferred_element_type=F32, precision=HIGH)


class Scatter:
    def __init__(self, me, src, out, bufs, ss, rs, ls, lss, lrs):
        self.me, self.src, self.out, self.ss, self.rs, self.ls = me, src, out, ss, rs, ls
        self.acc, self.cbuf, self.x1, self.y1, self.ox, self.oy, boxes = bufs
        self.cut = self.x1.shape[-1]
        self.line = Line(me, lambda z: self.acc.at[z, me.x, me.y], boxes, lss, lrs)

    def part(self, ref, half):
        width = self.acc.shape[-1]
        return ref.at[:, pl.ds(self.cut, width - self.cut)] if half else ref.at[:, pl.ds(0, self.cut)]

    def load(self, z):
        return pltpu.make_async_copy(self.src.at[pl.ds(2 * z, 2), :, self.me.c], self.acc.at[z], self.ls.at[z])

    def feed(self, stage, z):
        me = self.me
        send(stage.at[:, :, 1 - me.c], self.cbuf.at[z], self.ss.at[1 + z], self.rs.at[z], me.at(c=1 - me.c))
        for i in range(4):
            self.acc[z, i // 2, i % 2] = stage[i // 2, i % 2, me.c]

    def fed(self, z):
        sent(self.cbuf.at[z], self.ss.at[1 + z], self.rs.at[0], self.me)

    def begin(self):
        me = self.me

        def event(z):
            send(self.src.at[pl.ds(2 * z, 2), :, 1 - me.c], self.cbuf.at[z], self.ss.at[1 + z], self.rs.at[z], me.at(c=1 - me.c))
            self.load(z).start()
        return far_first(me, event)

    def core(self):
        me = self.me

        def event(z):
            if self.src is not None:
                self.load(z).wait()
            landed(self.cbuf.at[z], self.ss.at[0], self.rs.at[z], me)
            mine = self.acc.at[z]

            @pl.loop(0, 4)
            def _(i):
                x, y = i // 2, i % 2
                mine[x, y] = (mine[x, y].astype(F32) + self.cbuf[z, x, y].astype(F32)).astype(BF16)
            x_to, y_to = me.at(x=1 - me.x), me.at(y=1 - me.y)
            diag = mine.at[1 - me.x, 1 - me.y]
            send(self.part(diag, 0), self.x1.at[z], self.ss.at[0], self.rs.at[1 * me.nz + z], x_to)
            send(self.part(diag, 1), self.y1.at[z], self.ss.at[0], self.rs.at[2 * me.nz + z], y_to)
            send(self.part(mine.at[1 - me.x, me.y], 0), self.part(self.ox.at[z], 0), self.ss.at[0], self.rs.at[3 * me.nz + z], x_to)
            send(self.part(mine.at[me.x, 1 - me.y], 1), self.part(self.oy.at[z], 1), self.ss.at[0], self.rs.at[3 * me.nz + z], y_to)
        return far_first(me, event)

    def middle(self):
        me = self.me

        def event(z):
            landed(self.x1.at[z], self.ss.at[0], self.rs.at[me.nz + z], me)
            ref = self.part(self.acc.at[z, me.x, 1 - me.y], 0)
            ref[...] = add(ref, self.x1.at[z]).astype(BF16)
            send(ref, self.part(self.oy.at[z], 0), self.ss.at[0], self.rs.at[3 * me.nz + z], me.at(y=1 - me.y))
            landed(self.y1.at[z], self.ss.at[0], self.rs.at[2 * me.nz + z], me)
            ref = self.part(self.acc.at[z, 1 - me.x, me.y], 1)
            ref[...] = add(ref, self.y1.at[z]).astype(BF16)
            send(ref, self.part(self.ox.at[z], 1), self.ss.at[0], self.rs.at[3 * me.nz + z], me.at(x=1 - me.x))
        return far_first(me, event)

    def fold(self):
        me = self.me

        def event(z):
            landed(self.acc.at[z, 0], self.ss.at[0], self.rs.at[3 * me.nz + z], me)
            mine = self.acc.at[z, me.x, me.y]
            mine[...] = add(mine, self.ox.at[z], self.oy.at[z]).astype(BF16)
            self.line.event(z)
        return far_first(me, event)

    def finish(self):
        return [lambda: self.line.total(self.out)]

    def drain(self):
        me = self.me
        found = far_first(me, self.fed) if self.src is not None else []
        found.append(lambda: sent(self.acc.at[pl.ds(0, me.nz * 3 // 4)], self.ss.at[0], self.rs.at[0], me))
        return found + self.line.drain()

    def groups(self):
        begin = self.begin() if self.src is not None else []
        return dict(begin=begin, core=self.core(), middle=self.middle(), fold=self.fold(), finish=self.finish())

    @staticmethod
    def scratch(nz, rows, cols):
        buf = lambda *s: pltpu.VMEM(s + (rows, cols), BF16)
        cut = cols * 2 // 3 // 128 * 128
        return [buf(nz, 2, 2), buf(nz, 2, 2), pltpu.VMEM((nz, rows, cut), BF16), pltpu.VMEM((nz, rows, cols - cut), BF16), buf(nz), buf(nz), buf(nz),
                DMA((1 + nz,)), DMA((4 * nz,)), DMA((nz,)), DMA((1,)), DMA((1,))]


class SeqScatter:
    def __init__(self, me, src, then, acc, cbuf, oy, ss, rs, ls):
        self.me, self.src, self.then, self.acc, self.cbuf, self.oy = me, src, then, acc, cbuf, oy
        self.ss, self.rs = ss, rs
        self.load = pltpu.make_async_copy(src.at[:, :, me.c], acc, ls.at[0])

    def begin(self):
        me = self.me
        send(self.src.at[:, :, 1 - me.c], self.cbuf, self.ss.at[0], self.rs.at[0], me.at(c=1 - me.c))
        self.load.start()

    def core(self):
        me = self.me
        self.load.wait()
        landed(self.cbuf, self.ss.at[0], self.rs.at[0], me)

        @pl.loop(0, self.acc.shape[0])
        def _(i):
            for y in (0, 1):
                self.acc[i, y] = (self.acc[i, y].astype(F32) + self.cbuf[i, y].astype(F32)).astype(BF16)
        send(self.acc.at[:, 1 - me.y], self.oy, self.ss.at[1], self.rs.at[1], me.at(y=1 - me.y))

    def fold(self):
        me = self.me
        landed(self.oy, self.ss.at[0], self.rs.at[1], me)

        @pl.loop(0, self.acc.shape[0])
        def _(i):
            self.oy[i] = (self.acc[i, me.y].astype(F32) + self.oy[i].astype(F32)).astype(BF16)

    def finish(self):
        self.then(self.oy)

    def drain(self):
        sent(self.cbuf, self.ss.at[0], self.rs.at[0], self.me)
        sent(self.oy, self.ss.at[1], self.rs.at[0], self.me)

    def groups(self):
        return dict(begin=[self.begin], core=[self.core], fold=[self.fold], finish=[self.finish])

    @staticmethod
    def scratch(count, rows, cols):
        buf = lambda *s: pltpu.VMEM(s + (rows, cols), BF16)
        return [buf(count, 2), buf(count, 2), buf(count), DMA((2,)), DMA((2,)), DMA((1,))]


class Regrouped(SeqScatter):
    def __init__(self, me, dp_count, src, out, inbox, up_ss, up_rs, *rest):
        super().__init__(me, src, self.pass_on, *rest)
        self.n, self.out, self.inbox, self.up_ss, self.up_rs = dp_count, out, inbox, up_ss, up_rs

    def pass_on(self, total):
        me = self.me
        for k in range(1, self.n):
            to = lax.rem(me.dp + k, self.n)
            send(total.at[to], self.inbox.at[me.dp], self.up_ss.at[to], self.up_rs.at[me.dp], (to, me.seq))
        self.inbox[me.dp] = total[me.dp]

    def collect(self):
        cols = self.inbox.shape[2]
        for dp in range(self.n):
            pl.when(dp != self.me.dp)(lambda: landed(self.inbox.at[dp], self.up_ss.at[0], self.up_rs.at[dp], self.me))
            self.out[:, dp * cols:(dp + 1) * cols] = self.inbox[dp].astype(F32)

    def drain(self):
        super().drain()
        for k in range(1, self.n):
            sent(self.inbox.at[0], self.up_ss.at[lax.rem(self.me.dp + k, self.n)], self.up_rs.at[0], self.me)

    @staticmethod
    def scratch(count, rows, cols):
        return [pltpu.VMEM((count, rows, cols), BF16), DMA((count,)), DMA((count,))] + SeqScatter.scratch(count, rows, cols)


class SumAll:
    def __init__(self, me, ref, inbox, ss, rs):
        self.me, self.ref, self.inbox, self.ss, self.rs = me, ref, inbox, ss, rs

    def step(self, i, to):
        def begin():
            send(self.ref.at[i], self.inbox.at[i], self.ss.at[i], self.rs.at[i], to)

        def end():
            landed(self.inbox.at[i], self.ss.at[0], self.rs.at[i], self.me)
            self.ref[i + 1] = self.ref[i] + self.inbox[i]
        return begin, end

    def phases(self):
        me = self.me
        n = me.nz

        def begin_z():
            for k in range(1, n):
                to = lax.rem(me.z + k, n)
                send(self.ref.at[3], self.inbox.at[2 + k], self.ss.at[2 + k], self.rs.at[2 + k], me.at(z=to))

        def end_z():
            total = self.ref[3]
            for k in range(1, n):
                landed(self.inbox.at[2 + k], self.ss.at[0], self.rs.at[2 + k], me)
                total = total + self.inbox[2 + k]
            self.ref[4] = total

        def drain():
            for i in range(2 + n):
                sent(self.ref.at[0], self.ss.at[i], self.rs.at[0], me)
        first = self.step(0, me.at(c=1 - me.c))
        second = self.step(1, me.at(x=1 - me.x))
        third = self.step(2, me.at(y=1 - me.y))
        both = lambda one, other: (lambda: (one(), other()))
        return [[e] for e in (first[0], both(first[1], second[0]), both(second[1], third[0]), both(third[1], begin_z), end_z, drain)]


CUT, LATE_CUT = 640, 384


def laid_out(order, groups, steps):
    places, count = {}, 0
    for name, number in steps.items():
        places[name] = (count, number)
        count += number
    ahead = [[] for _ in range(count)]
    placed = [(position, name, phase) for name, phases in order.items() for phase, position in phases.items()]
    for position, name, phase in sorted(placed):
        ahead[min(count - 1, max(0, math.ceil(position)))] += groups[name][phase]
    return lambda name: ahead[places[name][0]:places[name][0] + places[name][1]]


def unpacked(packs, own_cols):
    count = packs.shape[0]
    group = 8
    rows = []
    for g in range(count // group):
        left = jnp.concatenate([packs[g * group + i] for i in range(group)], axis=1).astype(BF16)
        row = lax.broadcasted_iota(jnp.int32, (group * 128, group * own_cols), 0)
        column = lax.broadcasted_iota(jnp.int32, (group * 128, group * own_cols), 1)
        piece, place = row // 128, row % 128
        chosen = (place < own_cols) & (column == piece * own_cols + place)
        rows.append(dot(left, jnp.where(chosen, 1.0, 0.0).astype(BF16)))
    return jnp.concatenate(rows, axis=1)


def forward_kernel(dp_count, block_rows, own_cols, owner, media, pack, lat, sq, sk, sv, so, sg, sd, su,
                   wq, wk, wv, n_out, nl_out, q_out, k_out, v_out, gwo, gwu, gwd,
                   gains, lat_out, grad_hidden, do_all, stat_all, sums,
                   packs, lat_all, wo, og, dn, up, med, n, nl, q, k, v, expo, acc_f, acc, tops, stats, packed, wbuf,
                   acc_in, stat_in, nf_all, ga, act, gp, part_g, ox_g, zz_g, part_y, ox_y, zz_y,
                   own_sum, row_a, row_b, do_in, st_in, gwo_v, gwu_v, gwd_v,
                   local, ws, ms, outs, xs, xr, *sems):
    me = Here(dp_count)
    (rss, rrs, es, er), g_sems, y_sems, sems = sems[:4], sems[4:8], sems[8:12], sems[12:]
    nf_sems, do_sems, st_sems = sems[14:16], sems[16:18], sems[18:20]
    seq_count, lat_rows, width = lat_all.shape
    half = width // 2
    seq_peers = [lax.rem(me.seq + i, seq_count) for i in range(1, seq_count)]
    blocks, parts = n.shape[0] // block_rows, HEADS // PART
    media_rows = media.shape[0]
    greet_all(me, dp_count)
    gather = lambda i, src, dst, axes, halves: Gather(me, src, dst, *sems[2 * i:2 * i + 2], axes, halves)
    regroup = Regroup(me, dp_count, su, up, rss, rrs, up.shape[2])
    items = [
        Everyone(me, dp_count, pack, packs, es, er), gather(0, lat, lat_all, "yc", 0),
        gather(1, sk, wk, "zxyc", CUT), gather(2, sq, wq, "zxyc", CUT), gather(3, sv, wv, "zxyc", CUT),
        gather(4, so, wo, "zxyc", LATE_CUT), gather(5, sg, og, "zx", 0), gather(6, sd, dn, "yc", 0), regroup,
    ]
    own = [(pack, packs.at[items[0].index])]
    own += [(src, item.shard(me.z, me.x, me.y, me.c)) for src, item in zip((lat, sk, sq, sv, so, sg, sd), items[1:8])]
    own += [(regroup.columns(me.dp), regroup.piece(me.dp, me.y, me.c))]
    own = [pltpu.make_async_copy(src, dst, local.at[i]) for i, (src, dst) in enumerate(own)]
    for copy in own:
        copy.start()
    spread_nf = Gather(me, nf_all.at[me.dp], nf_all, *nf_sems, "zx", 0)
    sum_g = DpScatter(me, part_g, own_sum, ox_g, zz_g, *g_sems)
    sum_y = DpScatter(me, part_y, own_sum, ox_y, zz_y, *y_sems)
    spread_do = Gather(me, do_in.at[me.seq], do_in, *do_sems, "yc", 0)
    spread_st = Gather(me, st_in.at[me.seq], st_in, *st_sems, "yc", 0)

    lane = lax.broadcasted_iota(jnp.int32, (lat_rows, 128), 1)

    def beside(one, other):
        return jnp.where(lane < HEADS, one, pltpu.roll(other, HEADS, 1))

    def exchange(part):
        cols = pl.ds(part * half, half)
        for i, to in enumerate(seq_peers):
            send(acc.at[to, :, cols], acc_in.at[me.seq, :, cols], xs.at[part, i], xr.at[part, me.seq], (me.dp, to))
            if part == 0:
                send(packed.at[to], stat_in.at[me.seq], xs.at[2, i], xr.at[2, me.seq], (me.dp, to))

    def exchanged():
        for source in seq_peers:
            landed(stat_in.at[source], xs.at[0, 0], xr.at[2, source], me)
            for part in range(2):
                landed(acc_in.at[source, :, pl.ds(part * half, half)], xs.at[0, 0], xr.at[part, source], me)
    column = spread_nf.column()
    way = 1 - 2 * (me.z // (me.nz // 2))

    def layer(k):
        return lax.rem(me.z + way * k + me.nz, me.nz)

    def arrived(z):
        spread_nf.here(spread_nf.shard(z, 1 - me.x, me.y, me.c), FROMX, z)

    def steps_of(first, second):
        return {**{"a%d" % k: first(k) for k in range(me.nz)}, **{"b%d" % k: second(k) for k in range(me.nz)}}
    groups = dict(
        pack=dict(own=items[0].own(), arrive=items[0].arrive()),
        x=dict(send0=[lambda: exchange(0)], send1=[lambda: exchange(1)], wait=[exchanged]),
        up=dict(own=[regroup.own], column=[regroup.column], neighbours=[regroup.neighbours], sibling=[regroup.sibling]),
        g=dict(**steps_of(lambda k: [lambda: sum_g.send_x(layer(k))], lambda k: [lambda: sum_g.fold_in(layer(k))]), finish=[sum_g.finish]),
        nf=dict(own=spread_nf.own(), **steps_of(lambda k: column[2 * k - 2:2 * k], lambda k: [lambda: arrived(layer(k))])),
        y=sum_y.groups(), do=spread_do.groups(), st=spread_st.groups(),
        **dict(zip(("lat", "k", "q", "v", "o", "og", "dn"), [item.groups() for item in items[1:8]])))
    steps = blocks * parts // 2
    ahead_of = laid_out(FORWARD_ORDER, groups, dict(
        gains=1, norm=blocks - 1, latnorm=1, kproj=2, qproj=2, tops=steps, best=1, expo=steps, sums=1,
        vproj0=1, acc0=steps // 2, cast0=1, vproj1=1, acc1=steps // 2, cast1=1, fold=1, hidden=1, ga=2, ffn=me.nz, ypart=me.nz, gwd=1,
        grad=1, gwo=2, gwu=1, latout=1, end=1))

    def ahead(name):
        run(ahead_of(name)[0])

    def media_load(b):
        rows = pl.ds(pl.multiple_of(b * block_rows, block_rows), block_rows)
        slot = lax.rem(b, 2)
        return pltpu.make_async_copy(media.at[rows, :], med.at[slot], ms.at[slot])
    media_load(0).start()
    ahead("gains")
    for copy in own:
        copy.wait()
    gains[...] = unpacked(packs, own_cols)

    norm_events = ahead_of("norm")

    @pl.loop(0, blocks - 1)
    def _(b):
        run_at(b, norm_events)
        pl.when(b + 1 < blocks - 1)(lambda: media_load(b + 1).start())
        media_load(b).wait()
        u, _ = scaled_rows(med[lax.rem(b, 2)].astype(F32))
        n[pl.ds(pl.multiple_of(b * block_rows, block_rows), block_rows), :] = (u * gains[2:3, :] + gains[3:4, :]).astype(BF16)
    ahead("latnorm")
    u, _ = scaled_rows(lat_all[...].reshape(seq_count * lat_rows, width).astype(F32))
    nl[...] = (u * gains[0:1, :] + gains[1:2, :]).astype(BF16).reshape(nl.shape)
    n[pl.ds(media_rows, lat_rows), :] = nl[me.seq]
    n[pl.ds(media_rows + lat_rows, block_rows - lat_rows), :] = jnp.zeros((block_rows - lat_rows, width), BF16)

    def weight(w, i):
        return pltpu.make_async_copy(w.at[:, :, pl.ds(pl.multiple_of(i * half, 128), half)], wbuf.at[i], ws.at[i])

    def project(rows, w, out, name):
        events = ahead_of(name)
        run(events[0])
        for i in range(2):
            weight(w, i).start()

        @pl.loop(0, 2)
        def _(i):
            run_at(i, [[], events[1]])
            weight(w, i).wait()
            cols = pl.ds(pl.multiple_of(i * half, 128), half)
            out[:, cols] = dot(rows[...], wbuf[i].reshape(width, half)).astype(BF16)
    project(n, wk, k, "kproj")
    project(nl.reshape(seq_count * lat_rows, width), wq, q.reshape(seq_count * lat_rows, width), "qproj")
    mask = part_mask(lat_rows)
    key = lax.broadcasted_iota(jnp.int32, (PART * lat_rows, block_rows), 1)

    def scores(b, part, item):
        cols = pl.ds(pl.multiple_of(part * PCOLS, 128), PCOLS)
        at = pl.ds(pl.multiple_of(b * block_rows, block_rows), block_rows)
        found = dot_t(stacked(q[item, :, cols], mask), k[at, cols]) * SCALE
        return jnp.where(key < jnp.where(b == blocks - 1, lat_rows, block_rows), found, NEG)

    def replicated(stat, part):
        pieces = []
        for h in range(PART):
            column = jnp.sum(jnp.where(lane == part * PART + h, stat, 0.0), axis=-1, keepdims=True)
            pieces.append(jnp.broadcast_to(column, (lat_rows, 128)))
        return jnp.concatenate(pieces, axis=0)

    def place(stat, column, part):
        for h in range(PART):
            stat = jnp.where(lane == part * PART + h, column[h * lat_rows:(h + 1) * lat_rows], stat)
        return stat
    tops[...] = jnp.zeros_like(tops)
    top_events = ahead_of("tops")

    @pl.loop(0, steps)
    def _(i):
        b, pair = i // (parts // 2), i % (parts // 2)
        run_at(i, top_events)
        item = owner[b]
        for part in (pair * 2, pair * 2 + 1):
            tops[b, 0] = place(tops[b, 0], jnp.max(scores(b, part, item), axis=-1, keepdims=True), part)
    ahead("best")
    for i in range(seq_count):
        best = jnp.full((lat_rows, 128), NEG, F32)
        for b in range(blocks):
            best = jnp.maximum(best, jnp.where(owner[b] == i, tops[b, 0], NEG))
        stats[i, 0] = best
    expo_events = ahead_of("expo")

    @pl.loop(0, steps)
    def _(i):
        b, pair = i // (parts // 2), i % (parts // 2)
        run_at(i, expo_events)
        item = owner[b]
        for part in (pair * 2, pair * 2 + 1):
            e = jnp.exp(scores(b, part, item) - replicated(stats[item, 0], part))
            expo[b, part] = e.astype(BF16)
            tops[b, 1] = place(tops[b, 1], jnp.sum(e, axis=-1, keepdims=True), part)
    ahead("sums")
    for i in range(seq_count):
        packed[i] = beside(stats[i, 0], sum(jnp.where(owner[b] == i, tops[b, 1], 0.0) for b in range(blocks)))
    stat_in[me.seq] = packed[me.seq]
    acc_f[...] = jnp.zeros_like(acc_f)
    for part in range(2):
        ahead("vproj%d" % part)
        if part == 0:
            for i in range(2):
                weight(wv, i).start()
        weight(wv, part).wait()
        cols = pl.ds(part * half, half)
        v[:, cols] = dot(n[...], wbuf[part].reshape(width, half)).astype(BF16)
        acc_events = ahead_of("acc%d" % part)

        @pl.loop(0, steps // 2)
        def _(b):
            run_at(b, acc_events)
            item = owner[b]
            for head_part in range(part * parts // 2, (part + 1) * parts // 2):
                pcols = pl.ds(head_part * PCOLS, PCOLS)
                at = pl.ds(pl.multiple_of(b * block_rows, block_rows), block_rows)
                term = unstacked(dot(expo[b, head_part], v[at, pcols]), mask, lat_rows)
                for j in range(seq_count):
                    acc_f[j, :, pcols] += jnp.where(item == j, term, 0.0)
        ahead("cast%d" % part)
        acc[:, :, cols] = acc_f[:, :, cols].astype(BF16)
        acc_in[me.seq, :, cols] = acc[me.seq, :, cols]
    saves = [(n, n_out), (nl, nl_out), (q, q_out), (k, k_out), (v, v_out)]
    saves = [pltpu.make_async_copy(src, dst, outs.at[i]) for i, (src, dst) in enumerate(saves)]
    for copy in saves:
        copy.start()
    ahead("fold")
    tops_in = [stat_in[s] for s in range(seq_count)]
    best = functools.reduce(jnp.maximum, tops_in)
    weights = [jnp.exp(top - best) for top in tops_in]
    total = sum(w * pltpu.roll(top, 128 - HEADS, 1) for w, top in zip(weights, tops_in))
    total = jnp.where(lane < HEADS, total, 1.0)
    spread = head_columns(width)
    attended = sum(exact(w / total, spread) * acc_in[s].astype(F32) for s, w in enumerate(weights))
    row_a[...] = attended
    lse = best + jnp.log(total)
    ahead("hidden")
    hidden = lat_all[me.seq].astype(F32) + dot(attended.astype(BF16), wo[...].reshape(width, width))
    row_b[...] = hidden
    scaled, _ = scaled_rows(hidden)
    nf_all[me.dp] = (scaled * gains[4:5, :] + gains[5:6, :]).astype(BF16)
    all_rows = dp_count * lat_rows
    hidden_cols = gp.shape[1]
    og_all = lambda: og[...].reshape(all_rows, width)
    tile = hidden_cols // 2
    per = seq_count // 2
    ga_events = ahead_of("ga")

    @pl.loop(0, 2)
    def _(t):
        run_at(t, ga_events)
        at = pl.ds(pl.multiple_of(t * tile, 128), tile)
        ga[:, at] = dot_t(og_all(), dn[pl.ds(t * per, per)].reshape(tile, width))
    ffn_events = ahead_of("ffn")
    pair_rows = 2 * lat_rows

    def pair(z):
        return pl.ds(2 * z, 2), pl.ds(pl.multiple_of(z * pair_rows, pair_rows), pair_rows)

    @pl.loop(0, me.nz)
    def _(k):
        run_at(k, ffn_events)
        both, at = pair(layer(k))
        pre = dot(nf_all[both].reshape(pair_rows, width), up[...].reshape(width, hidden_cols))
        phi = 0.5 * (1.0 + lax.erf(pre * 0.7071067811865476))
        act[at, :] = (pre * phi).astype(BF16)
        slope = phi + pre * jnp.exp(pre * pre * -0.5) * 0.3989422804014327
        gp[at, :] = (ga[at, :] * slope).astype(BF16)
        part_g[both] = dot_t(gp[at, :], up[...].reshape(width, hidden_cols)).astype(BF16).reshape(2, lat_rows, width)
    y_events = ahead_of("ypart")

    @pl.loop(0, me.nz)
    def _(k):
        run_at(k, y_events)
        both, at = pair(layer(k))
        part_y[both] = dot(act[at, :], dn[...].reshape(hidden_cols, width)).astype(BF16).reshape(2, lat_rows, width)
    ahead("gwd")
    gwd_v[...] = t_dot(act[...], og_all()).astype(BF16)
    save_d = pltpu.make_async_copy(gwd_v, gwd, outs.at[5])
    save_d.start()
    ahead("grad")
    gathered = own_sum[...]
    scaled, inverse = scaled_rows(row_b[...])
    sums[...] = jnp.zeros_like(sums)
    sums[0:1, :] = jnp.sum(gathered * scaled, axis=0, keepdims=True)
    sums[1:2, :] = jnp.sum(gathered, axis=0, keepdims=True)
    grad = og[me.dp].astype(F32) + norm_back(gathered, scaled, inverse, gains[4:5, :])
    grad_hidden[...] = grad
    low = grad.astype(BF16)
    grad_att = dot_t(low, wo[...].reshape(width, width)).astype(BF16)
    do_in[me.seq] = grad_att
    st_in[me.seq] = beside(lse, exact_t(grad_att.astype(F32) * row_a[...], spread))
    save_o = []
    for i in range(2):
        cols = pl.ds(i * half, half)
        run(ahead_of("gwo")[i])
        if i:
            save_o[0].wait()
        gwo_v[...] = t_dot(row_a[...].astype(BF16), low[:, i * half:(i + 1) * half]).astype(BF16)
        save_o.append(pltpu.make_async_copy(gwo_v, gwo.at[:, cols], outs.at[6 + i]))
        save_o[-1].start()
    ahead("gwu")
    gwu_v[...] = t_dot(nf_all[...].reshape(all_rows, width), gp[...]).astype(BF16)
    save_u = pltpu.make_async_copy(gwu_v, gwu, outs.at[8])
    save_u.start()
    ahead("latout")
    lat_out[...] = (row_b[...] + own_sum[...]).astype(BF16)
    ahead("end")
    do_all[...] = do_in[...]
    stat_all[...] = st_in[...]
    for i in range(len(seq_peers)):
        for part in range(2):
            sent(acc_in.at[0, :, pl.ds(part * half, half)], xs.at[part, i], xr.at[0, 0], me)
        sent(stat_in.at[0], xs.at[2, i], xr.at[0, 0], me)
    for item in items[:8]:
        run(item.drain())
    regroup.drain()
    for item in (spread_nf, sum_g, sum_y, spread_do, spread_st):
        run(item.drain())
    for copy in saves + save_o[1:] + [save_d, save_u]:
        copy.wait()


def forward(dp_count, owner, media, pack, lat, sq, sk, sv, so, sg, sd, su, block_rows, own_cols):
    nz = dp_count // 2
    rows, width = lat.shape
    items, count = 4, dp_count * 4
    hidden = su.shape[1] // dp_count
    total = media.shape[0] + block_rows
    blocks = total // block_rows
    parts = HEADS // PART
    all_rows = dp_count * rows
    shape = jax.ShapeDtypeStruct
    buf = lambda *s: pltpu.VMEM(s, BF16)
    flt = lambda *s: pltpu.VMEM(s, F32)
    square = shape((count, width // count, width), BF16)
    stat = (items, rows, 128)
    line = [buf(nz, rows, width), buf(nz, rows, width)]
    return pl.pallas_call(
        functools.partial(forward_kernel, dp_count, block_rows, own_cols),
        out_shape=(
            square, square, square, shape((total, width), BF16), shape((items, rows, width), BF16), shape((items, rows, width), BF16),
            shape((total, width), BF16), shape((total, width), BF16),
            shape((width, width), BF16), shape((width, hidden), BF16), shape((hidden, width), BF16),
            shape((8, width), F32), shape((rows, width), BF16), shape((rows, width), F32),
            shape((items, rows, width), BF16), shape(stat, F32), shape((8, width), F32),
        ),
        in_specs=[pl.BlockSpec(memory_space=pltpu.SMEM)] + [ANY] * 10,
        out_specs=tuple([ANY] * 11 + [VMEM] * 6),
        scratch_shapes=[
            flt(count, 8, 128), buf(items, rows, width), buf(count, width // count, width), buf(dp_count, rows, width),
            buf(items, hidden // items, width), buf(count, width // count, hidden), buf(2, block_rows, width),
            buf(total, width), buf(items, rows, width), buf(items, rows, width), buf(total, width), buf(total, width),
            buf(blocks, parts, PART * rows, block_rows), flt(items, rows, width), buf(items, rows, width),
            flt(blocks, 2, rows, 128), flt(items, 1, rows, 128), flt(*stat), buf(2, count, width // count, width // 2),
            buf(items, rows, width), flt(*stat), buf(dp_count, rows, width), flt(all_rows, hidden), buf(all_rows, hidden), buf(all_rows, hidden),
            buf(dp_count, rows, width), *line, buf(dp_count, rows, width), *line,
            flt(rows, width), flt(rows, width), flt(rows, width), buf(items, rows, width), flt(*stat),
            buf(width, width // 2), buf(width, hidden), buf(hidden, width),
            DMA((9,)), DMA((2,)), DMA((2,)), DMA((9,)), DMA((3, items)), DMA((3, items)),
            *Regroup.semaphores(dp_count), DMA((1,)), DMA((1,)), *DpScatter.semaphores(nz), *DpScatter.semaphores(nz),
            *[sem for axes in ("yc", "zxyc", "zxyc", "zxyc", "zxyc", "zx", "yc", "zx", "yc", "yc") for sem in Gather.semaphores(axes, nz)],
        ],
        compiler_params=pltpu.CompilerParams(collective_id=1, has_side_effects=True, vmem_limit_bytes=WIDE),
    )(owner, media, pack, lat, sq, sk, sv, so, sg, sd, su)


def backward_kernel(dp_count, block_rows, owner, lat, grad_hidden, gains, sums_ffn,
                    n_in, nl_in, q_in, k_in, v_in, do_in, stat_in, gwo, gwu, gwd, media, wq, wk, wv,
                    media_grad, lat_grad, sums, out_q, out_k, out_v, out_o, out_up, out_dn,
                    n, nl, q, do, k, v, stats, dq, g, gq, med, stage, sums_ref, *scratch):
    me = Here(dp_count)
    items, lat_rows, width = q.shape
    rows = k.shape[0]
    media_rows = media.shape[0]
    blocks, parts = rows // block_rows, HEADS // PART
    scratch = list(scratch)
    take = lambda count: [scratch.pop(0) for _ in range(count)]
    o_s, fulls, up_s, dn_s, lat_s, small = take(12), [take(12) for _ in range(3)], take(9), take(6), take(6), take(4)
    in_sem, tile_sem, med_sem, out_sem = scratch
    loads = [(stat_in, stats), (q_in, q), (do_in, do), (k_in, k), (v_in, v), (n_in, n), (nl_in, nl)]
    loads = [pltpu.make_async_copy(src, dst, in_sem.at[i]) for i, (src, dst) in enumerate(loads)]
    for load in loads:
        load.start()
    all_sum = SumAll(me, *small)

    def latents(total):
        scaled, inverse = scaled_rows(lat[...].astype(F32))
        grad = total[0].astype(F32)
        lat_grad[...] = grad_hidden[...] + norm_back(grad, scaled, inverse, gains[0:1, :])
        first = small[0]
        first[0, 0:1, :] = jnp.sum(grad * scaled, axis=0, keepdims=True)
        first[0, 1:2, :] = jnp.sum(grad, axis=0, keepdims=True)
        first[0, 2:4, :] = sums_ref[0:2, :]
        first[0, 4:6, :] = sums_ffn[0:2, :]
        first[0, 6:8, :] = jnp.zeros_like(sums_ffn[0:2, :])

    def down(total):
        out_dn[...] = total[0].astype(F32)
    f_o = Scatter(me, gwo, out_o, o_s[:7], *o_s[7:])
    f_k, f_v, f_q = [Scatter(me, None, out, f[:7], *f[7:]) for out, f in zip((out_k, out_v, out_q), fulls)]
    up, dn = Regrouped(me, dp_count, gwu, out_up, *up_s), SeqScatter(me, gwd, down, *dn_s)
    lat_item = SeqScatter(me, gq, latents, *lat_s)
    greet(dp_peers(me, dp_count) + [me.at(y=1 - me.y), me.at(c=1 - me.c)])
    mask = part_mask(lat_rows)
    lane = lax.broadcasted_iota(jnp.int32, (lat_rows, 128), 1)
    key = lax.broadcasted_iota(jnp.int32, (PART * lat_rows, block_rows), 1)
    held = pl.ds(0, items * lat_rows)
    g[held, :] = jnp.zeros((items * lat_rows, width), F32)

    def replicated(stat, part, base=0):
        pieces = []
        for h in range(PART):
            column = jnp.sum(jnp.where(lane == base + part * PART + h, stat, 0.0), axis=-1, keepdims=True)
            pieces.append(jnp.broadcast_to(column, (lat_rows, 128)))
        return jnp.concatenate(pieces, axis=0)

    def block(b, part, item):
        cols = pl.ds(pl.multiple_of(part * PCOLS, 128), PCOLS)
        at = pl.ds(pl.multiple_of(b * block_rows, block_rows), block_rows)
        query, grad = stacked(q[item, :, cols], mask), stacked(do[item, :, cols], mask)
        keys, values = k[at, cols], v[at, cols]
        lse, delta = replicated(stats[item], part), replicated(stats[item], part, HEADS)
        prob = jnp.exp(dot_t(query, keys) * SCALE - lse)
        prob = jnp.where(key < jnp.where(b == blocks - 1, lat_rows, block_rows), prob, 0.0)
        score = (prob * (dot_t(grad, values) - delta)).astype(BF16)
        term = unstacked(dot(score, keys), mask, lat_rows) * SCALE
        k[at, cols] = (t_dot(score, query) * SCALE).astype(BF16)
        v[at, cols] = t_dot(prob.astype(BF16), grad).astype(BF16)
        for i in range(items):
            g[i * lat_rows:(i + 1) * lat_rows, cols] += jnp.where(item == i, term, 0.0)
    steps = blocks * parts // 2
    span = rows // 2
    turns = (span, 0)
    tile = items * lat_rows
    tiles = width // tile
    norms = [(min(media_rows, start + span) - start) // lat_rows for start in turns]
    groups = dict(
        o=f_o.groups(), k=f_k.groups(), v=f_v.groups(), q=f_q.groups(), lat=lat_item.groups(), dn=dn.groups(),
        up=dict(collect=[up.collect], **up.groups()), sum=dict(zip(("s0", "s1", "s2", "s3", "s4"), all_sum.phases())))
    ahead_of = laid_out(BACK_ORDER, groups, dict(
        attention=steps, dq=1, gwk=me.nz, gwv=me.nz, gwq=me.nz, tiles0=tiles, norms0=norms[0], tiles1=tiles, norms1=norms[1], end=1))
    for load in loads[:5]:
        load.wait()

    shares = ahead_of("attention")

    @pl.loop(0, steps)
    def _(i):
        b, pair = i // (parts // 2), i % (parts // 2)
        run_at(i, shares)
        item = owner[b]
        block(b, pair * 2, item)
        block(b, pair * 2 + 1, item)
    run(ahead_of("dq")[0])
    dq[...] = g[held, :].astype(BF16)
    for load in loads[5:]:
        load.wait()
    layer = width // me.nz

    def produce(full, left, right, name):
        shares = ahead_of(name)

        @pl.loop(0, me.nz)
        def _(t):
            run_at(t, shares)
            slot = lax.rem(t, 2)
            z = lax.rem(me.z + 1 + t, me.nz)
            pl.when(t >= 2)(lambda: full.fed(lax.rem(me.z + t - 1, me.nz)))
            cols = pl.ds(pl.multiple_of(z * layer, 128), layer)
            found = t_dot(left(cols), right()).astype(BF16)
            stage[slot] = found.reshape(stage.shape[1:])
            full.feed(stage.at[slot], z)
        full.fed(lax.rem(me.z + me.nz - 1, me.nz))
        full.fed(me.z)
    n_cols = lambda cols: n[:, :, cols].reshape(rows, layer)
    produce(f_k, n_cols, lambda: k[...], "gwk")
    produce(f_v, n_cols, lambda: v[...], "gwv")
    produce(f_q, lambda cols: nl[:, :, cols].reshape(items * lat_rows, layer), lambda: dq[...], "gwq")
    per = items
    slots = ((n.at[pl.ds(0, per)], n.at[pl.ds(per, per)], n.at[pl.ds(2 * per, per)]), (q, nl, do))

    def fetch(t, slot):
        return [pltpu.make_async_copy(w.at[pl.ds(t * per, per)], dst, tile_sem.at[slot, i]) for i, (w, dst) in enumerate(zip((wk, wv, wq), slots[slot]))]

    def media_load(i, start):
        at = pl.ds(pl.multiple_of(start + i * lat_rows, lat_rows), lat_rows)
        slot = lax.rem(i, 2)
        return pltpu.make_async_copy(media.at[at, :], med.at[slot], med_sem.at[slot])
    sums_ref[...] = jnp.zeros_like(sums_ref)
    for turn, start in enumerate(turns):
        shares = ahead_of("tiles%d" % turn)
        for copy in fetch(0, 0) + fetch(1, 1):
            copy.start()

        @pl.loop(0, tiles // 2)
        def _(pair):
            for slot in (0, 1):
                t = pair * 2 + slot
                run_at(t, shares)
                for copy in fetch(t, slot):
                    copy.wait()
                at = pl.ds(pl.multiple_of(t * tile, 128), tile)
                w_k, w_v, w_q = [ref[...].reshape(tile, width) for ref in slots[slot]]
                grad = dot_t(k[pl.ds(start, span), :], w_k) + dot_t(v[pl.ds(start, span), :], w_v)
                g[:, at] = grad
                if turn == 0:
                    own = dot_t(dq[...], w_q)
                    extra = grad[media_rows - start:media_rows - start + lat_rows]
                    for i in range(items):
                        term = own[i * lat_rows:(i + 1) * lat_rows]
                        gq[0, i // 2, i % 2, :, at] = jnp.where(me.seq == i, term + extra, term).astype(BF16)

                @pl.when(t + 2 < tiles)
                def _():
                    for copy in fetch(t + 2, slot):
                        copy.start()
        count = norms[turn]
        norm_shares = ahead_of("norms%d" % turn)
        media_load(0, start).start()

        def out_copy(first, length):
            at = pl.ds(pl.multiple_of(start + first, lat_rows), length)
            return pltpu.make_async_copy(g.at[pl.ds(pl.multiple_of(first, lat_rows), length), :], media_grad.at[at, :], out_sem)

        @pl.loop(0, count)
        def _(i):
            run_at(i, norm_shares)
            pl.when(i + 1 < count)(lambda: media_load(i + 1, start).start())
            media_load(i, start).wait()
            at = pl.ds(pl.multiple_of(i * lat_rows, lat_rows), lat_rows)
            u, inverse = scaled_rows(med[lax.rem(i, 2)].astype(F32))
            grad = g[at, :]
            g[at, :] = norm_back(grad, u, inverse, gains[2:3, :])
            out_copy(i * lat_rows, lat_rows).start()
            sums_ref[0:1, :] += jnp.sum(grad * u, axis=0, keepdims=True)
            sums_ref[1:2, :] += jnp.sum(grad, axis=0, keepdims=True)
        out_copy(0, count * lat_rows).wait()
    run(ahead_of("end")[0])
    sums[...] = small[0][4]
    for item in (f_o, f_k, f_v, f_q):
        run(item.drain())
    for item in (up, dn, lat_item):
        item.drain()
    run(all_sum.phases()[-1])


def backward(dp_count, owner, lat, grad_hidden, gains, sums_ffn, n, nl, q, k, v, do_all, stats, gwo, gwu, gwd, media, wq, wk, wv, block_rows):
    nz = dp_count // 2
    items, lat_rows, width = q.shape
    rows = n.shape[0]
    hidden = gwu.shape[1]
    count = dp_count * 4
    shape = jax.ShapeDtypeStruct
    buf = lambda *s: pltpu.VMEM(s, BF16)
    flt = lambda *s: pltpu.VMEM(s, F32)
    pieces = lambda w: w.reshape(width // lat_rows, lat_rows, width)
    arrays = (owner, lat, grad_hidden, gains, sums_ffn, n.reshape(rows // lat_rows, lat_rows, width), nl, q, k, v, do_all, stats,
              gwo.reshape(dp_count, 2, 2, width // count, width),
              gwu.reshape(dp_count, 2, 2, width // count, hidden), gwd.reshape(1, 2, 2, hidden // 4, width),
              media, pieces(wq), pieces(wk), pieces(wv))
    return pl.pallas_call(
        functools.partial(backward_kernel, dp_count, block_rows),
        out_shape=(
            shape(media.shape, F32), shape((lat_rows, width), F32), shape((8, width), F32), *[shape((width // count, width), F32)] * 4,
            shape((width // count, hidden * dp_count), F32), shape((hidden // 4, width), F32),
        ),
        in_specs=[pl.BlockSpec(memory_space=pltpu.SMEM)] + [VMEM] * 4 + [ANY] * 14,
        out_specs=tuple([ANY] + [VMEM] * 8),
        scratch_shapes=[
            buf(rows // lat_rows, lat_rows, width), buf(items, lat_rows, width), buf(items, lat_rows, width), buf(items, lat_rows, width),
            buf(rows, width), buf(rows, width), flt(*stats.shape), buf(items * lat_rows, width), flt(rows // 2, width),
            buf(1, 2, 2, lat_rows, width), buf(2, lat_rows, width), buf(2, 2, 2, 2, width // count, width), flt(8, width),
            *Scatter.scratch(nz, width // count, width), *(Scatter.scratch(nz, width // count, width) * 3), *Regrouped.scratch(dp_count, width // count, hidden),
            *SeqScatter.scratch(1, hidden // 4, width), *SeqScatter.scratch(1, lat_rows, width),
            flt(5, 8, width), flt(2 + nz, 8, width), DMA((2 + nz,)), DMA((2 + nz,)),
            DMA((7,)), DMA((2, 3)), DMA((2,)), DMA,
        ],
        compiler_params=pltpu.CompilerParams(collective_id=2, has_side_effects=True, vmem_limit_bytes=WIDE),
    )(*arrays)


def copy_kernel(*refs):
    n = (len(refs) - 2) // 3
    arrays, outs, held, first, second = refs[:n], refs[n:2 * n], refs[2 * n:3 * n], refs[-2], refs[-1]
    ins = [pltpu.make_async_copy(arrays[i], held[i], first.at[i]) for i in range(n)]
    backs = [pltpu.make_async_copy(held[i], outs[i], second.at[i]) for i in range(n)]
    for copy in ins:
        copy.start()
    for copy, after in zip(ins, backs):
        copy.wait()
        after.start()
    for copy in backs:
        copy.wait()


def copied(*arrays):
    n = len(arrays)
    return pl.pallas_call(
        copy_kernel, out_shape=tuple(jax.ShapeDtypeStruct(a.shape, a.dtype) for a in arrays),
        in_specs=[ANY] * n, out_specs=tuple([ANY] * n),
        scratch_shapes=[*[pltpu.VMEM(a.shape, a.dtype) for a in arrays], DMA((n,)), DMA((n,))],
        compiler_params=pltpu.CompilerParams(vmem_limit_bytes=WIDE),
    )(*arrays)


def local_fast(
    media, latents, out_grad, frame_counts, block_position, w_query, w_key, w_value, w_out, w_up, w_down,
    gain_lat, shift_lat, gain_media, shift_media, gain_ffn, shift_ffn,
):
    dp_count, seq_count = lax.axis_size("dp"), lax.axis_size("seq")
    seq = lax.axis_index("seq")
    blocks, block_rows, width = media.shape
    items, lat_rows = seq_count, latents.shape[1]
    own_cols = gain_lat.shape[0]
    ends = FRAME_BLOCKS * jnp.cumsum(frame_counts[0])
    position = lax.dynamic_slice_in_dim(block_position[0], seq * blocks, blocks)
    owner = jnp.sum((ends[None, :] <= position[:, None]).astype(jnp.int32), axis=1)
    owner = jnp.concatenate([owner, seq[None]])
    vectors = jnp.stack([gain_lat, shift_lat, gain_media, shift_media, gain_ffn, shift_ffn]).astype(F32)
    pack = jnp.pad(vectors, ((0, 2), (0, 128 - own_cols)))
    lat, og = latents.reshape(lat_rows, width), out_grad.reshape(lat_rows, width)
    med = media.reshape(-1, width)
    (wq, wk, wv, n, nl, q, k, v, gwo, gwu, gwd, gains, lat_out, grad_hidden, do_all, stat_all, sums_ffn) = forward(
        dp_count, owner, med, pack, lat, w_query, w_key, w_value, w_out, og, w_down, w_up, block_rows, own_cols)
    wq, wk, wv = [w.reshape(width, width) for w in (wq, wk, wv)]
    media_grad, lat_grad, sums, out_q, out_k, out_v, out_o, out_up, out_dn = backward(
        dp_count, owner, lat, grad_hidden, gains, sums_ffn, n, nl, q, k, v, do_all, stat_all, gwo, gwu, gwd, med, wq, wk, wv, block_rows)
    place = (lax.axis_index("dp") * seq_count + seq) * own_cols
    own = lax.dynamic_slice_in_dim(sums, place, own_cols, axis=1)
    lat_out, lat_grad, media_grad, *grads = copied(lat_out, lat_grad, media_grad, out_q, out_k, out_v, out_o, out_up, out_dn)
    return (lat_out.reshape(latents.shape), lat_grad.reshape(latents.shape), media_grad.reshape(media.shape), *grads, *[own[i] for i in range(6)])


def fits(mesh):
    return mesh.shape["seq"] == 4 and mesh.shape["dp"] % 2 == 0 and 1536 % (mesh.shape["dp"] * 64) == 0


def norm_forward(rows, gain, shift):
    mean = jnp.mean(rows, axis=-1, keepdims=True)
    centred = rows - mean
    variance = jnp.mean(centred * centred, axis=-1, keepdims=True)
    inverse = lax.rsqrt(variance + EPS)
    scaled = centred * inverse
    return (scaled * gain + shift, scaled, inverse)


def norm_backward(incoming, scaled, inverse, gain):
    inner = incoming * gain
    first = jnp.mean(inner, axis=-1, keepdims=True)
    second = jnp.mean(inner * scaled, axis=-1, keepdims=True)
    return (
        inverse * (inner - first - scaled * second),
        jnp.sum(incoming * scaled, axis=0),
        jnp.sum(incoming, axis=0),
    )


def matmul(left, right):
    return jnp.dot(left, right, preferred_element_type=jnp.float32)


def matmul_left_t(left, right):
    return lax.dot_general(
        left, right, (((0,), (0,)), ((), ())), preferred_element_type=jnp.float32
    )


def matmul_right_t(left, right):
    return lax.dot_general(
        left, right, (((1,), (1,)), ((), ())), preferred_element_type=jnp.float32
    )


def swap_rows(stat):
    return jnp.swapaxes(stat, 1, 2)[..., None]


def fold_sources(tops, totals, accums):
    best = jnp.max(tops, axis=0)
    factor = jnp.exp(tops - best[None])
    total = jnp.sum(factor * totals, axis=0)
    width = accums.shape[-1]
    spread = jnp.repeat(jnp.swapaxes(factor, 2, 3), width // factor.shape[2], axis=3)
    return (best, total, jnp.sum(accums * spread, axis=0))


def local(
    media,
    latents,
    out_grad,
    frame_counts,
    block_position,
    w_query,
    w_key,
    w_value,
    w_out,
    w_up,
    w_down,
    gain_lat,
    shift_lat,
    gain_media,
    shift_media,
    gain_ffn,
    shift_ffn,
):
    gathered = (
        lax.all_gather(w_query, ("dp", "seq"), axis=0, tiled=True),
        lax.all_gather(w_key, ("dp", "seq"), axis=0, tiled=True),
        lax.all_gather(w_value, ("dp", "seq"), axis=0, tiled=True),
        lax.all_gather(w_out, ("dp", "seq"), axis=0, tiled=True),
        lax.all_gather(w_up, ("dp", "seq"), axis=0, tiled=True),
        lax.all_gather(w_down, ("dp", "seq"), axis=0, tiled=True),
        lax.all_gather(gain_lat, ("dp", "seq"), axis=0, tiled=True),
        lax.all_gather(shift_lat, ("dp", "seq"), axis=0, tiled=True),
        lax.all_gather(gain_media, ("dp", "seq"), axis=0, tiled=True),
        lax.all_gather(shift_media, ("dp", "seq"), axis=0, tiled=True),
        lax.all_gather(gain_ffn, ("dp", "seq"), axis=0, tiled=True),
        lax.all_gather(shift_ffn, ("dp", "seq"), axis=0, tiled=True),
    )
    full_query, full_key, full_value, full_out, full_up, full_down = gathered[:6]
    lat_gain, lat_shift, med_gain, med_shift, ffn_gain, ffn_shift = [
        piece.astype(jnp.float32) for piece in gathered[6:]
    ]
    seq_rank = lax.axis_index("seq")
    seq_count = lax.axis_size("seq")
    blocks, block_rows, width = media.shape
    local_items, lat_rows, _ = latents.shape
    group_items = frame_counts.shape[1]
    heads = HEADS
    head_size = HEAD_DIM
    score_scale = head_size ** (-0.5)
    ends = FRAME_BLOCKS * jnp.cumsum(frame_counts[0])
    position = lax.dynamic_slice_in_dim(block_position[0], seq_rank * blocks, blocks)
    owner_item = jnp.sum((ends[None, :] <= position[:, None]).astype(jnp.int32), axis=1)
    member = (owner_item[:, None] == jnp.arange(group_items, dtype=jnp.int32)[None, :]).astype(
        jnp.float32
    )
    lat_input = latents.astype(jnp.float32).reshape(-1, width)
    normed_lat, scaled_lat, inverse_lat = norm_forward(lat_input, lat_gain, lat_shift)
    normed_lat = normed_lat.astype(jnp.bfloat16)
    query = matmul(normed_lat, full_query).astype(jnp.bfloat16)
    key_lat = (
        matmul(normed_lat, full_key)
        .astype(jnp.bfloat16)
        .reshape(local_items, lat_rows, heads, head_size)
    )
    value_lat = (
        matmul(normed_lat, full_value)
        .astype(jnp.bfloat16)
        .reshape(local_items, lat_rows, heads, head_size)
    )
    query_all = lax.all_gather(
        query.reshape(local_items, lat_rows, width), "seq", axis=0, tiled=True
    )
    med_input = media.astype(jnp.float32).reshape(-1, width)
    normed_med, scaled_med, inverse_med = norm_forward(med_input, med_gain, med_shift)
    normed_med = normed_med.astype(jnp.bfloat16)

    def media_keys(weight_key, weight_value):
        keys_out = (
            matmul(normed_med, weight_key)
            .astype(jnp.bfloat16)
            .reshape(blocks, block_rows, heads, head_size)
        )
        values_out = (
            matmul(normed_med, weight_value)
            .astype(jnp.bfloat16)
            .reshape(blocks, block_rows, heads, head_size)
        )
        return (keys_out, values_out)

    key_med, value_med = media_keys(full_key, full_value)
    query_blk = query_all[owner_item].reshape(blocks, lat_rows, heads, head_size)
    scores_med = (
        jnp.einsum("bqhd,bkhd->bhqk", query_blk, key_med, preferred_element_type=jnp.float32)
        * score_scale
    )
    block_top = jnp.max(scores_med, axis=-1)
    expo_med = jnp.exp(scores_med - block_top[..., None])
    expo_med_low = expo_med.astype(jnp.bfloat16)
    local_top = jnp.max(jnp.where(member.T[:, :, None, None] > 0, block_top[None], NEG), axis=1)
    to_local = jnp.exp(block_top - local_top[owner_item])
    local_total = jnp.einsum(
        "bi,bhq->ihq", member, to_local * jnp.sum(expo_med, axis=-1), precision=HIGH
    )
    accum_blk = jnp.einsum(
        "bhqk,bkhd->bqhd", expo_med_low, value_med, preferred_element_type=jnp.float32
    ) * swap_rows(to_local)
    local_accum = jnp.einsum("bi,bqhd->iqhd", member, accum_blk, precision=HIGH).reshape(
        group_items, lat_rows, width
    )
    part_top, part_total, part_accum = (
        lax.all_to_all(local_top, "seq", split_axis=0, concat_axis=0, tiled=True),
        lax.all_to_all(local_total, "seq", split_axis=0, concat_axis=0, tiled=True),
        lax.all_to_all(local_accum, "seq", split_axis=0, concat_axis=0, tiled=True),
    )
    top_own, total_own, accum_flat = fold_sources(
        part_top.reshape(seq_count, local_items, heads, lat_rows),
        part_total.reshape(seq_count, local_items, heads, lat_rows),
        part_accum.reshape(seq_count, local_items, lat_rows, width),
    )
    med_top = lax.all_gather(top_own, "seq", axis=0, tiled=True)
    accum_own = accum_flat.reshape(local_items, lat_rows, heads, head_size)
    query_lat = query.reshape(local_items, lat_rows, heads, head_size)
    scores_lat = (
        jnp.einsum("iqhd,ikhd->ihqk", query_lat, key_lat, preferred_element_type=jnp.float32)
        * score_scale
    )
    lat_top = jnp.max(scores_lat, axis=-1)
    expo_lat = jnp.exp(scores_lat - lat_top[..., None])
    expo_lat_low = expo_lat.astype(jnp.bfloat16)
    item_top = jnp.maximum(top_own, lat_top)
    media_weight = jnp.exp(top_own - item_top)
    lat_weight = jnp.exp(lat_top - item_top)
    item_total = total_own * media_weight + lat_weight * jnp.sum(expo_lat, axis=-1)
    inverse_total = 1.0 / item_total
    accum_lat = jnp.einsum(
        "ihqk,ikhd->iqhd", expo_lat_low, value_lat, preferred_element_type=jnp.float32
    ) * swap_rows(lat_weight)
    attended = (accum_own * swap_rows(media_weight) + accum_lat) * swap_rows(inverse_total)
    attended_low = attended.reshape(-1, width).astype(jnp.bfloat16)
    hidden = lat_input + matmul(attended_low, full_out)
    normed_ffn, scaled_ffn, inverse_ffn = norm_forward(hidden, ffn_gain, ffn_shift)
    normed_ffn = normed_ffn.astype(jnp.bfloat16)
    pre_act = matmul(normed_ffn, full_up)
    activated, gelu_back = jax.vjp(partial(jax.nn.gelu, approximate=False), pre_act)
    activated = activated.astype(jnp.bfloat16)
    result = hidden + matmul(activated, full_down)
    latents_out = result.astype(jnp.bfloat16).reshape(latents.shape)
    again = (
        lax.all_gather(w_query, ("dp", "seq"), axis=0, tiled=True),
        lax.all_gather(w_key, ("dp", "seq"), axis=0, tiled=True),
        lax.all_gather(w_value, ("dp", "seq"), axis=0, tiled=True),
        lax.all_gather(w_out, ("dp", "seq"), axis=0, tiled=True),
        lax.all_gather(w_up, ("dp", "seq"), axis=0, tiled=True),
        lax.all_gather(w_down, ("dp", "seq"), axis=0, tiled=True),
        lax.all_gather(gain_lat, ("dp", "seq"), axis=0, tiled=True),
        lax.all_gather(shift_lat, ("dp", "seq"), axis=0, tiled=True),
        lax.all_gather(gain_media, ("dp", "seq"), axis=0, tiled=True),
        lax.all_gather(shift_media, ("dp", "seq"), axis=0, tiled=True),
        lax.all_gather(gain_ffn, ("dp", "seq"), axis=0, tiled=True),
        lax.all_gather(shift_ffn, ("dp", "seq"), axis=0, tiled=True),
    )
    back_query, back_key, back_value, back_out, back_up, back_down = again[:6]
    grad_rows = out_grad.reshape(-1, width)
    cotangent = grad_rows.astype(jnp.float32)
    grad_down = matmul_left_t(activated, grad_rows)
    grad_act = matmul_right_t(grad_rows, back_down)
    grad_pre = gelu_back(grad_act)[0].astype(jnp.bfloat16)
    grad_up = matmul_left_t(normed_ffn, grad_pre)
    grad_normed_ffn = matmul_right_t(grad_pre, back_up)
    grad_hidden_norm, grad_gain_ffn, grad_shift_ffn = norm_backward(
        grad_normed_ffn, scaled_ffn, inverse_ffn, ffn_gain
    )
    grad_hidden = cotangent + grad_hidden_norm
    grad_hidden_low = grad_hidden.astype(jnp.bfloat16)
    grad_out = matmul_left_t(attended_low, grad_hidden_low)
    grad_att = matmul_right_t(grad_hidden_low, back_out).astype(jnp.bfloat16)
    grad_att_heads = grad_att.reshape(local_items, lat_rows, heads, head_size)
    delta = jnp.einsum(
        "iqhd,iqhd->ihq", grad_att_heads.astype(jnp.float32), attended, precision=HIGH
    )
    media_factor = media_weight * inverse_total
    grad_att_all = lax.all_gather(
        grad_att.reshape(local_items, lat_rows, width), "seq", axis=0, tiled=True
    )
    factor_all, delta_all = (
        lax.all_gather(media_factor, "seq", axis=0, tiled=True),
        lax.all_gather(delta, "seq", axis=0, tiled=True),
    )
    key_med, value_med = media_keys(back_key, back_value)
    grad_blk = grad_att_all[owner_item].reshape(blocks, lat_rows, heads, head_size)
    factor_blk = jnp.exp(block_top - med_top[owner_item]) * factor_all[owner_item]
    delta_blk = delta_all[owner_item]
    grad_prob_med = jnp.einsum(
        "bqhd,bkhd->bhqk", grad_blk, value_med, preferred_element_type=jnp.float32
    )
    grad_score_med = (
        expo_med * factor_blk[..., None] * (grad_prob_med - delta_blk[..., None])
    ).astype(jnp.bfloat16)
    grad_query_blk = (
        jnp.einsum("bhqk,bkhd->bqhd", grad_score_med, key_med, preferred_element_type=jnp.float32)
        * score_scale
    )
    grad_query_part = jnp.einsum("bi,bqhd->iqhd", member, grad_query_blk, precision=HIGH).reshape(
        group_items, lat_rows, width
    )
    grad_key_med = (
        (
            jnp.einsum(
                "bhqk,bqhd->bkhd", grad_score_med, query_blk, preferred_element_type=jnp.float32
            )
            * score_scale
        )
        .astype(jnp.bfloat16)
        .reshape(-1, width)
    )
    grad_value_med = (
        jnp.einsum(
            "bhqk,bqhd->bkhd",
            expo_med_low.astype(jnp.float32) * factor_blk[..., None],
            grad_blk.astype(jnp.float32),
            precision=HIGH,
        )
        .astype(jnp.bfloat16)
        .reshape(-1, width)
    )
    grad_query_own = lax.psum_scatter(
        grad_query_part.astype(jnp.bfloat16), "seq", scatter_dimension=0, tiled=True
    ).astype(jnp.float32)
    grad_normed_med = matmul_right_t(grad_key_med, back_key) + matmul_right_t(
        grad_value_med, back_value
    )
    grad_key = matmul_left_t(normed_med, grad_key_med)
    grad_value = matmul_left_t(normed_med, grad_value_med)
    media_grad, grad_gain_media, grad_shift_media = norm_backward(
        grad_normed_med, scaled_med, inverse_med, med_gain
    )
    lat_factor = lat_weight * inverse_total
    grad_prob_lat = jnp.einsum(
        "iqhd,ikhd->ihqk", grad_att_heads, value_lat, preferred_element_type=jnp.float32
    )
    grad_score_lat = (expo_lat * lat_factor[..., None] * (grad_prob_lat - delta[..., None])).astype(
        jnp.bfloat16
    )
    grad_query_lat = (
        jnp.einsum("ihqk,ikhd->iqhd", grad_score_lat, key_lat, preferred_element_type=jnp.float32)
        * score_scale
    )
    grad_key_lat = (
        (
            jnp.einsum(
                "ihqk,iqhd->ikhd", grad_score_lat, query_lat, preferred_element_type=jnp.float32
            )
            * score_scale
        )
        .astype(jnp.bfloat16)
        .reshape(-1, width)
    )
    grad_value_lat = (
        jnp.einsum(
            "ihqk,iqhd->ikhd",
            expo_lat_low.astype(jnp.float32) * lat_factor[..., None],
            grad_att_heads.astype(jnp.float32),
            precision=HIGH,
        )
        .astype(jnp.bfloat16)
        .reshape(-1, width)
    )
    grad_query = (
        (grad_query_own + grad_query_lat.reshape(local_items, lat_rows, width))
        .astype(jnp.bfloat16)
        .reshape(-1, width)
    )
    grad_normed_lat = (
        matmul_right_t(grad_query, back_query)
        + matmul_right_t(grad_key_lat, back_key)
        + matmul_right_t(grad_value_lat, back_value)
    )
    grad_query_weight = matmul_left_t(normed_lat, grad_query)
    grad_key = grad_key + matmul_left_t(normed_lat, grad_key_lat)
    grad_value = grad_value + matmul_left_t(normed_lat, grad_value_lat)
    grad_lat_norm, grad_gain_lat, grad_shift_lat = norm_backward(
        grad_normed_lat, scaled_lat, inverse_lat, lat_gain
    )
    latents_grad = (grad_hidden + grad_lat_norm).reshape(latents.shape)
    sharded = (
        lax.psum_scatter(grad_query_weight, ("dp", "seq"), scatter_dimension=0, tiled=True),
        lax.psum_scatter(grad_key, ("dp", "seq"), scatter_dimension=0, tiled=True),
        lax.psum_scatter(grad_value, ("dp", "seq"), scatter_dimension=0, tiled=True),
        lax.psum_scatter(grad_out, ("dp", "seq"), scatter_dimension=0, tiled=True),
        lax.psum_scatter(grad_up, ("dp", "seq"), scatter_dimension=0, tiled=True),
        lax.psum_scatter(grad_down, ("dp", "seq"), scatter_dimension=0, tiled=True),
        lax.psum_scatter(grad_gain_lat, ("dp", "seq"), scatter_dimension=0, tiled=True),
        lax.psum_scatter(grad_shift_lat, ("dp", "seq"), scatter_dimension=0, tiled=True),
        lax.psum_scatter(grad_gain_media, ("dp", "seq"), scatter_dimension=0, tiled=True),
        lax.psum_scatter(grad_shift_media, ("dp", "seq"), scatter_dimension=0, tiled=True),
        lax.psum_scatter(grad_gain_ffn, ("dp", "seq"), scatter_dimension=0, tiled=True),
        lax.psum_scatter(grad_shift_ffn, ("dp", "seq"), scatter_dimension=0, tiled=True),
    )
    return (latents_out, latents_grad, media_grad.reshape(media.shape)) + tuple(sharded)


def solution(mesh):
    return jax.shard_map(
        local_fast if fits(mesh) else local,
        mesh=mesh,
        in_specs=(
            P(("dp", "seq"), None, None),
            P(("dp", "seq"), None, None),
            P(("dp", "seq"), None, None),
            P("dp", None),
            P("dp", None),
            P(("dp", "seq"), None),
            P(("dp", "seq"), None),
            P(("dp", "seq"), None),
            P(("dp", "seq"), None),
            P(("dp", "seq"), None),
            P(("dp", "seq"), None),
            P(("dp", "seq")),
            P(("dp", "seq")),
            P(("dp", "seq")),
            P(("dp", "seq")),
            P(("dp", "seq")),
            P(("dp", "seq")),
        ),
        out_specs=(
            P(("dp", "seq"), None, None),
            P(("dp", "seq"), None, None),
            P(("dp", "seq"), None, None),
            P(("dp", "seq"), None),
            P(("dp", "seq"), None),
            P(("dp", "seq"), None),
            P(("dp", "seq"), None),
            P(("dp", "seq"), None),
            P(("dp", "seq"), None),
            P(("dp", "seq")),
            P(("dp", "seq")),
            P(("dp", "seq")),
            P(("dp", "seq")),
            P(("dp", "seq")),
            P(("dp", "seq")),
        ),
        check_vma=False,
    )
```

```python
import math
from functools import partial
from jax.sharding import PartitionSpec as P
import functools
import jax
import jax.numpy as jnp
from jax import lax
from jax.experimental import pallas as pl
from jax.experimental.pallas import tpu as pltpu

MESH = pl.DeviceIdType.MESH
ANY = pl.BlockSpec(memory_space=pl.ANY)
VMEM = pl.BlockSpec(memory_space=pltpu.VMEM)
DMA = pltpu.SemaphoreType.DMA


class Here:
    def __init__(self, dp_count):
        dp, seq = lax.axis_index("dp"), lax.axis_index("seq")
        self.nz = dp_count // 2
        self.z, self.x, self.y, self.c = dp // 2, dp % 2, seq // 2, seq % 2
        self.dp, self.seq = dp, seq

    def at(self, z=None, x=None, y=None, c=None):
        z = self.z if z is None else z
        x = self.x if x is None else x
        y = self.y if y is None else y
        c = self.c if c is None else c
        return (z * 2 + x, y * 2 + c)


def send(src, dst, ss, rs, to):
    copy = pltpu.make_async_remote_copy(
        src_ref=src, dst_ref=dst, send_sem=ss, recv_sem=rs, device_id=to, device_id_type=MESH
    )
    copy.start()


def landed(dst, ss, rs, me):
    pltpu.make_async_remote_copy(
        src_ref=dst, dst_ref=dst, send_sem=ss, recv_sem=rs, device_id=me.at(c=1 - me.c), device_id_type=MESH
    ).wait_recv()


def sent(src, ss, rs, me):
    pltpu.make_async_remote_copy(
        src_ref=src, dst_ref=src, send_sem=ss, recv_sem=rs, device_id=me.at(c=1 - me.c), device_id_type=MESH
    ).wait_send()


def greet(devices):
    barrier = pltpu.get_barrier_semaphore()
    for device in devices:
        pl.semaphore_signal(barrier, inc=1, device_id=device, device_id_type=MESH)
    pl.semaphore_wait(barrier, len(devices))


COL, FROMX, FROMY, DIAGA, DIAGB = range(5)
TOUP, TODOWN, TOX, TOY, FWDY, FWDX, TOC = range(7)


class Gather:
    def __init__(self, me, src, dst, ss, rs, axes, halves):
        self.me, self.src, self.dst, self.ss, self.rs = me, src, dst, ss, rs
        self.axes, self.halves = axes, halves
        self.sends = []
        self.depth = me.nz if "z" in axes else 1

    def slot(self, z, x, y, c):
        if self.axes == "zxyc":
            return ((z * 2 + x) * 2 + y) * 2 + c
        if self.axes == "zx":
            return z * 2 + x
        return y * 2 + c

    def shard(self, z, x, y, c, half=None):
        ref = self.dst.at[self.slot(z, x, y, c)]
        if half is None or not self.halves:
            return ref
        cut, width = self.halves, self.dst.shape[-1]
        return ref.at[:, pl.ds(0, cut)] if half == 0 else ref.at[:, pl.ds(cut, width - cut)]

    def key(self, z):
        return z if "z" in self.axes else 0

    def start(self, src, dst, out_kind, in_kind, z, to):
        send(src, dst, self.leaves(out_kind, z), self.arrives(in_kind, z), to)

    def leaves(self, kind, z):
        return self.ss.at[1 + kind * self.depth + z] if kind in (TOUP, TODOWN) else self.ss.at[0]

    def arrives(self, kind, z):
        return self.rs.at[5 * self.depth if kind >= 5 else kind * self.depth + self.key(z)]

    def whole(self, count):
        return self.dst.at[pl.ds(0, count)]

    def gone(self, ref, kind, z):
        sent(ref, self.leaves(kind, z), self.rs.at[0], self.me)

    def here(self, ref, kind, z):
        landed(ref, self.ss.at[0], self.arrives(kind, z), self.me)

    def groups(self):
        return dict(own=self.own(), column=self.column(), neighbours=self.neighbours(), diagonal=self.diagonal(), sibling=self.sibling())

    @staticmethod
    def semaphores(axes, nz):
        depth = nz if "z" in axes else 1
        return [DMA((1 + 2 * depth,)), DMA((5 * depth + 1,))]

    def hand_over(self, ref, kind, z):
        if "c" in self.axes:
            self.start(ref, ref, TOC + kind, 5 + kind, z, self.me.at(c=1 - self.me.c))

    def spread(self, ref, z):
        me = self.me
        if "x" in self.axes:
            self.start(ref, ref, TOX, FROMX, z, me.at(x=1 - me.x))
        if "y" in self.axes:
            self.start(ref, ref, TOY, FROMY, z, me.at(y=1 - me.y))
        self.hand_over(ref, COL, z)

    def own(self):
        return [self.send_own]

    def send_own(self):
        me = self.me
        ref = self.shard(me.z, me.x, me.y, me.c)
        if "z" in self.axes:
            @pl.when(me.z + 1 < me.nz)
            def _():
                self.start(self.src, ref, TOUP, COL, me.z, me.at(z=me.z + 1))

            @pl.when(me.z > 0)
            def _():
                self.start(self.src, ref, TODOWN, COL, me.z, me.at(z=me.z - 1))
        if "x" in self.axes:
            self.start(self.src, ref, TOX, FROMX, me.z, me.at(x=1 - me.x))
        if "y" in self.axes:
            self.start(self.src, ref, TOY, FROMY, me.z, me.at(y=1 - me.y))
        if "c" in self.axes:
            self.start(self.src, ref, TOC, 5, me.z, me.at(c=1 - me.c))

    def around(self, event):
        me = self.me
        found = [lambda: event(me.z)]
        for d in range(1, self.depth):
            found.append(lambda d=d: pl.when(me.z >= d)(lambda: event(me.z - d)))
            found.append(lambda d=d: pl.when(me.z + d < me.nz)(lambda: event(me.z + d)))
        return found

    def column(self):
        me = self.me

        def event(d, below):
            there = me.z - d if below else me.z + d
            ahead = me.z + 1 if below else me.z - 1

            @pl.when(there >= 0 if below else there < me.nz)
            def _():
                ref = self.shard(there, me.x, me.y, me.c)
                self.here(ref, COL, there)

                @pl.when(ahead < me.nz if below else ahead >= 0)
                def _():
                    self.start(ref, ref, TOUP if below else TODOWN, COL, there, me.at(z=ahead))
                self.spread(ref, there)
        return [functools.partial(event, d, below) for d in range(1, self.depth) for below in (True, False)]

    def neighbours(self):
        me = self.me

        def event(z):
            if "x" in self.axes:
                ref = self.shard(z, 1 - me.x, me.y, me.c)
                self.here(ref, FROMX, z)
                if "y" in self.axes:
                    half = self.shard(z, 1 - me.x, me.y, me.c, 0)
                    self.start(half, half, FWDY, DIAGA, z, me.at(y=1 - me.y))
                self.hand_over(ref, FROMX, z)
            if "y" in self.axes:
                ref = self.shard(z, me.x, 1 - me.y, me.c)
                self.here(ref, FROMY, z)
                if "x" in self.axes and self.halves:
                    half = self.shard(z, me.x, 1 - me.y, me.c, 1)
                    self.start(half, half, FWDX, DIAGB, z, me.at(x=1 - me.x))
                self.hand_over(ref, FROMY, z)
        return self.around(event)

    def diagonal(self):
        me = self.me
        if "x" not in self.axes or "y" not in self.axes:
            return []

        def event(z):
            for half in range(2 if self.halves else 1):
                ref = self.shard(z, 1 - me.x, 1 - me.y, me.c, half)
                self.here(ref, DIAGA + half, z)
                self.hand_over(ref, DIAGA + half, z)
        return self.around(event)

    def kinds(self):
        me = self.me
        found = [(COL, me.x, me.y, None)]
        if "x" in self.axes:
            found.append((FROMX, 1 - me.x, me.y, None))
        if "y" in self.axes:
            found.append((FROMY, me.x, 1 - me.y, None))
        if "x" in self.axes and "y" in self.axes:
            found.append((DIAGA, 1 - me.x, 1 - me.y, 0))
            if self.halves:
                found.append((DIAGB, 1 - me.x, 1 - me.y, 1))
        return found

    def sibling(self):
        if "c" not in self.axes:
            return []
        count = self.depth * (1 + ("x" in self.axes)) * (1 + ("y" in self.axes))
        return [lambda: self.here(self.whole(count), 5, 0)]

    def drain(self):
        me = self.me
        x, y, c = ["xyc".index(a) >= 0 and a in self.axes for a in "xyc"]
        count = self.depth * (x + y + (x and y) + c * (1 + x) * (1 + y))
        found = [lambda: self.gone(self.whole(count), TOC, 0)]
        if "z" in self.axes:
            shard = self.shard(me.z, me.x, me.y, me.c)

            def event(z):
                pl.when((z <= me.z) & (me.z + 1 < me.nz))(lambda: self.gone(shard, TOUP, z))
                pl.when((z >= me.z) & (me.z > 0))(lambda: self.gone(shard, TODOWN, z))
            found += self.around(event)
        return found

    def phases(self):
        return [self.own(), self.column(), self.neighbours(), self.diagonal(), self.sibling(), self.drain()]


def skewed(items):
    lists = [item.phases() for item in items]
    found = []
    for step in range(len(lists) + max(map(len, lists)) - 1):
        for i, phases in enumerate(lists):
            if 0 <= step - i < len(phases):
                found += phases[step - i]
    return found


def run(events):
    for event in events:
        event()


def share(events, count):
    cuts = [len(events) * i // count for i in range(count + 1)]
    return [events[a:b] for a, b in zip(cuts, cuts[1:])]


def run_at(step, lists):
    for i, events in enumerate(lists):
        if events:
            pl.when(step == i)(functools.partial(run, events))


class Regroup:
    def __init__(self, me, dp_count, src, dst, ss, rs, width):
        self.me, self.n, self.src, self.dst, self.ss, self.rs, self.width = me, dp_count, src, dst, ss, rs, width

    def piece(self, dp, y, c):
        return self.dst.at[dp * 4 + y * 2 + c]

    def columns(self, dp):
        return self.src.at[:, pl.ds(pl.multiple_of(dp * self.width, 128), self.width)]

    def hand(self, src, dp, y, place, to):
        send(src, self.piece(dp, y, self.me.c), self.ss.at[0], self.rs.at[place], to)

    def own(self):
        me = self.me
        for k in range(1, self.n):
            to = lax.rem(me.dp + k, self.n)
            self.hand(self.columns(to), me.dp, me.y, me.dp, (to, me.seq))
        self.share(self.columns(me.dp), me.dp)

    def share(self, src, dp):
        me = self.me
        self.hand(src, dp, me.y, self.n + dp, me.at(y=1 - me.y))
        self.hand(src, dp, me.y, 2 * self.n, me.at(c=1 - me.c))

    def here(self, ref, place):
        landed(ref, self.ss.at[0], self.rs.at[place], self.me)

    def column(self):
        me = self.me
        for k in range(1, self.n):
            dp = lax.rem(me.dp + k, self.n)
            ref = self.piece(dp, me.y, me.c)
            self.here(ref, dp)
            self.share(ref, dp)

    def neighbours(self):
        me = self.me
        for k in range(self.n):
            dp = lax.rem(me.dp + k, self.n)
            ref = self.piece(dp, 1 - me.y, me.c)
            self.here(ref, self.n + dp)
            self.hand(ref, dp, 1 - me.y, 2 * self.n, me.at(c=1 - me.c))

    def sibling(self):
        self.here(self.dst.at[pl.ds(0, 2 * self.n)], 2 * self.n)

    def drain(self):
        sent(self.dst.at[pl.ds(0, 4 * self.n - 1)], self.ss.at[0], self.rs.at[0], self.me)

    def phases(self):
        return [[self.own], [self.column], [self.neighbours], [self.sibling], [self.drain]]

    @staticmethod
    def semaphores(dp_count):
        return [DMA((1,)), DMA((2 * dp_count + 1,))]


class Everyone:
    def __init__(self, me, dp_count, src, dst, ss, rs):
        self.me, self.n, self.src, self.dst, self.ss, self.rs = me, dp_count * 4, src, dst, ss, rs
        self.index = me.dp * 4 + me.seq

    def own(self):
        def event():
            @pl.loop(1, self.n)
            def _(k):
                to = lax.rem(self.index + k, self.n)
                send(self.src, self.dst.at[self.index], self.ss.at[0], self.rs.at[0], (to // 4, to % 4))
        return [event]

    def arrive(self):
        return [lambda: landed(self.dst.at[pl.ds(0, self.n - 1)], self.ss.at[0], self.rs.at[0], self.me)]

    def drain(self):
        return [lambda: sent(self.dst.at[pl.ds(0, self.n - 1)], self.ss.at[0], self.rs.at[0], self.me)]

    def phases(self):
        return [self.own(), self.arrive(), self.drain()]


def greet_all(me, dp_count):
    barrier = pltpu.get_barrier_semaphore()
    count = dp_count * 4

    @pl.loop(1, count)
    def _(k):
        to = lax.rem(me.dp * 4 + me.seq + k, count)
        pl.semaphore_signal(barrier, inc=1, device_id=(to // 4, to % 4), device_id_type=MESH)
    pl.semaphore_wait(barrier, count - 1)


FORWARD_ORDER = dict(
    q=dict(own=-1.671, column=-0.997, neighbours=2.973, diagonal=8.049, sibling=9.285),
    pack=dict(own=-1.0, arrive=-0.731),
    lat=dict(own=-0.999, neighbours=-0.917, sibling=-0.732),
    k=dict(own=-0.998, column=-0.996, neighbours=2.5, diagonal=4.61, sibling=7.657),
    v=dict(own=-0.336, column=3.046, neighbours=14.914, diagonal=28.532, sibling=40.12),
    o=dict(own=8.048, column=23.68, neighbours=44.275, diagonal=59.459, sibling=59.943),
    og=dict(own=27.572, column=59.273, neighbours=61.672),
    up=dict(own=28.241, column=59.555, neighbours=61.854, sibling=62.713),
    dn=dict(own=28.533, neighbours=58.926, sibling=59.917),
    x=dict(send0=50.963, send1=59.241, wait=59.918),
    nf=dict(own=61.183, a1=61.853, a2=62.093, b0=62.272, b1=64.105, b2=65.251, a3=65.818, b3=66.796),
    g=dict(a0=64.191, a1=66.009, a2=66.274, a3=67.798, b0=69.586, b1=70.423, b2=71.005, b3=71.804, finish=71.853),
    y=dict(start=71.382, fold=72.623, finish=76.92),
    st=dict(own=73.217, neighbours=74.655, sibling=76.353),
    do=dict(own=73.218, neighbours=76.825, sibling=78.0),
)
BACK_ORDER = dict(
    o=dict(begin=-1.0, core=0.257, middle=14.163, fold=21.903, finish=28.444),
    up=dict(begin=1.335, core=6.978, fold=24.753, finish=24.894, collect=50.506),
    k=dict(core=18.955, middle=28.229, fold=40.734, finish=48.103),
    v=dict(core=24.416, middle=37.863, fold=48.42, finish=51.002),
    dn=dict(begin=24.67, core=37.79, fold=50.639, finish=51.001),
    lat=dict(begin=34.007, core=37.914, fold=48.961, finish=50.002),
    q=dict(core=40.466, middle=50.058, fold=50.129, finish=51.003),
    sum=dict(s0=50.057, s1=50.128, s2=50.64, s3=51.0, s4=450.823),
)


HEADS = 16
HEAD_DIM = 96
FRAME_BLOCKS = 2
EPS = 1e-05
NEG = -1e30
HIGH = lax.Precision.HIGHEST
F32, BF16 = jnp.float32, jnp.bfloat16
WIDE = 62 << 20
PART = 4
PCOLS = PART * HEAD_DIM
SCALE = HEAD_DIM ** (-0.5)


def dot(left, right):
    return jnp.dot(left, right, preferred_element_type=F32)


def dot_t(left, right):
    return lax.dot_general(left, right, (((1,), (1,)), ((), ())), preferred_element_type=F32)


def t_dot(left, right):
    return lax.dot_general(left, right, (((0,), (0,)), ((), ())), preferred_element_type=F32)


def scaled_rows(rows):
    mean = jnp.mean(rows, axis=-1, keepdims=True)
    centred = rows - mean
    inverse = lax.rsqrt(jnp.mean(centred * centred, axis=-1, keepdims=True) + EPS)
    return centred * inverse, inverse


def norm_back(incoming, scaled, inverse, gain):
    inner = incoming * gain
    first = jnp.mean(inner, axis=-1, keepdims=True)
    second = jnp.mean(inner * scaled, axis=-1, keepdims=True)
    return inverse * (inner - first - scaled * second)


def part_mask(rows):
    row = lax.broadcasted_iota(jnp.int32, (PART * rows, PCOLS), 0)
    column = lax.broadcasted_iota(jnp.int32, (PART * rows, PCOLS), 1)
    low = (row // rows) * HEAD_DIM
    return (column >= low) & (column < low + HEAD_DIM)


def stacked(rows, mask):
    return jnp.where(mask, jnp.concatenate([rows] * PART, axis=0), jnp.zeros((), rows.dtype))


def unstacked(rows, mask, count):
    kept = jnp.where(mask, rows, 0.0)
    return sum(kept[h * count:(h + 1) * count] for h in range(PART))


def blocks_of(media_rows, block_rows, lat_rows):
    found = [(b * block_rows, block_rows) for b in range(media_rows // block_rows)]
    return found + [(media_rows, lat_rows)]


def attend_kernel(block_rows, items, owner, media, lat_all, gains, wq, wk, wv,
                  acc, stats, n_out, nl_out, q_out, k_out, v_out, wbuf, a_ref, m_ref, l_ref, sems):
    width = media.shape[1]
    half = width // 2
    media_rows = media.shape[0]
    lat_rows = lat_all.shape[0] // items
    seq = lax.axis_index("seq")

    def fetch(step, slot):
        cols = pl.ds(pl.multiple_of(step * half, 128), half)
        return [pltpu.make_async_copy(w.at[:, cols], wbuf.at[slot, i], sems.at[slot, i]) for i, w in enumerate((wq, wk, wv))]
    for copy in fetch(0, 0):
        copy.start()

    @pl.loop(0, media_rows // block_rows)
    def _(b):
        rows = pl.ds(pl.multiple_of(b * block_rows, block_rows), block_rows)
        u, _ = scaled_rows(media[rows, :].astype(F32))
        n_out[rows, :] = (u * gains[2:3, :] + gains[3:4, :]).astype(BF16)

    @pl.loop(0, items)
    def _(i):
        rows = pl.ds(pl.multiple_of(i * lat_rows, lat_rows), lat_rows)
        u, _ = scaled_rows(lat_all[rows, :].astype(F32))
        nl_out[rows, :] = (u * gains[0:1, :] + gains[1:2, :]).astype(BF16)
    n_out[pl.ds(media_rows, lat_rows), :] = nl_out[pl.ds(pl.multiple_of(seq * lat_rows, lat_rows), lat_rows), :]
    padding = n_out.shape[0] - media_rows - lat_rows
    n_out[pl.ds(media_rows + lat_rows, padding), :] = jnp.zeros((padding, width), BF16)
    stats[...] = jnp.zeros_like(stats)
    mask = part_mask(lat_rows)
    lane = lax.broadcasted_iota(jnp.int32, (lat_rows, 128), 1)

    @pl.loop(0, 2)
    def _(step):
        slot = lax.rem(step, 2)
        cols = pl.ds(pl.multiple_of(step * half, 128), half)
        for copy in fetch(step, slot):
            copy.wait()

        @pl.when(step == 0)
        def _():
            for copy in fetch(1, 1):
                copy.start()
        q_out[:, cols] = dot(nl_out[...], wbuf[slot, 0]).astype(BF16)
        k_out[:, cols] = dot(n_out[...], wbuf[slot, 1]).astype(BF16)
        v_out[:, cols] = dot(n_out[...], wbuf[slot, 2]).astype(BF16)

        @pl.loop(0, half // PCOLS)
        def _(inner):
            part = step * (half // PCOLS) + inner
            pcols = pl.ds(pl.multiple_of(part * PCOLS, 128), PCOLS)
            a_ref[...] = jnp.zeros_like(a_ref)
            l_ref[...] = jnp.zeros_like(l_ref)
            m_ref[...] = jnp.full_like(m_ref, NEG)

            def block(start, count, item):
                rows = q_out[pl.ds(pl.multiple_of(item * lat_rows, lat_rows), lat_rows), pcols]
                query = stacked(rows, mask)
                keys, values = k_out[pl.ds(start, count), pcols], v_out[pl.ds(start, count), pcols]
                scores = dot_t(query, keys) * SCALE
                old = m_ref[item]
                new = jnp.maximum(old, jnp.max(scores, axis=-1, keepdims=True))
                factor = jnp.exp(old - new)
                expo = jnp.exp(scores - new[:, :count])
                m_ref[item] = new
                l_ref[item] = l_ref[item] * factor + jnp.sum(expo, axis=-1, keepdims=True)
                wide = jnp.concatenate([factor] * (PCOLS // 128), axis=1)
                a_ref[item] = a_ref[item] * wide + dot(expo.astype(BF16), values)
            for b, (start, count) in enumerate(blocks_of(media_rows, block_rows, lat_rows)):
                block(start, count, seq if count == lat_rows and start == media_rows else owner[b])
            for item in range(items):
                acc[item, :, pcols] = unstacked(a_ref[item], mask, lat_rows).astype(BF16)
                for h in range(PART):
                    chosen = lane == part * PART + h
                    at = pl.ds(h * lat_rows, lat_rows)
                    stats[item, 0] = jnp.where(chosen, m_ref[item, at, :], stats[item, 0])
                    stats[item, 1] = jnp.where(chosen, l_ref[item, at, :], stats[item, 1])


def attend(owner, media, lat_all, gains, wq, wk, wv, block_rows, items):
    width = media.shape[1]
    lat_rows = lat_all.shape[0] // items
    rows = media.shape[0] + block_rows
    shape = jax.ShapeDtypeStruct
    return pl.pallas_call(
        functools.partial(attend_kernel, block_rows, items),
        out_shape=(
            shape((items, lat_rows, width), BF16), shape((items, 2, lat_rows, 128), F32),
            shape((rows, width), BF16), shape((items * lat_rows, width), BF16),
            shape((items * lat_rows, width), BF16), shape((rows, width), BF16), shape((rows, width), BF16),
        ),
        in_specs=[pl.BlockSpec(memory_space=pltpu.SMEM), VMEM, VMEM, VMEM, ANY, ANY, ANY],
        out_specs=tuple([VMEM] * 7),
        scratch_shapes=[
            pltpu.VMEM((2, 3, width, width // 2), BF16),
            pltpu.VMEM((items, PART * lat_rows, PCOLS), F32),
            pltpu.VMEM((items, PART * lat_rows, 128), F32), pltpu.VMEM((items, PART * lat_rows, 128), F32),
            DMA((2, 3)),
        ],
        compiler_params=pltpu.CompilerParams(vmem_limit_bytes=WIDE),
    )(owner, media, lat_all, gains, wq, wk, wv)


def dp_peers(me, dp_count):
    return [(lax.rem(me.dp + k, dp_count), me.seq) for k in range(1, dp_count)]


def far_first(me, event):
    found = []
    for d in range(me.nz - 1, 0, -1):
        found.append(lambda d=d: pl.when(me.z >= d)(lambda: event(me.z - d)))
        found.append(lambda d=d: pl.when(me.z + d < me.nz)(lambda: event(me.z + d)))
    return found + [lambda: event(me.z)]


def add(*refs):
    total = refs[0][...].astype(F32)
    for ref in refs[1:]:
        total = total + ref[...].astype(F32)
    return total


class Line:
    def __init__(self, me, column, boxes, ss, rs):
        self.me, self.column, self.boxes, self.ss, self.rs = me, column, boxes, ss, rs

    def event(self, z):
        me = self.me

        @pl.when(z != me.z)
        def _():
            send(self.column(z), self.boxes.at[me.z], self.ss.at[0], self.rs.at[0], me.at(z=z))

    def total(self, out):
        me = self.me
        landed(self.boxes.at[pl.ds(0, me.nz - 1)], self.ss.at[0], self.rs.at[0], me)
        out[...] = self.column(me.z)[...].astype(F32)
        for z in range(me.nz):
            @pl.when(z != me.z)
            def _():
                out[...] += self.boxes.at[z][...].astype(F32)

    def drain(self):
        return [lambda: sent(self.boxes.at[pl.ds(0, self.me.nz - 1)], self.ss.at[0], self.rs.at[0], self.me)]


class DpScatter:
    def __init__(self, me, part, out, ox, boxes, ss, rs, lss, lrs):
        self.me, self.part, self.out, self.ox, self.ss, self.rs = me, part, out, ox, ss, rs
        self.line = Line(me, lambda z: part.at[z * 2 + me.x], boxes, lss, lrs)

    def order(self):
        n = self.me.nz
        return [lax.rem(self.me.z + k, n) for k in sorted(range(1, n), key=lambda k: -min(k, n - k))] + [self.me.z]

    def send_x(self, z):
        me = self.me
        send(self.part.at[z * 2 + 1 - me.x], self.ox.at[z], self.ss.at[0], self.rs.at[z], me.at(x=1 - me.x))

    def start(self):
        return [functools.partial(self.send_x, z) for z in self.order()]

    def fold_in(self, z):
        landed(self.ox.at[z], self.ss.at[0], self.rs.at[z], self.me)
        mine = self.part.at[z * 2 + self.me.x]
        mine[...] = add(mine, self.ox.at[z]).astype(mine.dtype)
        self.line.event(z)

    def fold(self):
        return [functools.partial(self.fold_in, z) for z in self.order()]

    def finish(self):
        self.line.total(self.out)

    def groups(self):
        return dict(start=self.start(), fold=self.fold(), finish=[self.finish])

    def drain(self):
        return [lambda: sent(self.ox, self.ss.at[0], self.rs.at[0], self.me)] + self.line.drain()

    @staticmethod
    def semaphores(nz):
        return [DMA((1,)), DMA((nz,)), DMA((1,)), DMA((1,))]


def head_columns(width):
    row = lax.broadcasted_iota(jnp.int32, (128, width), 0) * HEAD_DIM
    column = lax.broadcasted_iota(jnp.int32, (128, width), 1)
    return ((column >= row) & (column < row + HEAD_DIM)).astype(F32)


def exact(left, right):
    return jnp.dot(left, right, preferred_element_type=F32, precision=HIGH)


def exact_t(left, right):
    return lax.dot_general(left, right, (((1,), (1,)), ((), ())), preferred_element_type=F32, precision=HIGH)


class Scatter:
    def __init__(self, me, src, out, bufs, ss, rs, ls, lss, lrs):
        self.me, self.src, self.out, self.ss, self.rs, self.ls = me, src, out, ss, rs, ls
        self.acc, self.cbuf, self.x1, self.y1, self.ox, self.oy, boxes = bufs
        self.cut = self.x1.shape[-1]
        self.line = Line(me, lambda z: self.acc.at[z, me.x, me.y], boxes, lss, lrs)

    def part(self, ref, half):
        width = self.acc.shape[-1]
        return ref.at[:, pl.ds(self.cut, width - self.cut)] if half else ref.at[:, pl.ds(0, self.cut)]

    def load(self, z):
        return pltpu.make_async_copy(self.src.at[pl.ds(2 * z, 2), :, self.me.c], self.acc.at[z], self.ls.at[z])

    def feed(self, stage, z):
        me = self.me
        send(stage.at[:, :, 1 - me.c], self.cbuf.at[z], self.ss.at[1 + z], self.rs.at[z], me.at(c=1 - me.c))
        for i in range(4):
            self.acc[z, i // 2, i % 2] = stage[i // 2, i % 2, me.c]

    def fed(self, z):
        sent(self.cbuf.at[z], self.ss.at[1 + z], self.rs.at[0], self.me)

    def begin(self):
        me = self.me

        def event(z):
            send(self.src.at[pl.ds(2 * z, 2), :, 1 - me.c], self.cbuf.at[z], self.ss.at[1 + z], self.rs.at[z], me.at(c=1 - me.c))
            self.load(z).start()
        return far_first(me, event)

    def core(self):
        me = self.me

        def event(z):
            if self.src is not None:
                self.load(z).wait()
            landed(self.cbuf.at[z], self.ss.at[0], self.rs.at[z], me)
            mine = self.acc.at[z]

            @pl.loop(0, 4)
            def _(i):
                x, y = i // 2, i % 2
                mine[x, y] = (mine[x, y].astype(F32) + self.cbuf[z, x, y].astype(F32)).astype(BF16)
            x_to, y_to = me.at(x=1 - me.x), me.at(y=1 - me.y)
            diag = mine.at[1 - me.x, 1 - me.y]
            send(self.part(diag, 0), self.x1.at[z], self.ss.at[0], self.rs.at[1 * me.nz + z], x_to)
            send(self.part(diag, 1), self.y1.at[z], self.ss.at[0], self.rs.at[2 * me.nz + z], y_to)
            send(self.part(mine.at[1 - me.x, me.y], 0), self.part(self.ox.at[z], 0), self.ss.at[0], self.rs.at[3 * me.nz + z], x_to)
            send(self.part(mine.at[me.x, 1 - me.y], 1), self.part(self.oy.at[z], 1), self.ss.at[0], self.rs.at[3 * me.nz + z], y_to)
        return far_first(me, event)

    def middle(self):
        me = self.me

        def event(z):
            landed(self.x1.at[z], self.ss.at[0], self.rs.at[me.nz + z], me)
            ref = self.part(self.acc.at[z, me.x, 1 - me.y], 0)
            ref[...] = add(ref, self.x1.at[z]).astype(BF16)
            send(ref, self.part(self.oy.at[z], 0), self.ss.at[0], self.rs.at[3 * me.nz + z], me.at(y=1 - me.y))
            landed(self.y1.at[z], self.ss.at[0], self.rs.at[2 * me.nz + z], me)
            ref = self.part(self.acc.at[z, 1 - me.x, me.y], 1)
            ref[...] = add(ref, self.y1.at[z]).astype(BF16)
            send(ref, self.part(self.ox.at[z], 1), self.ss.at[0], self.rs.at[3 * me.nz + z], me.at(x=1 - me.x))
        return far_first(me, event)

    def fold(self):
        me = self.me

        def event(z):
            landed(self.acc.at[z, 0], self.ss.at[0], self.rs.at[3 * me.nz + z], me)
            mine = self.acc.at[z, me.x, me.y]
            mine[...] = add(mine, self.ox.at[z], self.oy.at[z]).astype(BF16)
            self.line.event(z)
        return far_first(me, event)

    def finish(self):
        return [lambda: self.line.total(self.out)]

    def drain(self):
        me = self.me
        found = far_first(me, self.fed) if self.src is not None else []
        found.append(lambda: sent(self.acc.at[pl.ds(0, me.nz * 3 // 4)], self.ss.at[0], self.rs.at[0], me))
        return found + self.line.drain()

    def groups(self):
        begin = self.begin() if self.src is not None else []
        return dict(begin=begin, core=self.core(), middle=self.middle(), fold=self.fold(), finish=self.finish())

    @staticmethod
    def scratch(nz, rows, cols):
        buf = lambda *s: pltpu.VMEM(s + (rows, cols), BF16)
        cut = cols * 2 // 3 // 128 * 128
        return [buf(nz, 2, 2), buf(nz, 2, 2), pltpu.VMEM((nz, rows, cut), BF16), pltpu.VMEM((nz, rows, cols - cut), BF16), buf(nz), buf(nz), buf(nz),
                DMA((1 + nz,)), DMA((4 * nz,)), DMA((nz,)), DMA((1,)), DMA((1,))]


class SeqScatter:
    def __init__(self, me, src, then, acc, cbuf, oy, ss, rs, ls):
        self.me, self.src, self.then, self.acc, self.cbuf, self.oy = me, src, then, acc, cbuf, oy
        self.ss, self.rs = ss, rs
        self.load = pltpu.make_async_copy(src.at[:, :, me.c], acc, ls.at[0])

    def begin(self):
        me = self.me
        send(self.src.at[:, :, 1 - me.c], self.cbuf, self.ss.at[0], self.rs.at[0], me.at(c=1 - me.c))
        self.load.start()

    def core(self):
        me = self.me
        self.load.wait()
        landed(self.cbuf, self.ss.at[0], self.rs.at[0], me)

        @pl.loop(0, self.acc.shape[0])
        def _(i):
            for y in (0, 1):
                self.acc[i, y] = (self.acc[i, y].astype(F32) + self.cbuf[i, y].astype(F32)).astype(BF16)
        send(self.acc.at[:, 1 - me.y], self.oy, self.ss.at[1], self.rs.at[1], me.at(y=1 - me.y))

    def fold(self):
        me = self.me
        landed(self.oy, self.ss.at[0], self.rs.at[1], me)

        @pl.loop(0, self.acc.shape[0])
        def _(i):
            self.oy[i] = (self.acc[i, me.y].astype(F32) + self.oy[i].astype(F32)).astype(BF16)

    def finish(self):
        self.then(self.oy)

    def drain(self):
        sent(self.cbuf, self.ss.at[0], self.rs.at[0], self.me)
        sent(self.oy, self.ss.at[1], self.rs.at[0], self.me)

    def groups(self):
        return dict(begin=[self.begin], core=[self.core], fold=[self.fold], finish=[self.finish])

    @staticmethod
    def scratch(count, rows, cols):
        buf = lambda *s: pltpu.VMEM(s + (rows, cols), BF16)
        return [buf(count, 2), buf(count, 2), buf(count), DMA((2,)), DMA((2,)), DMA((1,))]


class Regrouped(SeqScatter):
    def __init__(self, me, dp_count, src, out, inbox, up_ss, up_rs, *rest):
        super().__init__(me, src, self.pass_on, *rest)
        self.n, self.out, self.inbox, self.up_ss, self.up_rs = dp_count, out, inbox, up_ss, up_rs

    def pass_on(self, total):
        me = self.me
        for k in range(1, self.n):
            to = lax.rem(me.dp + k, self.n)
            send(total.at[to], self.inbox.at[me.dp], self.up_ss.at[to], self.up_rs.at[me.dp], (to, me.seq))
        self.inbox[me.dp] = total[me.dp]

    def collect(self):
        cols = self.inbox.shape[2]
        for dp in range(self.n):
            pl.when(dp != self.me.dp)(lambda: landed(self.inbox.at[dp], self.up_ss.at[0], self.up_rs.at[dp], self.me))
            self.out[:, dp * cols:(dp + 1) * cols] = self.inbox[dp].astype(F32)

    def drain(self):
        super().drain()
        for k in range(1, self.n):
            sent(self.inbox.at[0], self.up_ss.at[lax.rem(self.me.dp + k, self.n)], self.up_rs.at[0], self.me)

    @staticmethod
    def scratch(count, rows, cols):
        return [pltpu.VMEM((count, rows, cols), BF16), DMA((count,)), DMA((count,))] + SeqScatter.scratch(count, rows, cols)


class SumAll:
    def __init__(self, me, ref, inbox, ss, rs):
        self.me, self.ref, self.inbox, self.ss, self.rs = me, ref, inbox, ss, rs

    def step(self, i, to):
        def begin():
            send(self.ref.at[i], self.inbox.at[i], self.ss.at[i], self.rs.at[i], to)

        def end():
            landed(self.inbox.at[i], self.ss.at[0], self.rs.at[i], self.me)
            self.ref[i + 1] = self.ref[i] + self.inbox[i]
        return begin, end

    def phases(self):
        me = self.me
        n = me.nz

        def begin_z():
            for k in range(1, n):
                to = lax.rem(me.z + k, n)
                send(self.ref.at[3], self.inbox.at[2 + k], self.ss.at[2 + k], self.rs.at[2 + k], me.at(z=to))

        def end_z():
            total = self.ref[3]
            for k in range(1, n):
                landed(self.inbox.at[2 + k], self.ss.at[0], self.rs.at[2 + k], me)
                total = total + self.inbox[2 + k]
            self.ref[4] = total

        def drain():
            for i in range(2 + n):
                sent(self.ref.at[0], self.ss.at[i], self.rs.at[0], me)
        first = self.step(0, me.at(c=1 - me.c))
        second = self.step(1, me.at(x=1 - me.x))
        third = self.step(2, me.at(y=1 - me.y))
        both = lambda one, other: (lambda: (one(), other()))
        return [[e] for e in (first[0], both(first[1], second[0]), both(second[1], third[0]), both(third[1], begin_z), end_z, drain)]


CUT, LATE_CUT = 640, 384


def laid_out(order, groups, steps):
    places, count = {}, 0
    for name, number in steps.items():
        places[name] = (count, number)
        count += number
    ahead = [[] for _ in range(count)]
    placed = [(position, name, phase) for name, phases in order.items() for phase, position in phases.items()]
    for position, name, phase in sorted(placed):
        ahead[min(count - 1, max(0, math.ceil(position)))] += groups[name][phase]
    return lambda name: ahead[places[name][0]:places[name][0] + places[name][1]]


def unpacked(packs, own_cols):
    count = packs.shape[0]
    group = 8
    rows = []
    for g in range(count // group):
        left = jnp.concatenate([packs[g * group + i] for i in range(group)], axis=1).astype(BF16)
        row = lax.broadcasted_iota(jnp.int32, (group * 128, group * own_cols), 0)
        column = lax.broadcasted_iota(jnp.int32, (group * 128, group * own_cols), 1)
        piece, place = row // 128, row % 128
        chosen = (place < own_cols) & (column == piece * own_cols + place)
        rows.append(dot(left, jnp.where(chosen, 1.0, 0.0).astype(BF16)))
    return jnp.concatenate(rows, axis=1)


def forward_kernel(dp_count, block_rows, own_cols, owner, media, pack, lat, sq, sk, sv, so, sg, sd, su,
                   wq, wk, wv, n_out, nl_out, q_out, k_out, v_out, gwo, gwu, gwd,
                   gains, lat_out, grad_hidden, do_all, stat_all, sums,
                   packs, lat_all, wo, og, dn, up, med, n, nl, q, k, v, expo, acc_f, acc, tops, stats, packed, wbuf,
                   acc_in, stat_in, nf_all, ga, act, gp, part_g, ox_g, zz_g, part_y, ox_y, zz_y,
                   own_sum, row_a, row_b, do_in, st_in, gwo_v, gwu_v, gwd_v,
                   local, ws, ms, outs, xs, xr, *sems):
    me = Here(dp_count)
    (rss, rrs, es, er), g_sems, y_sems, sems = sems[:4], sems[4:8], sems[8:12], sems[12:]
    nf_sems, do_sems, st_sems = sems[14:16], sems[16:18], sems[18:20]
    seq_count, lat_rows, width = lat_all.shape
    half = width // 2
    seq_peers = [lax.rem(me.seq + i, seq_count) for i in range(1, seq_count)]
    blocks, parts = n.shape[0] // block_rows, HEADS // PART
    media_rows = media.shape[0]
    greet_all(me, dp_count)
    gather = lambda i, src, dst, axes, halves: Gather(me, src, dst, *sems[2 * i:2 * i + 2], axes, halves)
    regroup = Regroup(me, dp_count, su, up, rss, rrs, up.shape[2])
    items = [
        Everyone(me, dp_count, pack, packs, es, er), gather(0, lat, lat_all, "yc", 0),
        gather(1, sk, wk, "zxyc", CUT), gather(2, sq, wq, "zxyc", CUT), gather(3, sv, wv, "zxyc", CUT),
        gather(4, so, wo, "zxyc", LATE_CUT), gather(5, sg, og, "zx", 0), gather(6, sd, dn, "yc", 0), regroup,
    ]
    own = [(pack, packs.at[items[0].index])]
    own += [(src, item.shard(me.z, me.x, me.y, me.c)) for src, item in zip((lat, sk, sq, sv, so, sg, sd), items[1:8])]
    own += [(regroup.columns(me.dp), regroup.piece(me.dp, me.y, me.c))]
    own = [pltpu.make_async_copy(src, dst, local.at[i]) for i, (src, dst) in enumerate(own)]
    for copy in own:
        copy.start()
    spread_nf = Gather(me, nf_all.at[me.dp], nf_all, *nf_sems, "zx", 0)
    sum_g = DpScatter(me, part_g, own_sum, ox_g, zz_g, *g_sems)
    sum_y = DpScatter(me, part_y, own_sum, ox_y, zz_y, *y_sems)
    spread_do = Gather(me, do_in.at[me.seq], do_in, *do_sems, "yc", 0)
    spread_st = Gather(me, st_in.at[me.seq], st_in, *st_sems, "yc", 0)

    lane = lax.broadcasted_iota(jnp.int32, (lat_rows, 128), 1)

    def beside(one, other):
        return jnp.where(lane < HEADS, one, pltpu.roll(other, HEADS, 1))

    def exchange(part):
        cols = pl.ds(part * half, half)
        for i, to in enumerate(seq_peers):
            send(acc.at[to, :, cols], acc_in.at[me.seq, :, cols], xs.at[part, i], xr.at[part, me.seq], (me.dp, to))
            if part == 0:
                send(packed.at[to], stat_in.at[me.seq], xs.at[2, i], xr.at[2, me.seq], (me.dp, to))

    def exchanged():
        for source in seq_peers:
            landed(stat_in.at[source], xs.at[0, 0], xr.at[2, source], me)
            for part in range(2):
                landed(acc_in.at[source, :, pl.ds(part * half, half)], xs.at[0, 0], xr.at[part, source], me)
    column = spread_nf.column()
    way = 1 - 2 * (me.z // (me.nz // 2))

    def layer(k):
        return lax.rem(me.z + way * k + me.nz, me.nz)

    def arrived(z):
        spread_nf.here(spread_nf.shard(z, 1 - me.x, me.y, me.c), FROMX, z)

    def steps_of(first, second):
        return {**{"a%d" % k: first(k) for k in range(me.nz)}, **{"b%d" % k: second(k) for k in range(me.nz)}}
    groups = dict(
        pack=dict(own=items[0].own(), arrive=items[0].arrive()),
        x=dict(send0=[lambda: exchange(0)], send1=[lambda: exchange(1)], wait=[exchanged]),
        up=dict(own=[regroup.own], column=[regroup.column], neighbours=[regroup.neighbours], sibling=[regroup.sibling]),
        g=dict(**steps_of(lambda k: [lambda: sum_g.send_x(layer(k))], lambda k: [lambda: sum_g.fold_in(layer(k))]), finish=[sum_g.finish]),
        nf=dict(own=spread_nf.own(), **steps_of(lambda k: column[2 * k - 2:2 * k], lambda k: [lambda: arrived(layer(k))])),
        y=sum_y.groups(), do=spread_do.groups(), st=spread_st.groups(),
        **dict(zip(("lat", "k", "q", "v", "o", "og", "dn"), [item.groups() for item in items[1:8]])))
    steps = blocks * parts // 2
    ahead_of = laid_out(FORWARD_ORDER, groups, dict(
        gains=1, norm=blocks - 1, latnorm=1, kproj=2, qproj=2, tops=steps, best=1, expo=steps, sums=1,
        vproj0=1, acc0=steps // 2, cast0=1, vproj1=1, acc1=steps // 2, cast1=1, fold=1, hidden=1, ga=2, ffn=me.nz, ypart=me.nz, gwd=1,
        grad=1, gwo=2, gwu=1, latout=1, end=1))

    def ahead(name):
        run(ahead_of(name)[0])

    def media_load(b):
        rows = pl.ds(pl.multiple_of(b * block_rows, block_rows), block_rows)
        slot = lax.rem(b, 2)
        return pltpu.make_async_copy(media.at[rows, :], med.at[slot], ms.at[slot])
    media_load(0).start()
    ahead("gains")
    for copy in own:
        copy.wait()
    gains[...] = unpacked(packs, own_cols)

    norm_events = ahead_of("norm")

    @pl.loop(0, blocks - 1)
    def _(b):
        run_at(b, norm_events)
        pl.when(b + 1 < blocks - 1)(lambda: media_load(b + 1).start())
        media_load(b).wait()
        u, _ = scaled_rows(med[lax.rem(b, 2)].astype(F32))
        n[pl.ds(pl.multiple_of(b * block_rows, block_rows), block_rows), :] = (u * gains[2:3, :] + gains[3:4, :]).astype(BF16)
    ahead("latnorm")
    u, _ = scaled_rows(lat_all[...].reshape(seq_count * lat_rows, width).astype(F32))
    nl[...] = (u * gains[0:1, :] + gains[1:2, :]).astype(BF16).reshape(nl.shape)
    n[pl.ds(media_rows, lat_rows), :] = nl[me.seq]
    n[pl.ds(media_rows + lat_rows, block_rows - lat_rows), :] = jnp.zeros((block_rows - lat_rows, width), BF16)

    def weight(w, i):
        return pltpu.make_async_copy(w.at[:, :, pl.ds(pl.multiple_of(i * half, 128), half)], wbuf.at[i], ws.at[i])

    def project(rows, w, out, name):
        events = ahead_of(name)
        run(events[0])
        for i in range(2):
            weight(w, i).start()

        @pl.loop(0, 2)
        def _(i):
            run_at(i, [[], events[1]])
            weight(w, i).wait()
            cols = pl.ds(pl.multiple_of(i * half, 128), half)
            out[:, cols] = dot(rows[...], wbuf[i].reshape(width, half)).astype(BF16)
    project(n, wk, k, "kproj")
    project(nl.reshape(seq_count * lat_rows, width), wq, q.reshape(seq_count * lat_rows, width), "qproj")
    mask = part_mask(lat_rows)
    key = lax.broadcasted_iota(jnp.int32, (PART * lat_rows, block_rows), 1)

    def scores(b, part, item):
        cols = pl.ds(pl.multiple_of(part * PCOLS, 128), PCOLS)
        at = pl.ds(pl.multiple_of(b * block_rows, block_rows), block_rows)
        found = dot_t(stacked(q[item, :, cols], mask), k[at, cols]) * SCALE
        return jnp.where(key < jnp.where(b == blocks - 1, lat_rows, block_rows), found, NEG)

    def replicated(stat, part):
        pieces = []
        for h in range(PART):
            column = jnp.sum(jnp.where(lane == part * PART + h, stat, 0.0), axis=-1, keepdims=True)
            pieces.append(jnp.broadcast_to(column, (lat_rows, 128)))
        return jnp.concatenate(pieces, axis=0)

    def place(stat, column, part):
        for h in range(PART):
            stat = jnp.where(lane == part * PART + h, column[h * lat_rows:(h + 1) * lat_rows], stat)
        return stat
    tops[...] = jnp.zeros_like(tops)
    top_events = ahead_of("tops")

    @pl.loop(0, steps)
    def _(i):
        b, pair = i // (parts // 2), i % (parts // 2)
        run_at(i, top_events)
        item = owner[b]
        for part in (pair * 2, pair * 2 + 1):
            tops[b, 0] = place(tops[b, 0], jnp.max(scores(b, part, item), axis=-1, keepdims=True), part)
    ahead("best")
    for i in range(seq_count):
        best = jnp.full((lat_rows, 128), NEG, F32)
        for b in range(blocks):
            best = jnp.maximum(best, jnp.where(owner[b] == i, tops[b, 0], NEG))
        stats[i, 0] = best
    expo_events = ahead_of("expo")

    @pl.loop(0, steps)
    def _(i):
        b, pair = i // (parts // 2), i % (parts // 2)
        run_at(i, expo_events)
        item = owner[b]
        for part in (pair * 2, pair * 2 + 1):
            e = jnp.exp(scores(b, part, item) - replicated(stats[item, 0], part))
            expo[b, part] = e.astype(BF16)
            tops[b, 1] = place(tops[b, 1], jnp.sum(e, axis=-1, keepdims=True), part)
    ahead("sums")
    for i in range(seq_count):
        packed[i] = beside(stats[i, 0], sum(jnp.where(owner[b] == i, tops[b, 1], 0.0) for b in range(blocks)))
    stat_in[me.seq] = packed[me.seq]
    acc_f[...] = jnp.zeros_like(acc_f)
    for part in range(2):
        ahead("vproj%d" % part)
        if part == 0:
            for i in range(2):
                weight(wv, i).start()
        weight(wv, part).wait()
        cols = pl.ds(part * half, half)
        v[:, cols] = dot(n[...], wbuf[part].reshape(width, half)).astype(BF16)
        acc_events = ahead_of("acc%d" % part)

        @pl.loop(0, steps // 2)
        def _(b):
            run_at(b, acc_events)
            item = owner[b]
            for head_part in range(part * parts // 2, (part + 1) * parts // 2):
                pcols = pl.ds(head_part * PCOLS, PCOLS)
                at = pl.ds(pl.multiple_of(b * block_rows, block_rows), block_rows)
                term = unstacked(dot(expo[b, head_part], v[at, pcols]), mask, lat_rows)
                for j in range(seq_count):
                    acc_f[j, :, pcols] += jnp.where(item == j, term, 0.0)
        ahead("cast%d" % part)
        acc[:, :, cols] = acc_f[:, :, cols].astype(BF16)
        acc_in[me.seq, :, cols] = acc[me.seq, :, cols]
    saves = [(n, n_out), (nl, nl_out), (q, q_out), (k, k_out), (v, v_out)]
    saves = [pltpu.make_async_copy(src, dst, outs.at[i]) for i, (src, dst) in enumerate(saves)]
    for copy in saves:
        copy.start()
    ahead("fold")
    tops_in = [stat_in[s] for s in range(seq_count)]
    best = functools.reduce(jnp.maximum, tops_in)
    weights = [jnp.exp(top - best) for top in tops_in]
    total = sum(w * pltpu.roll(top, 128 - HEADS, 1) for w, top in zip(weights, tops_in))
    total = jnp.where(lane < HEADS, total, 1.0)
    spread = head_columns(width)
    attended = sum(exact(w / total, spread) * acc_in[s].astype(F32) for s, w in enumerate(weights))
    row_a[...] = attended
    lse = best + jnp.log(total)
    ahead("hidden")
    hidden = lat_all[me.seq].astype(F32) + dot(attended.astype(BF16), wo[...].reshape(width, width))
    row_b[...] = hidden
    scaled, _ = scaled_rows(hidden)
    nf_all[me.dp] = (scaled * gains[4:5, :] + gains[5:6, :]).astype(BF16)
    all_rows = dp_count * lat_rows
    hidden_cols = gp.shape[1]
    og_all = lambda: og[...].reshape(all_rows, width)
    tile = hidden_cols // 2
    per = seq_count // 2
    ga_events = ahead_of("ga")

    @pl.loop(0, 2)
    def _(t):
        run_at(t, ga_events)
        at = pl.ds(pl.multiple_of(t * tile, 128), tile)
        ga[:, at] = dot_t(og_all(), dn[pl.ds(t * per, per)].reshape(tile, width))
    ffn_events = ahead_of("ffn")
    pair_rows = 2 * lat_rows

    def pair(z):
        return pl.ds(2 * z, 2), pl.ds(pl.multiple_of(z * pair_rows, pair_rows), pair_rows)

    @pl.loop(0, me.nz)
    def _(k):
        run_at(k, ffn_events)
        both, at = pair(layer(k))
        pre = dot(nf_all[both].reshape(pair_rows, width), up[...].reshape(width, hidden_cols))
        phi = 0.5 * (1.0 + lax.erf(pre * 0.7071067811865476))
        act[at, :] = (pre * phi).astype(BF16)
        slope = phi + pre * jnp.exp(pre * pre * -0.5) * 0.3989422804014327
        gp[at, :] = (ga[at, :] * slope).astype(BF16)
        part_g[both] = dot_t(gp[at, :], up[...].reshape(width, hidden_cols)).astype(BF16).reshape(2, lat_rows, width)
    y_events = ahead_of("ypart")

    @pl.loop(0, me.nz)
    def _(k):
        run_at(k, y_events)
        both, at = pair(layer(k))
        part_y[both] = dot(act[at, :], dn[...].reshape(hidden_cols, width)).astype(BF16).reshape(2, lat_rows, width)
    ahead("gwd")
    gwd_v[...] = t_dot(act[...], og_all()).astype(BF16)
    save_d = pltpu.make_async_copy(gwd_v, gwd, outs.at[5])
    save_d.start()
    ahead("grad")
    gathered = own_sum[...]
    scaled, inverse = scaled_rows(row_b[...])
    sums[...] = jnp.zeros_like(sums)
    sums[0:1, :] = jnp.sum(gathered * scaled, axis=0, keepdims=True)
    sums[1:2, :] = jnp.sum(gathered, axis=0, keepdims=True)
    grad = og[me.dp].astype(F32) + norm_back(gathered, scaled, inverse, gains[4:5, :])
    grad_hidden[...] = grad
    low = grad.astype(BF16)
    grad_att = dot_t(low, wo[...].reshape(width, width)).astype(BF16)
    do_in[me.seq] = grad_att
    st_in[me.seq] = beside(lse, exact_t(grad_att.astype(F32) * row_a[...], spread))
    save_o = []
    for i in range(2):
        cols = pl.ds(i * half, half)
        run(ahead_of("gwo")[i])
        if i:
            save_o[0].wait()
        gwo_v[...] = t_dot(row_a[...].astype(BF16), low[:, i * half:(i + 1) * half]).astype(BF16)
        save_o.append(pltpu.make_async_copy(gwo_v, gwo.at[:, cols], outs.at[6 + i]))
        save_o[-1].start()
    ahead("gwu")
    gwu_v[...] = t_dot(nf_all[...].reshape(all_rows, width), gp[...]).astype(BF16)
    save_u = pltpu.make_async_copy(gwu_v, gwu, outs.at[8])
    save_u.start()
    ahead("latout")
    lat_out[...] = (row_b[...] + own_sum[...]).astype(BF16)
    ahead("end")
    do_all[...] = do_in[...]
    stat_all[...] = st_in[...]
    for i in range(len(seq_peers)):
        for part in range(2):
            sent(acc_in.at[0, :, pl.ds(part * half, half)], xs.at[part, i], xr.at[0, 0], me)
        sent(stat_in.at[0], xs.at[2, i], xr.at[0, 0], me)
    for item in items[:8]:
        run(item.drain())
    regroup.drain()
    for item in (spread_nf, sum_g, sum_y, spread_do, spread_st):
        run(item.drain())
    for copy in saves + save_o[1:] + [save_d, save_u]:
        copy.wait()


def forward(dp_count, owner, media, pack, lat, sq, sk, sv, so, sg, sd, su, block_rows, own_cols):
    nz = dp_count // 2
    rows, width = lat.shape
    items, count = 4, dp_count * 4
    hidden = su.shape[1] // dp_count
    total = media.shape[0] + block_rows
    blocks = total // block_rows
    parts = HEADS // PART
    all_rows = dp_count * rows
    shape = jax.ShapeDtypeStruct
    buf = lambda *s: pltpu.VMEM(s, BF16)
    flt = lambda *s: pltpu.VMEM(s, F32)
    square = shape((count, width // count, width), BF16)
    stat = (items, rows, 128)
    line = [buf(nz, rows, width), buf(nz, rows, width)]
    return pl.pallas_call(
        functools.partial(forward_kernel, dp_count, block_rows, own_cols),
        out_shape=(
            square, square, square, shape((total, width), BF16), shape((items, rows, width), BF16), shape((items, rows, width), BF16),
            shape((total, width), BF16), shape((total, width), BF16),
            shape((width, width), BF16), shape((width, hidden), BF16), shape((hidden, width), BF16),
            shape((8, width), F32), shape((rows, width), BF16), shape((rows, width), F32),
            shape((items, rows, width), BF16), shape(stat, F32), shape((8, width), F32),
        ),
        in_specs=[pl.BlockSpec(memory_space=pltpu.SMEM)] + [ANY] * 10,
        out_specs=tuple([ANY] * 11 + [VMEM] * 6),
        scratch_shapes=[
            flt(count, 8, 128), buf(items, rows, width), buf(count, width // count, width), buf(dp_count, rows, width),
            buf(items, hidden // items, width), buf(count, width // count, hidden), buf(2, block_rows, width),
            buf(total, width), buf(items, rows, width), buf(items, rows, width), buf(total, width), buf(total, width),
            buf(blocks, parts, PART * rows, block_rows), flt(items, rows, width), buf(items, rows, width),
            flt(blocks, 2, rows, 128), flt(items, 1, rows, 128), flt(*stat), buf(2, count, width // count, width // 2),
            buf(items, rows, width), flt(*stat), buf(dp_count, rows, width), flt(all_rows, hidden), buf(all_rows, hidden), buf(all_rows, hidden),
            buf(dp_count, rows, width), *line, buf(dp_count, rows, width), *line,
            flt(rows, width), flt(rows, width), flt(rows, width), buf(items, rows, width), flt(*stat),
            buf(width, width // 2), buf(width, hidden), buf(hidden, width),
            DMA((9,)), DMA((2,)), DMA((2,)), DMA((9,)), DMA((3, items)), DMA((3, items)),
            *Regroup.semaphores(dp_count), DMA((1,)), DMA((1,)), *DpScatter.semaphores(nz), *DpScatter.semaphores(nz),
            *[sem for axes in ("yc", "zxyc", "zxyc", "zxyc", "zxyc", "zx", "yc", "zx", "yc", "yc") for sem in Gather.semaphores(axes, nz)],
        ],
        compiler_params=pltpu.CompilerParams(collective_id=1, has_side_effects=True, vmem_limit_bytes=WIDE),
    )(owner, media, pack, lat, sq, sk, sv, so, sg, sd, su)


def backward_kernel(dp_count, block_rows, owner, lat, grad_hidden, gains, sums_ffn,
                    n_in, nl_in, q_in, k_in, v_in, do_in, stat_in, gwo, gwu, gwd, media, wq, wk, wv,
                    media_grad, lat_grad, sums, out_q, out_k, out_v, out_o, out_up, out_dn,
                    n, nl, q, do, k, v, stats, dq, g, gq, med, stage, sums_ref, *scratch):
    me = Here(dp_count)
    items, lat_rows, width = q.shape
    rows = k.shape[0]
    media_rows = media.shape[0]
    blocks, parts = rows // block_rows, HEADS // PART
    scratch = list(scratch)
    take = lambda count: [scratch.pop(0) for _ in range(count)]
    o_s, fulls, up_s, dn_s, lat_s, small = take(12), [take(12) for _ in range(3)], take(9), take(6), take(6), take(4)
    in_sem, tile_sem, med_sem, out_sem = scratch
    loads = [(stat_in, stats), (q_in, q), (do_in, do), (k_in, k), (v_in, v), (n_in, n), (nl_in, nl)]
    loads = [pltpu.make_async_copy(src, dst, in_sem.at[i]) for i, (src, dst) in enumerate(loads)]
    for load in loads:
        load.start()
    all_sum = SumAll(me, *small)

    def latents(total):
        scaled, inverse = scaled_rows(lat[...].astype(F32))
        grad = total[0].astype(F32)
        lat_grad[...] = grad_hidden[...] + norm_back(grad, scaled, inverse, gains[0:1, :])
        first = small[0]
        first[0, 0:1, :] = jnp.sum(grad * scaled, axis=0, keepdims=True)
        first[0, 1:2, :] = jnp.sum(grad, axis=0, keepdims=True)
        first[0, 2:4, :] = sums_ref[0:2, :]
        first[0, 4:6, :] = sums_ffn[0:2, :]
        first[0, 6:8, :] = jnp.zeros_like(sums_ffn[0:2, :])

    def down(total):
        out_dn[...] = total[0].astype(F32)
    f_o = Scatter(me, gwo, out_o, o_s[:7], *o_s[7:])
    f_k, f_v, f_q = [Scatter(me, None, out, f[:7], *f[7:]) for out, f in zip((out_k, out_v, out_q), fulls)]
    up, dn = Regrouped(me, dp_count, gwu, out_up, *up_s), SeqScatter(me, gwd, down, *dn_s)
    lat_item = SeqScatter(me, gq, latents, *lat_s)
    greet(dp_peers(me, dp_count) + [me.at(y=1 - me.y), me.at(c=1 - me.c)])
    mask = part_mask(lat_rows)
    lane = lax.broadcasted_iota(jnp.int32, (lat_rows, 128), 1)
    key = lax.broadcasted_iota(jnp.int32, (PART * lat_rows, block_rows), 1)
    held = pl.ds(0, items * lat_rows)
    g[held, :] = jnp.zeros((items * lat_rows, width), F32)

    def replicated(stat, part, base=0):
        pieces = []
        for h in range(PART):
            column = jnp.sum(jnp.where(lane == base + part * PART + h, stat, 0.0), axis=-1, keepdims=True)
            pieces.append(jnp.broadcast_to(column, (lat_rows, 128)))
        return jnp.concatenate(pieces, axis=0)

    def block(b, part, item):
        cols = pl.ds(pl.multiple_of(part * PCOLS, 128), PCOLS)
        at = pl.ds(pl.multiple_of(b * block_rows, block_rows), block_rows)
        query, grad = stacked(q[item, :, cols], mask), stacked(do[item, :, cols], mask)
        keys, values = k[at, cols], v[at, cols]
        lse, delta = replicated(stats[item], part), replicated(stats[item], part, HEADS)
        prob = jnp.exp(dot_t(query, keys) * SCALE - lse)
        prob = jnp.where(key < jnp.where(b == blocks - 1, lat_rows, block_rows), prob, 0.0)
        score = (prob * (dot_t(grad, values) - delta)).astype(BF16)
        term = unstacked(dot(score, keys), mask, lat_rows) * SCALE
        k[at, cols] = (t_dot(score, query) * SCALE).astype(BF16)
        v[at, cols] = t_dot(prob.astype(BF16), grad).astype(BF16)
        for i in range(items):
            g[i * lat_rows:(i + 1) * lat_rows, cols] += jnp.where(item == i, term, 0.0)
    steps = blocks * parts // 2
    span = rows // 2
    turns = (span, 0)
    tile = items * lat_rows
    tiles = width // tile
    norms = [(min(media_rows, start + span) - start) // lat_rows for start in turns]
    groups = dict(
        o=f_o.groups(), k=f_k.groups(), v=f_v.groups(), q=f_q.groups(), lat=lat_item.groups(), dn=dn.groups(),
        up=dict(collect=[up.collect], **up.groups()), sum=dict(zip(("s0", "s1", "s2", "s3", "s4"), all_sum.phases())))
    ahead_of = laid_out(BACK_ORDER, groups, dict(
        attention=steps, dq=1, gwk=me.nz, gwv=me.nz, gwq=me.nz, tiles0=tiles, norms0=norms[0], tiles1=tiles, norms1=norms[1], end=1))
    for load in loads[:5]:
        load.wait()

    shares = ahead_of("attention")

    @pl.loop(0, steps)
    def _(i):
        b, pair = i // (parts // 2), i % (parts // 2)
        run_at(i, shares)
        item = owner[b]
        block(b, pair * 2, item)
        block(b, pair * 2 + 1, item)
    run(ahead_of("dq")[0])
    dq[...] = g[held, :].astype(BF16)
    for load in loads[5:]:
        load.wait()
    layer = width // me.nz

    def produce(full, left, right, name):
        shares = ahead_of(name)

        @pl.loop(0, me.nz)
        def _(t):
            run_at(t, shares)
            slot = lax.rem(t, 2)
            z = lax.rem(me.z + 1 + t, me.nz)
            pl.when(t >= 2)(lambda: full.fed(lax.rem(me.z + t - 1, me.nz)))
            cols = pl.ds(pl.multiple_of(z * layer, 128), layer)
            found = t_dot(left(cols), right()).astype(BF16)
            stage[slot] = found.reshape(stage.shape[1:])
            full.feed(stage.at[slot], z)
        full.fed(lax.rem(me.z + me.nz - 1, me.nz))
        full.fed(me.z)
    n_cols = lambda cols: n[:, :, cols].reshape(rows, layer)
    produce(f_k, n_cols, lambda: k[...], "gwk")
    produce(f_v, n_cols, lambda: v[...], "gwv")
    produce(f_q, lambda cols: nl[:, :, cols].reshape(items * lat_rows, layer), lambda: dq[...], "gwq")
    per = items
    slots = ((n.at[pl.ds(0, per)], n.at[pl.ds(per, per)], n.at[pl.ds(2 * per, per)]), (q, nl, do))

    def fetch(t, slot):
        return [pltpu.make_async_copy(w.at[pl.ds(t * per, per)], dst, tile_sem.at[slot, i]) for i, (w, dst) in enumerate(zip((wk, wv, wq), slots[slot]))]

    def media_load(i, start):
        at = pl.ds(pl.multiple_of(start + i * lat_rows, lat_rows), lat_rows)
        slot = lax.rem(i, 2)
        return pltpu.make_async_copy(media.at[at, :], med.at[slot], med_sem.at[slot])
    sums_ref[...] = jnp.zeros_like(sums_ref)
    for turn, start in enumerate(turns):
        shares = ahead_of("tiles%d" % turn)
        for copy in fetch(0, 0) + fetch(1, 1):
            copy.start()

        @pl.loop(0, tiles // 2)
        def _(pair):
            for slot in (0, 1):
                t = pair * 2 + slot
                run_at(t, shares)
                for copy in fetch(t, slot):
                    copy.wait()
                at = pl.ds(pl.multiple_of(t * tile, 128), tile)
                w_k, w_v, w_q = [ref[...].reshape(tile, width) for ref in slots[slot]]
                grad = dot_t(k[pl.ds(start, span), :], w_k) + dot_t(v[pl.ds(start, span), :], w_v)
                g[:, at] = grad
                if turn == 0:
                    own = dot_t(dq[...], w_q)
                    extra = grad[media_rows - start:media_rows - start + lat_rows]
                    for i in range(items):
                        term = own[i * lat_rows:(i + 1) * lat_rows]
                        gq[0, i // 2, i % 2, :, at] = jnp.where(me.seq == i, term + extra, term).astype(BF16)

                @pl.when(t + 2 < tiles)
                def _():
                    for copy in fetch(t + 2, slot):
                        copy.start()
        count = norms[turn]
        norm_shares = ahead_of("norms%d" % turn)
        media_load(0, start).start()

        def out_copy(first, length):
            at = pl.ds(pl.multiple_of(start + first, lat_rows), length)
            return pltpu.make_async_copy(g.at[pl.ds(pl.multiple_of(first, lat_rows), length), :], media_grad.at[at, :], out_sem)

        @pl.loop(0, count)
        def _(i):
            run_at(i, norm_shares)
            pl.when(i + 1 < count)(lambda: media_load(i + 1, start).start())
            media_load(i, start).wait()
            at = pl.ds(pl.multiple_of(i * lat_rows, lat_rows), lat_rows)
            u, inverse = scaled_rows(med[lax.rem(i, 2)].astype(F32))
            grad = g[at, :]
            g[at, :] = norm_back(grad, u, inverse, gains[2:3, :])
            out_copy(i * lat_rows, lat_rows).start()
            sums_ref[0:1, :] += jnp.sum(grad * u, axis=0, keepdims=True)
            sums_ref[1:2, :] += jnp.sum(grad, axis=0, keepdims=True)
        out_copy(0, count * lat_rows).wait()
    run(ahead_of("end")[0])
    sums[...] = small[0][4]
    for item in (f_o, f_k, f_v, f_q):
        run(item.drain())
    for item in (up, dn, lat_item):
        item.drain()
    run(all_sum.phases()[-1])


def backward(dp_count, owner, lat, grad_hidden, gains, sums_ffn, n, nl, q, k, v, do_all, stats, gwo, gwu, gwd, media, wq, wk, wv, block_rows):
    nz = dp_count // 2
    items, lat_rows, width = q.shape
    rows = n.shape[0]
    hidden = gwu.shape[1]
    count = dp_count * 4
    shape = jax.ShapeDtypeStruct
    buf = lambda *s: pltpu.VMEM(s, BF16)
    flt = lambda *s: pltpu.VMEM(s, F32)
    pieces = lambda w: w.reshape(width // lat_rows, lat_rows, width)
    arrays = (owner, lat, grad_hidden, gains, sums_ffn, n.reshape(rows // lat_rows, lat_rows, width), nl, q, k, v, do_all, stats,
              gwo.reshape(dp_count, 2, 2, width // count, width),
              gwu.reshape(dp_count, 2, 2, width // count, hidden), gwd.reshape(1, 2, 2, hidden // 4, width),
              media, pieces(wq), pieces(wk), pieces(wv))
    return pl.pallas_call(
        functools.partial(backward_kernel, dp_count, block_rows),
        out_shape=(
            shape(media.shape, F32), shape((lat_rows, width), F32), shape((8, width), F32), *[shape((width // count, width), F32)] * 4,
            shape((width // count, hidden * dp_count), F32), shape((hidden // 4, width), F32),
        ),
        in_specs=[pl.BlockSpec(memory_space=pltpu.SMEM)] + [VMEM] * 4 + [ANY] * 14,
        out_specs=tuple([ANY] + [VMEM] * 8),
        scratch_shapes=[
            buf(rows // lat_rows, lat_rows, width), buf(items, lat_rows, width), buf(items, lat_rows, width), buf(items, lat_rows, width),
            buf(rows, width), buf(rows, width), flt(*stats.shape), buf(items * lat_rows, width), flt(rows // 2, width),
            buf(1, 2, 2, lat_rows, width), buf(2, lat_rows, width), buf(2, 2, 2, 2, width // count, width), flt(8, width),
            *Scatter.scratch(nz, width // count, width), *(Scatter.scratch(nz, width // count, width) * 3), *Regrouped.scratch(dp_count, width // count, hidden),
            *SeqScatter.scratch(1, hidden // 4, width), *SeqScatter.scratch(1, lat_rows, width),
            flt(5, 8, width), flt(2 + nz, 8, width), DMA((2 + nz,)), DMA((2 + nz,)),
            DMA((7,)), DMA((2, 3)), DMA((2,)), DMA,
        ],
        compiler_params=pltpu.CompilerParams(collective_id=2, has_side_effects=True, vmem_limit_bytes=WIDE),
    )(*arrays)


def copy_kernel(*refs):
    n = (len(refs) - 2) // 3
    arrays, outs, held, first, second = refs[:n], refs[n:2 * n], refs[2 * n:3 * n], refs[-2], refs[-1]
    ins = [pltpu.make_async_copy(arrays[i], held[i], first.at[i]) for i in range(n)]
    backs = [pltpu.make_async_copy(held[i], outs[i], second.at[i]) for i in range(n)]
    for copy in ins:
        copy.start()
    for copy, after in zip(ins, backs):
        copy.wait()
        after.start()
    for copy in backs:
        copy.wait()


def copied(*arrays):
    n = len(arrays)
    return pl.pallas_call(
        copy_kernel, out_shape=tuple(jax.ShapeDtypeStruct(a.shape, a.dtype) for a in arrays),
        in_specs=[ANY] * n, out_specs=tuple([ANY] * n),
        scratch_shapes=[*[pltpu.VMEM(a.shape, a.dtype) for a in arrays], DMA((n,)), DMA((n,))],
        compiler_params=pltpu.CompilerParams(vmem_limit_bytes=WIDE),
    )(*arrays)


def local_fast(
    media, latents, out_grad, frame_counts, block_position, w_query, w_key, w_value, w_out, w_up, w_down,
    gain_lat, shift_lat, gain_media, shift_media, gain_ffn, shift_ffn,
):
    dp_count, seq_count = lax.axis_size("dp"), lax.axis_size("seq")
    seq = lax.axis_index("seq")
    blocks, block_rows, width = media.shape
    items, lat_rows = seq_count, latents.shape[1]
    own_cols = gain_lat.shape[0]
    ends = FRAME_BLOCKS * jnp.cumsum(frame_counts[0])
    position = lax.dynamic_slice_in_dim(block_position[0], seq * blocks, blocks)
    owner = jnp.sum((ends[None, :] <= position[:, None]).astype(jnp.int32), axis=1)
    owner = jnp.concatenate([owner, seq[None]])
    vectors = jnp.stack([gain_lat, shift_lat, gain_media, shift_media, gain_ffn, shift_ffn]).astype(F32)
    pack = jnp.pad(vectors, ((0, 2), (0, 128 - own_cols)))
    lat, og = latents.reshape(lat_rows, width), out_grad.reshape(lat_rows, width)
    med = media.reshape(-1, width)
    (wq, wk, wv, n, nl, q, k, v, gwo, gwu, gwd, gains, lat_out, grad_hidden, do_all, stat_all, sums_ffn) = forward(
        dp_count, owner, med, pack, lat, w_query, w_key, w_value, w_out, og, w_down, w_up, block_rows, own_cols)
    wq, wk, wv = [w.reshape(width, width) for w in (wq, wk, wv)]
    media_grad, lat_grad, sums, out_q, out_k, out_v, out_o, out_up, out_dn = backward(
        dp_count, owner, lat, grad_hidden, gains, sums_ffn, n, nl, q, k, v, do_all, stat_all, gwo, gwu, gwd, med, wq, wk, wv, block_rows)
    place = (lax.axis_index("dp") * seq_count + seq) * own_cols
    own = lax.dynamic_slice_in_dim(sums, place, own_cols, axis=1)
    media_grad, lat_out, lat_grad, *grads = copied(media_grad, lat_out, lat_grad, out_q, out_k, out_v, out_o, out_up, out_dn)
    return (lat_out.reshape(latents.shape), lat_grad.reshape(latents.shape), media_grad.reshape(media.shape), *grads, *[own[i] for i in range(6)])


def fits(mesh):
    return mesh.shape["seq"] == 4 and mesh.shape["dp"] % 2 == 0 and 1536 % (mesh.shape["dp"] * 64) == 0


def norm_forward(rows, gain, shift):
    mean = jnp.mean(rows, axis=-1, keepdims=True)
    centred = rows - mean
    variance = jnp.mean(centred * centred, axis=-1, keepdims=True)
    inverse = lax.rsqrt(variance + EPS)
    scaled = centred * inverse
    return (scaled * gain + shift, scaled, inverse)


def norm_backward(incoming, scaled, inverse, gain):
    inner = incoming * gain
    first = jnp.mean(inner, axis=-1, keepdims=True)
    second = jnp.mean(inner * scaled, axis=-1, keepdims=True)
    return (
        inverse * (inner - first - scaled * second),
        jnp.sum(incoming * scaled, axis=0),
        jnp.sum(incoming, axis=0),
    )


def matmul(left, right):
    return jnp.dot(left, right, preferred_element_type=jnp.float32)


def matmul_left_t(left, right):
    return lax.dot_general(
        left, right, (((0,), (0,)), ((), ())), preferred_element_type=jnp.float32
    )


def matmul_right_t(left, right):
    return lax.dot_general(
        left, right, (((1,), (1,)), ((), ())), preferred_element_type=jnp.float32
    )


def swap_rows(stat):
    return jnp.swapaxes(stat, 1, 2)[..., None]


def fold_sources(tops, totals, accums):
    best = jnp.max(tops, axis=0)
    factor = jnp.exp(tops - best[None])
    total = jnp.sum(factor * totals, axis=0)
    width = accums.shape[-1]
    spread = jnp.repeat(jnp.swapaxes(factor, 2, 3), width // factor.shape[2], axis=3)
    return (best, total, jnp.sum(accums * spread, axis=0))


def local(
    media,
    latents,
    out_grad,
    frame_counts,
    block_position,
    w_query,
    w_key,
    w_value,
    w_out,
    w_up,
    w_down,
    gain_lat,
    shift_lat,
    gain_media,
    shift_media,
    gain_ffn,
    shift_ffn,
):
    gathered = (
        lax.all_gather(w_query, ("dp", "seq"), axis=0, tiled=True),
        lax.all_gather(w_key, ("dp", "seq"), axis=0, tiled=True),
        lax.all_gather(w_value, ("dp", "seq"), axis=0, tiled=True),
        lax.all_gather(w_out, ("dp", "seq"), axis=0, tiled=True),
        lax.all_gather(w_up, ("dp", "seq"), axis=0, tiled=True),
        lax.all_gather(w_down, ("dp", "seq"), axis=0, tiled=True),
        lax.all_gather(gain_lat, ("dp", "seq"), axis=0, tiled=True),
        lax.all_gather(shift_lat, ("dp", "seq"), axis=0, tiled=True),
        lax.all_gather(gain_media, ("dp", "seq"), axis=0, tiled=True),
        lax.all_gather(shift_media, ("dp", "seq"), axis=0, tiled=True),
        lax.all_gather(gain_ffn, ("dp", "seq"), axis=0, tiled=True),
        lax.all_gather(shift_ffn, ("dp", "seq"), axis=0, tiled=True),
    )
    full_query, full_key, full_value, full_out, full_up, full_down = gathered[:6]
    lat_gain, lat_shift, med_gain, med_shift, ffn_gain, ffn_shift = [
        piece.astype(jnp.float32) for piece in gathered[6:]
    ]
    seq_rank = lax.axis_index("seq")
    seq_count = lax.axis_size("seq")
    blocks, block_rows, width = media.shape
    local_items, lat_rows, _ = latents.shape
    group_items = frame_counts.shape[1]
    heads = HEADS
    head_size = HEAD_DIM
    score_scale = head_size ** (-0.5)
    ends = FRAME_BLOCKS * jnp.cumsum(frame_counts[0])
    position = lax.dynamic_slice_in_dim(block_position[0], seq_rank * blocks, blocks)
    owner_item = jnp.sum((ends[None, :] <= position[:, None]).astype(jnp.int32), axis=1)
    member = (owner_item[:, None] == jnp.arange(group_items, dtype=jnp.int32)[None, :]).astype(
        jnp.float32
    )
    lat_input = latents.astype(jnp.float32).reshape(-1, width)
    normed_lat, scaled_lat, inverse_lat = norm_forward(lat_input, lat_gain, lat_shift)
    normed_lat = normed_lat.astype(jnp.bfloat16)
    query = matmul(normed_lat, full_query).astype(jnp.bfloat16)
    key_lat = (
        matmul(normed_lat, full_key)
        .astype(jnp.bfloat16)
        .reshape(local_items, lat_rows, heads, head_size)
    )
    value_lat = (
        matmul(normed_lat, full_value)
        .astype(jnp.bfloat16)
        .reshape(local_items, lat_rows, heads, head_size)
    )
    query_all = lax.all_gather(
        query.reshape(local_items, lat_rows, width), "seq", axis=0, tiled=True
    )
    med_input = media.astype(jnp.float32).reshape(-1, width)
    normed_med, scaled_med, inverse_med = norm_forward(med_input, med_gain, med_shift)
    normed_med = normed_med.astype(jnp.bfloat16)

    def media_keys(weight_key, weight_value):
        keys_out = (
            matmul(normed_med, weight_key)
            .astype(jnp.bfloat16)
            .reshape(blocks, block_rows, heads, head_size)
        )
        values_out = (
            matmul(normed_med, weight_value)
            .astype(jnp.bfloat16)
            .reshape(blocks, block_rows, heads, head_size)
        )
        return (keys_out, values_out)

    key_med, value_med = media_keys(full_key, full_value)
    query_blk = query_all[owner_item].reshape(blocks, lat_rows, heads, head_size)
    scores_med = (
        jnp.einsum("bqhd,bkhd->bhqk", query_blk, key_med, preferred_element_type=jnp.float32)
        * score_scale
    )
    block_top = jnp.max(scores_med, axis=-1)
    expo_med = jnp.exp(scores_med - block_top[..., None])
    expo_med_low = expo_med.astype(jnp.bfloat16)
    local_top = jnp.max(jnp.where(member.T[:, :, None, None] > 0, block_top[None], NEG), axis=1)
    to_local = jnp.exp(block_top - local_top[owner_item])
    local_total = jnp.einsum(
        "bi,bhq->ihq", member, to_local * jnp.sum(expo_med, axis=-1), precision=HIGH
    )
    accum_blk = jnp.einsum(
        "bhqk,bkhd->bqhd", expo_med_low, value_med, preferred_element_type=jnp.float32
    ) * swap_rows(to_local)
    local_accum = jnp.einsum("bi,bqhd->iqhd", member, accum_blk, precision=HIGH).reshape(
        group_items, lat_rows, width
    )
    part_top, part_total, part_accum = (
        lax.all_to_all(local_top, "seq", split_axis=0, concat_axis=0, tiled=True),
        lax.all_to_all(local_total, "seq", split_axis=0, concat_axis=0, tiled=True),
        lax.all_to_all(local_accum, "seq", split_axis=0, concat_axis=0, tiled=True),
    )
    top_own, total_own, accum_flat = fold_sources(
        part_top.reshape(seq_count, local_items, heads, lat_rows),
        part_total.reshape(seq_count, local_items, heads, lat_rows),
        part_accum.reshape(seq_count, local_items, lat_rows, width),
    )
    med_top = lax.all_gather(top_own, "seq", axis=0, tiled=True)
    accum_own = accum_flat.reshape(local_items, lat_rows, heads, head_size)
    query_lat = query.reshape(local_items, lat_rows, heads, head_size)
    scores_lat = (
        jnp.einsum("iqhd,ikhd->ihqk", query_lat, key_lat, preferred_element_type=jnp.float32)
        * score_scale
    )
    lat_top = jnp.max(scores_lat, axis=-1)
    expo_lat = jnp.exp(scores_lat - lat_top[..., None])
    expo_lat_low = expo_lat.astype(jnp.bfloat16)
    item_top = jnp.maximum(top_own, lat_top)
    media_weight = jnp.exp(top_own - item_top)
    lat_weight = jnp.exp(lat_top - item_top)
    item_total = total_own * media_weight + lat_weight * jnp.sum(expo_lat, axis=-1)
    inverse_total = 1.0 / item_total
    accum_lat = jnp.einsum(
        "ihqk,ikhd->iqhd", expo_lat_low, value_lat, preferred_element_type=jnp.float32
    ) * swap_rows(lat_weight)
    attended = (accum_own * swap_rows(media_weight) + accum_lat) * swap_rows(inverse_total)
    attended_low = attended.reshape(-1, width).astype(jnp.bfloat16)
    hidden = lat_input + matmul(attended_low, full_out)
    normed_ffn, scaled_ffn, inverse_ffn = norm_forward(hidden, ffn_gain, ffn_shift)
    normed_ffn = normed_ffn.astype(jnp.bfloat16)
    pre_act = matmul(normed_ffn, full_up)
    activated, gelu_back = jax.vjp(partial(jax.nn.gelu, approximate=False), pre_act)
    activated = activated.astype(jnp.bfloat16)
    result = hidden + matmul(activated, full_down)
    latents_out = result.astype(jnp.bfloat16).reshape(latents.shape)
    again = (
        lax.all_gather(w_query, ("dp", "seq"), axis=0, tiled=True),
        lax.all_gather(w_key, ("dp", "seq"), axis=0, tiled=True),
        lax.all_gather(w_value, ("dp", "seq"), axis=0, tiled=True),
        lax.all_gather(w_out, ("dp", "seq"), axis=0, tiled=True),
        lax.all_gather(w_up, ("dp", "seq"), axis=0, tiled=True),
        lax.all_gather(w_down, ("dp", "seq"), axis=0, tiled=True),
        lax.all_gather(gain_lat, ("dp", "seq"), axis=0, tiled=True),
        lax.all_gather(shift_lat, ("dp", "seq"), axis=0, tiled=True),
        lax.all_gather(gain_media, ("dp", "seq"), axis=0, tiled=True),
        lax.all_gather(shift_media, ("dp", "seq"), axis=0, tiled=True),
        lax.all_gather(gain_ffn, ("dp", "seq"), axis=0, tiled=True),
        lax.all_gather(shift_ffn, ("dp", "seq"), axis=0, tiled=True),
    )
    back_query, back_key, back_value, back_out, back_up, back_down = again[:6]
    grad_rows = out_grad.reshape(-1, width)
    cotangent = grad_rows.astype(jnp.float32)
    grad_down = matmul_left_t(activated, grad_rows)
    grad_act = matmul_right_t(grad_rows, back_down)
    grad_pre = gelu_back(grad_act)[0].astype(jnp.bfloat16)
    grad_up = matmul_left_t(normed_ffn, grad_pre)
    grad_normed_ffn = matmul_right_t(grad_pre, back_up)
    grad_hidden_norm, grad_gain_ffn, grad_shift_ffn = norm_backward(
        grad_normed_ffn, scaled_ffn, inverse_ffn, ffn_gain
    )
    grad_hidden = cotangent + grad_hidden_norm
    grad_hidden_low = grad_hidden.astype(jnp.bfloat16)
    grad_out = matmul_left_t(attended_low, grad_hidden_low)
    grad_att = matmul_right_t(grad_hidden_low, back_out).astype(jnp.bfloat16)
    grad_att_heads = grad_att.reshape(local_items, lat_rows, heads, head_size)
    delta = jnp.einsum(
        "iqhd,iqhd->ihq", grad_att_heads.astype(jnp.float32), attended, precision=HIGH
    )
    media_factor = media_weight * inverse_total
    grad_att_all = lax.all_gather(
        grad_att.reshape(local_items, lat_rows, width), "seq", axis=0, tiled=True
    )
    factor_all, delta_all = (
        lax.all_gather(media_factor, "seq", axis=0, tiled=True),
        lax.all_gather(delta, "seq", axis=0, tiled=True),
    )
    key_med, value_med = media_keys(back_key, back_value)
    grad_blk = grad_att_all[owner_item].reshape(blocks, lat_rows, heads, head_size)
    factor_blk = jnp.exp(block_top - med_top[owner_item]) * factor_all[owner_item]
    delta_blk = delta_all[owner_item]
    grad_prob_med = jnp.einsum(
        "bqhd,bkhd->bhqk", grad_blk, value_med, preferred_element_type=jnp.float32
    )
    grad_score_med = (
        expo_med * factor_blk[..., None] * (grad_prob_med - delta_blk[..., None])
    ).astype(jnp.bfloat16)
    grad_query_blk = (
        jnp.einsum("bhqk,bkhd->bqhd", grad_score_med, key_med, preferred_element_type=jnp.float32)
        * score_scale
    )
    grad_query_part = jnp.einsum("bi,bqhd->iqhd", member, grad_query_blk, precision=HIGH).reshape(
        group_items, lat_rows, width
    )
    grad_key_med = (
        (
            jnp.einsum(
                "bhqk,bqhd->bkhd", grad_score_med, query_blk, preferred_element_type=jnp.float32
            )
            * score_scale
        )
        .astype(jnp.bfloat16)
        .reshape(-1, width)
    )
    grad_value_med = (
        jnp.einsum(
            "bhqk,bqhd->bkhd",
            expo_med_low.astype(jnp.float32) * factor_blk[..., None],
            grad_blk.astype(jnp.float32),
            precision=HIGH,
        )
        .astype(jnp.bfloat16)
        .reshape(-1, width)
    )
    grad_query_own = lax.psum_scatter(
        grad_query_part.astype(jnp.bfloat16), "seq", scatter_dimension=0, tiled=True
    ).astype(jnp.float32)
    grad_normed_med = matmul_right_t(grad_key_med, back_key) + matmul_right_t(
        grad_value_med, back_value
    )
    grad_key = matmul_left_t(normed_med, grad_key_med)
    grad_value = matmul_left_t(normed_med, grad_value_med)
    media_grad, grad_gain_media, grad_shift_media = norm_backward(
        grad_normed_med, scaled_med, inverse_med, med_gain
    )
    lat_factor = lat_weight * inverse_total
    grad_prob_lat = jnp.einsum(
        "iqhd,ikhd->ihqk", grad_att_heads, value_lat, preferred_element_type=jnp.float32
    )
    grad_score_lat = (expo_lat * lat_factor[..., None] * (grad_prob_lat - delta[..., None])).astype(
        jnp.bfloat16
    )
    grad_query_lat = (
        jnp.einsum("ihqk,ikhd->iqhd", grad_score_lat, key_lat, preferred_element_type=jnp.float32)
        * score_scale
    )
    grad_key_lat = (
        (
            jnp.einsum(
                "ihqk,iqhd->ikhd", grad_score_lat, query_lat, preferred_element_type=jnp.float32
            )
            * score_scale
        )
        .astype(jnp.bfloat16)
        .reshape(-1, width)
    )
    grad_value_lat = (
        jnp.einsum(
            "ihqk,iqhd->ikhd",
            expo_lat_low.astype(jnp.float32) * lat_factor[..., None],
            grad_att_heads.astype(jnp.float32),
            precision=HIGH,
        )
        .astype(jnp.bfloat16)
        .reshape(-1, width)
    )
    grad_query = (
        (grad_query_own + grad_query_lat.reshape(local_items, lat_rows, width))
        .astype(jnp.bfloat16)
        .reshape(-1, width)
    )
    grad_normed_lat = (
        matmul_right_t(grad_query, back_query)
        + matmul_right_t(grad_key_lat, back_key)
        + matmul_right_t(grad_value_lat, back_value)
    )
    grad_query_weight = matmul_left_t(normed_lat, grad_query)
    grad_key = grad_key + matmul_left_t(normed_lat, grad_key_lat)
    grad_value = grad_value + matmul_left_t(normed_lat, grad_value_lat)
    grad_lat_norm, grad_gain_lat, grad_shift_lat = norm_backward(
        grad_normed_lat, scaled_lat, inverse_lat, lat_gain
    )
    latents_grad = (grad_hidden + grad_lat_norm).reshape(latents.shape)
    sharded = (
        lax.psum_scatter(grad_query_weight, ("dp", "seq"), scatter_dimension=0, tiled=True),
        lax.psum_scatter(grad_key, ("dp", "seq"), scatter_dimension=0, tiled=True),
        lax.psum_scatter(grad_value, ("dp", "seq"), scatter_dimension=0, tiled=True),
        lax.psum_scatter(grad_out, ("dp", "seq"), scatter_dimension=0, tiled=True),
        lax.psum_scatter(grad_up, ("dp", "seq"), scatter_dimension=0, tiled=True),
        lax.psum_scatter(grad_down, ("dp", "seq"), scatter_dimension=0, tiled=True),
        lax.psum_scatter(grad_gain_lat, ("dp", "seq"), scatter_dimension=0, tiled=True),
        lax.psum_scatter(grad_shift_lat, ("dp", "seq"), scatter_dimension=0, tiled=True),
        lax.psum_scatter(grad_gain_media, ("dp", "seq"), scatter_dimension=0, tiled=True),
        lax.psum_scatter(grad_shift_media, ("dp", "seq"), scatter_dimension=0, tiled=True),
        lax.psum_scatter(grad_gain_ffn, ("dp", "seq"), scatter_dimension=0, tiled=True),
        lax.psum_scatter(grad_shift_ffn, ("dp", "seq"), scatter_dimension=0, tiled=True),
    )
    return (latents_out, latents_grad, media_grad.reshape(media.shape)) + tuple(sharded)


def solution(mesh):
    return jax.shard_map(
        local_fast if fits(mesh) else local,
        mesh=mesh,
        in_specs=(
            P(("dp", "seq"), None, None),
            P(("dp", "seq"), None, None),
            P(("dp", "seq"), None, None),
            P("dp", None),
            P("dp", None),
            P(("dp", "seq"), None),
            P(("dp", "seq"), None),
            P(("dp", "seq"), None),
            P(("dp", "seq"), None),
            P(("dp", "seq"), None),
            P(("dp", "seq"), None),
            P(("dp", "seq")),
            P(("dp", "seq")),
            P(("dp", "seq")),
            P(("dp", "seq")),
            P(("dp", "seq")),
            P(("dp", "seq")),
        ),
        out_specs=(
            P(("dp", "seq"), None, None),
            P(("dp", "seq"), None, None),
            P(("dp", "seq"), None, None),
            P(("dp", "seq"), None),
            P(("dp", "seq"), None),
            P(("dp", "seq"), None),
            P(("dp", "seq"), None),
            P(("dp", "seq"), None),
            P(("dp", "seq"), None),
            P(("dp", "seq")),
            P(("dp", "seq")),
            P(("dp", "seq")),
            P(("dp", "seq")),
            P(("dp", "seq")),
            P(("dp", "seq")),
        ),
        check_vma=False,
    )
```
